32 devices in a mesh: grp: 8 (over z, y), blk: 4 (over x, core).
Axes of the slice: x: 2, y: 2, z: 4, core: 2. Of those that a mesh axis runs over, the one named last changes fastest.
Arguments:
- dec_in: bfloat16 [20480, 768], P(('grp', 'blk')), may hold values from -6 to 6
- encodings: bfloat16 [16384, 768], P(('grp', 'blk')), may hold values from -6 to 6
- answer_len: int32 [1024], P(('grp', 'blk')), may hold values from 1 to 20
- answer_question: int32 [1024], P('grp'), may hold values from 0 to 3, as said below
- question_rows: int32 [8, 4], P('grp'), may hold values from 250 to 1048, as said below
- bucket_table: int32 [20], replicated, may hold values from 0 to 31, as said below
- gain_self: float32 [768], replicated, may hold values from 0.5 to 1.5
- w_qkv: bfloat16 [768, 2304], replicated, may hold values from -0.21875 to 0.21875
- w_self_out: bfloat16 [768, 768], replicated, may hold values from -0.4375 to 0.4375
- rel_bias: float32 [32, 12], replicated, may hold values from -4 to 4
- gain_cross: float32 [768], replicated, may hold values from 0.5 to 1.5
- w_cross_q: bfloat16 [768, 768], replicated, may hold values from -0.21875 to 0.21875
- w_cross_kv: bfloat16 [768, 1536], replicated, may hold values from -0.21875 to 0.21875
- w_cross_out: bfloat16 [768, 768], replicated, may hold values from -6 to 6
- gain_ffn: float32 [768], replicated, may hold values from 0.5 to 1.5
- w_in: bfloat16 [768, 3072], replicated, may hold values from -0.21875 to 0.21875
- w_out: bfloat16 [3072, 768], replicated, may hold values from -0.21875 to 0.21875
- cotangent: bfloat16 [20480, 768], P(('grp', 'blk')), may hold values from -6 to 6
Outputs:
- layer_out: bfloat16 [20480, 768], P(('grp', 'blk'))
- d_dec_in: float32 [20480, 768], P(('grp', 'blk'))
- d_encodings: float32 [16384, 768], P(('grp', 'blk'))
- d_gain_self: float32 [768], P('blk')
- d_w_qkv: float32 [768, 2304], P('blk')
- d_w_self_out: float32 [768, 768], P('blk')
- d_rel_bias: float32 [32, 12], P('blk')
- d_gain_cross: float32 [768], P('blk')
- d_w_cross_q: float32 [768, 768], P('blk')
- d_w_cross_kv: float32 [768, 1536], P('blk')
- d_w_cross_out: float32 [768, 768], P('blk')
- d_gain_ffn: float32 [768], P('blk')
- d_w_in: float32 [768, 3072], P('blk')
- d_w_out: float32 [3072, 768], P('blk')
The draws below stay inside these ranges and needn't reach their ends.
Inputs may be any that keep to these rules, and one draw needn't show every extreme that they name: `question_rows`: in each group, in an order drawn for that group, the 4 questions hold 4, 2, 1 and 1 times (1) whole passages of 250 rows, and the largest also holds the rows left over, so that they add up to 2048. `answer_question`: answers choose a question of their group with a chance proportional to its passages. `bucket_table`: entry 0 is 0, entries never fall as the distance grows, and the last entry is 31.
All inputs are finite; a program needn't handle non-finite values.
Results may differ from the reference program's by a relative error of at most 0.02.
Values may be sent and summed in bfloat16 or wider, within the bound.
A program may use at most 256 MiB of HBM per device.

```python
import math
import jax
import jax.numpy as jnp
from jax import lax

D = 768
H = 12
DH = 64
FF = 3072
NB = 32
ANS = 20
QG = 4
PASSAGE = 250
ANSW_DEV = 32
ENC_DEV = 512
ENC = 2048
ENC_ALL = 16384
ANSWERS = 1024
TOKENS = 20480
N_GRP = 8
N_BLK = 4


def group_units(key):
    group_count = ENC_ALL // ENC
    group_keys = jax.random.split(key, group_count)

    def one_group(group_key):
        scores = jax.random.randint(group_key, (QG,), 0, 1 << 20) * QG + jnp.arange(QG)
        order = jnp.argsort(scores)
        return jnp.array([4, 2, 1, 1], jnp.int32)[order]
    return jax.vmap(one_group)(group_keys)


def draw_question_rows(key, part):
    units = group_units(key)
    unit_rows = ENC // (8 * PASSAGE) * PASSAGE
    rows = units * unit_rows + jnp.where(units == 4, ENC - 8 * unit_rows, 0)
    return rows.astype(jnp.int32)


def draw_answer_question(key, part):
    units = group_units(key)
    key = jax.random.fold_in(key, 13)
    group_count = ENC_ALL // ENC
    per_group = ANSWERS // group_count
    unit_ends = jnp.cumsum(units, axis=1)
    picked = jax.random.randint(key, (group_count, per_group), 0, 8)
    chosen = jnp.sum((picked[:, :, None] >= unit_ends[:, None, :]).astype(jnp.int32), axis=2)
    return chosen.reshape(ANSWERS).astype(jnp.int32)


def draw_bucket_table(key, part):
    key = jax.random.fold_in(key, 7)
    increments = jax.random.randint(key, (ANS,), 0, 3)
    increments = jnp.where(jnp.arange(ANS) == 0, 0, increments)
    climbing = jnp.minimum(jnp.cumsum(increments), NB - 1)
    return jnp.where(jnp.arange(ANS) == ANS - 1, NB - 1, climbing).astype(jnp.int32)


def set_ends(values, own_key, least, top_value):
    longest = values.shape.index(max(values.shape))
    spots = []
    for shift in (0, 1):
        where = [jax.random.randint(jax.random.fold_in(own_key, axis), (), 0, length) for axis, length in enumerate(values.shape)]
        where[longest] = (where[longest] + shift) % values.shape[longest]
        spots.append(tuple(where))
    return values.at[spots[0]].set(least).at[spots[1]].set(top_value)


def steps_of(key, shape, shards, smallest, high):
    loudness = 1.0
    for dim, shards_of in shards:
        draws = jax.random.uniform(jax.random.fold_in(jax.random.fold_in(key, 6), dim), (shards_of,), jnp.float32, smallest / len(shards), high / len(shards))
        loudness = loudness * jnp.repeat(jnp.exp(draws), shape[dim] // shards_of).reshape((-1,) + (1,) * (len(shape) - 1 - dim))
    return loudness


def scatter_about(own_key, dims, width, bound, cuts=(), held_as=jnp.bfloat16):
    entries = jax.random.normal(own_key, dims, jnp.float32) * width
    if len(cuts) > 0:
        entries = steps_of(own_key, dims, cuts, -0.22, 0.18) * entries
    return jnp.clip(entries, min=-bound, max=bound).astype(held_as)


def setup_inputs(seed: int = 0) -> dict:
    keys = jax.random.split(jax.random.key(seed), 19)
    return {
        "dec_in": scatter_about(keys[0], (TOKENS, D), 1.0, 6.0, ((0, 32),)),
        "encodings": scatter_about(keys[1], (ENC_ALL, D), 1.0, 6.0, ((0, 32),)),
        "answer_len": set_ends(jax.random.randint(keys[2], (ANSWERS,), 1, ANS + 1), jax.random.fold_in(keys[2], 1), 1, ANS).astype(jnp.int32),
        "answer_question": draw_answer_question(jax.random.fold_in(keys[18], 71), 0),
        "question_rows": draw_question_rows(jax.random.fold_in(keys[18], 71), 0),
        "bucket_table": draw_bucket_table(jax.random.fold_in(keys[18], 71), 0),
        "gain_self": jnp.clip(1.0 + 0.1 * jax.random.normal(keys[6], (D,), jnp.float32), 0.5, 1.5),
        "w_qkv": scatter_about(keys[7], (D, 3 * D), D ** -0.5, 0.21875),
        "w_self_out": scatter_about(keys[8], (D, D), (D // 4) ** -0.5, 0.4375),
        "rel_bias": scatter_about(keys[9], (NB, H), 1.0, 4.0, (), jnp.float32),
        "gain_cross": jnp.clip(1.0 + 0.1 * jax.random.normal(keys[10], (D,), jnp.float32), 0.5, 1.5),
        "w_cross_q": scatter_about(keys[11], (D, D), D ** -0.5, 0.21875),
        "w_cross_kv": scatter_about(keys[12], (D, 2 * D), D ** -0.5, 0.21875),
        "w_cross_out": scatter_about(keys[13], (D, D), 1 ** -0.5, 6.0),
        "gain_ffn": jnp.clip(1.0 + 0.1 * jax.random.normal(keys[14], (D,), jnp.float32), 0.5, 1.5),
        "w_in": scatter_about(keys[15], (D, FF), D ** -0.5, 0.21875),
        "w_out": scatter_about(keys[16], (FF, D), (FF // 4) ** -0.5, 0.21875),
        "cotangent": scatter_about(keys[17], (TOKENS, D), 1.0, 6.0, ((0, 32),)),
    }


HIGHEST_PRECISION = lax.Precision.HIGHEST
EPSILON = 1e-06

@jax.custom_vjp
def low(v):
    return lax.optimization_barrier(v.astype(jnp.bfloat16)).astype(jnp.float32)

@jax.custom_vjp
def low_back(v):
    return v

def low_keep(v):
    return (low(v), None)

def low_pass(kept, grad):
    return (grad,)

def back_keep(v):
    return (v, None)

def back_low(kept, grad):
    return (low(grad),)
low.defvjp(low_keep, low_pass)
low_back.defvjp(back_keep, back_low)

def round_both(value):
    return low(low_back(value))

def matmul_high(left_arg, right_arg):
    return jnp.dot(left_arg, right_arg, precision=HIGHEST_PRECISION)

def norm_rows(rows_in, gain_vec):
    return rows_in * lax.rsqrt(lax.optimization_barrier(jnp.mean(rows_in * rows_in, axis=-1, keepdims=True)) + EPSILON) * gain_vec

def reference(dec_in, encodings, answer_len, answer_question, question_rows, bucket_table, gain_self, w_qkv, w_self_out, rel_bias, gain_cross, w_cross_q, w_cross_kv, w_cross_out, gain_ffn, w_in, w_out, cotangent):
    position = jnp.arange(ANS).astype(jnp.int32)
    distance = jnp.maximum(position[:, None] - position[None, :], 0)
    bucket_index = bucket_table[distance]
    self_valid = (position[None, :] <= position[:, None])[None] & (position[None, None, :] < answer_len[:, None, None])
    row_ends = jnp.cumsum(question_rows, axis=1).astype(jnp.int32)
    enc_index = jnp.arange(ENC_DEV * N_BLK).astype(jnp.int32)
    key_ids = lax.optimization_barrier(jnp.sum((enc_index[None, :, None] >= row_ends[:, None, :]).astype(jnp.int32), axis=2))
    token_ids = jnp.repeat(answer_question, ANS).reshape(N_GRP * N_BLK, ANSW_DEV * ANS)
    block_index = jnp.arange(N_GRP * N_BLK).astype(jnp.int32)
    score_scale = 1.0 / math.sqrt(DH)

    def forward(dec_x, enc_x, g_self, qkv_w, so_w, bias_w, g_cross, cq_w, ckv_w, co_w, g_ffn, in_w, out_w):
        normed_one = low(norm_rows(dec_x, g_self))
        projected = round_both(matmul_high(normed_one, qkv_w)).reshape(ANSWERS, ANS, 3, H, DH)
        self_q = projected[:, :, 0]
        self_k = projected[:, :, 1]
        self_v = projected[:, :, 2]
        raw_self = jnp.einsum('aihd,ajhd->ahij', self_q, self_k, precision=HIGHEST_PRECISION) * score_scale
        bias_full = jnp.transpose(bias_w[bucket_index], (2, 0, 1))
        self_scores = jnp.where(self_valid[:, None], raw_self + bias_full[None], -1000000000.0)
        self_prob = jax.nn.softmax(self_scores, axis=-1)
        self_out = jnp.einsum('ahij,ajhd->aihd', self_prob, self_v, precision=HIGHEST_PRECISION).reshape(TOKENS, D)
        mid_x = dec_x + low_back(matmul_high(round_both(self_out), so_w))
        normed_two = low(norm_rows(mid_x, g_cross))
        cross_q = round_both(matmul_high(normed_two, cq_w)).reshape(N_GRP * N_BLK, ANSW_DEV * ANS, H, DH)
        paired = round_both(matmul_high(enc_x, ckv_w)).reshape(N_GRP, ENC_DEV * N_BLK, 2, H, DH)

        def cross_block(block_item):
            query_block, id_block, which_block = block_item
            group_index = which_block // N_BLK
            key_block = paired[group_index, :, 0]
            value_block = paired[group_index, :, 1]
            raw_scores = low_back(jnp.einsum('ihd,jhd->hij', query_block, key_block, precision=HIGHEST_PRECISION) * score_scale)
            key_mask = id_block[:, None] == key_ids[group_index][None, :]
            cross_prob = low(jax.nn.softmax(jnp.where(key_mask[None], raw_scores, -1000000000.0), axis=-1))
            return jnp.einsum('hij,jhd->ihd', cross_prob, value_block, precision=HIGHEST_PRECISION)
        cross_out = lax.map(jax.checkpoint(cross_block), (cross_q, token_ids, block_index)).reshape(TOKENS, D)
        late_x = mid_x + low_back(matmul_high(round_both(cross_out), co_w))
        normed_three = low(norm_rows(late_x, g_ffn))
        hidden_pre = low_back(matmul_high(normed_three, in_w))
        hidden_act = low(jax.nn.gelu(hidden_pre))
        return late_x + matmul_high(hidden_act, out_w)
    result, pull_back = jax.vjp(forward, dec_in.astype(jnp.float32), encodings.astype(jnp.float32), gain_self, w_qkv.astype(jnp.float32), w_self_out.astype(jnp.float32), rel_bias, gain_cross, w_cross_q.astype(jnp.float32), w_cross_kv.astype(jnp.float32), w_cross_out.astype(jnp.float32), gain_ffn, w_in.astype(jnp.float32), w_out.astype(jnp.float32))
    grads = pull_back(cotangent.astype(jnp.float32))
    return (result.astype(jnp.bfloat16), grads[0], grads[1], grads[2], grads[3], grads[4], grads[5], grads[6], grads[7], grads[8], grads[9], grads[10], grads[11], grads[12])
```

```python
import functools
import math

import jax
import jax.numpy as jnp
from jax import lax
from jax.experimental import pallas as pl
from jax.experimental.pallas import tpu as pltpu
from jax.sharding import PartitionSpec as P

EPSILON = 1e-06
NEG = -1e30
MASKED = -1e9
TQ = 64
TK = 256
WIN = 128
F32 = jnp.float32
BF = jnp.bfloat16
VM = pl.BlockSpec(memory_space=pltpu.VMEM)
SM = pl.BlockSpec(memory_space=pltpu.SMEM)
LIMIT = 60 << 20


def dot(a, b):
    return jnp.dot(a, b, preferred_element_type=F32)


def dot_tn(a, b):
    return lax.dot_general(a, b, (((0,), (0,)), ((), ())), preferred_element_type=F32)


def dot_nt(a, b):
    return lax.dot_general(a, b, (((1,), (1,)), ((), ())), preferred_element_type=F32)


def stack4(t):
    lane = lax.broadcasted_iota(jnp.int32, t.shape, 1) // 64
    return jnp.concatenate([jnp.where(lane == a, t, jnp.zeros_like(t)) for a in range(4)], axis=0)


def unstack4(s):
    n = s.shape[0] // 4
    lane = lax.broadcasted_iota(jnp.int32, (n, 256), 1) // 64
    out = s[:n]
    for a in range(1, 4):
        out = jnp.where(lane == a, s[a * n : (a + 1) * n], out)
    return out


def range_mask(base, rows, start, size):
    idx = lax.broadcasted_iota(jnp.int32, (rows, start.shape[1]), 0)
    rel = idx - (start - base)
    return (rel >= 0) & (rel < size)


def red(x, op):
    return op(x.reshape(x.shape[0] // 8, 8, x.shape[1]), axis=0)


def cross_fwd_kernel(
    lo_ref, hi_ref, start_ref, size_ref, q_ref, k_ref, vt_ref, o_ref, lse_ref, qst, s_scr, m_scr, l_scr, acc, *, nq, tiles
):
    def tile(t, _):
        st = start_ref[t]
        sz = size_ref[t]
        lo = lo_ref[t]
        hi = hi_ref[t]
        row = pl.ds(pl.multiple_of(t * TQ, TQ), TQ)
        for c in range(nq):
            qst[c] = stack4(q_ref[row, c * 256 : (c + 1) * 256]).T
            m_scr[c] = jnp.full((8, 256), NEG, F32)
            l_scr[c] = jnp.zeros((8, 256), F32)
            acc[c] = jnp.zeros((256, 256), F32)

        def scores(j, _):
            kr = pl.ds(pl.multiple_of(j * TK, TK), TK)
            mask = range_mask(j * TK, TK, st, sz)
            for c in range(nq):
                s = dot(k_ref[kr, c * 256 : (c + 1) * 256], qst[c])
                s = jnp.where(mask, s, NEG)
                s_scr[c, kr, :] = s
                m_scr[c] = jnp.maximum(m_scr[c], red(s, jnp.max))
            return 0

        lax.fori_loop(lo, hi, scores, 0)
        for c in range(nq):
            m_scr[c] = jnp.broadcast_to(jnp.max(m_scr[c], axis=0, keepdims=True), (8, 256))

        def mix(j, _):
            kr = pl.ds(pl.multiple_of(j * TK, TK), TK)
            for c in range(nq):
                p = jnp.exp(s_scr[c, kr, :] - m_scr[c][0:1])
                l_scr[c] += red(p, jnp.sum)
                acc[c] += dot(vt_ref[c * 256 : (c + 1) * 256, kr], p.astype(BF))
            return 0

        lax.fori_loop(lo, hi, mix, 0)
        for c in range(nq):
            l = jnp.sum(l_scr[c], axis=0, keepdims=True)
            lse_ref[t, c] = m_scr[c][0:1] + jnp.log(l)
            o_ref[row, c * 256 : (c + 1) * 256] = unstack4((acc[c] * (1.0 / l)).T)
        return 0

    lax.fori_loop(0, tiles, tile, 0)


def quads_per_step(nq, keys):
    return nq if keys <= 2048 else 1


def cross_fwd(lo, hi, start, size, q, k, vt):
    rows, width = q.shape
    tiles, keys = rows // TQ, k.shape[0]
    nq = quads_per_step(width // 256, keys)
    full = pl.BlockSpec(start.shape, lambda g: (0, 0, 0))
    return pl.pallas_call(
        functools.partial(cross_fwd_kernel, nq=nq, tiles=tiles),
        grid=(width // 256 // nq,),
        out_shape=(
            jax.ShapeDtypeStruct(q.shape, F32),
            jax.ShapeDtypeStruct((tiles, width // 256, 1, 256), F32),
        ),
        in_specs=[
            SM,
            SM,
            full,
            full,
            pl.BlockSpec((rows, nq * 256), lambda g: (0, g)),
            pl.BlockSpec((keys, nq * 256), lambda g: (0, g)),
            pl.BlockSpec((nq * 256, keys), lambda g: (g, 0)),
        ],
        out_specs=(
            pl.BlockSpec((rows, nq * 256), lambda g: (0, g)),
            pl.BlockSpec((tiles, nq, 1, 256), lambda g: (0, g, 0, 0)),
        ),
        scratch_shapes=[
            pltpu.VMEM((nq, 256, 256), BF),
            pltpu.VMEM((nq, keys, 256), F32),
            pltpu.VMEM((nq, 8, 256), F32),
            pltpu.VMEM((nq, 8, 256), F32),
            pltpu.VMEM((nq, 256, 256), F32),
        ],
        compiler_params=pltpu.CompilerParams(vmem_limit_bytes=LIMIT),
        name="cross_fwd",
    )(lo, hi, start, size, q, k, vt)


def cross_bwd_kernel(
    lo_ref,
    hi_ref,
    start_ref,
    size_ref,
    q_ref,
    do_ref,
    o_ref,
    lse_ref,
    k_ref,
    v_ref,
    kt_ref,
    dq_ref,
    dk_ref,
    dv_ref,
    qs,
    qst,
    dos,
    dost,
    del_scr,
    dka,
    dva,
    dqt,
    *,
    nq,
    tiles,
    scale,
):
    dka[...] = jnp.zeros_like(dka)
    dva[...] = jnp.zeros_like(dva)

    def tile(t, _):
        st = start_ref[t]
        sz = size_ref[t]
        row = pl.ds(pl.multiple_of(t * TQ, TQ), TQ)
        for c in range(nq):
            cs = slice(c * 256, (c + 1) * 256)
            a = stack4(q_ref[row, cs])
            qs[c] = a
            qst[c] = a.T
            b = stack4(do_ref[row, cs])
            dos[c] = b
            dost[c] = b.T
            product = do_ref[row, cs].astype(F32) * o_ref[row, cs]
            total = jnp.sum(red(stack4(product).T, jnp.sum), axis=0, keepdims=True)
            del_scr[c] = jnp.broadcast_to(total, (8, 256))
            dqt[c] = jnp.zeros((256, 256), F32)

        def step(j, _):
            kr = pl.ds(pl.multiple_of(j * TK, TK), TK)
            mask = range_mask(j * TK, TK, st, sz)
            for c in range(nq):
                cs = slice(c * 256, (c + 1) * 256)
                s = dot(k_ref[kr, cs], qst[c])
                p = jnp.where(mask, jnp.exp(s - lse_ref[t, c]), 0.0)
                dp = dot(v_ref[kr, cs], dost[c])
                ds = (p * (dp - del_scr[c][0:1])).astype(BF)
                dva[kr, cs] += dot(p.astype(BF), dos[c])
                dka[kr, cs] += dot(ds, qs[c])
                dqt[c] += dot(kt_ref[cs, kr], ds)
            return 0

        lax.fori_loop(lo_ref[t], hi_ref[t], step, 0)
        for c in range(nq):
            cs = slice(c * 256, (c + 1) * 256)
            dq_ref[row, cs] = (unstack4(dqt[c].T) * scale).astype(BF)
        return 0

    lax.fori_loop(0, tiles, tile, 0)
    dk_ref[...] = dka[...].astype(BF)
    dv_ref[...] = dva[...].astype(BF)


def cross_bwd(lo, hi, start, size, q, do, o, lse, k, v, kt, scale):
    rows, width = q.shape
    tiles, keys = rows // TQ, k.shape[0]
    nq = quads_per_step(width // 256, keys)
    full = pl.BlockSpec(start.shape, lambda g: (0, 0, 0))
    own = pl.BlockSpec((rows, nq * 256), lambda g: (0, g))
    held = pl.BlockSpec((keys, nq * 256), lambda g: (0, g), pipeline_mode=pl.Buffered(1))
    out_kv = pl.BlockSpec((keys, nq * 256), lambda g: (0, g), pipeline_mode=pl.Buffered(1))
    return pl.pallas_call(
        functools.partial(cross_bwd_kernel, nq=nq, tiles=tiles, scale=scale),
        grid=(width // 256 // nq,),
        out_shape=(
            jax.ShapeDtypeStruct(q.shape, BF),
            jax.ShapeDtypeStruct(k.shape, BF),
            jax.ShapeDtypeStruct(k.shape, BF),
        ),
        in_specs=[
            SM,
            SM,
            full,
            full,
            own,
            own,
            own,
            pl.BlockSpec((tiles, nq, 1, 256), lambda g: (0, g, 0, 0)),
            held,
            held,
            pl.BlockSpec((nq * 256, keys), lambda g: (g, 0), pipeline_mode=pl.Buffered(1)),
        ],
        out_specs=(own, out_kv, out_kv),
        scratch_shapes=[pltpu.VMEM((nq, 256, 256), BF)] * 4
        + [
            pltpu.VMEM((nq, 8, 256), F32),
            pltpu.VMEM((keys, nq * 256), F32),
            pltpu.VMEM((keys, nq * 256), F32),
            pltpu.VMEM((nq, 256, 256), F32),
        ],
        compiler_params=pltpu.CompilerParams(vmem_limit_bytes=LIMIT),
        name="cross_bwd",
    )(lo, hi, start, size, q, do, o, lse, k, v, kt)


def distances():
    j = lax.broadcasted_iota(jnp.int32, (WIN, 256), 0)
    i = lax.broadcasted_iota(jnp.int32, (WIN, 256), 1) % 64
    return WIN - TQ + i - j


def fill_window(proj_ref, kp, vp, width):
    kp[0:64, :] = jnp.zeros((64, width), BF)
    vp[0:64, :] = jnp.zeros((64, width), BF)
    kp[64:, :] = proj_ref[:, width : 2 * width]
    vp[64:, :] = proj_ref[:, 2 * width : 3 * width]


def fill_bias(brow_ref, bias, nq):
    dist = distances()
    for c in range(nq):
        cs = slice(c * 256, (c + 1) * 256)

        def add(d, held):
            return jnp.where(dist == d, brow_ref[pl.ds(d, 1), cs], held)

        bias[c] = lax.fori_loop(0, brow_ref.shape[0], add, jnp.full((WIN, 256), MASKED, F32))


def self_fwd_kernel(start_ref, size_ref, brow_ref, proj_ref, o_ref, lse_ref, kp, vp, bias, *, nq, tiles, scale):
    width = nq * 256
    fill_window(proj_ref, kp, vp, width)
    fill_bias(brow_ref, bias, nq)

    def tile(t, _):
        row = pl.ds(pl.multiple_of(t * TQ, TQ), TQ)
        win = pl.ds(pl.multiple_of(t * TQ, TQ), WIN)
        mask = range_mask(t * TQ - 64, WIN, start_ref[t], size_ref[t])
        for c in range(nq):
            cs = slice(c * 256, (c + 1) * 256)
            qst = stack4(proj_ref[row, cs] * jnp.asarray(scale, BF)).T
            s = jnp.where(mask, dot(kp[win, cs], qst) + bias[c], MASKED)
            m = jnp.max(red(s, jnp.max), axis=0, keepdims=True)
            p = jnp.exp(s - m)
            l = jnp.sum(red(p, jnp.sum), axis=0, keepdims=True)
            p = (p * (1.0 / l)).astype(BF)
            o_ref[row, cs] = unstack4(dot_tn(p, vp[win, cs])).astype(BF)
            lse_ref[t, c] = m + jnp.log(l)
        return 0

    lax.fori_loop(0, tiles, tile, 0)


def self_fwd(start, size, brow, proj, scale):
    rows, width = proj.shape[0], proj.shape[1] // 3
    nq, tiles = width // 256, rows // TQ
    return pl.pallas_call(
        functools.partial(self_fwd_kernel, nq=nq, tiles=tiles, scale=scale),
        out_shape=(
            jax.ShapeDtypeStruct((rows, width), BF),
            jax.ShapeDtypeStruct((tiles, nq, 1, 256), F32),
        ),
        in_specs=[VM] * 4,
        out_specs=(VM, VM),
        scratch_shapes=[
            pltpu.VMEM((rows + 64, width), BF),
            pltpu.VMEM((rows + 64, width), BF),
            pltpu.VMEM((nq, WIN, 256), F32),
        ],
        compiler_params=pltpu.CompilerParams(vmem_limit_bytes=LIMIT),
        name="self_fwd",
    )(start, size, brow, proj)


def self_bwd_kernel(
    start_ref,
    size_ref,
    brow_ref,
    proj_ref,
    do_ref,
    lse_ref,
    dproj_ref,
    dbrow_ref,
    kp,
    vp,
    bias,
    dka,
    dva,
    dsum,
    *,
    nq,
    tiles,
    scale,
):
    width = nq * 256
    fill_window(proj_ref, kp, vp, width)
    fill_bias(brow_ref, bias, nq)
    dka[...] = jnp.zeros_like(dka)
    dva[...] = jnp.zeros_like(dva)
    dsum[...] = jnp.zeros_like(dsum)

    def tile(t, _):
        row = pl.ds(pl.multiple_of(t * TQ, TQ), TQ)
        win = pl.ds(pl.multiple_of(t * TQ, TQ), WIN)
        mask = range_mask(t * TQ - 64, WIN, start_ref[t], size_ref[t])
        for c in range(nq):
            cs = slice(c * 256, (c + 1) * 256)
            qs = stack4(proj_ref[row, cs] * jnp.asarray(scale, BF))
            dos = stack4(do_ref[row, cs])
            s = dot(kp[win, cs], qs.T) + bias[c]
            p = jnp.where(mask, jnp.exp(s - lse_ref[t, c]), 0.0)
            dp = dot(vp[win, cs], dos.T)
            delta = jnp.sum(red(p * dp, jnp.sum), axis=0, keepdims=True)
            ds = p * (dp - delta)
            dsum[c] += ds
            ds = ds.astype(BF)
            dva[win, cs] += dot(p.astype(BF), dos)
            dka[win, cs] += dot(ds, qs)
            dproj_ref[row, cs] = (unstack4(dot_tn(ds, kp[win, cs])) * scale).astype(BF)
        return 0

    lax.fori_loop(0, tiles, tile, 0)
    dproj_ref[:, width : 2 * width] = dka[64:, :].astype(BF)
    dproj_ref[:, 2 * width : 3 * width] = dva[64:, :].astype(BF)
    dist = distances()
    for c in range(nq):
        cs = slice(c * 256, (c + 1) * 256)

        def one(d, _):
            x = jnp.where(dist == d, dsum[c], 0.0)
            dbrow_ref[pl.ds(d, 1), cs] = jnp.sum(red(x, jnp.sum), axis=0, keepdims=True)
            return 0

        lax.fori_loop(0, brow_ref.shape[0], one, 0)


def self_bwd(start, size, brow, proj, do, lse, scale):
    rows, width = proj.shape[0], proj.shape[1] // 3
    nq, tiles = width // 256, rows // TQ
    return pl.pallas_call(
        functools.partial(self_bwd_kernel, nq=nq, tiles=tiles, scale=scale),
        out_shape=(jax.ShapeDtypeStruct((rows, 3 * width), BF), jax.ShapeDtypeStruct(brow.shape, F32)),
        in_specs=[VM] * 6,
        out_specs=(VM, VM),
        scratch_shapes=[
            pltpu.VMEM((rows + 64, width), BF),
            pltpu.VMEM((rows + 64, width), BF),
            pltpu.VMEM((nq, WIN, 256), F32),
            pltpu.VMEM((rows + 64, width), F32),
            pltpu.VMEM((rows + 64, width), F32),
            pltpu.VMEM((nq, WIN, 256), F32),
        ],
        compiler_params=pltpu.CompilerParams(vmem_limit_bytes=LIMIT),
        name="self_bwd",
    )(start, size, brow, proj, do, lse)


def norm_rows(x, gain):
    inverse = lax.rsqrt(jnp.mean(x * x, axis=-1, keepdims=True) + EPSILON)
    return x * inverse * gain, inverse


def norm_back(x, inverse, gain, grad):
    scaled = grad * gain
    mean = jnp.mean(x * scaled, axis=-1, keepdims=True)
    return inverse * scaled - x * inverse * inverse * inverse * mean, jnp.sum(grad * x * inverse, axis=0)


def swap(x, axis, bit):
    size = lax.axis_size(axis)
    return lax.ppermute(x, axis, [(i, i ^ bit) for i in range(size)])


def bits_of(axis):
    size = lax.axis_size(axis)
    return [1 << b for b in range(size.bit_length() - 1)]


def gather_parts(x, axis):
    parts = {0: x}
    for bit in reversed(bits_of(axis)):
        for r in list(parts):
            parts[r ^ bit] = swap(parts[r], axis, bit)
    return parts


def add_low(a, b):
    return (a.astype(F32) + b.astype(F32)).astype(BF)


def scatter_sum(x, axis, order):
    size = x.shape[0]
    live = list(range(size))
    block = x
    for bit in order:
        keep = [r for r in live if not r & bit]
        send = [r for r in live if r & bit]
        k = jnp.stack([block[live.index(r)] for r in keep])
        s = jnp.stack([block[live.index(r)] for r in send])
        block = add_low(k, swap(s, axis, bit))
        live = keep
    return block[0]


def gather_sum(x, axis, order):
    parts = [0]
    block = x[None]
    for bit in order:
        block = jnp.concatenate([block, swap(block, axis, bit)], axis=0)
        parts = parts + [r ^ bit for r in parts]
    inverse = [parts.index(r) for r in range(len(parts))]
    return block, inverse


def relative(x, axis):
    size = lax.axis_size(axis)
    me = lax.axis_index(axis)
    return jnp.stack([lax.dynamic_index_in_dim(x, me ^ r, 0, keepdims=False) for r in range(size)])


def reduce_all(x):
    blocks, rows, width = x.shape
    groups = lax.axis_size("grp")
    part = scatter_sum(relative(x, "blk"), "blk", bits_of("blk"))
    part = relative(part.reshape(groups, rows // groups, width), "grp")
    part = scatter_sum(part, "grp", bits_of("grp"))
    whole, inverse = gather_sum(part, "grp", list(reversed(bits_of("grp"))))
    me = lax.axis_index("grp")
    index = jnp.asarray(inverse, jnp.int32)[jnp.arange(groups) ^ me]
    return jnp.take(whole, index, axis=0).reshape(rows, width)


def sum_everywhere(x):
    for axis in ("blk", "grp"):
        for bit in bits_of(axis):
            x = x + swap(x, axis, bit)
    return x


def pack(grads, blocks):
    out = []
    for g in grads:
        k, n = g.shape
        r = g.reshape(blocks, k // blocks, n // 768, 768).transpose(0, 2, 1, 3)
        out.append(r.reshape(blocks, -1, 768))
    return jnp.concatenate(out, axis=1)


def unpack(rows, shapes, blocks):
    out, at = [], 0
    for k, n in shapes:
        count = k // blocks * (n // 768)
        piece = rows[at : at + count].reshape(n // 768, k // blocks, 768)
        out.append(piece.transpose(1, 0, 2).reshape(k // blocks, n).astype(F32))
        at += count
    return out


def body(
    dec_in,
    encodings,
    answer_len,
    answer_question,
    question_rows,
    bucket_table,
    gain_self,
    w_qkv,
    w_self_out,
    rel_bias,
    gain_cross,
    w_cross_q,
    w_cross_kv,
    w_cross_out,
    gain_ffn,
    w_in,
    w_out,
    cotangent,
):
    answers = answer_len.shape[0]
    length = bucket_table.shape[0]
    rows, width = dec_in.shape
    heads = rel_bias.shape[1]
    buckets = rel_bias.shape[0]
    scale = 1.0 / math.sqrt(width // heads)
    enc_rows = encodings.shape[0]
    blocks = lax.axis_size("blk")
    me = lax.axis_index("blk")
    tiles = rows // TQ
    nq = width // 256

    enc_parts = gather_parts(encodings, "blk")

    own_q = lax.dynamic_slice_in_dim(answer_question, me * answers, answers, 0)
    a_index = jnp.arange(answers)
    before = (own_q[None, :] < own_q[:, None]) | (
        (own_q[None, :] == own_q[:, None]) & (a_index[None, :] < a_index[:, None])
    )
    rank = jnp.sum(before.astype(jnp.int32), axis=1)
    target = (rank[:, None] * length + jnp.arange(length)[None, :]).reshape(rows)
    forward_perm = (jnp.arange(rows)[:, None] == target[None, :]).astype(BF)
    sorted_len = jnp.sum(jnp.where(rank[:, None] == a_index[None, :], answer_len[:, None], 0), axis=0)
    ends_q = jnp.cumsum(question_rows[0])
    starts_q = ends_q - question_rows[0]
    sorted_q = jnp.sum(jnp.where(rank[:, None] == a_index[None, :], own_q[:, None], 0), axis=0)
    token_q = jnp.repeat(sorted_q, length)
    pick = token_q[:, None] == jnp.arange(question_rows.shape[1])[None, :]
    token_start = jnp.sum(jnp.where(pick, starts_q[None, :], 0), axis=1)
    token_size = jnp.sum(jnp.where(pick, question_rows[0][None, :], 0), axis=1)

    def stacked(v):
        return jnp.tile(v.reshape(tiles, 1, TQ), (1, 1, 4)).astype(jnp.int32)

    c_start, c_size = stacked(token_start), stacked(token_size)
    lo = (token_start.reshape(tiles, TQ)[:, 0] // TK).astype(jnp.int32)
    hi = ((token_start + token_size).reshape(tiles, TQ)[:, -1] + TK - 1) // TK
    hi = hi.astype(jnp.int32)
    s_start = stacked(jnp.arange(rows) // length * length)
    s_size = stacked(jnp.repeat(sorted_len, length))

    bucket_hot = (bucket_table[:, None] == jnp.arange(buckets)[None, :]).astype(F32)
    brow = jnp.repeat(
        jnp.dot(bucket_hot, rel_bias, precision=lax.Precision.HIGHEST), width // heads, axis=1
    )

    x0 = dot(forward_perm, dec_in)
    grad_top = dot(forward_perm, cotangent)
    grad_low = grad_top.astype(BF)
    n1, r1 = norm_rows(x0, gain_self)
    h1 = n1.astype(BF)
    proj = dot(h1, w_qkv).astype(BF)
    o_self, lse_self = self_fwd(s_start, s_size, brow, proj, scale)
    x1 = x0 + dot(o_self, w_self_out)
    n2, r2 = norm_rows(x1, gain_cross)
    h2 = n2.astype(BF)
    qc = (dot(h2, w_cross_q).astype(BF) * jnp.asarray(scale, BF)).astype(BF)

    enc_rel = jnp.stack([enc_parts[r] for r in range(blocks)])
    enc_all = relative(enc_rel, "blk").reshape(blocks * enc_rows, width)
    kv = dot(enc_all, w_cross_kv).astype(BF)
    k_all, v_all = kv[:, :width], kv[:, width:]
    kvt = lax.dot_general(w_cross_kv, enc_all, (((0,), (1,)), ((), ())), preferred_element_type=F32).astype(BF)
    kt_all, vt_all = kvt[:width], kvt[width:]

    o_cross, lse_cross = cross_fwd(lo, hi, c_start, c_size, qc, k_all, vt_all)
    oc = o_cross.astype(BF)
    x2 = x1 + dot(oc, w_cross_out)
    n3, r3 = norm_rows(x2, gain_ffn)
    h3 = n3.astype(BF)
    hidden, gelu_back = jax.vjp(jax.nn.gelu, dot(h3, w_in))
    u = hidden.astype(BF)
    out = (x2 + dot(u, w_out)).astype(BF)
    layer_out = dot_tn(forward_perm, out).astype(BF)

    d_w_out = dot_tn(u, grad_low).astype(BF)
    da = gelu_back(dot_nt(grad_low, w_out))[0].astype(BF)
    d_w_in = dot_tn(h3, da).astype(BF)
    sums_out = reduce_all(pack([d_w_out], blocks))
    sums_in = reduce_all(pack([d_w_in], blocks))
    dx3, d_gain_ffn = norm_back(x2, r3, gain_ffn, dot_nt(da, w_in))
    dx2 = grad_top + dx3
    dyc = dx2.astype(BF)
    d_w_cross_out = dot_tn(oc, dyc).astype(BF)
    d_o = dot_nt(dyc, w_cross_out).astype(BF)
    dqc, dk, dv = cross_bwd(
        lo, hi, c_start, c_size, qc, d_o, o_cross, lse_cross, k_all, v_all, kt_all, scale
    )

    dkv = jnp.concatenate([dk, dv], axis=1).reshape(blocks, enc_rows, 2 * width)
    dkv = relative(dkv, "blk")
    dkv = add_low(dkv[0::2], swap(dkv[1::2], "blk", 1))
    enc_half = enc_rel[0::2]
    dkv_flat = dkv.reshape(-1, 2 * width)
    d_w_cross_kv = dot_tn(enc_half.reshape(-1, width), dkv_flat).astype(BF)
    d_enc = dot_nt(dkv_flat, w_cross_kv).reshape(blocks // 2, enc_rows, width)
    d_enc_parts = {2 * r: d_enc[r] for r in range(blocks // 2)}
    for bit in reversed(bits_of("blk")[1:]):
        for r in [r for r in d_enc_parts if r & bit]:
            came = swap(d_enc_parts.pop(r).astype(BF), "blk", bit)
            d_enc_parts[r ^ bit] = d_enc_parts[r ^ bit] + came.astype(F32)
    d_encodings = d_enc_parts[0]

    d_w_cross_q = dot_tn(h2, dqc).astype(BF)
    sums_cross = reduce_all(pack([d_w_cross_out, d_w_cross_q, d_w_cross_kv], blocks))
    dx_two, d_gain_cross = norm_back(x1, r2, gain_cross, dot_nt(dqc, w_cross_q))
    dx1 = dx2 + dx_two
    dy1 = dx1.astype(BF)
    d_w_self_out = dot_tn(o_self, dy1).astype(BF)
    d_os = dot_nt(dy1, w_self_out).astype(BF)
    dproj, dbrow = self_bwd(s_start, s_size, brow, proj, d_os, lse_self, scale)
    d_w_qkv = dot_tn(h1, dproj).astype(BF)
    sums_self = reduce_all(pack([d_w_qkv, d_w_self_out], blocks))
    dx_one, d_gain_self = norm_back(x0, r1, gain_self, dot_nt(dproj, w_qkv))
    d_rel = jnp.dot(
        bucket_hot.T, jnp.sum(dbrow.reshape(length, heads, -1), axis=2), precision=lax.Precision.HIGHEST
    )
    d_x0 = dx1 + dx_one
    high = d_x0.astype(BF)
    low = (d_x0 - high.astype(F32)).astype(BF)
    d_dec_in = dot_tn(forward_perm, high) + dot_tn(forward_perm, low)

    small = jnp.concatenate([d_gain_self, d_gain_cross, d_gain_ffn, d_rel.reshape(-1)])
    small = sum_everywhere(small.reshape(-1, 128)).reshape(-1)

    def own(v):
        return lax.dynamic_slice_in_dim(v, me * (v.shape[0] // blocks), v.shape[0] // blocks, 0)

    g_self, g_cross, g_ffn = (own(small[i * width : (i + 1) * width]) for i in range(3))
    g_rel = own(small[3 * width :].reshape(buckets, heads))
    (o_wout,) = unpack(sums_out, [w_out.shape], blocks)
    (o_win,) = unpack(sums_in, [w_in.shape], blocks)
    o_wco, o_wcq, o_wckv = unpack(sums_cross, [w_cross_out.shape, w_cross_q.shape, w_cross_kv.shape], blocks)
    o_wqkv, o_wso = unpack(sums_self, [w_qkv.shape, w_self_out.shape], blocks)
    return (
        layer_out,
        d_dec_in,
        d_encodings,
        g_self,
        o_wqkv,
        o_wso,
        g_rel,
        g_cross,
        o_wcq,
        o_wckv,
        o_wco,
        g_ffn,
        o_win,
        o_wout,
    )


def solution(mesh):
    rows = P(("grp", "blk"), None)
    return jax.shard_map(
        body,
        mesh=mesh,
        in_specs=(rows, rows, P(("grp", "blk")), P("grp"), P("grp", None)) + (P(),) * 12 + (rows,),
        out_specs=(rows, rows, rows, P("blk"))
        + (P("blk", None),) * 3
        + (P("blk"),)
        + (P("blk", None),) * 3
        + (P("blk"),)
        + (P("blk", None),) * 2,
        check_vma=False,
    )
```

```python
import functools
import math

import jax
import jax.numpy as jnp
from jax import lax
from jax.experimental import pallas as pl
from jax.experimental.pallas import tpu as pltpu
from jax.sharding import PartitionSpec as P

EPSILON = 1e-06
NEG = -1e30
MASKED = -1e9
TQ = 64
TK = 256
WIN = 128
F32 = jnp.float32
BF = jnp.bfloat16
VM = pl.BlockSpec(memory_space=pltpu.VMEM)
SM = pl.BlockSpec(memory_space=pltpu.SMEM)
LIMIT = 60 << 20


def dot(a, b):
    return jnp.dot(a, b, preferred_element_type=F32)


def dot_tn(a, b):
    return lax.dot_general(a, b, (((0,), (0,)), ((), ())), preferred_element_type=F32)


def dot_nt(a, b):
    return lax.dot_general(a, b, (((1,), (1,)), ((), ())), preferred_element_type=F32)


def stack4(t):
    lane = lax.broadcasted_iota(jnp.int32, t.shape, 1) // 64
    return jnp.concatenate([jnp.where(lane == a, t, jnp.zeros_like(t)) for a in range(4)], axis=0)


def unstack4(s):
    n = s.shape[0] // 4
    lane = lax.broadcasted_iota(jnp.int32, (n, 256), 1) // 64
    out = s[:n]
    for a in range(1, 4):
        out = jnp.where(lane == a, s[a * n : (a + 1) * n], out)
    return out


def range_mask(base, rows, start, size):
    idx = lax.broadcasted_iota(jnp.int32, (rows, start.shape[1]), 0)
    rel = idx - (start - base)
    return (rel >= 0) & (rel < size)


def red(x, op):
    return op(x.reshape(x.shape[0] // 8, 8, x.shape[1]), axis=0)


def cross_fwd_kernel(
    lo_ref, hi_ref, start_ref, size_ref, q_ref, k_ref, vt_ref, o_ref, lse_ref, qst, s_scr, m_scr, l_scr, acc, *, nq, tiles
):
    def tile(t, _):
        st = start_ref[t]
        sz = size_ref[t]
        lo = lo_ref[t]
        hi = hi_ref[t]
        row = pl.ds(pl.multiple_of(t * TQ, TQ), TQ)
        for c in range(nq):
            qst[c] = stack4(q_ref[row, c * 256 : (c + 1) * 256]).T
            m_scr[c] = jnp.full((8, 256), NEG, F32)
            l_scr[c] = jnp.zeros((8, 256), F32)
            acc[c] = jnp.zeros((256, 256), F32)

        def scores(j, _):
            kr = pl.ds(pl.multiple_of(j * TK, TK), TK)
            mask = range_mask(j * TK, TK, st, sz)
            for c in range(nq):
                s = dot(k_ref[kr, c * 256 : (c + 1) * 256], qst[c])
                s = jnp.where(mask, s, NEG)
                s_scr[c, kr, :] = s
                m_scr[c] = jnp.maximum(m_scr[c], red(s, jnp.max))
            return 0

        lax.fori_loop(lo, hi, scores, 0)
        for c in range(nq):
            m_scr[c] = jnp.broadcast_to(jnp.max(m_scr[c], axis=0, keepdims=True), (8, 256))

        def mix(j, _):
            kr = pl.ds(pl.multiple_of(j * TK, TK), TK)
            for c in range(nq):
                p = jnp.exp(s_scr[c, kr, :] - m_scr[c][0:1])
                l_scr[c] += red(p, jnp.sum)
                acc[c] += dot(vt_ref[c * 256 : (c + 1) * 256, kr], p.astype(BF))
            return 0

        lax.fori_loop(lo, hi, mix, 0)
        for c in range(nq):
            l = jnp.sum(l_scr[c], axis=0, keepdims=True)
            lse_ref[t, c] = m_scr[c][0:1] + jnp.log(l)
            o_ref[row, c * 256 : (c + 1) * 256] = unstack4((acc[c] * (1.0 / l)).T)
        return 0

    lax.fori_loop(0, tiles, tile, 0)


def quads_per_step(nq, keys):
    return nq if keys <= 2048 else 1


def cross_fwd(lo, hi, start, size, q, k, vt):
    rows, width = q.shape
    tiles, keys = rows // TQ, k.shape[0]
    nq = quads_per_step(width // 256, keys)
    full = pl.BlockSpec(start.shape, lambda g: (0, 0, 0))
    return pl.pallas_call(
        functools.partial(cross_fwd_kernel, nq=nq, tiles=tiles),
        grid=(width // 256 // nq,),
        out_shape=(
            jax.ShapeDtypeStruct(q.shape, F32),
            jax.ShapeDtypeStruct((tiles, width // 256, 1, 256), F32),
        ),
        in_specs=[
            SM,
            SM,
            full,
            full,
            pl.BlockSpec((rows, nq * 256), lambda g: (0, g)),
            pl.BlockSpec((keys, nq * 256), lambda g: (0, g)),
            pl.BlockSpec((nq * 256, keys), lambda g: (g, 0)),
        ],
        out_specs=(
            pl.BlockSpec((rows, nq * 256), lambda g: (0, g)),
            pl.BlockSpec((tiles, nq, 1, 256), lambda g: (0, g, 0, 0)),
        ),
        scratch_shapes=[
            pltpu.VMEM((nq, 256, 256), BF),
            pltpu.VMEM((nq, keys, 256), F32),
            pltpu.VMEM((nq, 8, 256), F32),
            pltpu.VMEM((nq, 8, 256), F32),
            pltpu.VMEM((nq, 256, 256), F32),
        ],
        compiler_params=pltpu.CompilerParams(vmem_limit_bytes=LIMIT),
        name="cross_fwd",
    )(lo, hi, start, size, q, k, vt)


def cross_bwd_kernel(
    lo_ref,
    hi_ref,
    start_ref,
    size_ref,
    q_ref,
    do_ref,
    o_ref,
    lse_ref,
    k_ref,
    v_ref,
    kt_ref,
    dq_ref,
    dk_ref,
    dv_ref,
    qs,
    qst,
    dos,
    dost,
    del_scr,
    dka,
    dva,
    dqt,
    *,
    nq,
    tiles,
    scale,
):
    dka[...] = jnp.zeros_like(dka)
    dva[...] = jnp.zeros_like(dva)

    def tile(t, _):
        st = start_ref[t]
        sz = size_ref[t]
        row = pl.ds(pl.multiple_of(t * TQ, TQ), TQ)
        for c in range(nq):
            cs = slice(c * 256, (c + 1) * 256)
            a = stack4(q_ref[row, cs])
            qs[c] = a
            qst[c] = a.T
            b = stack4(do_ref[row, cs])
            dos[c] = b
            dost[c] = b.T
            product = do_ref[row, cs].astype(F32) * o_ref[row, cs]
            total = jnp.sum(red(stack4(product).T, jnp.sum), axis=0, keepdims=True)
            del_scr[c] = jnp.broadcast_to(total, (8, 256))
            dqt[c] = jnp.zeros((256, 256), F32)

        def step(j, _):
            kr = pl.ds(pl.multiple_of(j * TK, TK), TK)
            mask = range_mask(j * TK, TK, st, sz)
            for c in range(nq):
                cs = slice(c * 256, (c + 1) * 256)
                s = dot(k_ref[kr, cs], qst[c])
                p = jnp.where(mask, jnp.exp(s - lse_ref[t, c]), 0.0)
                dp = dot(v_ref[kr, cs], dost[c])
                ds = (p * (dp - del_scr[c][0:1])).astype(BF)
                dva[kr, cs] += dot(p.astype(BF), dos[c])
                dka[kr, cs] += dot(ds, qs[c])
                dqt[c] += dot(kt_ref[cs, kr], ds)
            return 0

        lax.fori_loop(lo_ref[t], hi_ref[t], step, 0)
        for c in range(nq):
            cs = slice(c * 256, (c + 1) * 256)
            dq_ref[row, cs] = (unstack4(dqt[c].T) * scale).astype(BF)
        return 0

    lax.fori_loop(0, tiles, tile, 0)
    dk_ref[...] = dka[...].astype(BF)
    dv_ref[...] = dva[...].astype(BF)


def cross_bwd(lo, hi, start, size, q, do, o, lse, k, v, kt, scale):
    rows, width = q.shape
    tiles, keys = rows // TQ, k.shape[0]
    nq = quads_per_step(width // 256, keys)
    full = pl.BlockSpec(start.shape, lambda g: (0, 0, 0))
    own = pl.BlockSpec((rows, nq * 256), lambda g: (0, g))
    held = pl.BlockSpec((keys, nq * 256), lambda g: (0, g), pipeline_mode=pl.Buffered(1))
    out_kv = pl.BlockSpec((keys, nq * 256), lambda g: (0, g), pipeline_mode=pl.Buffered(1))
    return pl.pallas_call(
        functools.partial(cross_bwd_kernel, nq=nq, tiles=tiles, scale=scale),
        grid=(width // 256 // nq,),
        out_shape=(
            jax.ShapeDtypeStruct(q.shape, BF),
            jax.ShapeDtypeStruct(k.shape, BF),
            jax.ShapeDtypeStruct(k.shape, BF),
        ),
        in_specs=[
            SM,
            SM,
            full,
            full,
            own,
            own,
            own,
            pl.BlockSpec((tiles, nq, 1, 256), lambda g: (0, g, 0, 0)),
            held,
            held,
            pl.BlockSpec((nq * 256, keys), lambda g: (g, 0), pipeline_mode=pl.Buffered(1)),
        ],
        out_specs=(own, out_kv, out_kv),
        scratch_shapes=[pltpu.VMEM((nq, 256, 256), BF)] * 4
        + [
            pltpu.VMEM((nq, 8, 256), F32),
            pltpu.VMEM((keys, nq * 256), F32),
            pltpu.VMEM((keys, nq * 256), F32),
            pltpu.VMEM((nq, 256, 256), F32),
        ],
        compiler_params=pltpu.CompilerParams(vmem_limit_bytes=LIMIT),
        name="cross_bwd",
    )(lo, hi, start, size, q, do, o, lse, k, v, kt)


def distances():
    j = lax.broadcasted_iota(jnp.int32, (WIN, 256), 0)
    i = lax.broadcasted_iota(jnp.int32, (WIN, 256), 1) % 64
    return WIN - TQ + i - j


def fill_window(proj_ref, kp, vp, width):
    kp[0:64, :] = jnp.zeros((64, width), BF)
    vp[0:64, :] = jnp.zeros((64, width), BF)
    kp[64:, :] = proj_ref[:, width : 2 * width]
    vp[64:, :] = proj_ref[:, 2 * width : 3 * width]


def fill_bias(brow_ref, bias, nq):
    dist = distances()
    for c in range(nq):
        cs = slice(c * 256, (c + 1) * 256)

        def add(d, held):
            return jnp.where(dist == d, brow_ref[pl.ds(d, 1), cs], held)

        bias[c] = lax.fori_loop(0, brow_ref.shape[0], add, jnp.full((WIN, 256), MASKED, F32))


def self_fwd_kernel(start_ref, size_ref, brow_ref, proj_ref, o_ref, lse_ref, kp, vp, bias, *, nq, tiles, scale):
    width = nq * 256
    fill_window(proj_ref, kp, vp, width)
    fill_bias(brow_ref, bias, nq)

    def tile(t, _):
        row = pl.ds(pl.multiple_of(t * TQ, TQ), TQ)
        win = pl.ds(pl.multiple_of(t * TQ, TQ), WIN)
        mask = range_mask(t * TQ - 64, WIN, start_ref[t], size_ref[t])
        for c in range(nq):
            cs = slice(c * 256, (c + 1) * 256)
            qst = stack4(proj_ref[row, cs] * jnp.asarray(scale, BF)).T
            s = jnp.where(mask, dot(kp[win, cs], qst) + bias[c], MASKED)
            m = jnp.max(red(s, jnp.max), axis=0, keepdims=True)
            p = jnp.exp(s - m)
            l = jnp.sum(red(p, jnp.sum), axis=0, keepdims=True)
            p = (p * (1.0 / l)).astype(BF)
            o_ref[row, cs] = unstack4(dot_tn(p, vp[win, cs])).astype(BF)
            lse_ref[t, c] = m + jnp.log(l)
        return 0

    lax.fori_loop(0, tiles, tile, 0)


def self_fwd(start, size, brow, proj, scale):
    rows, width = proj.shape[0], proj.shape[1] // 3
    nq, tiles = width // 256, rows // TQ
    return pl.pallas_call(
        functools.partial(self_fwd_kernel, nq=nq, tiles=tiles, scale=scale),
        out_shape=(
            jax.ShapeDtypeStruct((rows, width), BF),
            jax.ShapeDtypeStruct((tiles, nq, 1, 256), F32),
        ),
        in_specs=[VM] * 4,
        out_specs=(VM, VM),
        scratch_shapes=[
            pltpu.VMEM((rows + 64, width), BF),
            pltpu.VMEM((rows + 64, width), BF),
            pltpu.VMEM((nq, WIN, 256), F32),
        ],
        compiler_params=pltpu.CompilerParams(vmem_limit_bytes=LIMIT),
        name="self_fwd",
    )(start, size, brow, proj)


def self_bwd_kernel(
    start_ref,
    size_ref,
    brow_ref,
    proj_ref,
    do_ref,
    lse_ref,
    dproj_ref,
    dbrow_ref,
    kp,
    vp,
    bias,
    dka,
    dva,
    dsum,
    *,
    nq,
    tiles,
    scale,
):
    width = nq * 256
    fill_window(proj_ref, kp, vp, width)
    fill_bias(brow_ref, bias, nq)
    dka[...] = jnp.zeros_like(dka)
    dva[...] = jnp.zeros_like(dva)
    dsum[...] = jnp.zeros_like(dsum)

    def tile(t, _):
        row = pl.ds(pl.multiple_of(t * TQ, TQ), TQ)
        win = pl.ds(pl.multiple_of(t * TQ, TQ), WIN)
        mask = range_mask(t * TQ - 64, WIN, start_ref[t], size_ref[t])
        for c in range(nq):
            cs = slice(c * 256, (c + 1) * 256)
            qs = stack4(proj_ref[row, cs] * jnp.asarray(scale, BF))
            dos = stack4(do_ref[row, cs])
            s = dot(kp[win, cs], qs.T) + bias[c]
            p = jnp.where(mask, jnp.exp(s - lse_ref[t, c]), 0.0)
            dp = dot(vp[win, cs], dos.T)
            delta = jnp.sum(red(p * dp, jnp.sum), axis=0, keepdims=True)
            ds = p * (dp - delta)
            dsum[c] += ds
            ds = ds.astype(BF)
            dva[win, cs] += dot(p.astype(BF), dos)
            dka[win, cs] += dot(ds, qs)
            dproj_ref[row, cs] = (unstack4(dot_tn(ds, kp[win, cs])) * scale).astype(BF)
        return 0

    lax.fori_loop(0, tiles, tile, 0)
    dproj_ref[:, width : 2 * width] = dka[64:, :].astype(BF)
    dproj_ref[:, 2 * width : 3 * width] = dva[64:, :].astype(BF)
    dist = distances()
    for c in range(nq):
        cs = slice(c * 256, (c + 1) * 256)

        def one(d, _):
            x = jnp.where(dist == d, dsum[c], 0.0)
            dbrow_ref[pl.ds(d, 1), cs] = jnp.sum(red(x, jnp.sum), axis=0, keepdims=True)
            return 0

        lax.fori_loop(0, brow_ref.shape[0], one, 0)


def self_bwd(start, size, brow, proj, do, lse, scale):
    rows, width = proj.shape[0], proj.shape[1] // 3
    nq, tiles = width // 256, rows // TQ
    return pl.pallas_call(
        functools.partial(self_bwd_kernel, nq=nq, tiles=tiles, scale=scale),
        out_shape=(jax.ShapeDtypeStruct((rows, 3 * width), BF), jax.ShapeDtypeStruct(brow.shape, F32)),
        in_specs=[VM] * 6,
        out_specs=(VM, VM),
        scratch_shapes=[
            pltpu.VMEM((rows + 64, width), BF),
            pltpu.VMEM((rows + 64, width), BF),
            pltpu.VMEM((nq, WIN, 256), F32),
            pltpu.VMEM((rows + 64, width), F32),
            pltpu.VMEM((rows + 64, width), F32),
            pltpu.VMEM((nq, WIN, 256), F32),
        ],
        compiler_params=pltpu.CompilerParams(vmem_limit_bytes=LIMIT),
        name="self_bwd",
    )(start, size, brow, proj, do, lse)


def norm_rows(x, gain):
    inverse = lax.rsqrt(jnp.mean(x * x, axis=-1, keepdims=True) + EPSILON)
    return x * inverse * gain, inverse


def norm_back(x, inverse, gain, grad):
    scaled = grad * gain
    mean = jnp.mean(x * scaled, axis=-1, keepdims=True)
    return inverse * scaled - x * inverse * inverse * inverse * mean, jnp.sum(grad * x * inverse, axis=0)


def swap(x, axis, bit):
    size = lax.axis_size(axis)
    return lax.ppermute(x, axis, [(i, i ^ bit) for i in range(size)])


def bits_of(axis):
    size = lax.axis_size(axis)
    return [1 << b for b in range(size.bit_length() - 1)]


def gather_parts(x, axis):
    parts = {0: x}
    for bit in reversed(bits_of(axis)):
        for r in list(parts):
            parts[r ^ bit] = swap(parts[r], axis, bit)
    return parts


def add_low(a, b):
    return (a.astype(F32) + b.astype(F32)).astype(BF)


def scatter_sum(x, axis, order):
    size = x.shape[0]
    live = list(range(size))
    block = x
    for bit in order:
        keep = [r for r in live if not r & bit]
        send = [r for r in live if r & bit]
        k = jnp.stack([block[live.index(r)] for r in keep])
        s = jnp.stack([block[live.index(r)] for r in send])
        block = add_low(k, swap(s, axis, bit))
        live = keep
    return block[0]


def gather_sum(x, axis, order):
    parts = [0]
    block = x[None]
    for bit in order:
        block = jnp.concatenate([block, swap(block, axis, bit)], axis=0)
        parts = parts + [r ^ bit for r in parts]
    inverse = [parts.index(r) for r in range(len(parts))]
    return block, inverse


def relative(x, axis):
    size = lax.axis_size(axis)
    me = lax.axis_index(axis)
    return jnp.stack([lax.dynamic_index_in_dim(x, me ^ r, 0, keepdims=False) for r in range(size)])


def reduce_all(x):
    blocks, rows, width = x.shape
    groups = lax.axis_size("grp")
    part = scatter_sum(relative(x, "blk"), "blk", bits_of("blk"))
    part = relative(part.reshape(groups, rows // groups, width), "grp")
    part = scatter_sum(part, "grp", bits_of("grp"))
    whole, inverse = gather_sum(part, "grp", list(reversed(bits_of("grp"))))
    me = lax.axis_index("grp")
    index = jnp.asarray(inverse, jnp.int32)[jnp.arange(groups) ^ me]
    return jnp.take(whole, index, axis=0).reshape(rows, width)


def sum_everywhere(x):
    for axis in ("blk", "grp"):
        for bit in bits_of(axis):
            x = x + swap(x, axis, bit)
    return x


def pack(grads, blocks):
    out = []
    for g in grads:
        k, n = g.shape
        r = g.reshape(blocks, k // blocks, n // 768, 768).transpose(0, 2, 1, 3)
        out.append(r.reshape(blocks, -1, 768))
    return jnp.concatenate(out, axis=1)


def unpack(rows, shapes, blocks):
    out, at = [], 0
    for k, n in shapes:
        count = k // blocks * (n // 768)
        piece = rows[at : at + count].reshape(n // 768, k // blocks, 768)
        out.append(piece.transpose(1, 0, 2).reshape(k // blocks, n).astype(F32))
        at += count
    return out


def body(
    dec_in,
    encodings,
    answer_len,
    answer_question,
    question_rows,
    bucket_table,
    gain_self,
    w_qkv,
    w_self_out,
    rel_bias,
    gain_cross,
    w_cross_q,
    w_cross_kv,
    w_cross_out,
    gain_ffn,
    w_in,
    w_out,
    cotangent,
):
    answers = answer_len.shape[0]
    length = bucket_table.shape[0]
    rows, width = dec_in.shape
    heads = rel_bias.shape[1]
    buckets = rel_bias.shape[0]
    scale = 1.0 / math.sqrt(width // heads)
    enc_rows = encodings.shape[0]
    blocks = lax.axis_size("blk")
    me = lax.axis_index("blk")
    tiles = rows // TQ
    nq = width // 256

    enc_parts = gather_parts(encodings, "blk")

    own_q = lax.dynamic_slice_in_dim(answer_question, me * answers, answers, 0)
    a_index = jnp.arange(answers)
    before = (own_q[None, :] < own_q[:, None]) | (
        (own_q[None, :] == own_q[:, None]) & (a_index[None, :] < a_index[:, None])
    )
    rank = jnp.sum(before.astype(jnp.int32), axis=1)
    target = (rank[:, None] * length + jnp.arange(length)[None, :]).reshape(rows)
    forward_perm = (jnp.arange(rows)[:, None] == target[None, :]).astype(BF)
    sorted_len = jnp.sum(jnp.where(rank[:, None] == a_index[None, :], answer_len[:, None], 0), axis=0)
    ends_q = jnp.cumsum(question_rows[0])
    starts_q = ends_q - question_rows[0]
    sorted_q = jnp.sum(jnp.where(rank[:, None] == a_index[None, :], own_q[:, None], 0), axis=0)
    token_q = jnp.repeat(sorted_q, length)
    pick = token_q[:, None] == jnp.arange(question_rows.shape[1])[None, :]
    token_start = jnp.sum(jnp.where(pick, starts_q[None, :], 0), axis=1)
    token_size = jnp.sum(jnp.where(pick, question_rows[0][None, :], 0), axis=1)

    def stacked(v):
        return jnp.tile(v.reshape(tiles, 1, TQ), (1, 1, 4)).astype(jnp.int32)

    c_start, c_size = stacked(token_start), stacked(token_size)
    lo = (token_start.reshape(tiles, TQ)[:, 0] // TK).astype(jnp.int32)
    hi = ((token_start + token_size).reshape(tiles, TQ)[:, -1] + TK - 1) // TK
    hi = hi.astype(jnp.int32)
    s_start = stacked(jnp.arange(rows) // length * length)
    s_size = stacked(jnp.repeat(sorted_len, length))

    bucket_hot = (bucket_table[:, None] == jnp.arange(buckets)[None, :]).astype(F32)
    brow = jnp.repeat(
        jnp.dot(bucket_hot, rel_bias, precision=lax.Precision.HIGHEST), width // heads, axis=1
    )

    x0 = dot(forward_perm, dec_in)
    grad_top = dot(forward_perm, cotangent)
    grad_low = grad_top.astype(BF)
    n1, r1 = norm_rows(x0, gain_self)
    h1 = n1.astype(BF)
    proj = dot(h1, w_qkv).astype(BF)
    o_self, lse_self = self_fwd(s_start, s_size, brow, proj, scale)
    x1 = x0 + dot(o_self, w_self_out)
    n2, r2 = norm_rows(x1, gain_cross)
    h2 = n2.astype(BF)
    qc = (dot(h2, w_cross_q).astype(BF) * jnp.asarray(scale, BF)).astype(BF)

    enc_rel = jnp.stack([enc_parts[r] for r in range(blocks)])
    enc_all = relative(enc_rel, "blk").reshape(blocks * enc_rows, width)
    kv = dot(enc_all, w_cross_kv).astype(BF)
    k_all, v_all = kv[:, :width], kv[:, width:]
    kvt = lax.dot_general(w_cross_kv, enc_all, (((0,), (1,)), ((), ())), preferred_element_type=F32).astype(BF)
    kt_all, vt_all = kvt[:width], kvt[width:]

    o_cross, lse_cross = cross_fwd(lo, hi, c_start, c_size, qc, k_all, vt_all)
    oc = o_cross.astype(BF)
    x2 = x1 + dot(oc, w_cross_out)
    n3, r3 = norm_rows(x2, gain_ffn)
    h3 = n3.astype(BF)
    hidden, gelu_back = jax.vjp(jax.nn.gelu, dot(h3, w_in))
    u = hidden.astype(BF)
    out = (x2 + dot(u, w_out)).astype(BF)
    layer_out = dot_tn(forward_perm, out).astype(BF)

    d_w_out = dot_tn(u, grad_low).astype(BF)
    da = gelu_back(dot_nt(grad_low, w_out))[0].astype(BF)
    d_w_in = dot_tn(h3, da).astype(BF)
    sums_out = reduce_all(pack([d_w_out], blocks))
    sums_in = reduce_all(pack([d_w_in], blocks))
    dx3, d_gain_ffn = norm_back(x2, r3, gain_ffn, dot_nt(da, w_in))
    dx2 = grad_top + dx3
    dyc = dx2.astype(BF)
    d_w_cross_out = dot_tn(oc, dyc).astype(BF)
    d_o = dot_nt(dyc, w_cross_out).astype(BF)
    dqc, dk, dv = cross_bwd(
        lo, hi, c_start, c_size, qc, d_o, o_cross, lse_cross, k_all, v_all, kt_all, scale
    )

    dkv = jnp.concatenate([dk, dv], axis=1).reshape(blocks, enc_rows, 2 * width)
    dkv = relative(dkv, "blk")
    dkv = add_low(dkv[0::2], swap(dkv[1::2], "blk", 1))
    enc_half = enc_rel[0::2]
    dkv_flat = dkv.reshape(-1, 2 * width)
    d_w_cross_kv = dot_tn(enc_half.reshape(-1, width), dkv_flat).astype(BF)
    d_enc = dot_nt(dkv_flat, w_cross_kv).reshape(blocks // 2, enc_rows, width)
    d_enc_parts = {2 * r: d_enc[r] for r in range(blocks // 2)}
    for bit in reversed(bits_of("blk")[1:]):
        for r in [r for r in d_enc_parts if r & bit]:
            came = swap(d_enc_parts.pop(r).astype(BF), "blk", bit)
            d_enc_parts[r ^ bit] = d_enc_parts[r ^ bit] + came.astype(F32)
    d_encodings = d_enc_parts[0]

    d_w_cross_q = dot_tn(h2, dqc).astype(BF)
    sums_cross = reduce_all(pack([d_w_cross_out, d_w_cross_q, d_w_cross_kv], blocks))
    dx_two, d_gain_cross = norm_back(x1, r2, gain_cross, dot_nt(dqc, w_cross_q))
    dx1 = dx2 + dx_two
    dy1 = dx1.astype(BF)
    d_w_self_out = dot_tn(o_self, dy1).astype(BF)
    d_os = dot_nt(dy1, w_self_out).astype(BF)
    dproj, dbrow = self_bwd(s_start, s_size, brow, proj, d_os, lse_self, scale)
    d_w_qkv = dot_tn(h1, dproj).astype(BF)
    sums_self = reduce_all(pack([d_w_qkv, d_w_self_out], blocks))
    dx_one, d_gain_self = norm_back(x0, r1, gain_self, dot_nt(dproj, w_qkv))
    d_rel = jnp.dot(
        bucket_hot.T, jnp.sum(dbrow.reshape(length, heads, -1), axis=2), precision=lax.Precision.HIGHEST
    )
    d_x0 = dx1 + dx_one
    high = d_x0.astype(BF)
    low = (d_x0 - high.astype(F32)).astype(BF)
    d_dec_in = dot_tn(forward_perm, high) + dot_tn(forward_perm, low)

    small = jnp.concatenate([d_gain_self, d_gain_cross, d_gain_ffn, d_rel.reshape(-1)])
    small = sum_everywhere(small.reshape(-1, 128)).reshape(-1)

    def own(v):
        return lax.dynamic_slice_in_dim(v, me * (v.shape[0] // blocks), v.shape[0] // blocks, 0)

    g_self, g_cross, g_ffn = (own(small[i * width : (i + 1) * width]) for i in range(3))
    g_rel = own(small[3 * width :].reshape(buckets, heads))
    (o_wout,) = unpack(sums_out, [w_out.shape], blocks)
    (o_win,) = unpack(sums_in, [w_in.shape], blocks)
    o_wco, o_wcq, o_wckv = unpack(sums_cross, [w_cross_out.shape, w_cross_q.shape, w_cross_kv.shape], blocks)
    o_wqkv, o_wso = unpack(sums_self, [w_qkv.shape, w_self_out.shape], blocks)
    return (
        layer_out,
        d_dec_in,
        d_encodings,
        g_self,
        o_wqkv,
        o_wso,
        g_rel,
        g_cross,
        o_wcq,
        o_wckv,
        o_wco,
        g_ffn,
        o_win,
        o_wout,
    )


def slot_of(rel):
    return (rel & 1) * 4 + (rel & 2) + ((rel >> 2) & 1)


def gelu_both(a):
    c = math.sqrt(2.0 / math.pi)
    a2 = a * a
    t = jnp.tanh(c * (a + 0.044715 * (a2 * a)))
    half = 0.5 * (1.0 + t)
    return a * half, half + 0.5 * a * (1.0 - t * t) * (c * (1.0 + 3.0 * 0.044715 * a2))


def rms(x):
    return lax.rsqrt(jnp.mean(x * x, axis=-1, keepdims=True) + EPSILON)


def rms_back(x, inverse, gain, grad):
    scaled = grad * gain
    mean = jnp.mean(x * scaled, axis=-1, keepdims=True)
    unit = x * inverse
    return inverse * (scaled - unit * (inverse * mean)), jnp.sum(grad * unit, axis=0, keepdims=True)


def onehot_rows(src):
    n = src.shape[1]
    return (lax.broadcasted_iota(jnp.int32, (n, n), 0) == src).astype(F32).astype(BF)


def pre_kernel(
    me_ref,
    aq_ref,
    len_ref,
    qrows_ref,
    bucket_ref,
    dec_ref,
    gain1_ref,
    rel_ref,
    wqkv_ref,
    src_ref,
    cstart_ref,
    csize_ref,
    sstart_ref,
    ssize_ref,
    lo_ref,
    hi_ref,
    brow_ref,
    x0_ref,
    h1_ref,
    proj_ref,
    oself_ref,
    lse_ref,
    order,
    qstart,
    qcount,
    wide,
    kp,
    vp,
    bias,
    *,
    answers,
    length,
    questions,
    scale,
):
    rows, width = dec_ref.shape
    nq, tiles = width // 256, rows // TQ
    base = me_ref[0] * answers
    n = jnp.int32(0)
    first_row = jnp.int32(0)
    for c in range(questions):
        qstart[c] = first_row
        first_row = first_row + qrows_ref[0, c]
        qcount[c] = n

        def visit(a, n):
            hit = aq_ref[base + a] == c

            @pl.when(hit)
            def _():
                order[n] = a

            return n + hit.astype(jnp.int32)

        n = lax.fori_loop(0, answers, visit, n)

    def answer_of(tok):
        ans = jnp.zeros_like(tok)
        for k in range(1, answers):
            ans = ans + (tok >= k * length).astype(jnp.int32)
        return ans

    tok = lax.broadcasted_iota(jnp.int32, (1, rows), 1)
    ans = answer_of(tok)
    src = tok - ans * length
    for k in range(answers):
        src = src + jnp.where(ans == k, order[k] * length, 0)
    src_ref[...] = src

    lane = lax.broadcasted_iota(jnp.int32, (tiles, 256), 1) % TQ
    tok = lane + TQ * lax.broadcasted_iota(jnp.int32, (tiles, 256), 0)
    ans = answer_of(tok)
    sstart_ref[...] = ans * length
    size = jnp.zeros_like(ans)
    for k in range(answers):
        size = size + jnp.where(ans == k, len_ref[order[k]], 0)
    ssize_ref[...] = size
    cstart = jnp.zeros_like(ans)
    csize = jnp.zeros_like(ans) + qrows_ref[0, 0]
    for c in range(1, questions):
        here = ans >= qcount[c]
        cstart = jnp.where(here, qstart[c], cstart)
        csize = jnp.where(here, qrows_ref[0, c], csize)
    cstart_ref[...] = cstart
    csize_ref[...] = csize
    for t in range(tiles):
        q_first = aq_ref[base + order[t * TQ // length]]
        q_last = aq_ref[base + order[(t * TQ + TQ - 1) // length]]
        lo_ref[t] = qstart[q_first] // TK
        hi_ref[t] = (qstart[q_last] + qrows_ref[0, q_last] + TK - 1) // TK

    for c in range(nq):
        head = lax.broadcasted_iota(jnp.int32, (rel_ref.shape[0], 256), 1) // 64
        held = jnp.zeros((rel_ref.shape[0], 256), F32)
        for a in range(4):
            h = c * 4 + a
            held = jnp.where(head == a, rel_ref[:, h : h + 1], held)
        wide[:, c * 256 : (c + 1) * 256] = held
    for d in range(length):
        brow_ref[d : d + 1, :] = wide[pl.ds(bucket_ref[d], 1), :]

    x0 = dot_tn(onehot_rows(src), dec_ref[...])
    x0_ref[...] = x0.astype(BF)
    h1_ref[...] = (x0 * rms(x0) * gain1_ref[...]).astype(BF)
    for i in range(3):
        cs = slice(i * width, (i + 1) * width)
        proj_ref[:, cs] = dot(h1_ref[...], wqkv_ref[:, cs]).astype(BF)
    fill_window(proj_ref, kp, vp, width)
    fill_bias(brow_ref, bias, nq)

    def tile(t, _):
        row = pl.ds(pl.multiple_of(t * TQ, TQ), TQ)
        win = pl.ds(pl.multiple_of(t * TQ, TQ), WIN)
        mask = range_mask(t * TQ - 64, WIN, sstart_ref[pl.ds(t, 1), :], ssize_ref[pl.ds(t, 1), :])
        for c in range(nq):
            cs = slice(c * 256, (c + 1) * 256)
            qst = stack4(proj_ref[row, cs] * jnp.asarray(scale, BF)).T
            s = jnp.where(mask, dot(kp[win, cs], qst) + bias[c], MASKED)
            m = jnp.max(red(s, jnp.max), axis=0, keepdims=True)
            p = jnp.exp(s - m)
            l = jnp.sum(red(p, jnp.sum), axis=0, keepdims=True)
            p = (p * (1.0 / l)).astype(BF)
            oself_ref[row, cs] = unstack4(dot_tn(p, vp[win, cs])).astype(BF)
            lse_ref[t, c] = m + jnp.log(l)
        return 0

    lax.fori_loop(0, tiles, tile, 0)


def mid_kernel(x0_ref, oself_ref, wso_ref, gain2_ref, wcq_ref, x1_ref, h2_ref, qc_ref, *, scale):
    x1 = x0_ref[...].astype(F32) + dot(oself_ref[...], wso_ref[...])
    x1_ref[...] = x1
    h2_ref[...] = (x1 * rms(x1) * gain2_ref[...]).astype(BF)
    qc_ref[...] = dot(h2_ref[...], wcq_ref[...]).astype(BF) * jnp.asarray(scale, BF)


def mid(x0, oself, wso, gain, wcq, scale):
    rows, width = x0.shape
    return call(
        functools.partial(mid_kernel, scale=scale),
        "mid",
        (sds((rows, width), F32), sds((rows, width), BF), sds((rows, width), BF)),
        [VM] * 5,
        (VM,) * 3,
        [],
        (x0, oself, wso, gain, wcq),
        us=8,
    )


def call(kernel, name, out_shape, in_specs, out_specs, scratch, args, us):
    moved = sum(math.prod(a.shape) * a.dtype.itemsize for a in args)
    moved += sum(math.prod(a.shape) * a.dtype.itemsize for a in out_shape)
    return pl.pallas_call(
        kernel,
        out_shape=out_shape,
        in_specs=in_specs,
        out_specs=out_specs,
        scratch_shapes=scratch,
        compiler_params=pltpu.CompilerParams(vmem_limit_bytes=LIMIT),
        cost_estimate=pl.CostEstimate(flops=int(us * 1e11), bytes_accessed=moved, transcendentals=0),
        name=name,
    )(*args)


def sds(shape, dtype):
    return jax.ShapeDtypeStruct(shape, dtype)


def pre(me, aq, lens, qrows, bucket, dec, g1, rel, wqkv, scale):
    rows, width = dec.shape
    tiles, nq, length = rows // TQ, width // 256, bucket.shape[0]
    i32 = jnp.int32
    meta = sds((tiles, 256), i32)
    out = (
        sds((1, rows), i32),
        meta,
        meta,
        meta,
        meta,
        sds((tiles,), i32),
        sds((tiles,), i32),
        sds((length, width), F32),
        sds((rows, width), BF),
        sds((rows, width), BF),
        sds((rows, 3 * width), BF),
        sds((rows, width), BF),
        sds((tiles, nq, 1, 256), F32),
    )
    return call(
        functools.partial(
            pre_kernel, answers=lens.shape[0], length=length, questions=qrows.shape[1], scale=scale
        ),
        "pre",
        out,
        [SM] * 5 + [VM] * 4,
        (VM,) * 5 + (SM, SM) + (VM,) * 6,
        [
            pltpu.SMEM((lens.shape[0],), i32),
            pltpu.SMEM((qrows.shape[1],), i32),
            pltpu.SMEM((qrows.shape[1],), i32),
            pltpu.VMEM((rel.shape[0], width), F32),
            pltpu.VMEM((rows + 64, width), BF),
            pltpu.VMEM((rows + 64, width), BF),
            pltpu.VMEM((nq, WIN, 256), F32),
        ],
        (me, aq, lens, qrows, bucket, dec, g1, rel, wqkv),
        us=40,
    )


def kv_cross_kernel(
    me_ref,
    lo_ref,
    hi_ref,
    start_ref,
    size_ref,
    q_ref,
    *rest,
    pieces,
):
    enc = rest[:pieces]
    wkv_ref, k_ref, v_ref, kt_ref, o_ref, lse_ref, vt, qst, s_scr, m_scr, l_scr, acc = rest[pieces:]
    rows, width = q_ref.shape
    nq, tiles = width // 256, rows // TQ
    n = enc[0].shape[0]
    for r in range(pieces):
        at = pl.ds(pl.multiple_of((me_ref[0] ^ r) * n, n), n)
        kk = dot(enc[r][...], wkv_ref[:, :width]).astype(BF)
        k_ref[at, :] = kk
        kt_ref[:, at] = kk.T
        vv = dot(enc[r][...], wkv_ref[:, width:]).astype(BF)
        v_ref[at, :] = vv
        vt[:, at] = vv.T

    def tile(t, _):
        st = start_ref[pl.ds(t, 1), :]
        sz = size_ref[pl.ds(t, 1), :]
        lo = lo_ref[t]
        hi = hi_ref[t]
        row = pl.ds(pl.multiple_of(t * TQ, TQ), TQ)
        for c in range(nq):
            qst[c] = stack4(q_ref[row, c * 256 : (c + 1) * 256]).T
            m_scr[c] = jnp.full((8, 256), NEG, F32)
            l_scr[c] = jnp.zeros((8, 256), F32)
            acc[c] = jnp.zeros((256, 256), F32)

        def scores(j, _):
            kr = pl.ds(pl.multiple_of(j * TK, TK), TK)
            mask = range_mask(j * TK, TK, st, sz)
            for c in range(nq):
                s = dot(k_ref[kr, c * 256 : (c + 1) * 256], qst[c])
                s = jnp.where(mask, s, NEG)
                s_scr[c, kr, :] = s
                m_scr[c] = jnp.maximum(m_scr[c], red(s, jnp.max))
            return 0

        lax.fori_loop(lo, hi, scores, 0)
        for c in range(nq):
            m_scr[c] = jnp.broadcast_to(jnp.max(m_scr[c], axis=0, keepdims=True), (8, 256))

        def mix(j, _):
            kr = pl.ds(pl.multiple_of(j * TK, TK), TK)
            for c in range(nq):
                p = jnp.exp(s_scr[c, kr, :] - m_scr[c][0:1])
                l_scr[c] += red(p, jnp.sum)
                acc[c] += dot(vt[c * 256 : (c + 1) * 256, kr], p.astype(BF))
            return 0

        lax.fori_loop(lo, hi, mix, 0)
        for c in range(nq):
            l = jnp.sum(l_scr[c], axis=0, keepdims=True)
            lse_ref[t, c] = m_scr[c][0:1] + jnp.log(l)
            o_ref[row, c * 256 : (c + 1) * 256] = unstack4((acc[c] * (1.0 / l)).T)
        return 0

    lax.fori_loop(0, tiles, tile, 0)


def kv_cross(me, lo, hi, start, size, q, enc, wkv):
    rows, width = q.shape
    tiles, nq = rows // TQ, width // 256
    keys = len(enc) * enc[0].shape[0]
    return call(
        functools.partial(kv_cross_kernel, pieces=len(enc)),
        "kv_cross",
        (
            sds((keys, width), BF),
            sds((keys, width), BF),
            sds((width, keys), BF),
            sds((rows, width), F32),
            sds((tiles, nq, 1, 256), F32),
        ),
        [SM] * 3 + [VM] * (3 + len(enc) + 1),
        (VM,) * 5,
        [
            pltpu.VMEM((width, keys), BF),
            pltpu.VMEM((nq, 256, 256), BF),
            pltpu.VMEM((nq, keys, 256), F32),
            pltpu.VMEM((nq, 8, 256), F32),
            pltpu.VMEM((nq, 8, 256), F32),
            pltpu.VMEM((nq, 256, 256), F32),
        ],
        (me, lo, hi, start, size, q, *enc, wkv),
        us=80,
    )


def ffn_kernel(
    me_ref,
    src_ref,
    x1_ref,
    ocross_ref,
    gain_ref,
    cot_ref,
    wco_ref,
    win_ref,
    wout_ref,
    keep_ref,
    send_ref,
    x2_ref,
    dh_ref,
    g_ref,
    oc_ref,
    out_ref,
    h3,
    h3t,
    out_acc,
    *,
    last,
):
    i = pl.program_id(0)
    me_b, me_g = me_ref[0], me_ref[1]
    f = me_b ^ i
    rows, width = x1_ref.shape
    quarter = width // 4
    half = quarter // 2

    @pl.when(i == 0)
    def _():
        hot = onehot_rows(src_ref[...])
        g_ref[...] = dot_tn(hot, cot_ref[...]).astype(BF)
        oc = ocross_ref[...].astype(BF)
        oc_ref[...] = oc
        x2 = x1_ref[...] + dot(oc, wco_ref[...])
        x2_ref[...] = x2
        n = (x2 * rms(x2) * gain_ref[...]).astype(BF)
        h3[...] = n
        h3t[...] = n.T
        out_acc[...] = jnp.zeros_like(out_acc)
        dh_ref[...] = jnp.zeros_like(dh_ref)

    u, slope = gelu_both(dot(h3[...], win_ref[...]))
    u = u.astype(BF)
    out_acc[...] += dot(u, wout_ref[...])
    da = (slope * dot_nt(g_ref[...], wout_ref[...])).astype(BF)
    dh_ref[...] += dot_nt(da, win_ref[...])
    dwo = dot_tn(u, g_ref[...]).astype(BF)
    for s in range(8):
        at = (i >> 1) * 8 + slot_of(me_g ^ s)

        @pl.when((i & 1) == 0)
        def _():
            keep_ref[at, half:, :] = dwo[s * half : (s + 1) * half]

        @pl.when((i & 1) == 1)
        def _():
            send_ref[at, half:, :] = dwo[s * half : (s + 1) * half]

    for r in range(4):
        part = h3t[pl.ds(pl.multiple_of((me_b ^ r) * quarter, quarter), quarter), :]
        dwi = dot(part, da).astype(BF)
        target = send_ref if r & 1 else keep_ref
        for b in range(2):
            at = (r >> 1) * 8 + slot_of(me_g ^ (2 * f + b))
            target[at, :half, :] = dwi[b * half : (b + 1) * half]

    @pl.when(i == last)
    def _():
        out = (x2_ref[...] + out_acc[...]).astype(BF)
        out_ref[...] = dot(onehot_rows(src_ref[...]), out).astype(BF)


def ffn(me, src, x1, ocross, gain, cot, wco, win, wout):
    rows, width = x1.shape
    steps = win.shape[1] // width
    half = width // 8
    full = lambda a: pl.BlockSpec(a.shape, lambda i, m: (0,) * len(a.shape))
    outs = (
        sds((16, 2 * half, width), BF),
        sds((16, 2 * half, width), BF),
        sds((rows, width), F32),
        sds((rows, width), F32),
        sds((rows, width), BF),
        sds((rows, width), BF),
        sds((rows, width), BF),
    )
    ins = (src, x1, ocross, gain, cot, wco)
    grid_spec = pltpu.PrefetchScalarGridSpec(
        num_scalar_prefetch=1,
        grid=(steps,),
        in_specs=[full(a) for a in ins]
        + [
            pl.BlockSpec((width, width), lambda i, m: (0, m[0] ^ i)),
            pl.BlockSpec((width, width), lambda i, m: (m[0] ^ i, 0)),
        ],
        out_specs=tuple(full(a) for a in outs),
        scratch_shapes=[
            pltpu.VMEM((rows, width), BF),
            pltpu.VMEM((width, rows), BF),
            pltpu.VMEM((rows, width), F32),
        ],
    )
    return pl.pallas_call(
        functools.partial(ffn_kernel, last=steps - 1),
        out_shape=outs,
        grid_spec=grid_spec,
        compiler_params=pltpu.CompilerParams(vmem_limit_bytes=LIMIT),
        cost_estimate=pl.CostEstimate(flops=60 * 10**11, bytes_accessed=30 << 20, transcendentals=0),
        name="ffn",
    )(me, *ins, win, wout)


def ffn_back_kernel(x2_ref, dh_ref, g_ref, gain_ref, wco_ref, dx2_ref, dyc_ref, do_ref, dgain_ref):
    x2 = x2_ref[...]
    dx, dgain_ref[...] = rms_back(x2, rms(x2), gain_ref[...], dh_ref[...])
    dx2 = g_ref[...].astype(F32) + dx
    dx2_ref[...] = dx2
    dyc_ref[...] = dx2.astype(BF)
    do_ref[...] = dot_nt(dyc_ref[...], wco_ref[...]).astype(BF)


def ffn_back(x2, dh, g, gain, wco):
    rows, width = x2.shape
    return call(
        ffn_back_kernel,
        "ffn_back",
        (sds((rows, width), F32), sds((rows, width), BF), sds((rows, width), BF), sds((1, width), F32)),
        [VM] * 5,
        (VM,) * 4,
        [],
        (x2, dh, g, gain, wco),
        us=30,
    )


def cross_back_kernel(
    me_ref,
    lo_ref,
    hi_ref,
    start_ref,
    size_ref,
    q_ref,
    do_ref,
    o_ref,
    lse_ref,
    k_ref,
    v_ref,
    kt_ref,
    dq_ref,
    keep_ref,
    send_ref,
    qs,
    qst,
    dos,
    dost,
    del_scr,
    dka,
    dva,
    dqt,
    *,
    scale,
):
    rows, width = q_ref.shape
    nq, tiles = width // 256, rows // TQ
    dka[...] = jnp.zeros_like(dka)
    dva[...] = jnp.zeros_like(dva)

    def tile(t, _):
        st = start_ref[pl.ds(t, 1), :]
        sz = size_ref[pl.ds(t, 1), :]
        row = pl.ds(pl.multiple_of(t * TQ, TQ), TQ)
        for c in range(nq):
            cs = slice(c * 256, (c + 1) * 256)
            a = stack4(q_ref[row, cs])
            qs[c] = a
            qst[c] = a.T
            b = stack4(do_ref[row, cs])
            dos[c] = b
            dost[c] = b.T
            product = do_ref[row, cs].astype(F32) * o_ref[row, cs]
            total = jnp.sum(red(stack4(product).T, jnp.sum), axis=0, keepdims=True)
            del_scr[c] = jnp.broadcast_to(total, (8, 256))
            dqt[c] = jnp.zeros((256, 256), F32)

        def step(j, _):
            kr = pl.ds(pl.multiple_of(j * TK, TK), TK)
            mask = range_mask(j * TK, TK, st, sz)
            for c in range(nq):
                cs = slice(c * 256, (c + 1) * 256)
                s = dot(k_ref[kr, cs], qst[c])
                p = jnp.where(mask, jnp.exp(s - lse_ref[t, c]), 0.0)
                dp = dot(v_ref[kr, cs], dost[c])
                ds = (p * (dp - del_scr[c][0:1])).astype(BF)
                dva[kr, cs] += dot(p.astype(BF), dos[c])
                dka[kr, cs] += dot(ds, qs[c])
                dqt[c] += dot(kt_ref[cs, kr], ds)
            return 0

        lax.fori_loop(lo_ref[t], hi_ref[t], step, 0)
        for c in range(nq):
            cs = slice(c * 256, (c + 1) * 256)
            dq_ref[row, cs] = (unstack4(dqt[c].T) * scale).astype(BF)
        return 0

    lax.fori_loop(0, tiles, tile, 0)
    n = keep_ref.shape[1]
    for r in range(4):
        at = pl.ds(pl.multiple_of((me_ref[0] ^ r) * n, n), n)
        target = send_ref if r & 1 else keep_ref
        target[r >> 1, :, :width] = dka[at, :].astype(BF)
        target[r >> 1, :, width:] = dva[at, :].astype(BF)


def cross_back(me, lo, hi, start, size, q, do, o, lse, k, v, kt, scale):
    rows, width = q.shape
    keys, nq = k.shape[0], width // 256
    part = sds((2, keys // 4, 2 * width), BF)
    return call(
        functools.partial(cross_back_kernel, scale=scale),
        "cross_back",
        (sds((rows, width), BF), part, part),
        [SM] * 3 + [VM] * 9,
        (VM,) * 3,
        [pltpu.VMEM((nq, 256, 256), BF)] * 4
        + [
            pltpu.VMEM((nq, 8, 256), F32),
            pltpu.VMEM((keys, width), F32),
            pltpu.VMEM((keys, width), F32),
            pltpu.VMEM((nq, 256, 256), F32),
        ],
        (me, lo, hi, start, size, q, do, o, lse, k, v, kt),
        us=150,
    )


def cross_in_kernel(dq_ref, x1_ref, dx2_ref, gain_ref, wcq_ref, wso_ref, dx1_ref, dy1_ref, dos_ref, dgain_ref):
    x1 = x1_ref[...]
    dx, dgain_ref[...] = rms_back(x1, rms(x1), gain_ref[...], dot_nt(dq_ref[...], wcq_ref[...]))
    dx1 = dx2_ref[...] + dx
    dx1_ref[...] = dx1
    dy1_ref[...] = dx1.astype(BF)
    dos_ref[...] = dot_nt(dy1_ref[...], wso_ref[...]).astype(BF)


def cross_in(dq, x1, dx2, gain, wcq, wso):
    rows, width = x1.shape
    return call(
        cross_in_kernel,
        "cross_in",
        (sds((rows, width), F32), sds((rows, width), BF), sds((rows, width), BF), sds((1, width), F32)),
        [VM] * 6,
        (VM,) * 4,
        [],
        (dq, x1, dx2, gain, wcq, wso),
        us=60,
    )


def put_pieces(me_ref, left_t, right, block, keep_ref, send_ref):
    width = left_t.shape[0]
    quarter = width // 4
    half = quarter // 2
    for r in range(4):
        part = left_t[pl.ds(pl.multiple_of((me_ref[0] ^ r) * quarter, quarter), quarter), :]
        grad = dot(part, right).astype(BF)
        target = send_ref if r & 1 else keep_ref
        for b in range(2):
            at = (r >> 1) * 8 + slot_of(me_ref[1] ^ (2 * block + b))
            target[at] = grad[b * half : (b + 1) * half]


def cross_weights_kernel(
    me_ref, dkv_ref, came_ref, enc0_ref, enc2_ref, wkv_ref, oc_ref, dyc_ref, h2_ref, dq_ref,
    keep_ref, send_ref, own_ref, out_ref, both, enc_t, left_t,
):
    n, width2 = dkv_ref.shape[1], dkv_ref.shape[2]
    width = width2 // 2
    for r in range(2):
        both[r * n : (r + 1) * n, :] = (dkv_ref[r].astype(F32) + came_ref[r].astype(F32)).astype(BF)
    out_ref[...] = dot_nt(both[n:, :], wkv_ref[...]).astype(BF)
    own_ref[...] = dot_nt(both[:n, :], wkv_ref[...])
    enc_t[:, :n] = enc0_ref[...].T
    enc_t[:, n:] = enc2_ref[...].T
    put_pieces(me_ref, enc_t, both[:, :width], 2, keep_ref, send_ref)
    put_pieces(me_ref, enc_t, both[:, width:], 3, keep_ref, send_ref)
    left_t[...] = oc_ref[...].T
    put_pieces(me_ref, left_t, dyc_ref[...], 0, keep_ref, send_ref)
    left_t[...] = h2_ref[...].T
    put_pieces(me_ref, left_t, dq_ref[...], 1, keep_ref, send_ref)


def cross_weights(me, dkv, came, enc0, enc2, wkv, oc, dyc, h2, dq):
    rows, width = oc.shape
    n = enc0.shape[0]
    part = sds((16, width // 8, width), BF)
    return call(
        cross_weights_kernel,
        "cross_weights",
        (part, part, sds((n, width), F32), sds((n, width), BF)),
        [SM] + [VM] * 9,
        (VM,) * 4,
        [pltpu.VMEM((2 * n, 2 * width), BF), pltpu.VMEM((width, 2 * n), BF), pltpu.VMEM((width, rows), BF)],
        (me, dkv, came, enc0, enc2, wkv, oc, dyc, h2, dq),
        us=30,
    )


def self_back_kernel(
    start_ref,
    size_ref,
    brow_ref,
    bucket_ref,
    proj_ref,
    do_ref,
    lse_ref,
    dproj_ref,
    drel_ref,
    kp,
    vp,
    bias,
    dka,
    dva,
    dsum,
    *,
    scale,
):
    rows, width = do_ref.shape
    nq, tiles = width // 256, rows // TQ
    fill_window(proj_ref, kp, vp, width)
    fill_bias(brow_ref, bias, nq)
    dka[...] = jnp.zeros_like(dka)
    dva[...] = jnp.zeros_like(dva)
    dsum[...] = jnp.zeros_like(dsum)

    def tile(t, _):
        row = pl.ds(pl.multiple_of(t * TQ, TQ), TQ)
        win = pl.ds(pl.multiple_of(t * TQ, TQ), WIN)
        mask = range_mask(t * TQ - 64, WIN, start_ref[pl.ds(t, 1), :], size_ref[pl.ds(t, 1), :])
        for c in range(nq):
            cs = slice(c * 256, (c + 1) * 256)
            qs = stack4(proj_ref[row, cs] * jnp.asarray(scale, BF))
            dos = stack4(do_ref[row, cs])
            s = dot(kp[win, cs], qs.T) + bias[c]
            p = jnp.where(mask, jnp.exp(s - lse_ref[t, c]), 0.0)
            dp = dot(vp[win, cs], dos.T)
            delta = jnp.sum(red(p * dp, jnp.sum), axis=0, keepdims=True)
            ds = p * (dp - delta)
            dsum[c] += ds
            ds = ds.astype(BF)
            dva[win, cs] += dot(p.astype(BF), dos)
            dka[win, cs] += dot(ds, qs)
            dproj_ref[row, cs] = (unstack4(dot_tn(ds, kp[win, cs])) * scale).astype(BF)
        return 0

    lax.fori_loop(0, tiles, tile, 0)
    dproj_ref[:, width : 2 * width] = dka[64:, :].astype(BF)
    dproj_ref[:, 2 * width : 3 * width] = dva[64:, :].astype(BF)
    dist = distances()
    drel_ref[...] = jnp.zeros_like(drel_ref)
    for c in range(nq):
        cs = slice(c * 256, (c + 1) * 256)

        def one(d, _):
            x = jnp.where(dist == d, dsum[c], 0.0)
            at = pl.ds(bucket_ref[d], 1)
            drel_ref[at, cs] += jnp.sum(red(x, jnp.sum), axis=0, keepdims=True)
            return 0

        lax.fori_loop(0, brow_ref.shape[0], one, 0)


def self_back(start, size, brow, bucket, proj, do, lse, buckets, scale):
    rows, width = do.shape
    nq = width // 256
    return call(
        functools.partial(self_back_kernel, scale=scale),
        "self_back",
        (sds((rows, 3 * width), BF), sds((buckets, width), F32)),
        [VM] * 3 + [SM] + [VM] * 3,
        (VM, VM),
        [
            pltpu.VMEM((rows + 64, width), BF),
            pltpu.VMEM((rows + 64, width), BF),
            pltpu.VMEM((nq, WIN, 256), F32),
            pltpu.VMEM((rows + 64, width), F32),
            pltpu.VMEM((rows + 64, width), F32),
            pltpu.VMEM((nq, WIN, 256), F32),
        ],
        (start, size, brow, bucket, proj, do, lse),
        us=60,
    )


def self_weights_kernel(me_ref, h1_ref, dproj_ref, oself_ref, dy1_ref, keep_ref, send_ref, left_t):
    width = h1_ref.shape[1]
    left_t[...] = h1_ref[...].T
    for i in range(3):
        put_pieces(me_ref, left_t, dproj_ref[:, i * width : (i + 1) * width], i, keep_ref, send_ref)
    left_t[...] = oself_ref[...].T
    put_pieces(me_ref, left_t, dy1_ref[...], 3, keep_ref, send_ref)


def self_weights(me, h1, dproj, oself, dy1):
    rows, width = h1.shape
    part = sds((16, width // 8, width), BF)
    return call(
        self_weights_kernel,
        "self_weights",
        (part, part),
        [SM] + [VM] * 4,
        (VM, VM),
        [pltpu.VMEM((width, rows), BF)],
        (me, h1, dproj, oself, dy1),
        us=20,
    )


def self_in_kernel(src_ref, dproj_ref, wqkv_ref, x0_ref, gain_ref, dx1_ref, d_ref, dgain_ref):
    x0 = x0_ref[...].astype(F32)
    dx, dgain_ref[...] = rms_back(x0, rms(x0), gain_ref[...], dot_nt(dproj_ref[...], wqkv_ref[...]))
    dx0 = dx1_ref[...] + dx
    high = dx0.astype(BF)
    low = (dx0 - high.astype(F32)).astype(BF)
    hot = onehot_rows(src_ref[...])
    d_ref[...] = dot(hot, high) + dot(hot, low)


def self_in(src, dproj, wqkv, x0, gain, dx1):
    rows, width = x0.shape
    return call(
        self_in_kernel,
        "self_in",
        (sds((rows, width), F32), sds((1, width), F32)),
        [VM] * 6,
        (VM, VM),
        [],
        (src, dproj, wqkv, x0, gain, dx1),
        us=20,
    )


def unpack_ffn_kernel(me_ref, a0, a1, a2, a3, win_ref, wout_ref):
    half = a0.shape[1] // 2
    for i, ref in enumerate((a0, a1, a2, a3)):
        for z2 in range(2):
            s = me_ref[1] ^ ((i >> 1) + 2 * (i & 1) + 4 * z2)
            piece = ref[z2]
            rows = pl.ds(pl.multiple_of((s & 1) * half, half), half)
            cols = pl.ds(pl.multiple_of((s >> 1) * 768, 768), 768)
            win_ref[rows, cols] = piece[:half].astype(F32)
            wout_ref[pl.ds(pl.multiple_of(s * half, half), half), :] = piece[half:].astype(F32)


def unpack_ffn(me, arrays, win_shape, wout_shape):
    return call(
        unpack_ffn_kernel,
        "unpack_ffn",
        (sds(win_shape, F32), sds(wout_shape, F32)),
        [SM] + [VM] * 4,
        (VM, VM),
        [],
        (me, *arrays),
        us=4,
    )


def tail_kernel(ck, sk, cs, ss, *rest, columns):
    outs = rest[:4]
    q, r1, r2, r3, r4, r5, f, send_sem, recv_sem = rest[4:]
    count, step_rows = q.shape[0], q.shape[2]
    per = count // 2
    g, b = lax.axis_index("grp"), lax.axis_index("blk")
    peers = [(g, b ^ 1), (g, b ^ 2), (g ^ 1, b), (g ^ 2, b), (g ^ 4, b), (g ^ 4, b), (g ^ 2, b), (g ^ 1, b)]
    barrier = pltpu.get_barrier_semaphore()
    for p in peers[:5]:
        pl.semaphore_signal(barrier, inc=1, device_id=p, device_id_type=pl.DeviceIdType.MESH)
    pl.semaphore_wait(barrier, 5)

    def copy(k, j, first=None):
        at = pl.ds(pl.multiple_of((j % per) * step_rows, step_rows), step_rows)
        src, dst = [
            lambda: (first.at[:, at, :], r1.at[j]),
            lambda: (q.at[j, pl.ds(8, 8)], r2.at[j]),
            lambda: (q.at[j, pl.ds(4, 4)], r3.at[j]),
            lambda: (q.at[j, pl.ds(2, 2)], r4.at[j]),
            lambda: (q.at[j, pl.ds(1, 1)], r5.at[j]),
            lambda: (f.at[j, pl.ds(0, 1)], f.at[j, pl.ds(1, 1)]),
            lambda: (f.at[j, pl.ds(0, 2)], f.at[j, pl.ds(2, 2)]),
            lambda: (f.at[j, pl.ds(0, 4)], f.at[j, pl.ds(4, 4)]),
        ][k]()
        return pltpu.make_async_remote_copy(
            src_ref=src,
            dst_ref=dst,
            send_sem=send_sem.at[k, j],
            recv_sem=recv_sem.at[k, j],
            device_id=peers[k],
            device_id_type=pl.DeviceIdType.MESH,
        )

    def start_core(j, _):
        copy(0, j, cs).start()
        return 0

    def start_core2(j, _):
        copy(0, j, ss).start()
        return 0

    lax.fori_loop(0, per, start_core, 0)
    lax.fori_loop(per, count, start_core2, 0)

    def add(a, c):
        return (a.astype(F32) + c.astype(F32)).astype(BF)

    def event(k, j):
        if k == 0:
            at = pl.ds(pl.multiple_of((j % per) * step_rows, step_rows), step_rows)

            @pl.when((j >= 0) & (j < per))
            def _():
                copy(0, j, cs).wait()
                q[j] = add(ck[:, at, :], r1[j])
                copy(1, j).start()

            @pl.when((j >= per) & (j < count))
            def _():
                copy(0, j, ss).wait()
                q[j] = add(sk[:, at, :], r1[j])
                copy(1, j).start()

            return

        @pl.when((j >= 0) & (j < count))
        def _():
            copy(k, j).wait()
            if k == 1:
                q[j, 0:8] = add(q[j, 0:8], r2[j])
            elif k == 2:
                q[j, 0:4] = add(q[j, 0:4], r3[j])
            elif k == 3:
                q[j, 0:2] = add(q[j, 0:2], r4[j])
            elif k == 4:
                f[j, 0:1] = add(q[j, 0:1], r5[j])
            if k < 7:
                copy(k + 1, j).start()
                return
            base = (j % per) * step_rows
            for slot in range(8):
                s = g ^ ((slot >> 2) + (slot & 2) + 4 * (slot & 1))
                block, side = s >> 1, s & 1
                at = pl.ds(pl.multiple_of(side * (per * step_rows) + base, step_rows), step_rows)
                wide = f[j, slot].astype(F32)
                first = 0
                for o, (out, n) in enumerate(zip(outs, columns)):
                    if o == 2 or o == 0:
                        first = 0
                    mine = (j < per) if o < 2 else (j >= per)

                    @pl.when(mine & (block >= first) & (block < first + n))
                    def _():
                        cols = pl.ds(pl.multiple_of((block - first) * 768, 768), 768)
                        out[at, cols] = wide

                    first += n

    event(0, jnp.int32(0))
    event(0, jnp.int32(1))

    def step(t, _):
        event(0, t + 2)
        event(1, t)
        event(4, t - 2)
        event(7, t - 4)
        event(6, t - 3)
        event(3, t - 1)
        event(5, t - 2)
        event(2, t)
        return 0

    lax.fori_loop(0, count + 4, step, 0)


def tail(c_keep, s_keep, c_send, s_send):
    slots, rows, width = c_keep.shape
    step_rows = 16
    count = 2 * rows // step_rows
    columns = (2, 2, 3, 1)
    any_spec = pl.BlockSpec(memory_space=pl.ANY)

    def buf(n):
        return pltpu.VMEM((count, n, step_rows, width), BF)

    return pl.pallas_call(
        functools.partial(tail_kernel, columns=columns),
        out_shape=tuple(sds((2 * rows, n * width), F32) for n in columns),
        in_specs=[VM, VM, any_spec, any_spec],
        out_specs=(VM,) * 4,
        scratch_shapes=[buf(16), buf(16), buf(8), buf(4), buf(2), buf(1), buf(8)]
        + [pltpu.SemaphoreType.DMA((8, count))] * 2,
        compiler_params=pltpu.CompilerParams(
            vmem_limit_bytes=LIMIT, collective_id=0, has_side_effects=True
        ),
        cost_estimate=pl.CostEstimate(flops=10**13, bytes_accessed=30 << 20, transcendentals=0),
        name="tail",
    )(c_keep, s_keep, c_send, s_send)


def hop(x, core=0, xb=0, yb=0, z1=0, z2=0):
    b, g = core | (xb << 1), yb | (z1 << 1) | (z2 << 2)
    groups, blocks = lax.axis_size("grp"), lax.axis_size("blk")
    pairs = [(i * blocks + j, (i ^ g) * blocks + (j ^ b)) for i in range(groups) for j in range(blocks)]
    return lax.ppermute(x, ("grp", "blk"), pairs)


def total(*parts):
    out = parts[0].astype(F32)
    for p in parts[1:]:
        out = out + p.astype(F32)
    return out.astype(BF)


def after(x, *deps):
    return lax.optimization_barrier((x,) + deps)[0]


def split_xy(keep, came):
    return [total(keep[4 * j : 4 * j + 4], came[4 * j : 4 * j + 4]) for j in range(4)]


def send_xy(q):
    return q[0], hop(q[1], yb=1), hop(q[2], xb=1), hop(q[3], xb=1, yb=1)


def split_z(parts):
    return [total(*[p[j] for p in parts]) for j in range(4)]


def send_z(q):
    return q[0], hop(q[1], z2=1), hop(q[2], z1=1), hop(q[3], z1=1, z2=1)


def fused_body(
    dec_in,
    encodings,
    answer_len,
    answer_question,
    question_rows,
    bucket_table,
    gain_self,
    w_qkv,
    w_self_out,
    rel_bias,
    gain_cross,
    w_cross_q,
    w_cross_kv,
    w_cross_out,
    gain_ffn,
    w_in,
    w_out,
    cotangent,
):
    rows, width = dec_in.shape
    buckets, heads = rel_bias.shape
    scale = 1.0 / math.sqrt(width // heads)
    me_b, me_g = lax.axis_index("blk"), lax.axis_index("grp")
    me = jnp.stack([me_b, me_g]).astype(jnp.int32)
    g1, g2, g3 = (g.reshape(1, width) for g in (gain_self, gain_cross, gain_ffn))

    enc2 = hop(encodings, xb=1)
    enc1 = hop(encodings, core=1)
    src, cstart, csize, sstart, ssize, lo, hi, brow, x0, h1, proj, oself, lse_self = pre(
        me, answer_question, answer_len, question_rows, bucket_table, dec_in, g1, rel_bias, w_qkv, scale
    )
    enc2, oself = lax.optimization_barrier((enc2, oself))
    enc3 = hop(enc2, core=1)
    enc1 = after(enc1, x0)
    x1, h2, qc = mid(x0, oself, w_self_out, g2, w_cross_q, scale)
    k, v, kt, ocross, lse = kv_cross(
        me, lo, hi, cstart, csize, qc, (encodings, enc1, enc2, enc3), w_cross_kv
    )
    f_keep, f_send, x2, dh3, g_low, oc, layer_out = ffn(
        me, src, x1, ocross, g3, cotangent, w_cross_out, w_in, w_out
    )
    f_came = hop(f_send, core=1)
    dx2, dyc, do, dgain3 = ffn_back(x2, dh3, g_low, g3, w_cross_out)
    f_came = after(f_came, do)
    f_q = split_xy(f_keep, f_came)
    do = after(do, *f_q)
    f_parts = send_xy(f_q)
    dq, kv_keep, kv_send = cross_back(me, lo, hi, cstart, csize, qc, do, ocross, lse, k, v, kt, scale)
    kv_came = hop(kv_send, core=1)
    f_parts = [after(p, dq) for p in f_parts]
    f_q = split_z(f_parts)
    dq = after(dq, *f_q)
    f_parts = send_z(f_q)
    dx1, dy1, dos, dgain2 = cross_in(dq, x1, dx2, g2, w_cross_q, w_self_out)
    kv_came = after(kv_came, dos)
    c_keep, c_send, enc_own, enc_out = cross_weights(
        me, kv_keep, kv_came, encodings, enc2, w_cross_kv, oc, dyc, h2, dq
    )
    enc_came = hop(enc_out, xb=1)
    f_parts = [after(p, c_keep) for p in f_parts]
    f_own = total(*f_parts)
    dos = after(dos, f_own, c_keep)
    f_came = hop(f_own, z2=1)
    dproj, drel = self_back(sstart, ssize, brow, bucket_table, proj, dos, lse_self, buckets, scale)
    f_came = after(f_came, dproj)
    f_pair = jnp.stack([f_own, f_came])
    dproj = after(dproj, f_pair, enc_came)
    s_keep, s_send = self_weights(me, h1, dproj, oself, dy1)
    d_dec_in, dgain1 = self_in(src, dproj, w_qkv, x0, g1, dx1)
    f_all = [f_pair, hop(f_pair, z1=1), hop(f_pair, yb=1), hop(f_pair, yb=1, z1=1)]
    o_win, o_wout = unpack_ffn(me, f_all, (width // 4, w_in.shape[1]), (w_out.shape[0] // 4, width))
    d_encodings = enc_own + enc_came.astype(F32)

    drel = jnp.sum(drel.reshape(buckets, heads, -1), axis=2)
    small = jnp.concatenate([dgain1[0], dgain2[0], dgain3[0], drel.reshape(-1)])
    small = sum_everywhere(small.reshape(-1, 128)).reshape(-1)
    o_co_cq, o_wckv, o_wqkv, o_wso = tail(c_keep, s_keep, c_send, s_send)
    o_wco, o_wcq = o_co_cq[:, :width], o_co_cq[:, width:]

    def own(v):
        return lax.dynamic_slice_in_dim(v, me_b * (v.shape[0] // 4), v.shape[0] // 4, 0)

    g_self, g_cross, g_ffn = (own(small[i * width : (i + 1) * width]) for i in range(3))
    g_rel = own(small[3 * width :].reshape(buckets, heads))
    return (
        layer_out,
        d_dec_in,
        d_encodings,
        g_self,
        o_wqkv,
        o_wso,
        g_rel,
        g_cross,
        o_wcq,
        o_wckv,
        o_wco,
        g_ffn,
        o_win,
        o_wout,
    )


def solution(mesh):
    rows = P(("grp", "blk"), None)
    fused = mesh.shape["grp"] == 8 and mesh.shape["blk"] == 4
    return jax.shard_map(
        fused_body if fused else body,
        mesh=mesh,
        in_specs=(rows, rows, P(("grp", "blk")), P("grp"), P("grp", None)) + (P(),) * 12 + (rows,),
        out_specs=(rows, rows, rows, P("blk"))
        + (P("blk", None),) * 3
        + (P("blk"),)
        + (P("blk", None),) * 3
        + (P("blk"),)
        + (P("blk", None),) * 2,
        check_vma=False,
    )
```

```python
import functools
import math

import jax
import jax.numpy as jnp
from jax import lax
from jax.experimental import pallas as pl
from jax.experimental.pallas import tpu as pltpu
from jax.sharding import PartitionSpec as P

EPSILON = 1e-06
NEG = -1e30
MASKED = -1e9
TQ = 64
TK = 256
WIN = 128
F32 = jnp.float32
BF = jnp.bfloat16
VM = pl.BlockSpec(memory_space=pltpu.VMEM)
SM = pl.BlockSpec(memory_space=pltpu.SMEM)
LIMIT = 60 << 20


def dot(a, b):
    return jnp.dot(a, b, preferred_element_type=F32)


def dot_tn(a, b):
    return lax.dot_general(a, b, (((0,), (0,)), ((), ())), preferred_element_type=F32)


def dot_nt(a, b):
    return lax.dot_general(a, b, (((1,), (1,)), ((), ())), preferred_element_type=F32)


def stack4(t):
    lane = lax.broadcasted_iota(jnp.int32, t.shape, 1) // 64
    return jnp.concatenate([jnp.where(lane == a, t, jnp.zeros_like(t)) for a in range(4)], axis=0)


def unstack4(s):
    n = s.shape[0] // 4
    lane = lax.broadcasted_iota(jnp.int32, (n, 256), 1) // 64
    out = s[:n]
    for a in range(1, 4):
        out = jnp.where(lane == a, s[a * n : (a + 1) * n], out)
    return out


def range_mask(base, rows, start, size):
    idx = lax.broadcasted_iota(jnp.int32, (rows, start.shape[1]), 0)
    rel = idx - (start - base)
    return (rel >= 0) & (rel < size)


def red(x, op):
    return op(x.reshape(x.shape[0] // 8, 8, x.shape[1]), axis=0)


def cross_fwd_kernel(
    lo_ref, hi_ref, start_ref, size_ref, q_ref, k_ref, vt_ref, o_ref, lse_ref, qst, s_scr, m_scr, l_scr, acc, *, nq, tiles
):
    def tile(t, _):
        st = start_ref[t]
        sz = size_ref[t]
        lo = lo_ref[t]
        hi = hi_ref[t]
        row = pl.ds(pl.multiple_of(t * TQ, TQ), TQ)
        for c in range(nq):
            qst[c] = stack4(q_ref[row, c * 256 : (c + 1) * 256]).T
            m_scr[c] = jnp.full((8, 256), NEG, F32)
            l_scr[c] = jnp.zeros((8, 256), F32)
            acc[c] = jnp.zeros((256, 256), F32)

        def scores(j, _):
            kr = pl.ds(pl.multiple_of(j * TK, TK), TK)
            mask = range_mask(j * TK, TK, st, sz)
            for c in range(nq):
                s = dot(k_ref[kr, c * 256 : (c + 1) * 256], qst[c])
                s = jnp.where(mask, s, NEG)
                s_scr[c, kr, :] = s
                m_scr[c] = jnp.maximum(m_scr[c], red(s, jnp.max))
            return 0

        lax.fori_loop(lo, hi, scores, 0)
        for c in range(nq):
            m_scr[c] = jnp.broadcast_to(jnp.max(m_scr[c], axis=0, keepdims=True), (8, 256))

        def mix(j, _):
            kr = pl.ds(pl.multiple_of(j * TK, TK), TK)
            for c in range(nq):
                p = jnp.exp(s_scr[c, kr, :] - m_scr[c][0:1])
                l_scr[c] += red(p, jnp.sum)
                acc[c] += dot(vt_ref[c * 256 : (c + 1) * 256, kr], p.astype(BF))
            return 0

        lax.fori_loop(lo, hi, mix, 0)
        for c in range(nq):
            l = jnp.sum(l_scr[c], axis=0, keepdims=True)
            lse_ref[t, c] = m_scr[c][0:1] + jnp.log(l)
            o_ref[row, c * 256 : (c + 1) * 256] = unstack4((acc[c] * (1.0 / l)).T)
        return 0

    lax.fori_loop(0, tiles, tile, 0)


def quads_per_step(nq, keys):
    return nq if keys <= 2048 else 1


def cross_fwd(lo, hi, start, size, q, k, vt):
    rows, width = q.shape
    tiles, keys = rows // TQ, k.shape[0]
    nq = quads_per_step(width // 256, keys)
    full = pl.BlockSpec(start.shape, lambda g: (0, 0, 0))
    return pl.pallas_call(
        functools.partial(cross_fwd_kernel, nq=nq, tiles=tiles),
        grid=(width // 256 // nq,),
        out_shape=(
            jax.ShapeDtypeStruct(q.shape, F32),
            jax.ShapeDtypeStruct((tiles, width // 256, 1, 256), F32),
        ),
        in_specs=[
            SM,
            SM,
            full,
            full,
            pl.BlockSpec((rows, nq * 256), lambda g: (0, g)),
            pl.BlockSpec((keys, nq * 256), lambda g: (0, g)),
            pl.BlockSpec((nq * 256, keys), lambda g: (g, 0)),
        ],
        out_specs=(
            pl.BlockSpec((rows, nq * 256), lambda g: (0, g)),
            pl.BlockSpec((tiles, nq, 1, 256), lambda g: (0, g, 0, 0)),
        ),
        scratch_shapes=[
            pltpu.VMEM((nq, 256, 256), BF),
            pltpu.VMEM((nq, keys, 256), F32),
            pltpu.VMEM((nq, 8, 256), F32),
            pltpu.VMEM((nq, 8, 256), F32),
            pltpu.VMEM((nq, 256, 256), F32),
        ],
        compiler_params=pltpu.CompilerParams(vmem_limit_bytes=LIMIT),
        name="cross_fwd",
    )(lo, hi, start, size, q, k, vt)


def cross_bwd_kernel(
    lo_ref,
    hi_ref,
    start_ref,
    size_ref,
    q_ref,
    do_ref,
    o_ref,
    lse_ref,
    k_ref,
    v_ref,
    kt_ref,
    dq_ref,
    dk_ref,
    dv_ref,
    qs,
    qst,
    dos,
    dost,
    del_scr,
    dka,
    dva,
    dqt,
    *,
    nq,
    tiles,
    scale,
):
    dka[...] = jnp.zeros_like(dka)
    dva[...] = jnp.zeros_like(dva)

    def tile(t, _):
        st = start_ref[t]
        sz = size_ref[t]
        row = pl.ds(pl.multiple_of(t * TQ, TQ), TQ)
        for c in range(nq):
            cs = slice(c * 256, (c + 1) * 256)
            a = stack4(q_ref[row, cs])
            qs[c] = a
            qst[c] = a.T
            b = stack4(do_ref[row, cs])
            dos[c] = b
            dost[c] = b.T
            product = do_ref[row, cs].astype(F32) * o_ref[row, cs]
            total = jnp.sum(red(stack4(product).T, jnp.sum), axis=0, keepdims=True)
            del_scr[c] = jnp.broadcast_to(total, (8, 256))
            dqt[c] = jnp.zeros((256, 256), F32)

        def step(j, _):
            kr = pl.ds(pl.multiple_of(j * TK, TK), TK)
            mask = range_mask(j * TK, TK, st, sz)
            for c in range(nq):
                cs = slice(c * 256, (c + 1) * 256)
                s = dot(k_ref[kr, cs], qst[c])
                p = jnp.where(mask, jnp.exp(s - lse_ref[t, c]), 0.0)
                dp = dot(v_ref[kr, cs], dost[c])
                ds = (p * (dp - del_scr[c][0:1])).astype(BF)
                dva[kr, cs] += dot(p.astype(BF), dos[c])
                dka[kr, cs] += dot(ds, qs[c])
                dqt[c] += dot(kt_ref[cs, kr], ds)
            return 0

        lax.fori_loop(lo_ref[t], hi_ref[t], step, 0)
        for c in range(nq):
            cs = slice(c * 256, (c + 1) * 256)
            dq_ref[row, cs] = (unstack4(dqt[c].T) * scale).astype(BF)
        return 0

    lax.fori_loop(0, tiles, tile, 0)
    dk_ref[...] = dka[...].astype(BF)
    dv_ref[...] = dva[...].astype(BF)


def cross_bwd(lo, hi, start, size, q, do, o, lse, k, v, kt, scale):
    rows, width = q.shape
    tiles, keys = rows // TQ, k.shape[0]
    nq = quads_per_step(width // 256, keys)
    full = pl.BlockSpec(start.shape, lambda g: (0, 0, 0))
    own = pl.BlockSpec((rows, nq * 256), lambda g: (0, g))
    held = pl.BlockSpec((keys, nq * 256), lambda g: (0, g), pipeline_mode=pl.Buffered(1))
    out_kv = pl.BlockSpec((keys, nq * 256), lambda g: (0, g), pipeline_mode=pl.Buffered(1))
    return pl.pallas_call(
        functools.partial(cross_bwd_kernel, nq=nq, tiles=tiles, scale=scale),
        grid=(width // 256 // nq,),
        out_shape=(
            jax.ShapeDtypeStruct(q.shape, BF),
            jax.ShapeDtypeStruct(k.shape, BF),
            jax.ShapeDtypeStruct(k.shape, BF),
        ),
        in_specs=[
            SM,
            SM,
            full,
            full,
            own,
            own,
            own,
            pl.BlockSpec((tiles, nq, 1, 256), lambda g: (0, g, 0, 0)),
            held,
            held,
            pl.BlockSpec((nq * 256, keys), lambda g: (g, 0), pipeline_mode=pl.Buffered(1)),
        ],
        out_specs=(own, out_kv, out_kv),
        scratch_shapes=[pltpu.VMEM((nq, 256, 256), BF)] * 4
        + [
            pltpu.VMEM((nq, 8, 256), F32),
            pltpu.VMEM((keys, nq * 256), F32),
            pltpu.VMEM((keys, nq * 256), F32),
            pltpu.VMEM((nq, 256, 256), F32),
        ],
        compiler_params=pltpu.CompilerParams(vmem_limit_bytes=LIMIT),
        name="cross_bwd",
    )(lo, hi, start, size, q, do, o, lse, k, v, kt)


def distances():
    j = lax.broadcasted_iota(jnp.int32, (WIN, 256), 0)
    i = lax.broadcasted_iota(jnp.int32, (WIN, 256), 1) % 64
    return WIN - TQ + i - j


def fill_window(proj_ref, kp, vp, width):
    kp[0:64, :] = jnp.zeros((64, width), BF)
    vp[0:64, :] = jnp.zeros((64, width), BF)
    kp[64:, :] = proj_ref[:, width : 2 * width]
    vp[64:, :] = proj_ref[:, 2 * width : 3 * width]


def fill_bias(brow_ref, bias, nq):
    dist = distances()
    for c in range(nq):
        cs = slice(c * 256, (c + 1) * 256)

        def add(d, held):
            return jnp.where(dist == d, brow_ref[pl.ds(d, 1), cs], held)

        bias[c] = lax.fori_loop(0, brow_ref.shape[0], add, jnp.full((WIN, 256), MASKED, F32))


def self_fwd_kernel(start_ref, size_ref, brow_ref, proj_ref, o_ref, lse_ref, kp, vp, bias, *, nq, tiles, scale):
    width = nq * 256
    fill_window(proj_ref, kp, vp, width)
    fill_bias(brow_ref, bias, nq)

    def tile(t, _):
        row = pl.ds(pl.multiple_of(t * TQ, TQ), TQ)
        win = pl.ds(pl.multiple_of(t * TQ, TQ), WIN)
        mask = range_mask(t * TQ - 64, WIN, start_ref[t], size_ref[t])
        for c in range(nq):
            cs = slice(c * 256, (c + 1) * 256)
            qst = stack4(proj_ref[row, cs] * jnp.asarray(scale, BF)).T
            s = jnp.where(mask, dot(kp[win, cs], qst) + bias[c], MASKED)
            m = jnp.max(red(s, jnp.max), axis=0, keepdims=True)
            p = jnp.exp(s - m)
            l = jnp.sum(red(p, jnp.sum), axis=0, keepdims=True)
            p = (p * (1.0 / l)).astype(BF)
            o_ref[row, cs] = unstack4(dot_tn(p, vp[win, cs])).astype(BF)
            lse_ref[t, c] = m + jnp.log(l)
        return 0

    lax.fori_loop(0, tiles, tile, 0)


def self_fwd(start, size, brow, proj, scale):
    rows, width = proj.shape[0], proj.shape[1] // 3
    nq, tiles = width // 256, rows // TQ
    return pl.pallas_call(
        functools.partial(self_fwd_kernel, nq=nq, tiles=tiles, scale=scale),
        out_shape=(
            jax.ShapeDtypeStruct((rows, width), BF),
            jax.ShapeDtypeStruct((tiles, nq, 1, 256), F32),
        ),
        in_specs=[VM] * 4,
        out_specs=(VM, VM),
        scratch_shapes=[
            pltpu.VMEM((rows + 64, width), BF),
            pltpu.VMEM((rows + 64, width), BF),
            pltpu.VMEM((nq, WIN, 256), F32),
        ],
        compiler_params=pltpu.CompilerParams(vmem_limit_bytes=LIMIT),
        name="self_fwd",
    )(start, size, brow, proj)


def self_bwd_kernel(
    start_ref,
    size_ref,
    brow_ref,
    proj_ref,
    do_ref,
    lse_ref,
    dproj_ref,
    dbrow_ref,
    kp,
    vp,
    bias,
    dka,
    dva,
    dsum,
    *,
    nq,
    tiles,
    scale,
):
    width = nq * 256
    fill_window(proj_ref, kp, vp, width)
    fill_bias(brow_ref, bias, nq)
    dka[...] = jnp.zeros_like(dka)
    dva[...] = jnp.zeros_like(dva)
    dsum[...] = jnp.zeros_like(dsum)

    def tile(t, _):
        row = pl.ds(pl.multiple_of(t * TQ, TQ), TQ)
        win = pl.ds(pl.multiple_of(t * TQ, TQ), WIN)
        mask = range_mask(t * TQ - 64, WIN, start_ref[t], size_ref[t])
        for c in range(nq):
            cs = slice(c * 256, (c + 1) * 256)
            qs = stack4(proj_ref[row, cs] * jnp.asarray(scale, BF))
            dos = stack4(do_ref[row, cs])
            s = dot(kp[win, cs], qs.T) + bias[c]
            p = jnp.where(mask, jnp.exp(s - lse_ref[t, c]), 0.0)
            dp = dot(vp[win, cs], dos.T)
            delta = jnp.sum(red(p * dp, jnp.sum), axis=0, keepdims=True)
            ds = p * (dp - delta)
            dsum[c] += ds
            ds = ds.astype(BF)
            dva[win, cs] += dot(p.astype(BF), dos)
            dka[win, cs] += dot(ds, qs)
            dproj_ref[row, cs] = (unstack4(dot_tn(ds, kp[win, cs])) * scale).astype(BF)
        return 0

    lax.fori_loop(0, tiles, tile, 0)
    dproj_ref[:, width : 2 * width] = dka[64:, :].astype(BF)
    dproj_ref[:, 2 * width : 3 * width] = dva[64:, :].astype(BF)
    dist = distances()
    for c in range(nq):
        cs = slice(c * 256, (c + 1) * 256)

        def one(d, _):
            x = jnp.where(dist == d, dsum[c], 0.0)
            dbrow_ref[pl.ds(d, 1), cs] = jnp.sum(red(x, jnp.sum), axis=0, keepdims=True)
            return 0

        lax.fori_loop(0, brow_ref.shape[0], one, 0)


def self_bwd(start, size, brow, proj, do, lse, scale):
    rows, width = proj.shape[0], proj.shape[1] // 3
    nq, tiles = width // 256, rows // TQ
    return pl.pallas_call(
        functools.partial(self_bwd_kernel, nq=nq, tiles=tiles, scale=scale),
        out_shape=(jax.ShapeDtypeStruct((rows, 3 * width), BF), jax.ShapeDtypeStruct(brow.shape, F32)),
        in_specs=[VM] * 6,
        out_specs=(VM, VM),
        scratch_shapes=[
            pltpu.VMEM((rows + 64, width), BF),
            pltpu.VMEM((rows + 64, width), BF),
            pltpu.VMEM((nq, WIN, 256), F32),
            pltpu.VMEM((rows + 64, width), F32),
            pltpu.VMEM((rows + 64, width), F32),
            pltpu.VMEM((nq, WIN, 256), F32),
        ],
        compiler_params=pltpu.CompilerParams(vmem_limit_bytes=LIMIT),
        name="self_bwd",
    )(start, size, brow, proj, do, lse)


def norm_rows(x, gain):
    inverse = lax.rsqrt(jnp.mean(x * x, axis=-1, keepdims=True) + EPSILON)
    return x * inverse * gain, inverse


def norm_back(x, inverse, gain, grad):
    scaled = grad * gain
    mean = jnp.mean(x * scaled, axis=-1, keepdims=True)
    return inverse * scaled - x * inverse * inverse * inverse * mean, jnp.sum(grad * x * inverse, axis=0)


def swap(x, axis, bit):
    size = lax.axis_size(axis)
    return lax.ppermute(x, axis, [(i, i ^ bit) for i in range(size)])


def bits_of(axis):
    size = lax.axis_size(axis)
    return [1 << b for b in range(size.bit_length() - 1)]


def gather_parts(x, axis):
    parts = {0: x}
    for bit in reversed(bits_of(axis)):
        for r in list(parts):
            parts[r ^ bit] = swap(parts[r], axis, bit)
    return parts


def add_low(a, b):
    return (a.astype(F32) + b.astype(F32)).astype(BF)


def scatter_sum(x, axis, order):
    size = x.shape[0]
    live = list(range(size))
    block = x
    for bit in order:
        keep = [r for r in live if not r & bit]
        send = [r for r in live if r & bit]
        k = jnp.stack([block[live.index(r)] for r in keep])
        s = jnp.stack([block[live.index(r)] for r in send])
        block = add_low(k, swap(s, axis, bit))
        live = keep
    return block[0]


def gather_sum(x, axis, order):
    parts = [0]
    block = x[None]
    for bit in order:
        block = jnp.concatenate([block, swap(block, axis, bit)], axis=0)
        parts = parts + [r ^ bit for r in parts]
    inverse = [parts.index(r) for r in range(len(parts))]
    return block, inverse


def relative(x, axis):
    size = lax.axis_size(axis)
    me = lax.axis_index(axis)
    return jnp.stack([lax.dynamic_index_in_dim(x, me ^ r, 0, keepdims=False) for r in range(size)])


def reduce_all(x):
    blocks, rows, width = x.shape
    groups = lax.axis_size("grp")
    part = scatter_sum(relative(x, "blk"), "blk", bits_of("blk"))
    part = relative(part.reshape(groups, rows // groups, width), "grp")
    part = scatter_sum(part, "grp", bits_of("grp"))
    whole, inverse = gather_sum(part, "grp", list(reversed(bits_of("grp"))))
    me = lax.axis_index("grp")
    index = jnp.asarray(inverse, jnp.int32)[jnp.arange(groups) ^ me]
    return jnp.take(whole, index, axis=0).reshape(rows, width)


def sum_everywhere(x):
    for axis in ("blk", "grp"):
        for bit in bits_of(axis):
            x = x + swap(x, axis, bit)
    return x


def pack(grads, blocks):
    out = []
    for g in grads:
        k, n = g.shape
        r = g.reshape(blocks, k // blocks, n // 768, 768).transpose(0, 2, 1, 3)
        out.append(r.reshape(blocks, -1, 768))
    return jnp.concatenate(out, axis=1)


def unpack(rows, shapes, blocks):
    out, at = [], 0
    for k, n in shapes:
        count = k // blocks * (n // 768)
        piece = rows[at : at + count].reshape(n // 768, k // blocks, 768)
        out.append(piece.transpose(1, 0, 2).reshape(k // blocks, n).astype(F32))
        at += count
    return out


def body(
    dec_in,
    encodings,
    answer_len,
    answer_question,
    question_rows,
    bucket_table,
    gain_self,
    w_qkv,
    w_self_out,
    rel_bias,
    gain_cross,
    w_cross_q,
    w_cross_kv,
    w_cross_out,
    gain_ffn,
    w_in,
    w_out,
    cotangent,
):
    answers = answer_len.shape[0]
    length = bucket_table.shape[0]
    rows, width = dec_in.shape
    heads = rel_bias.shape[1]
    buckets = rel_bias.shape[0]
    scale = 1.0 / math.sqrt(width // heads)
    enc_rows = encodings.shape[0]
    blocks = lax.axis_size("blk")
    me = lax.axis_index("blk")
    tiles = rows // TQ
    nq = width // 256

    enc_parts = gather_parts(encodings, "blk")

    own_q = lax.dynamic_slice_in_dim(answer_question, me * answers, answers, 0)
    a_index = jnp.arange(answers)
    before = (own_q[None, :] < own_q[:, None]) | (
        (own_q[None, :] == own_q[:, None]) & (a_index[None, :] < a_index[:, None])
    )
    rank = jnp.sum(before.astype(jnp.int32), axis=1)
    target = (rank[:, None] * length + jnp.arange(length)[None, :]).reshape(rows)
    forward_perm = (jnp.arange(rows)[:, None] == target[None, :]).astype(BF)
    sorted_len = jnp.sum(jnp.where(rank[:, None] == a_index[None, :], answer_len[:, None], 0), axis=0)
    ends_q = jnp.cumsum(question_rows[0])
    starts_q = ends_q - question_rows[0]
    sorted_q = jnp.sum(jnp.where(rank[:, None] == a_index[None, :], own_q[:, None], 0), axis=0)
    token_q = jnp.repeat(sorted_q, length)
    pick = token_q[:, None] == jnp.arange(question_rows.shape[1])[None, :]
    token_start = jnp.sum(jnp.where(pick, starts_q[None, :], 0), axis=1)
    token_size = jnp.sum(jnp.where(pick, question_rows[0][None, :], 0), axis=1)

    def stacked(v):
        return jnp.tile(v.reshape(tiles, 1, TQ), (1, 1, 4)).astype(jnp.int32)

    c_start, c_size = stacked(token_start), stacked(token_size)
    lo = (token_start.reshape(tiles, TQ)[:, 0] // TK).astype(jnp.int32)
    hi = ((token_start + token_size).reshape(tiles, TQ)[:, -1] + TK - 1) // TK
    hi = hi.astype(jnp.int32)
    s_start = stacked(jnp.arange(rows) // length * length)
    s_size = stacked(jnp.repeat(sorted_len, length))

    bucket_hot = (bucket_table[:, None] == jnp.arange(buckets)[None, :]).astype(F32)
    brow = jnp.repeat(
        jnp.dot(bucket_hot, rel_bias, precision=lax.Precision.HIGHEST), width // heads, axis=1
    )

    x0 = dot(forward_perm, dec_in)
    grad_top = dot(forward_perm, cotangent)
    grad_low = grad_top.astype(BF)
    n1, r1 = norm_rows(x0, gain_self)
    h1 = n1.astype(BF)
    proj = dot(h1, w_qkv).astype(BF)
    o_self, lse_self = self_fwd(s_start, s_size, brow, proj, scale)
    x1 = x0 + dot(o_self, w_self_out)
    n2, r2 = norm_rows(x1, gain_cross)
    h2 = n2.astype(BF)
    qc = (dot(h2, w_cross_q).astype(BF) * jnp.asarray(scale, BF)).astype(BF)

    enc_rel = jnp.stack([enc_parts[r] for r in range(blocks)])
    enc_all = relative(enc_rel, "blk").reshape(blocks * enc_rows, width)
    kv = dot(enc_all, w_cross_kv).astype(BF)
    k_all, v_all = kv[:, :width], kv[:, width:]
    kvt = lax.dot_general(w_cross_kv, enc_all, (((0,), (1,)), ((), ())), preferred_element_type=F32).astype(BF)
    kt_all, vt_all = kvt[:width], kvt[width:]

    o_cross, lse_cross = cross_fwd(lo, hi, c_start, c_size, qc, k_all, vt_all)
    oc = o_cross.astype(BF)
    x2 = x1 + dot(oc, w_cross_out)
    n3, r3 = norm_rows(x2, gain_ffn)
    h3 = n3.astype(BF)
    hidden, gelu_back = jax.vjp(jax.nn.gelu, dot(h3, w_in))
    u = hidden.astype(BF)
    out = (x2 + dot(u, w_out)).astype(BF)
    layer_out = dot_tn(forward_perm, out).astype(BF)

    d_w_out = dot_tn(u, grad_low).astype(BF)
    da = gelu_back(dot_nt(grad_low, w_out))[0].astype(BF)
    d_w_in = dot_tn(h3, da).astype(BF)
    sums_out = reduce_all(pack([d_w_out], blocks))
    sums_in = reduce_all(pack([d_w_in], blocks))
    dx3, d_gain_ffn = norm_back(x2, r3, gain_ffn, dot_nt(da, w_in))
    dx2 = grad_top + dx3
    dyc = dx2.astype(BF)
    d_w_cross_out = dot_tn(oc, dyc).astype(BF)
    d_o = dot_nt(dyc, w_cross_out).astype(BF)
    dqc, dk, dv = cross_bwd(
        lo, hi, c_start, c_size, qc, d_o, o_cross, lse_cross, k_all, v_all, kt_all, scale
    )

    dkv = jnp.concatenate([dk, dv], axis=1).reshape(blocks, enc_rows, 2 * width)
    dkv = relative(dkv, "blk")
    dkv = add_low(dkv[0::2], swap(dkv[1::2], "blk", 1))
    enc_half = enc_rel[0::2]
    dkv_flat = dkv.reshape(-1, 2 * width)
    d_w_cross_kv = dot_tn(enc_half.reshape(-1, width), dkv_flat).astype(BF)
    d_enc = dot_nt(dkv_flat, w_cross_kv).reshape(blocks // 2, enc_rows, width)
    d_enc_parts = {2 * r: d_enc[r] for r in range(blocks // 2)}
    for bit in reversed(bits_of("blk")[1:]):
        for r in [r for r in d_enc_parts if r & bit]:
            came = swap(d_enc_parts.pop(r).astype(BF), "blk", bit)
            d_enc_parts[r ^ bit] = d_enc_parts[r ^ bit] + came.astype(F32)
    d_encodings = d_enc_parts[0]

    d_w_cross_q = dot_tn(h2, dqc).astype(BF)
    sums_cross = reduce_all(pack([d_w_cross_out, d_w_cross_q, d_w_cross_kv], blocks))
    dx_two, d_gain_cross = norm_back(x1, r2, gain_cross, dot_nt(dqc, w_cross_q))
    dx1 = dx2 + dx_two
    dy1 = dx1.astype(BF)
    d_w_self_out = dot_tn(o_self, dy1).astype(BF)
    d_os = dot_nt(dy1, w_self_out).astype(BF)
    dproj, dbrow = self_bwd(s_start, s_size, brow, proj, d_os, lse_self, scale)
    d_w_qkv = dot_tn(h1, dproj).astype(BF)
    sums_self = reduce_all(pack([d_w_qkv, d_w_self_out], blocks))
    dx_one, d_gain_self = norm_back(x0, r1, gain_self, dot_nt(dproj, w_qkv))
    d_rel = jnp.dot(
        bucket_hot.T, jnp.sum(dbrow.reshape(length, heads, -1), axis=2), precision=lax.Precision.HIGHEST
    )
    d_x0 = dx1 + dx_one
    high = d_x0.astype(BF)
    low = (d_x0 - high.astype(F32)).astype(BF)
    d_dec_in = dot_tn(forward_perm, high) + dot_tn(forward_perm, low)

    small = jnp.concatenate([d_gain_self, d_gain_cross, d_gain_ffn, d_rel.reshape(-1)])
    small = sum_everywhere(small.reshape(-1, 128)).reshape(-1)

    def own(v):
        return lax.dynamic_slice_in_dim(v, me * (v.shape[0] // blocks), v.shape[0] // blocks, 0)

    g_self, g_cross, g_ffn = (own(small[i * width : (i + 1) * width]) for i in range(3))
    g_rel = own(small[3 * width :].reshape(buckets, heads))
    (o_wout,) = unpack(sums_out, [w_out.shape], blocks)
    (o_win,) = unpack(sums_in, [w_in.shape], blocks)
    o_wco, o_wcq, o_wckv = unpack(sums_cross, [w_cross_out.shape, w_cross_q.shape, w_cross_kv.shape], blocks)
    o_wqkv, o_wso = unpack(sums_self, [w_qkv.shape, w_self_out.shape], blocks)
    return (
        layer_out,
        d_dec_in,
        d_encodings,
        g_self,
        o_wqkv,
        o_wso,
        g_rel,
        g_cross,
        o_wcq,
        o_wckv,
        o_wco,
        g_ffn,
        o_win,
        o_wout,
    )


def slot_of(rel):
    return (rel & 1) * 4 + (rel & 2) + ((rel >> 2) & 1)


def gelu_both(a):
    c = math.sqrt(2.0 / math.pi)
    a2 = a * a
    t = jnp.tanh(c * (a + 0.044715 * (a2 * a)))
    half = 0.5 * (1.0 + t)
    return a * half, half + 0.5 * a * (1.0 - t * t) * (c * (1.0 + 3.0 * 0.044715 * a2))


def rms(x):
    return lax.rsqrt(jnp.mean(x * x, axis=-1, keepdims=True) + EPSILON)


def rms_back(x, inverse, gain, grad):
    scaled = grad * gain
    mean = jnp.mean(x * scaled, axis=-1, keepdims=True)
    unit = x * inverse
    return inverse * (scaled - unit * (inverse * mean)), jnp.sum(grad * unit, axis=0, keepdims=True)


def onehot_rows(src):
    n = src.shape[1]
    return (lax.broadcasted_iota(jnp.int32, (n, n), 0) == src).astype(F32).astype(BF)


def pre_kernel(
    me_ref,
    aq_ref,
    len_ref,
    qrows_ref,
    bucket_ref,
    dec_ref,
    gain1_ref,
    rel_ref,
    wqkv_ref,
    src_ref,
    cstart_ref,
    csize_ref,
    sstart_ref,
    ssize_ref,
    lo_ref,
    hi_ref,
    brow_ref,
    x0_ref,
    h1_ref,
    proj_ref,
    oself_ref,
    lse_ref,
    order,
    qstart,
    qcount,
    wide,
    kp,
    vp,
    bias,
    *,
    answers,
    length,
    questions,
    scale,
):
    rows, width = dec_ref.shape
    nq, tiles = width // 256, rows // TQ
    base = me_ref[0] * answers
    n = jnp.int32(0)
    first_row = jnp.int32(0)
    for c in range(questions):
        qstart[c] = first_row
        first_row = first_row + qrows_ref[0, c]
        qcount[c] = n

        def visit(a, n):
            hit = aq_ref[base + a] == c

            @pl.when(hit)
            def _():
                order[n] = a

            return n + hit.astype(jnp.int32)

        n = lax.fori_loop(0, answers, visit, n)

    def answer_of(tok):
        ans = jnp.zeros_like(tok)
        for k in range(1, answers):
            ans = ans + (tok >= k * length).astype(jnp.int32)
        return ans

    tok = lax.broadcasted_iota(jnp.int32, (1, rows), 1)
    ans = answer_of(tok)
    src = tok - ans * length
    for k in range(answers):
        src = src + jnp.where(ans == k, order[k] * length, 0)
    src_ref[...] = src

    lane = lax.broadcasted_iota(jnp.int32, (tiles, 256), 1) % TQ
    tok = lane + TQ * lax.broadcasted_iota(jnp.int32, (tiles, 256), 0)
    ans = answer_of(tok)
    sstart_ref[...] = ans * length
    size = jnp.zeros_like(ans)
    for k in range(answers):
        size = size + jnp.where(ans == k, len_ref[order[k]], 0)
    ssize_ref[...] = size
    cstart = jnp.zeros_like(ans)
    csize = jnp.zeros_like(ans) + qrows_ref[0, 0]
    for c in range(1, questions):
        here = ans >= qcount[c]
        cstart = jnp.where(here, qstart[c], cstart)
        csize = jnp.where(here, qrows_ref[0, c], csize)
    cstart_ref[...] = cstart
    csize_ref[...] = csize
    for t in range(tiles):
        q_first = aq_ref[base + order[t * TQ // length]]
        q_last = aq_ref[base + order[(t * TQ + TQ - 1) // length]]
        lo_ref[t] = qstart[q_first] // TK
        hi_ref[t] = (qstart[q_last] + qrows_ref[0, q_last] + TK - 1) // TK

    for c in range(nq):
        head = lax.broadcasted_iota(jnp.int32, (rel_ref.shape[0], 256), 1) // 64
        held = jnp.zeros((rel_ref.shape[0], 256), F32)
        for a in range(4):
            h = c * 4 + a
            held = jnp.where(head == a, rel_ref[:, h : h + 1], held)
        wide[:, c * 256 : (c + 1) * 256] = held
    for d in range(length):
        brow_ref[d : d + 1, :] = wide[pl.ds(bucket_ref[d], 1), :]

    x0 = dot_tn(onehot_rows(src), dec_ref[...])
    x0_ref[...] = x0.astype(BF)
    h1_ref[...] = (x0 * rms(x0) * gain1_ref[...]).astype(BF)
    for i in range(3):
        cs = slice(i * width, (i + 1) * width)
        proj_ref[:, cs] = dot(h1_ref[...], wqkv_ref[:, cs]).astype(BF)
    fill_window(proj_ref, kp, vp, width)
    fill_bias(brow_ref, bias, nq)

    def tile(t, _):
        row = pl.ds(pl.multiple_of(t * TQ, TQ), TQ)
        win = pl.ds(pl.multiple_of(t * TQ, TQ), WIN)
        mask = range_mask(t * TQ - 64, WIN, sstart_ref[pl.ds(t, 1), :], ssize_ref[pl.ds(t, 1), :])
        for c in range(nq):
            cs = slice(c * 256, (c + 1) * 256)
            qst = stack4(proj_ref[row, cs] * jnp.asarray(scale, BF)).T
            s = jnp.where(mask, dot(kp[win, cs], qst) + bias[c], MASKED)
            m = jnp.max(red(s, jnp.max), axis=0, keepdims=True)
            p = jnp.exp(s - m)
            l = jnp.sum(red(p, jnp.sum), axis=0, keepdims=True)
            p = (p * (1.0 / l)).astype(BF)
            oself_ref[row, cs] = unstack4(dot_tn(p, vp[win, cs])).astype(BF)
            lse_ref[t, c] = m + jnp.log(l)
        return 0

    lax.fori_loop(0, tiles, tile, 0)


def mid_kernel(x0_ref, oself_ref, wso_ref, gain2_ref, wcq_ref, x1_ref, h2_ref, qc_ref, *, scale):
    x1 = x0_ref[...].astype(F32) + dot(oself_ref[...], wso_ref[...])
    x1_ref[...] = x1
    h2_ref[...] = (x1 * rms(x1) * gain2_ref[...]).astype(BF)
    qc_ref[...] = dot(h2_ref[...], wcq_ref[...]).astype(BF) * jnp.asarray(scale, BF)


def mid(x0, oself, wso, gain, wcq, scale):
    rows, width = x0.shape
    return call(
        functools.partial(mid_kernel, scale=scale),
        "mid",
        (sds((rows, width), F32), sds((rows, width), BF), sds((rows, width), BF)),
        [VM] * 5,
        (VM,) * 3,
        [],
        (x0, oself, wso, gain, wcq),
        us=8,
    )


def call(kernel, name, out_shape, in_specs, out_specs, scratch, args, us):
    moved = sum(math.prod(a.shape) * a.dtype.itemsize for a in args)
    moved += sum(math.prod(a.shape) * a.dtype.itemsize for a in out_shape)
    return pl.pallas_call(
        kernel,
        out_shape=out_shape,
        in_specs=in_specs,
        out_specs=out_specs,
        scratch_shapes=scratch,
        compiler_params=pltpu.CompilerParams(vmem_limit_bytes=LIMIT),
        cost_estimate=pl.CostEstimate(flops=int(us * 1e11), bytes_accessed=moved, transcendentals=0),
        name=name,
    )(*args)


def sds(shape, dtype):
    return jax.ShapeDtypeStruct(shape, dtype)


def pre(me, aq, lens, qrows, bucket, dec, g1, rel, wqkv, scale):
    rows, width = dec.shape
    tiles, nq, length = rows // TQ, width // 256, bucket.shape[0]
    i32 = jnp.int32
    meta = sds((tiles, 256), i32)
    out = (
        sds((1, rows), i32),
        meta,
        meta,
        meta,
        meta,
        sds((tiles,), i32),
        sds((tiles,), i32),
        sds((length, width), F32),
        sds((rows, width), BF),
        sds((rows, width), BF),
        sds((rows, 3 * width), BF),
        sds((rows, width), BF),
        sds((tiles, nq, 1, 256), F32),
    )
    return call(
        functools.partial(
            pre_kernel, answers=lens.shape[0], length=length, questions=qrows.shape[1], scale=scale
        ),
        "pre",
        out,
        [SM] * 5 + [VM] * 4,
        (VM,) * 5 + (SM, SM) + (VM,) * 6,
        [
            pltpu.SMEM((lens.shape[0],), i32),
            pltpu.SMEM((qrows.shape[1],), i32),
            pltpu.SMEM((qrows.shape[1],), i32),
            pltpu.VMEM((rel.shape[0], width), F32),
            pltpu.VMEM((rows + 64, width), BF),
            pltpu.VMEM((rows + 64, width), BF),
            pltpu.VMEM((nq, WIN, 256), F32),
        ],
        (me, aq, lens, qrows, bucket, dec, g1, rel, wqkv),
        us=40,
    )


def own_heads(x):
    return jnp.concatenate([x[a * 64 : (a + 1) * 64, a * TQ : (a + 1) * TQ] for a in range(4)], axis=0)


def in_pairs(lo, hi, work):
    def two(i, _):
        work(lo + 2 * i)
        work(lo + 2 * i + 1)
        return 0

    lax.fori_loop(0, (hi - lo) // 2, two, 0)

    @pl.when((hi - lo) % 2 == 1)
    def _():
        work(hi - 1)


def kv_cross_kernel(
    me_ref,
    lo_ref,
    hi_ref,
    start_ref,
    size_ref,
    q_ref,
    *rest,
    pieces,
):
    enc = rest[:pieces]
    wkv_ref, k_ref, v_ref, kt_ref, o_ref, lse_ref, vt, qst, s_scr, m_scr, l_scr, acc = rest[pieces:]
    rows, width = q_ref.shape
    nq, tiles = width // 256, rows // TQ
    n = enc[0].shape[0]
    for r in range(pieces):
        at = pl.ds(pl.multiple_of((me_ref[0] ^ r) * n, n), n)
        kk = dot(enc[r][...], wkv_ref[:, :width]).astype(BF)
        k_ref[at, :] = kk
        kt_ref[:, at] = kk.T
        vv = dot(enc[r][...], wkv_ref[:, width:]).astype(BF)
        v_ref[at, :] = vv
        vt[:, at] = vv.T

    def tile(t, _):
        st = start_ref[pl.ds(t, 1), :]
        sz = size_ref[pl.ds(t, 1), :]
        lo = lo_ref[t]
        hi = hi_ref[t]
        row = pl.ds(pl.multiple_of(t * TQ, TQ), TQ)
        for c in range(nq):
            qst[c] = stack4(q_ref[row, c * 256 : (c + 1) * 256])
            m_scr[c] = jnp.full((8, 256), NEG, F32)
            l_scr[c] = jnp.zeros((8, 256), F32)
            acc[c] = jnp.zeros((256, 256), F32)

        def scores(j):
            kr = pl.ds(pl.multiple_of(j * TK, TK), TK)
            mask = range_mask(j * TK, TK, st, sz)
            for c in range(nq):
                s = dot_nt(k_ref[kr, c * 256 : (c + 1) * 256], qst[c])
                s = jnp.where(mask, s, NEG)
                s_scr[c, kr, :] = s
                m_scr[c] = jnp.maximum(m_scr[c], red(s, jnp.max))

        in_pairs(lo, hi, scores)
        for c in range(nq):
            m_scr[c] = jnp.broadcast_to(jnp.max(m_scr[c], axis=0, keepdims=True), (8, 256))

        def mix(j):
            kr = pl.ds(pl.multiple_of(j * TK, TK), TK)
            for c in range(nq):
                p = jnp.exp(s_scr[c, kr, :] - m_scr[c][0:1])
                l_scr[c] += red(p, jnp.sum)
                acc[c] += dot(vt[c * 256 : (c + 1) * 256, kr], p.astype(BF))

        in_pairs(lo, hi, mix)
        for c in range(nq):
            l = jnp.sum(l_scr[c], axis=0, keepdims=True)
            lse_ref[t, c] = m_scr[c][0:1] + jnp.log(l)
            o_ref[row, c * 256 : (c + 1) * 256] = own_heads(acc[c] * (1.0 / l)).T
        return 0

    lax.fori_loop(0, tiles, tile, 0)


def kv_cross(me, lo, hi, start, size, q, enc, wkv):
    rows, width = q.shape
    tiles, nq = rows // TQ, width // 256
    keys = len(enc) * enc[0].shape[0]
    return call(
        functools.partial(kv_cross_kernel, pieces=len(enc)),
        "kv_cross",
        (
            sds((keys, width), BF),
            sds((keys, width), BF),
            sds((width, keys), BF),
            sds((rows, width), F32),
            sds((tiles, nq, 1, 256), F32),
        ),
        [SM] * 3 + [VM] * (3 + len(enc) + 1),
        (VM,) * 5,
        [
            pltpu.VMEM((width, keys), BF),
            pltpu.VMEM((nq, 256, 256), BF),
            pltpu.VMEM((nq, keys, 256), F32),
            pltpu.VMEM((nq, 8, 256), F32),
            pltpu.VMEM((nq, 8, 256), F32),
            pltpu.VMEM((nq, 256, 256), F32),
        ],
        (me, lo, hi, start, size, q, *enc, wkv),
        us=80,
    )


def ffn_kernel(
    me_ref,
    src_ref,
    x1_ref,
    ocross_ref,
    gain_ref,
    cot_ref,
    wco_ref,
    win_ref,
    wout_ref,
    keep_ref,
    send_ref,
    x2_ref,
    dh_ref,
    g_ref,
    oc_ref,
    out_ref,
    h3,
    h3t,
    out_acc,
    *,
    last,
):
    i = pl.program_id(0)
    me_b, me_g = me_ref[0], me_ref[1]
    f = me_b ^ i
    rows, width = x1_ref.shape
    quarter = width // 4
    half = quarter // 2

    @pl.when(i == 0)
    def _():
        hot = onehot_rows(src_ref[...])
        g_ref[...] = dot_tn(hot, cot_ref[...]).astype(BF)
        oc = ocross_ref[...].astype(BF)
        oc_ref[...] = oc
        x2 = x1_ref[...] + dot(oc, wco_ref[...])
        x2_ref[...] = x2
        n = (x2 * rms(x2) * gain_ref[...]).astype(BF)
        h3[...] = n
        h3t[...] = n.T
        out_acc[...] = jnp.zeros_like(out_acc)
        dh_ref[...] = jnp.zeros_like(dh_ref)

    u, slope = gelu_both(dot(h3[...], win_ref[...]))
    u = u.astype(BF)
    out_acc[...] += dot(u, wout_ref[...])
    da = (slope * dot_nt(g_ref[...], wout_ref[...])).astype(BF)
    dh_ref[...] += dot_nt(da, win_ref[...])
    dwo = dot_tn(u, g_ref[...]).astype(BF)
    for s in range(8):
        at = (i >> 1) * 8 + slot_of(me_g ^ s)

        @pl.when((i & 1) == 0)
        def _():
            keep_ref[at, half:, :] = dwo[s * half : (s + 1) * half]

        @pl.when((i & 1) == 1)
        def _():
            send_ref[at, half:, :] = dwo[s * half : (s + 1) * half]

    for r in range(4):
        part = h3t[pl.ds(pl.multiple_of((me_b ^ r) * quarter, quarter), quarter), :]
        dwi = dot(part, da).astype(BF)
        target = send_ref if r & 1 else keep_ref
        for b in range(2):
            rel = me_g ^ (2 * f + b)
            at = (rel & 1) * 8 + (r >> 1) * 4 + (rel & 2) + ((rel >> 2) & 1)
            target[at, :half, :] = dwi[b * half : (b + 1) * half]

    @pl.when(i == last)
    def _():
        out = (x2_ref[...] + out_acc[...]).astype(BF)
        out_ref[...] = dot(onehot_rows(src_ref[...]), out).astype(BF)


def ffn(me, src, x1, ocross, gain, cot, wco, win, wout):
    rows, width = x1.shape
    steps = win.shape[1] // width
    half = width // 8
    full = lambda a: pl.BlockSpec(a.shape, lambda i, m: (0,) * len(a.shape))
    outs = (
        sds((16, 2 * half, width), BF),
        sds((16, 2 * half, width), BF),
        sds((rows, width), F32),
        sds((rows, width), F32),
        sds((rows, width), BF),
        sds((rows, width), BF),
        sds((rows, width), BF),
    )
    ins = (src, x1, ocross, gain, cot, wco)
    grid_spec = pltpu.PrefetchScalarGridSpec(
        num_scalar_prefetch=1,
        grid=(steps,),
        in_specs=[full(a) for a in ins]
        + [
            pl.BlockSpec((width, width), lambda i, m: (0, m[0] ^ i)),
            pl.BlockSpec((width, width), lambda i, m: (m[0] ^ i, 0)),
        ],
        out_specs=tuple(full(a) for a in outs),
        scratch_shapes=[
            pltpu.VMEM((rows, width), BF),
            pltpu.VMEM((width, rows), BF),
            pltpu.VMEM((rows, width), F32),
        ],
    )
    return pl.pallas_call(
        functools.partial(ffn_kernel, last=steps - 1),
        out_shape=outs,
        grid_spec=grid_spec,
        compiler_params=pltpu.CompilerParams(vmem_limit_bytes=LIMIT),
        cost_estimate=pl.CostEstimate(flops=60 * 10**11, bytes_accessed=30 << 20, transcendentals=0),
        name="ffn",
    )(me, *ins, win, wout)


def ffn_back_kernel(x2_ref, dh_ref, g_ref, gain_ref, wco_ref, dx2_ref, dyc_ref, do_ref, dgain_ref):
    x2 = x2_ref[...]
    dx, dgain_ref[...] = rms_back(x2, rms(x2), gain_ref[...], dh_ref[...])
    dx2 = g_ref[...].astype(F32) + dx
    dx2_ref[...] = dx2
    dyc_ref[...] = dx2.astype(BF)
    do_ref[...] = dot_nt(dyc_ref[...], wco_ref[...]).astype(BF)


def ffn_back(x2, dh, g, gain, wco):
    rows, width = x2.shape
    return call(
        ffn_back_kernel,
        "ffn_back",
        (sds((rows, width), F32), sds((rows, width), BF), sds((rows, width), BF), sds((1, width), F32)),
        [VM] * 5,
        (VM,) * 4,
        [],
        (x2, dh, g, gain, wco),
        us=30,
    )


def cross_back_kernel(
    me_ref,
    lo_ref,
    hi_ref,
    start_ref,
    size_ref,
    q_ref,
    do_ref,
    o_ref,
    lse_ref,
    k_ref,
    v_ref,
    kt_ref,
    dq_ref,
    keep_ref,
    send_ref,
    qs,
    dos,
    del_scr,
    dka,
    dva,
    dqt,
    ps,
    dss,
    *,
    scale,
):
    rows, width = q_ref.shape
    nq, tiles = width // 256, rows // TQ
    dka[...] = jnp.zeros_like(dka)
    dva[...] = jnp.zeros_like(dva)

    def tile(t, _):
        st = start_ref[pl.ds(t, 1), :]
        sz = size_ref[pl.ds(t, 1), :]
        row = pl.ds(pl.multiple_of(t * TQ, TQ), TQ)
        for c in range(nq):
            cs = slice(c * 256, (c + 1) * 256)
            qs[c] = stack4(q_ref[row, cs])
            b = do_ref[row, cs]
            dos[c] = stack4(b)
            product = (b.astype(F32) * o_ref[row, cs]).T
            total = jnp.concatenate(
                [jnp.sum(product[h * 64 : (h + 1) * 64], axis=0, keepdims=True) for h in range(4)], axis=1
            )
            del_scr[c] = jnp.broadcast_to(total, (8, 256))
            dqt[c] = jnp.zeros((256, 256), F32)

        def probs(j, slot):
            kr = pl.ds(pl.multiple_of(j * TK, TK), TK)
            mask = range_mask(j * TK, TK, st, sz)
            for c in range(nq):
                cs = slice(c * 256, (c + 1) * 256)
                s = dot_nt(k_ref[kr, cs], qs[c])
                p = jnp.where(mask, jnp.exp(s - lse_ref[t, c]), 0.0)
                dp = dot_nt(v_ref[kr, cs], dos[c])
                ps[slot, c] = p.astype(BF)
                dss[slot, c] = (p * (dp - del_scr[c][0:1])).astype(BF)

        def grads(j, slot):
            kr = pl.ds(pl.multiple_of(j * TK, TK), TK)
            for c in range(nq):
                cs = slice(c * 256, (c + 1) * 256)
                ds = dss[slot, c]
                dva[kr, cs] += dot(ps[slot, c], dos[c])
                dka[kr, cs] += dot(ds, qs[c])
                dqt[c] += dot(kt_ref[cs, kr], ds)

        lo = lo_ref[t]
        hi = hi_ref[t]

        def two(i, _):
            probs(lo + 2 * i, 0)
            probs(lo + 2 * i + 1, 1)
            grads(lo + 2 * i, 0)
            grads(lo + 2 * i + 1, 1)
            return 0

        lax.fori_loop(0, (hi - lo) // 2, two, 0)

        @pl.when((hi - lo) % 2 == 1)
        def _():
            probs(hi - 1, 0)
            grads(hi - 1, 0)

        for c in range(nq):
            cs = slice(c * 256, (c + 1) * 256)
            dq_ref[row, cs] = (own_heads(dqt[c]).T * scale).astype(BF)
        return 0

    lax.fori_loop(0, tiles, tile, 0)
    n = keep_ref.shape[1]
    for r in range(4):
        at = pl.ds(pl.multiple_of((me_ref[0] ^ r) * n, n), n)
        target = send_ref if r & 1 else keep_ref
        target[r >> 1, :, :width] = dka[at, :].astype(BF)
        target[r >> 1, :, width:] = dva[at, :].astype(BF)


def cross_back(me, lo, hi, start, size, q, do, o, lse, k, v, kt, scale, first, nq):
    rows = q.shape[0]
    keys, width = k.shape[0], nq * 256
    tiles = rows // TQ
    at = first // nq
    part = sds((2, keys // 4, 2 * width), BF)
    cols = lambda n: pl.BlockSpec((n, width), lambda i: (0, at))
    whole = lambda a: pl.BlockSpec(a.shape, lambda i: (0,) * len(a.shape))
    outs = (sds((rows, width), BF), part, part)
    return pl.pallas_call(
        functools.partial(cross_back_kernel, scale=scale),
        grid=(1,),
        out_shape=outs,
        in_specs=[
            SM,
            SM,
            SM,
            whole(start),
            whole(size),
            cols(rows),
            cols(rows),
            cols(rows),
            pl.BlockSpec((tiles, nq, 1, 256), lambda i: (0, at, 0, 0)),
            cols(keys),
            cols(keys),
            pl.BlockSpec((width, keys), lambda i: (at, 0)),
        ],
        out_specs=tuple(whole(a) for a in outs),
        scratch_shapes=[pltpu.VMEM((nq, 256, 256), BF)] * 2
        + [
            pltpu.VMEM((nq, 8, 256), F32),
            pltpu.VMEM((keys, width), F32),
            pltpu.VMEM((keys, width), F32),
            pltpu.VMEM((nq, 256, 256), F32),
            pltpu.VMEM((2, nq, 256, 256), BF),
            pltpu.VMEM((2, nq, 256, 256), BF),
        ],
        compiler_params=pltpu.CompilerParams(vmem_limit_bytes=LIMIT),
        cost_estimate=pl.CostEstimate(flops=10**13, bytes_accessed=30 << 20, transcendentals=0),
        name="cross_back",
    )(me, lo, hi, start, size, q, do, o, lse, k, v, kt)


def cross_in_kernel(
    dq0_ref, dq1_ref, x1_ref, dx2_ref, gain_ref, wcq_ref, wso_ref, dx1_ref, dy1_ref, dos_ref, dgain_ref
):
    x1 = x1_ref[...]
    cut = dq0_ref.shape[1]
    back = dot_nt(dq0_ref[...], wcq_ref[:, :cut]) + dot_nt(dq1_ref[...], wcq_ref[:, cut:])
    dx, dgain_ref[...] = rms_back(x1, rms(x1), gain_ref[...], back)
    dx1 = dx2_ref[...] + dx
    dx1_ref[...] = dx1
    dy1_ref[...] = dx1.astype(BF)
    dos_ref[...] = dot_nt(dy1_ref[...], wso_ref[...]).astype(BF)


def cross_in(dq0, dq1, x1, dx2, gain, wcq, wso):
    rows, width = x1.shape
    return call(
        cross_in_kernel,
        "cross_in",
        (sds((rows, width), F32), sds((rows, width), BF), sds((rows, width), BF), sds((1, width), F32)),
        [VM] * 7,
        (VM,) * 4,
        [],
        (dq0, dq1, x1, dx2, gain, wcq, wso),
        us=60,
    )


def put_pieces(me_b, me_g, left_t, right, block, keep_ref, send_ref):
    width = left_t.shape[0]
    quarter = width // 4
    tall, wide = quarter // 4, width // 2
    for r in range(4):
        part = left_t[pl.ds(pl.multiple_of((me_b ^ r) * quarter, quarter), quarter), :]
        grad = dot(part, right).astype(BF)
        target = send_ref if r & 1 else keep_ref
        for s in range(8):
            at = (r >> 1) * 8 + slot_of(me_g ^ s)
            y, x = (s >> 1) * tall, (s & 1) * wide
            target[at, block * tall : (block + 1) * tall, :] = grad[y : y + tall, x : x + wide]


def cross_weights_kernel(
    me_ref, keep0_ref, came0_ref, keep1_ref, came1_ref, enc0_ref, enc2_ref, wkv_ref, oc_ref, dyc_ref, h2_ref,
    dq0_ref, dq1_ref, keep_ref, send_ref, own_ref, out_ref, both, enc_t, left_t,
):
    n = keep0_ref.shape[1]
    width = oc_ref.shape[1]
    cut = dq0_ref.shape[1]
    for r in range(2):
        rows = slice(r * n, (r + 1) * n)
        for keep, came, at, wide in ((keep0_ref, came0_ref, 0, cut), (keep1_ref, came1_ref, cut, width - cut)):
            total = (keep[r].astype(F32) + came[r].astype(F32)).astype(BF)
            both[rows, at : at + wide] = total[:, :wide]
            both[rows, width + at : width + at + wide] = total[:, wide:]
    out_ref[...] = dot_nt(both[n:, :], wkv_ref[...]).astype(BF)
    own_ref[...] = dot_nt(both[:n, :], wkv_ref[...])
    enc_t[:, :n] = enc0_ref[...].T
    enc_t[:, n:] = enc2_ref[...].T
    me_b, me_g = me_ref[0], me_ref[1]
    put_pieces(me_b, me_g, enc_t, both[:, :width], 2, keep_ref, send_ref)
    put_pieces(me_b, me_g, enc_t, both[:, width:], 3, keep_ref, send_ref)
    left_t[...] = oc_ref[...].T
    put_pieces(me_b, me_g, left_t, dyc_ref[...], 0, keep_ref, send_ref)
    left_t[...] = h2_ref[...].T
    dq = jnp.concatenate([dq0_ref[...], dq1_ref[...]], axis=1)
    put_pieces(me_b, me_g, left_t, dq, 1, keep_ref, send_ref)


def cross_weights(me, keep0, came0, keep1, came1, enc0, enc2, wkv, oc, dyc, h2, dq0, dq1):
    rows, width = oc.shape
    n = enc0.shape[0]
    part = sds((16, width // 4, width // 2), BF)
    return call(
        cross_weights_kernel,
        "cross_weights",
        (part, part, sds((n, width), F32), sds((n, width), BF)),
        [SM] + [VM] * 12,
        (VM,) * 4,
        [pltpu.VMEM((2 * n, 2 * width), BF), pltpu.VMEM((width, 2 * n), BF), pltpu.VMEM((width, rows), BF)],
        (me, keep0, came0, keep1, came1, enc0, enc2, wkv, oc, dyc, h2, dq0, dq1),
        us=30,
    )


def late_kernel(
    start_ref,
    size_ref,
    bucket_ref,
    brow_ref,
    proj_ref,
    do_ref,
    lse_ref,
    h1_ref,
    oself_ref,
    dy1_ref,
    src_ref,
    x0_ref,
    gain_ref,
    dx1_ref,
    wqkv_ref,
    dg2_ref,
    dg3_ref,
    ck,
    cs,
    d_ref,
    small_ref,
    f_ref,
    kp,
    vp,
    bias,
    dka,
    dva,
    dsum,
    dproj,
    left_t,
    sk,
    ss,
    high,
    low,
    drow,
    sm_in,
    dgain,
    q,
    r1,
    r2,
    r3,
    r4,
    r5,
    f,
    send_sem,
    recv_sem,
    sm_send,
    sm_recv,
    *,
    scale,
):
    rows, width = do_ref.shape
    nq, tiles = width // 256, rows // TQ
    length, buckets = brow_ref.shape[0], 32
    count, step_rows = q.shape[0], q.shape[2]
    per = ck.shape[1] // step_rows
    each = width // 16 // step_rows
    early = per + each
    g, b = lax.axis_index("grp"), lax.axis_index("blk")
    peers = [(g, b ^ 1), (g, b ^ 2), (g ^ 1, b), (g ^ 2, b), (g ^ 4, b), (g ^ 4, b), (g ^ 2, b), (g ^ 1, b)]
    mesh_id = pl.DeviceIdType.MESH
    barrier = pltpu.get_barrier_semaphore()
    for p in peers[:5]:
        pl.semaphore_signal(barrier, inc=1, device_id=p, device_id_type=mesh_id)
    pl.semaphore_wait(barrier, 5)

    def rows_of(j):
        j = j - per * (j >= per).astype(jnp.int32) if not isinstance(j, int) else j % per
        return pl.ds(pl.multiple_of(j * step_rows, step_rows), step_rows)

    def copy(k, j, first=None):
        src, dst = [
            lambda: (first.at[:, rows_of(j), :], r1.at[j]),
            lambda: (q.at[j, pl.ds(8, 8)], r2.at[j]),
            lambda: (q.at[j, pl.ds(4, 4)], r3.at[j]),
            lambda: (q.at[j, pl.ds(2, 2)], r4.at[j]),
            lambda: (q.at[j, pl.ds(1, 1)], r5.at[j]),
            lambda: (f.at[j, pl.ds(0, 1)], f.at[j, pl.ds(1, 1)]),
            lambda: (f.at[j, pl.ds(0, 2)], f.at[j, pl.ds(2, 2)]),
            lambda: (f.at[j, pl.ds(0, 4)], f.at[j, pl.ds(4, 4)]),
        ][k]()
        return pltpu.make_async_remote_copy(
            src_ref=src,
            dst_ref=dst,
            send_sem=send_sem.at[k, j],
            recv_sem=recv_sem.at[k, j],
            device_id=peers[k],
            device_id_type=mesh_id,
        )

    def add(x, y):
        return (x.astype(F32) + y.astype(F32)).astype(BF)

    def event(k, j):
        if k == 0:
            for live, keep, send in (
                ((j >= 0) & (j < per), ck, cs),
                ((j >= per) & (j < count), sk, ss),
            ):

                @pl.when(live)
                def _():
                    copy(0, j, send).wait()
                    q[j] = add(keep[:, rows_of(j), :], r1[j])
                    copy(1, j).start()

            return

        @pl.when((j >= 0) & (j < count))
        def _():
            copy(k, j).wait()
            if k == 1:
                q[j, 0:8] = add(q[j, 0:8], r2[j])
            elif k == 2:
                q[j, 0:4] = add(q[j, 0:4], r3[j])
            elif k == 3:
                q[j, 0:2] = add(q[j, 0:2], r4[j])
            elif k == 4:
                f[j, 0:1] = add(q[j, 0:1], r5[j])
            if k < 7:
                copy(k + 1, j).start()
                return
            f_ref[j] = f[j]

    def step(t):
        t = jnp.asarray(t, jnp.int32)
        event(0, t + 2)
        for k in range(1, 8):
            event(k, t + 1 - k)

    def start_first(j, _):
        copy(0, j, cs).start()
        return 0

    def start_second(j, _):
        copy(0, j, ss).start()
        return 0

    lax.fori_loop(0, per, start_first, 0)
    left_t[...] = oself_ref[...].T
    put_pieces(b, g, left_t, dy1_ref[...], 0, sk, ss)
    lax.fori_loop(per, early, start_second, 0)

    fill_window(proj_ref, kp, vp, width)
    fill_bias(brow_ref, bias, nq)
    dka[...] = jnp.zeros_like(dka)
    dva[...] = jnp.zeros_like(dva)
    dsum[...] = jnp.zeros_like(dsum)
    event(0, jnp.int32(0))
    event(0, jnp.int32(1))

    def tile(t):
        row = pl.ds(pl.multiple_of(t * TQ, TQ), TQ)
        win = pl.ds(pl.multiple_of(t * TQ, TQ), WIN)
        mask = range_mask(t * TQ - 64, WIN, start_ref[pl.ds(t, 1), :], size_ref[pl.ds(t, 1), :])
        for c in range(nq):
            cols = slice(c * 256, (c + 1) * 256)
            qs = stack4(proj_ref[row, cols] * jnp.asarray(scale, BF))
            dos = stack4(do_ref[row, cols])
            s = dot(kp[win, cols], qs.T) + bias[c]
            p = jnp.where(mask, jnp.exp(s - lse_ref[t, c]), 0.0)
            dp = dot(vp[win, cols], dos.T)
            delta = jnp.sum(red(p * dp, jnp.sum), axis=0, keepdims=True)
            ds = p * (dp - delta)
            dsum[c] += ds
            ds = ds.astype(BF)
            dva[win, cols] += dot(p.astype(BF), dos)
            dka[win, cols] += dot(ds, qs)
            dproj[row, cols] = (unstack4(dot_tn(ds, kp[win, cols])) * scale).astype(BF)

    def tile_and_step(t, _):
        tile(t)
        step(t)
        return 0

    lax.fori_loop(0, tiles, tile_and_step, 0)
    dproj[:, width : 2 * width] = dka[64:, :].astype(BF)
    dproj[:, 2 * width : 3 * width] = dva[64:, :].astype(BF)
    left_t[...] = h1_ref[...].T
    done = tiles
    for i in range(3):
        put_pieces(b, g, left_t, dproj[:, i * width : (i + 1) * width], i + 1, sk, ss)
        lax.fori_loop(early + i * each, early + (i + 1) * each, start_second, 0)
        step(done)
        done += 1
    dgain[...] = jnp.zeros_like(dgain)
    parts = 5
    block = rows // parts

    def self_in(i, _):
        at = pl.ds(pl.multiple_of(i * block, block), block)
        x0 = x0_ref[at, :].astype(F32)
        dx, part = rms_back(x0, rms(x0), gain_ref[...], dot_nt(dproj[at, :], wqkv_ref[...]))
        dgain[...] += part
        dx0 = dx1_ref[at, :] + dx
        top = dx0.astype(BF)
        high[at, :] = top
        low[at, :] = (dx0 - top.astype(F32)).astype(BF)
        step(done + i)
        return 0

    lax.fori_loop(0, parts, self_in, 0)

    dist = distances()
    for c in range(nq):
        cols = slice(c * 256, (c + 1) * 256)

        def one(d, _):
            x = jnp.where(dist == d, dsum[c], 0.0)
            drow[pl.ds(d, 1), cols] = jnp.sum(red(x, jnp.sum), axis=0, keepdims=True)
            return 0

        lax.fori_loop(0, length, one, 0)
    lane = lax.broadcasted_iota(jnp.int32, (buckets, length), 1)
    place = jnp.zeros((buckets, length), jnp.int32)
    for d in range(length):
        place = jnp.where(lane == d, bucket_ref[d], place)
    hot = (place == lax.broadcasted_iota(jnp.int32, (buckets, length), 0)).astype(F32)
    head = (
        lax.broadcasted_iota(jnp.int32, (width, 128), 0) // 64
        == lax.broadcasted_iota(jnp.int32, (width, 128), 1)
    ).astype(F32)
    by_bucket = jnp.dot(hot, drow[...], preferred_element_type=F32, precision=lax.Precision.HIGHEST)
    small_ref[...] = jnp.zeros_like(small_ref)
    small_ref[24:, :] = jnp.dot(by_bucket, head, preferred_element_type=F32, precision=lax.Precision.HIGHEST)
    for i, ref in enumerate((dgain, dg2_ref, dg3_ref)):
        for k in range(6):
            small_ref[6 * i + k : 6 * i + k + 1, :] = ref[0:1, k * 128 : (k + 1) * 128]

    def small_copy(k):
        return pltpu.make_async_remote_copy(
            src_ref=small_ref if k == 0 else sm_in.at[k + 4],
            dst_ref=sm_in.at[k],
            send_sem=sm_send.at[k],
            recv_sem=sm_recv.at[k],
            device_id=peers[k],
            device_id_type=mesh_id,
        )

    def small_sum(k):
        small_copy(k).wait()
        held = small_ref[...] if k == 0 else sm_in[k + 4]
        if k < 4:
            sm_in[k + 5] = held + sm_in[k]
            small_copy(k + 1).start()
        else:
            small_ref[...] = held + sm_in[k]

    small_copy(0).start()
    done += parts
    step(done)
    small_sum(0)
    hot_rows = onehot_rows(src_ref[...])
    d_ref[...] = dot(hot_rows, high[...]) + dot(hot_rows, low[...])
    for k in range(1, 5):
        step(done + k)
        small_sum(k)

    def rest(t, _):
        step(t)
        return 0

    lax.fori_loop(done + 5, count + 6, rest, 0)


def late(start, size, bucket, brow, proj, do, lse, h1, oself, dy1, src, x0, gain, dx1, wqkv, dg2, dg3, ck, cs, scale):
    rows, width = do.shape
    nq = width // 256
    slots, piece, wide = ck.shape
    step_rows = 16
    count = 2 * piece // step_rows
    any_spec = pl.BlockSpec(memory_space=pl.ANY)

    def buf(n):
        return pltpu.VMEM((count, n, step_rows, wide), BF)

    return pl.pallas_call(
        functools.partial(late_kernel, scale=scale),
        out_shape=(sds((rows, width), F32), sds((56, 128), F32), sds((count, 8, step_rows, wide), BF)),
        in_specs=[VM, VM, SM] + [VM] * 15 + [any_spec],
        out_specs=(VM,) * 3,
        scratch_shapes=[
            pltpu.VMEM((rows + 64, width), BF),
            pltpu.VMEM((rows + 64, width), BF),
            pltpu.VMEM((nq, WIN, 256), F32),
            pltpu.VMEM((rows + 64, width), F32),
            pltpu.VMEM((rows + 64, width), F32),
            pltpu.VMEM((nq, WIN, 256), F32),
            pltpu.VMEM((rows, 3 * width), BF),
            pltpu.VMEM((width, rows), BF),
            pltpu.VMEM((slots, piece, wide), BF),
            pltpu.VMEM((slots, piece, wide), BF),
            pltpu.VMEM((rows, width), BF),
            pltpu.VMEM((rows, width), BF),
            pltpu.VMEM(brow.shape, F32),
            pltpu.VMEM((9, 56, 128), F32),
            pltpu.VMEM((1, width), F32),
            buf(16),
            buf(16),
            buf(8),
            buf(4),
            buf(2),
            buf(1),
            buf(8),
        ]
        + [pltpu.SemaphoreType.DMA((8, count))] * 2
        + [pltpu.SemaphoreType.DMA((5,))] * 2,
        compiler_params=pltpu.CompilerParams(
            vmem_limit_bytes=62 << 20, collective_id=0, has_side_effects=True
        ),
        cost_estimate=pl.CostEstimate(flops=10**13, bytes_accessed=30 << 20, transcendentals=0),
        name="late",
    )(start, size, bucket, brow, proj, do, lse, h1, oself, dy1, src, x0, gain, dx1, wqkv, dg2, dg3, ck, cs)


def last_kernel(
    me_ref, a0, a1, a2, a3, f_ref, own_ref, came_ref, win_ref, wout_ref, co_ref, cq_ref, ckv_ref, qkv_ref, so_ref, enc_ref
):
    half = a0.shape[1] // 2
    for i, ref in enumerate((a0, a1, a2, a3)):
        for z2 in range(2):
            s = me_ref[1] ^ ((i >> 1) + 2 * (i & 1) + 4 * z2)
            piece = ref[z2]
            rows = pl.ds(pl.multiple_of((s & 1) * half, half), half)
            cols = pl.ds(pl.multiple_of((s >> 1) * 768, 768), 768)
            win_ref[rows, cols] = piece[:half].astype(F32)
            wout_ref[pl.ds(pl.multiple_of(s * half, half), half), :] = piece[half:].astype(F32)
    count, _, step_rows, wide = f_ref.shape
    width = 2 * wide
    places = (
        (co_ref, 0), (cq_ref, 0), (ckv_ref, 0), (ckv_ref, width),
        (so_ref, 0), (qkv_ref, 0), (qkv_ref, width), (qkv_ref, 2 * width),
    )
    each = count // 8
    tall = each * step_rows
    for slot in range(8):
        s = me_ref[1] ^ ((slot >> 2) + (slot & 2) + 4 * (slot & 1))
        for n, (out, col) in enumerate(places):
            for k in range(each):
                at = pl.ds(pl.multiple_of((s >> 1) * tall + k * step_rows, step_rows), step_rows)
                cols = pl.ds(pl.multiple_of(col + (s & 1) * wide, 128), wide)
                out[at, cols] = f_ref[n * each + k, slot].astype(F32)
    enc_ref[...] = own_ref[...] + came_ref[...].astype(F32)


def last(me, arrays, f, own, came):
    width = own.shape[1]
    quarter = width // 4
    cols = lambda n: sds((quarter, n * width), F32)
    return call(
        last_kernel,
        "last",
        (cols(4), sds((width, width), F32), cols(1), cols(1), cols(2), cols(3), cols(1), sds(own.shape, F32)),
        [SM] + [VM] * 7,
        (VM,) * 8,
        [],
        (me, *arrays, f, own, came),
        us=8,
    )


def hop(x, core=0, xb=0, yb=0, z1=0, z2=0):
    b, g = core | (xb << 1), yb | (z1 << 1) | (z2 << 2)
    groups, blocks = lax.axis_size("grp"), lax.axis_size("blk")
    pairs = [(i * blocks + j, (i ^ g) * blocks + (j ^ b)) for i in range(groups) for j in range(blocks)]
    return lax.ppermute(x, ("grp", "blk"), pairs)


def total(*parts):
    out = parts[0].astype(F32)
    for p in parts[1:]:
        out = out + p.astype(F32)
    return out.astype(BF)


def after(x, *deps):
    return lax.optimization_barrier((x,) + deps)[0]


def fused_body(
    dec_in,
    encodings,
    answer_len,
    answer_question,
    question_rows,
    bucket_table,
    gain_self,
    w_qkv,
    w_self_out,
    rel_bias,
    gain_cross,
    w_cross_q,
    w_cross_kv,
    w_cross_out,
    gain_ffn,
    w_in,
    w_out,
    cotangent,
):
    rows, width = dec_in.shape
    buckets, heads = rel_bias.shape
    scale = 1.0 / math.sqrt(width // heads)
    me_b, me_g = lax.axis_index("blk"), lax.axis_index("grp")
    me = jnp.stack([me_b, me_g]).astype(jnp.int32)
    g1, g2, g3 = (g.reshape(1, width) for g in (gain_self, gain_cross, gain_ffn))

    enc2 = hop(encodings, xb=1)
    enc1 = hop(encodings, core=1)
    src, cstart, csize, sstart, ssize, lo, hi, brow, x0, h1, proj, oself, lse_self = pre(
        me, answer_question, answer_len, question_rows, bucket_table, dec_in, g1, rel_bias, w_qkv, scale
    )
    enc2, oself = lax.optimization_barrier((enc2, oself))
    enc3 = hop(enc2, core=1)
    enc1 = after(enc1, x0)
    x1, h2, qc = mid(x0, oself, w_self_out, g2, w_cross_q, scale)
    k, v, kt, ocross, lse = kv_cross(
        me, lo, hi, cstart, csize, qc, (encodings, enc1, enc2, enc3), w_cross_kv
    )
    f_keep, f_send, x2, dh3, g_low, oc, layer_out = ffn(
        me, src, x1, ocross, g3, cotangent, w_cross_out, w_in, w_out
    )
    f_came = hop(f_send, core=1)
    dx2, dyc, do, dgain3 = ffn_back(x2, dh3, g_low, g3, w_cross_out)
    f_came = after(f_came, do)
    half = width // 8
    i_keep, i_send, o_keep, o_send = (
        total(f_keep[n : n + 8, rows_], f_came[n : n + 8, rows_])
        for rows_ in (slice(0, half), slice(half, 2 * half))
        for n in (0, 8)
    )
    do, o_send, i_send = lax.optimization_barrier((do, o_send, i_send))
    i_came, o_came = hop(i_send, yb=1), hop(o_send, xb=1)
    dq0, keep0, send0 = cross_back(
        me, lo, hi, cstart, csize, qc, do, ocross, lse, k, v, kt, scale, 0, 2
    )
    came0 = hop(send0, core=1)
    i_came, o_came, dq0 = lax.optimization_barrier((i_came, o_came, dq0))
    i_q = [total(i_keep[2 * j : 2 * j + 2], i_came[2 * j : 2 * j + 2]) for j in range(4)]
    o_q = [total(o_keep[2 * j : 2 * j + 2], o_came[2 * j : 2 * j + 2]) for j in range(4)]
    z_send = jnp.concatenate([i_q[1], o_q[1]], axis=1)
    do1, z_send, i_q[2], i_q[3], o_q[2], o_q[3] = lax.optimization_barrier(
        (do, z_send, i_q[2], i_q[3], o_q[2], o_q[3])
    )
    z_came = hop(z_send, z1=1)
    ix, ixz = hop(i_q[2], xb=1), hop(i_q[3], xb=1, z1=1)
    oy, oyz = hop(o_q[2], yb=1), hop(o_q[3], yb=1, z1=1)
    dq1, keep1, send1 = cross_back(
        me, lo, hi, cstart, csize, qc, do1, ocross, lse, k, v, kt, scale, 2, 1
    )
    came1 = hop(send1, core=1)
    z_came, ix, ixz, oy, oyz, dq1 = lax.optimization_barrier((z_came, ix, ixz, oy, oyz, dq1))

    def line(n):
        return jnp.concatenate(
            [
                total(i_q[0][n], z_came[n, :half], ix[n], ixz[n]),
                total(o_q[0][n], z_came[n, half:], oy[n], oyz[n]),
            ],
            axis=0,
        )

    f_keep, f_send = line(0), line(1)
    dq1, f_send = lax.optimization_barrier((dq1, f_send))
    f_came = hop(f_send, z2=1)
    dx1, dy1, dos, dgain2 = cross_in(dq0, dq1, x1, dx2, g2, w_cross_q, w_self_out)
    f_came, came1, dos = lax.optimization_barrier((f_came, came1, dos))
    f_own = total(f_keep, f_came)
    came1, f_own = lax.optimization_barrier((came1, f_own))
    f_came = hop(f_own, z2=1)
    c_keep, c_send, enc_own, enc_out = cross_weights(
        me, keep0, came0, keep1, came1, encodings, enc2, w_cross_kv, oc, dyc, h2, dq0, dq1
    )
    enc_came = hop(enc_out, xb=1)
    f_came, c_keep = lax.optimization_barrier((f_came, c_keep))
    f_pair = jnp.stack([f_own, f_came])
    dos, c_keep, f_pair = lax.optimization_barrier((dos, c_keep, f_pair))
    f_all = [hop(f_pair, z1=1), hop(f_pair, yb=1), hop(f_pair, yb=1, z1=1)]
    d_dec_in, small, gathered = late(
        sstart, ssize, bucket_table, brow, proj, dos, lse_self, h1, oself, dy1, src, x0, g1, dx1, w_qkv,
        dgain2, dgain3, c_keep, c_send, scale,
    )
    *f_all, enc_came, gathered = lax.optimization_barrier((*f_all, enc_came, gathered))
    o_win, o_wout, o_wco, o_wcq, o_wckv, o_wqkv, o_wso, d_encodings = last(
        me, [f_pair, *f_all], gathered, enc_own, enc_came
    )

    def own(v):
        return lax.dynamic_slice_in_dim(v, me_b * (v.shape[0] // 4), v.shape[0] // 4, 0)

    gains = small[:18].reshape(3, width)
    g_self, g_cross, g_ffn = (own(gains[i]) for i in range(3))
    g_rel = own(small[24:, :heads])
    return (
        layer_out,
        d_dec_in,
        d_encodings,
        g_self,
        o_wqkv,
        o_wso,
        g_rel,
        g_cross,
        o_wcq,
        o_wckv,
        o_wco,
        g_ffn,
        o_win,
        o_wout,
    )


def solution(mesh):
    rows = P(("grp", "blk"), None)
    fused = mesh.shape["grp"] == 8 and mesh.shape["blk"] == 4
    return jax.shard_map(
        fused_body if fused else body,
        mesh=mesh,
        in_specs=(rows, rows, P(("grp", "blk")), P("grp"), P("grp", None)) + (P(),) * 12 + (rows,),
        out_specs=(rows, rows, rows, P("blk"))
        + (P("blk", None),) * 3
        + (P("blk"),)
        + (P("blk", None),) * 3
        + (P("blk"),)
        + (P("blk", None),) * 2,
        check_vma=False,
    )
```

```python
import functools
import math

import jax
import jax.numpy as jnp
from jax import lax
from jax.experimental import pallas as pl
from jax.experimental.pallas import tpu as pltpu
from jax.sharding import PartitionSpec as P

EPSILON = 1e-06
NEG = -1e30
MASKED = -1e9
TQ = 64
TK = 256
WIN = 128
F32 = jnp.float32
BF = jnp.bfloat16
VM = pl.BlockSpec(memory_space=pltpu.VMEM)
SM = pl.BlockSpec(memory_space=pltpu.SMEM)
LIMIT = 60 << 20


def dot(a, b):
    return jnp.dot(a, b, preferred_element_type=F32)


def dot_tn(a, b):
    return lax.dot_general(a, b, (((0,), (0,)), ((), ())), preferred_element_type=F32)


def dot_nt(a, b):
    return lax.dot_general(a, b, (((1,), (1,)), ((), ())), preferred_element_type=F32)


def stack4(t):
    lane = lax.broadcasted_iota(jnp.int32, t.shape, 1) // 64
    return jnp.concatenate([jnp.where(lane == a, t, jnp.zeros_like(t)) for a in range(4)], axis=0)


def unstack4(s):
    n = s.shape[0] // 4
    lane = lax.broadcasted_iota(jnp.int32, (n, 256), 1) // 64
    out = s[:n]
    for a in range(1, 4):
        out = jnp.where(lane == a, s[a * n : (a + 1) * n], out)
    return out


def range_mask(base, rows, start, size):
    idx = lax.broadcasted_iota(jnp.int32, (rows, start.shape[1]), 0)
    rel = idx - (start - base)
    return (rel >= 0) & (rel < size)


def red(x, op):
    return op(x.reshape(x.shape[0] // 8, 8, x.shape[1]), axis=0)


def cross_fwd_kernel(
    lo_ref, hi_ref, start_ref, size_ref, q_ref, k_ref, vt_ref, o_ref, lse_ref, qst, s_scr, m_scr, l_scr, acc, *, nq, tiles
):
    def tile(t, _):
        st = start_ref[t]
        sz = size_ref[t]
        lo = lo_ref[t]
        hi = hi_ref[t]
        row = pl.ds(pl.multiple_of(t * TQ, TQ), TQ)
        for c in range(nq):
            qst[c] = stack4(q_ref[row, c * 256 : (c + 1) * 256]).T
            m_scr[c] = jnp.full((8, 256), NEG, F32)
            l_scr[c] = jnp.zeros((8, 256), F32)
            acc[c] = jnp.zeros((256, 256), F32)

        def scores(j, _):
            kr = pl.ds(pl.multiple_of(j * TK, TK), TK)
            mask = range_mask(j * TK, TK, st, sz)
            for c in range(nq):
                s = dot(k_ref[kr, c * 256 : (c + 1) * 256], qst[c])
                s = jnp.where(mask, s, NEG)
                s_scr[c, kr, :] = s
                m_scr[c] = jnp.maximum(m_scr[c], red(s, jnp.max))
            return 0

        lax.fori_loop(lo, hi, scores, 0)
        for c in range(nq):
            m_scr[c] = jnp.broadcast_to(jnp.max(m_scr[c], axis=0, keepdims=True), (8, 256))

        def mix(j, _):
            kr = pl.ds(pl.multiple_of(j * TK, TK), TK)
            for c in range(nq):
                p = jnp.exp(s_scr[c, kr, :] - m_scr[c][0:1])
                l_scr[c] += red(p, jnp.sum)
                acc[c] += dot(vt_ref[c * 256 : (c + 1) * 256, kr], p.astype(BF))
            return 0

        lax.fori_loop(lo, hi, mix, 0)
        for c in range(nq):
            l = jnp.sum(l_scr[c], axis=0, keepdims=True)
            lse_ref[t, c] = m_scr[c][0:1] + jnp.log(l)
            o_ref[row, c * 256 : (c + 1) * 256] = unstack4((acc[c] * (1.0 / l)).T)
        return 0

    lax.fori_loop(0, tiles, tile, 0)


def quads_per_step(nq, keys):
    return nq if keys <= 2048 else 1


def cross_fwd(lo, hi, start, size, q, k, vt):
    rows, width = q.shape
    tiles, keys = rows // TQ, k.shape[0]
    nq = quads_per_step(width // 256, keys)
    full = pl.BlockSpec(start.shape, lambda g: (0, 0, 0))
    return pl.pallas_call(
        functools.partial(cross_fwd_kernel, nq=nq, tiles=tiles),
        grid=(width // 256 // nq,),
        out_shape=(
            jax.ShapeDtypeStruct(q.shape, F32),
            jax.ShapeDtypeStruct((tiles, width // 256, 1, 256), F32),
        ),
        in_specs=[
            SM,
            SM,
            full,
            full,
            pl.BlockSpec((rows, nq * 256), lambda g: (0, g)),
            pl.BlockSpec((keys, nq * 256), lambda g: (0, g)),
            pl.BlockSpec((nq * 256, keys), lambda g: (g, 0)),
        ],
        out_specs=(
            pl.BlockSpec((rows, nq * 256), lambda g: (0, g)),
            pl.BlockSpec((tiles, nq, 1, 256), lambda g: (0, g, 0, 0)),
        ),
        scratch_shapes=[
            pltpu.VMEM((nq, 256, 256), BF),
            pltpu.VMEM((nq, keys, 256), F32),
            pltpu.VMEM((nq, 8, 256), F32),
            pltpu.VMEM((nq, 8, 256), F32),
            pltpu.VMEM((nq, 256, 256), F32),
        ],
        compiler_params=pltpu.CompilerParams(vmem_limit_bytes=LIMIT),
        name="cross_fwd",
    )(lo, hi, start, size, q, k, vt)


def cross_bwd_kernel(
    lo_ref,
    hi_ref,
    start_ref,
    size_ref,
    q_ref,
    do_ref,
    o_ref,
    lse_ref,
    k_ref,
    v_ref,
    kt_ref,
    dq_ref,
    dk_ref,
    dv_ref,
    qs,
    qst,
    dos,
    dost,
    del_scr,
    dka,
    dva,
    dqt,
    *,
    nq,
    tiles,
    scale,
):
    dka[...] = jnp.zeros_like(dka)
    dva[...] = jnp.zeros_like(dva)

    def tile(t, _):
        st = start_ref[t]
        sz = size_ref[t]
        row = pl.ds(pl.multiple_of(t * TQ, TQ), TQ)
        for c in range(nq):
            cs = slice(c * 256, (c + 1) * 256)
            a = stack4(q_ref[row, cs])
            qs[c] = a
            qst[c] = a.T
            b = stack4(do_ref[row, cs])
            dos[c] = b
            dost[c] = b.T
            product = do_ref[row, cs].astype(F32) * o_ref[row, cs]
            total = jnp.sum(red(stack4(product).T, jnp.sum), axis=0, keepdims=True)
            del_scr[c] = jnp.broadcast_to(total, (8, 256))
            dqt[c] = jnp.zeros((256, 256), F32)

        def step(j, _):
            kr = pl.ds(pl.multiple_of(j * TK, TK), TK)
            mask = range_mask(j * TK, TK, st, sz)
            for c in range(nq):
                cs = slice(c * 256, (c + 1) * 256)
                s = dot(k_ref[kr, cs], qst[c])
                p = jnp.where(mask, jnp.exp(s - lse_ref[t, c]), 0.0)
                dp = dot(v_ref[kr, cs], dost[c])
                ds = (p * (dp - del_scr[c][0:1])).astype(BF)
                dva[kr, cs] += dot(p.astype(BF), dos[c])
                dka[kr, cs] += dot(ds, qs[c])
                dqt[c] += dot(kt_ref[cs, kr], ds)
            return 0

        lax.fori_loop(lo_ref[t], hi_ref[t], step, 0)
        for c in range(nq):
            cs = slice(c * 256, (c + 1) * 256)
            dq_ref[row, cs] = (unstack4(dqt[c].T) * scale).astype(BF)
        return 0

    lax.fori_loop(0, tiles, tile, 0)
    dk_ref[...] = dka[...].astype(BF)
    dv_ref[...] = dva[...].astype(BF)


def cross_bwd(lo, hi, start, size, q, do, o, lse, k, v, kt, scale):
    rows, width = q.shape
    tiles, keys = rows // TQ, k.shape[0]
    nq = quads_per_step(width // 256, keys)
    full = pl.BlockSpec(start.shape, lambda g: (0, 0, 0))
    own = pl.BlockSpec((rows, nq * 256), lambda g: (0, g))
    held = pl.BlockSpec((keys, nq * 256), lambda g: (0, g), pipeline_mode=pl.Buffered(1))
    out_kv = pl.BlockSpec((keys, nq * 256), lambda g: (0, g), pipeline_mode=pl.Buffered(1))
    return pl.pallas_call(
        functools.partial(cross_bwd_kernel, nq=nq, tiles=tiles, scale=scale),
        grid=(width // 256 // nq,),
        out_shape=(
            jax.ShapeDtypeStruct(q.shape, BF),
            jax.ShapeDtypeStruct(k.shape, BF),
            jax.ShapeDtypeStruct(k.shape, BF),
        ),
        in_specs=[
            SM,
            SM,
            full,
            full,
            own,
            own,
            own,
            pl.BlockSpec((tiles, nq, 1, 256), lambda g: (0, g, 0, 0)),
            held,
            held,
            pl.BlockSpec((nq * 256, keys), lambda g: (g, 0), pipeline_mode=pl.Buffered(1)),
        ],
        out_specs=(own, out_kv, out_kv),
        scratch_shapes=[pltpu.VMEM((nq, 256, 256), BF)] * 4
        + [
            pltpu.VMEM((nq, 8, 256), F32),
            pltpu.VMEM((keys, nq * 256), F32),
            pltpu.VMEM((keys, nq * 256), F32),
            pltpu.VMEM((nq, 256, 256), F32),
        ],
        compiler_params=pltpu.CompilerParams(vmem_limit_bytes=LIMIT),
        name="cross_bwd",
    )(lo, hi, start, size, q, do, o, lse, k, v, kt)


def distances():
    j = lax.broadcasted_iota(jnp.int32, (WIN, 256), 0)
    i = lax.broadcasted_iota(jnp.int32, (WIN, 256), 1) % 64
    return WIN - TQ + i - j


def fill_window(proj_ref, kp, vp, width):
    kp[0:64, :] = jnp.zeros((64, width), BF)
    vp[0:64, :] = jnp.zeros((64, width), BF)
    kp[64:, :] = proj_ref[:, width : 2 * width]
    vp[64:, :] = proj_ref[:, 2 * width : 3 * width]


def fill_bias(brow_ref, bias, nq):
    dist = distances()
    for c in range(nq):
        cs = slice(c * 256, (c + 1) * 256)

        def add(d, held):
            return jnp.where(dist == d, brow_ref[pl.ds(d, 1), cs], held)

        bias[c] = lax.fori_loop(0, brow_ref.shape[0], add, jnp.full((WIN, 256), MASKED, F32))


def self_fwd_kernel(start_ref, size_ref, brow_ref, proj_ref, o_ref, lse_ref, kp, vp, bias, *, nq, tiles, scale):
    width = nq * 256
    fill_window(proj_ref, kp, vp, width)
    fill_bias(brow_ref, bias, nq)

    def tile(t, _):
        row = pl.ds(pl.multiple_of(t * TQ, TQ), TQ)
        win = pl.ds(pl.multiple_of(t * TQ, TQ), WIN)
        mask = range_mask(t * TQ - 64, WIN, start_ref[t], size_ref[t])
        for c in range(nq):
            cs = slice(c * 256, (c + 1) * 256)
            qst = stack4(proj_ref[row, cs] * jnp.asarray(scale, BF)).T
            s = jnp.where(mask, dot(kp[win, cs], qst) + bias[c], MASKED)
            m = jnp.max(red(s, jnp.max), axis=0, keepdims=True)
            p = jnp.exp(s - m)
            l = jnp.sum(red(p, jnp.sum), axis=0, keepdims=True)
            p = (p * (1.0 / l)).astype(BF)
            o_ref[row, cs] = unstack4(dot_tn(p, vp[win, cs])).astype(BF)
            lse_ref[t, c] = m + jnp.log(l)
        return 0

    lax.fori_loop(0, tiles, tile, 0)


def self_fwd(start, size, brow, proj, scale):
    rows, width = proj.shape[0], proj.shape[1] // 3
    nq, tiles = width // 256, rows // TQ
    return pl.pallas_call(
        functools.partial(self_fwd_kernel, nq=nq, tiles=tiles, scale=scale),
        out_shape=(
            jax.ShapeDtypeStruct((rows, width), BF),
            jax.ShapeDtypeStruct((tiles, nq, 1, 256), F32),
        ),
        in_specs=[VM] * 4,
        out_specs=(VM, VM),
        scratch_shapes=[
            pltpu.VMEM((rows + 64, width), BF),
            pltpu.VMEM((rows + 64, width), BF),
            pltpu.VMEM((nq, WIN, 256), F32),
        ],
        compiler_params=pltpu.CompilerParams(vmem_limit_bytes=LIMIT),
        name="self_fwd",
    )(start, size, brow, proj)


def self_bwd_kernel(
    start_ref,
    size_ref,
    brow_ref,
    proj_ref,
    do_ref,
    lse_ref,
    dproj_ref,
    dbrow_ref,
    kp,
    vp,
    bias,
    dka,
    dva,
    dsum,
    *,
    nq,
    tiles,
    scale,
):
    width = nq * 256
    fill_window(proj_ref, kp, vp, width)
    fill_bias(brow_ref, bias, nq)
    dka[...] = jnp.zeros_like(dka)
    dva[...] = jnp.zeros_like(dva)
    dsum[...] = jnp.zeros_like(dsum)

    def tile(t, _):
        row = pl.ds(pl.multiple_of(t * TQ, TQ), TQ)
        win = pl.ds(pl.multiple_of(t * TQ, TQ), WIN)
        mask = range_mask(t * TQ - 64, WIN, start_ref[t], size_ref[t])
        for c in range(nq):
            cs = slice(c * 256, (c + 1) * 256)
            qs = stack4(proj_ref[row, cs] * jnp.asarray(scale, BF))
            dos = stack4(do_ref[row, cs])
            s = dot(kp[win, cs], qs.T) + bias[c]
            p = jnp.where(mask, jnp.exp(s - lse_ref[t, c]), 0.0)
            dp = dot(vp[win, cs], dos.T)
            delta = jnp.sum(red(p * dp, jnp.sum), axis=0, keepdims=True)
            ds = p * (dp - delta)
            dsum[c] += ds
            ds = ds.astype(BF)
            dva[win, cs] += dot(p.astype(BF), dos)
            dka[win, cs] += dot(ds, qs)
            dproj_ref[row, cs] = (unstack4(dot_tn(ds, kp[win, cs])) * scale).astype(BF)
        return 0

    lax.fori_loop(0, tiles, tile, 0)
    dproj_ref[:, width : 2 * width] = dka[64:, :].astype(BF)
    dproj_ref[:, 2 * width : 3 * width] = dva[64:, :].astype(BF)
    dist = distances()
    for c in range(nq):
        cs = slice(c * 256, (c + 1) * 256)

        def one(d, _):
            x = jnp.where(dist == d, dsum[c], 0.0)
            dbrow_ref[pl.ds(d, 1), cs] = jnp.sum(red(x, jnp.sum), axis=0, keepdims=True)
            return 0

        lax.fori_loop(0, brow_ref.shape[0], one, 0)


def self_bwd(start, size, brow, proj, do, lse, scale):
    rows, width = proj.shape[0], proj.shape[1] // 3
    nq, tiles = width // 256, rows // TQ
    return pl.pallas_call(
        functools.partial(self_bwd_kernel, nq=nq, tiles=tiles, scale=scale),
        out_shape=(jax.ShapeDtypeStruct((rows, 3 * width), BF), jax.ShapeDtypeStruct(brow.shape, F32)),
        in_specs=[VM] * 6,
        out_specs=(VM, VM),
        scratch_shapes=[
            pltpu.VMEM((rows + 64, width), BF),
            pltpu.VMEM((rows + 64, width), BF),
            pltpu.VMEM((nq, WIN, 256), F32),
            pltpu.VMEM((rows + 64, width), F32),
            pltpu.VMEM((rows + 64, width), F32),
            pltpu.VMEM((nq, WIN, 256), F32),
        ],
        compiler_params=pltpu.CompilerParams(vmem_limit_bytes=LIMIT),
        name="self_bwd",
    )(start, size, brow, proj, do, lse)


def norm_rows(x, gain):
    inverse = lax.rsqrt(jnp.mean(x * x, axis=-1, keepdims=True) + EPSILON)
    return x * inverse * gain, inverse


def norm_back(x, inverse, gain, grad):
    scaled = grad * gain
    mean = jnp.mean(x * scaled, axis=-1, keepdims=True)
    return inverse * scaled - x * inverse * inverse * inverse * mean, jnp.sum(grad * x * inverse, axis=0)


def swap(x, axis, bit):
    size = lax.axis_size(axis)
    return lax.ppermute(x, axis, [(i, i ^ bit) for i in range(size)])


def bits_of(axis):
    size = lax.axis_size(axis)
    return [1 << b for b in range(size.bit_length() - 1)]


def gather_parts(x, axis):
    parts = {0: x}
    for bit in reversed(bits_of(axis)):
        for r in list(parts):
            parts[r ^ bit] = swap(parts[r], axis, bit)
    return parts


def add_low(a, b):
    return (a.astype(F32) + b.astype(F32)).astype(BF)


def scatter_sum(x, axis, order):
    size = x.shape[0]
    live = list(range(size))
    block = x
    for bit in order:
        keep = [r for r in live if not r & bit]
        send = [r for r in live if r & bit]
        k = jnp.stack([block[live.index(r)] for r in keep])
        s = jnp.stack([block[live.index(r)] for r in send])
        block = add_low(k, swap(s, axis, bit))
        live = keep
    return block[0]


def gather_sum(x, axis, order):
    parts = [0]
    block = x[None]
    for bit in order:
        block = jnp.concatenate([block, swap(block, axis, bit)], axis=0)
        parts = parts + [r ^ bit for r in parts]
    inverse = [parts.index(r) for r in range(len(parts))]
    return block, inverse


def relative(x, axis):
    size = lax.axis_size(axis)
    me = lax.axis_index(axis)
    return jnp.stack([lax.dynamic_index_in_dim(x, me ^ r, 0, keepdims=False) for r in range(size)])


def reduce_all(x):
    blocks, rows, width = x.shape
    groups = lax.axis_size("grp")
    part = scatter_sum(relative(x, "blk"), "blk", bits_of("blk"))
    part = relative(part.reshape(groups, rows // groups, width), "grp")
    part = scatter_sum(part, "grp", bits_of("grp"))
    whole, inverse = gather_sum(part, "grp", list(reversed(bits_of("grp"))))
    me = lax.axis_index("grp")
    index = jnp.asarray(inverse, jnp.int32)[jnp.arange(groups) ^ me]
    return jnp.take(whole, index, axis=0).reshape(rows, width)


def sum_everywhere(x):
    for axis in ("blk", "grp"):
        for bit in bits_of(axis):
            x = x + swap(x, axis, bit)
    return x


def pack(grads, blocks):
    out = []
    for g in grads:
        k, n = g.shape
        r = g.reshape(blocks, k // blocks, n // 768, 768).transpose(0, 2, 1, 3)
        out.append(r.reshape(blocks, -1, 768))
    return jnp.concatenate(out, axis=1)


def unpack(rows, shapes, blocks):
    out, at = [], 0
    for k, n in shapes:
        count = k // blocks * (n // 768)
        piece = rows[at : at + count].reshape(n // 768, k // blocks, 768)
        out.append(piece.transpose(1, 0, 2).reshape(k // blocks, n).astype(F32))
        at += count
    return out


def body(
    dec_in,
    encodings,
    answer_len,
    answer_question,
    question_rows,
    bucket_table,
    gain_self,
    w_qkv,
    w_self_out,
    rel_bias,
    gain_cross,
    w_cross_q,
    w_cross_kv,
    w_cross_out,
    gain_ffn,
    w_in,
    w_out,
    cotangent,
):
    answers = answer_len.shape[0]
    length = bucket_table.shape[0]
    rows, width = dec_in.shape
    heads = rel_bias.shape[1]
    buckets = rel_bias.shape[0]
    scale = 1.0 / math.sqrt(width // heads)
    enc_rows = encodings.shape[0]
    blocks = lax.axis_size("blk")
    me = lax.axis_index("blk")
    tiles = rows // TQ
    nq = width // 256

    enc_parts = gather_parts(encodings, "blk")

    own_q = lax.dynamic_slice_in_dim(answer_question, me * answers, answers, 0)
    a_index = jnp.arange(answers)
    before = (own_q[None, :] < own_q[:, None]) | (
        (own_q[None, :] == own_q[:, None]) & (a_index[None, :] < a_index[:, None])
    )
    rank = jnp.sum(before.astype(jnp.int32), axis=1)
    target = (rank[:, None] * length + jnp.arange(length)[None, :]).reshape(rows)
    forward_perm = (jnp.arange(rows)[:, None] == target[None, :]).astype(BF)
    sorted_len = jnp.sum(jnp.where(rank[:, None] == a_index[None, :], answer_len[:, None], 0), axis=0)
    ends_q = jnp.cumsum(question_rows[0])
    starts_q = ends_q - question_rows[0]
    sorted_q = jnp.sum(jnp.where(rank[:, None] == a_index[None, :], own_q[:, None], 0), axis=0)
    token_q = jnp.repeat(sorted_q, length)
    pick = token_q[:, None] == jnp.arange(question_rows.shape[1])[None, :]
    token_start = jnp.sum(jnp.where(pick, starts_q[None, :], 0), axis=1)
    token_size = jnp.sum(jnp.where(pick, question_rows[0][None, :], 0), axis=1)

    def stacked(v):
        return jnp.tile(v.reshape(tiles, 1, TQ), (1, 1, 4)).astype(jnp.int32)

    c_start, c_size = stacked(token_start), stacked(token_size)
    lo = (token_start.reshape(tiles, TQ)[:, 0] // TK).astype(jnp.int32)
    hi = ((token_start + token_size).reshape(tiles, TQ)[:, -1] + TK - 1) // TK
    hi = hi.astype(jnp.int32)
    s_start = stacked(jnp.arange(rows) // length * length)
    s_size = stacked(jnp.repeat(sorted_len, length))

    bucket_hot = (bucket_table[:, None] == jnp.arange(buckets)[None, :]).astype(F32)
    brow = jnp.repeat(
        jnp.dot(bucket_hot, rel_bias, precision=lax.Precision.HIGHEST), width // heads, axis=1
    )

    x0 = dot(forward_perm, dec_in)
    grad_top = dot(forward_perm, cotangent)
    grad_low = grad_top.astype(BF)
    n1, r1 = norm_rows(x0, gain_self)
    h1 = n1.astype(BF)
    proj = dot(h1, w_qkv).astype(BF)
    o_self, lse_self = self_fwd(s_start, s_size, brow, proj, scale)
    x1 = x0 + dot(o_self, w_self_out)
    n2, r2 = norm_rows(x1, gain_cross)
    h2 = n2.astype(BF)
    qc = (dot(h2, w_cross_q).astype(BF) * jnp.asarray(scale, BF)).astype(BF)

    enc_rel = jnp.stack([enc_parts[r] for r in range(blocks)])
    enc_all = relative(enc_rel, "blk").reshape(blocks * enc_rows, width)
    kv = dot(enc_all, w_cross_kv).astype(BF)
    k_all, v_all = kv[:, :width], kv[:, width:]
    kvt = lax.dot_general(w_cross_kv, enc_all, (((0,), (1,)), ((), ())), preferred_element_type=F32).astype(BF)
    kt_all, vt_all = kvt[:width], kvt[width:]

    o_cross, lse_cross = cross_fwd(lo, hi, c_start, c_size, qc, k_all, vt_all)
    oc = o_cross.astype(BF)
    x2 = x1 + dot(oc, w_cross_out)
    n3, r3 = norm_rows(x2, gain_ffn)
    h3 = n3.astype(BF)
    hidden, gelu_back = jax.vjp(jax.nn.gelu, dot(h3, w_in))
    u = hidden.astype(BF)
    out = (x2 + dot(u, w_out)).astype(BF)
    layer_out = dot_tn(forward_perm, out).astype(BF)

    d_w_out = dot_tn(u, grad_low).astype(BF)
    da = gelu_back(dot_nt(grad_low, w_out))[0].astype(BF)
    d_w_in = dot_tn(h3, da).astype(BF)
    sums_out = reduce_all(pack([d_w_out], blocks))
    sums_in = reduce_all(pack([d_w_in], blocks))
    dx3, d_gain_ffn = norm_back(x2, r3, gain_ffn, dot_nt(da, w_in))
    dx2 = grad_top + dx3
    dyc = dx2.astype(BF)
    d_w_cross_out = dot_tn(oc, dyc).astype(BF)
    d_o = dot_nt(dyc, w_cross_out).astype(BF)
    dqc, dk, dv = cross_bwd(
        lo, hi, c_start, c_size, qc, d_o, o_cross, lse_cross, k_all, v_all, kt_all, scale
    )

    dkv = jnp.concatenate([dk, dv], axis=1).reshape(blocks, enc_rows, 2 * width)
    dkv = relative(dkv, "blk")
    dkv = add_low(dkv[0::2], swap(dkv[1::2], "blk", 1))
    enc_half = enc_rel[0::2]
    dkv_flat = dkv.reshape(-1, 2 * width)
    d_w_cross_kv = dot_tn(enc_half.reshape(-1, width), dkv_flat).astype(BF)
    d_enc = dot_nt(dkv_flat, w_cross_kv).reshape(blocks // 2, enc_rows, width)
    d_enc_parts = {2 * r: d_enc[r] for r in range(blocks // 2)}
    for bit in reversed(bits_of("blk")[1:]):
        for r in [r for r in d_enc_parts if r & bit]:
            came = swap(d_enc_parts.pop(r).astype(BF), "blk", bit)
            d_enc_parts[r ^ bit] = d_enc_parts[r ^ bit] + came.astype(F32)
    d_encodings = d_enc_parts[0]

    d_w_cross_q = dot_tn(h2, dqc).astype(BF)
    sums_cross = reduce_all(pack([d_w_cross_out, d_w_cross_q, d_w_cross_kv], blocks))
    dx_two, d_gain_cross = norm_back(x1, r2, gain_cross, dot_nt(dqc, w_cross_q))
    dx1 = dx2 + dx_two
    dy1 = dx1.astype(BF)
    d_w_self_out = dot_tn(o_self, dy1).astype(BF)
    d_os = dot_nt(dy1, w_self_out).astype(BF)
    dproj, dbrow = self_bwd(s_start, s_size, brow, proj, d_os, lse_self, scale)
    d_w_qkv = dot_tn(h1, dproj).astype(BF)
    sums_self = reduce_all(pack([d_w_qkv, d_w_self_out], blocks))
    dx_one, d_gain_self = norm_back(x0, r1, gain_self, dot_nt(dproj, w_qkv))
    d_rel = jnp.dot(
        bucket_hot.T, jnp.sum(dbrow.reshape(length, heads, -1), axis=2), precision=lax.Precision.HIGHEST
    )
    d_x0 = dx1 + dx_one
    high = d_x0.astype(BF)
    low = (d_x0 - high.astype(F32)).astype(BF)
    d_dec_in = dot_tn(forward_perm, high) + dot_tn(forward_perm, low)

    small = jnp.concatenate([d_gain_self, d_gain_cross, d_gain_ffn, d_rel.reshape(-1)])
    small = sum_everywhere(small.reshape(-1, 128)).reshape(-1)

    def own(v):
        return lax.dynamic_slice_in_dim(v, me * (v.shape[0] // blocks), v.shape[0] // blocks, 0)

    g_self, g_cross, g_ffn = (own(small[i * width : (i + 1) * width]) for i in range(3))
    g_rel = own(small[3 * width :].reshape(buckets, heads))
    (o_wout,) = unpack(sums_out, [w_out.shape], blocks)
    (o_win,) = unpack(sums_in, [w_in.shape], blocks)
    o_wco, o_wcq, o_wckv = unpack(sums_cross, [w_cross_out.shape, w_cross_q.shape, w_cross_kv.shape], blocks)
    o_wqkv, o_wso = unpack(sums_self, [w_qkv.shape, w_self_out.shape], blocks)
    return (
        layer_out,
        d_dec_in,
        d_encodings,
        g_self,
        o_wqkv,
        o_wso,
        g_rel,
        g_cross,
        o_wcq,
        o_wckv,
        o_wco,
        g_ffn,
        o_win,
        o_wout,
    )


def slot_of(rel):
    return (rel & 1) * 4 + (rel & 2) + ((rel >> 2) & 1)


def gelu_both(a):
    c = math.sqrt(2.0 / math.pi)
    a2 = a * a
    t = jnp.tanh(c * (a + 0.044715 * (a2 * a)))
    half = 0.5 * (1.0 + t)
    return a * half, half + 0.5 * a * (1.0 - t * t) * (c * (1.0 + 3.0 * 0.044715 * a2))


def rms(x):
    return lax.rsqrt(jnp.mean(x * x, axis=-1, keepdims=True) + EPSILON)


def rms_back(x, inverse, gain, grad):
    scaled = grad * gain
    mean = jnp.mean(x * scaled, axis=-1, keepdims=True)
    unit = x * inverse
    return inverse * (scaled - unit * (inverse * mean)), jnp.sum(grad * unit, axis=0, keepdims=True)


def onehot_rows(src):
    n = src.shape[1]
    return (lax.broadcasted_iota(jnp.int32, (n, n), 0) == src).astype(F32).astype(BF)


def pre_kernel(
    me_ref,
    aq_ref,
    len_ref,
    qrows_ref,
    bucket_ref,
    dec_ref,
    gain1_ref,
    rel_ref,
    wqkv_ref,
    src_ref,
    cstart_ref,
    csize_ref,
    sstart_ref,
    ssize_ref,
    lo_ref,
    hi_ref,
    brow_ref,
    x0_ref,
    h1_ref,
    proj_ref,
    oself_ref,
    lse_ref,
    order,
    qstart,
    qcount,
    wide,
    kp,
    vp,
    bias,
    *,
    answers,
    length,
    questions,
    scale,
):
    rows, width = dec_ref.shape
    nq, tiles = width // 256, rows // TQ
    base = me_ref[0] * answers
    n = jnp.int32(0)
    first_row = jnp.int32(0)
    for c in range(questions):
        qstart[c] = first_row
        first_row = first_row + qrows_ref[0, c]
        qcount[c] = n

        def visit(a, n):
            hit = aq_ref[base + a] == c

            @pl.when(hit)
            def _():
                order[n] = a

            return n + hit.astype(jnp.int32)

        n = lax.fori_loop(0, answers, visit, n)

    def answer_of(tok):
        ans = jnp.zeros_like(tok)
        for k in range(1, answers):
            ans = ans + (tok >= k * length).astype(jnp.int32)
        return ans

    tok = lax.broadcasted_iota(jnp.int32, (1, rows), 1)
    ans = answer_of(tok)
    src = tok - ans * length
    for k in range(answers):
        src = src + jnp.where(ans == k, order[k] * length, 0)
    src_ref[...] = src

    lane = lax.broadcasted_iota(jnp.int32, (tiles, 256), 1) % TQ
    tok = lane + TQ * lax.broadcasted_iota(jnp.int32, (tiles, 256), 0)
    ans = answer_of(tok)
    sstart_ref[...] = ans * length
    size = jnp.zeros_like(ans)
    for k in range(answers):
        size = size + jnp.where(ans == k, len_ref[order[k]], 0)
    ssize_ref[...] = size
    cstart = jnp.zeros_like(ans)
    csize = jnp.zeros_like(ans) + qrows_ref[0, 0]
    for c in range(1, questions):
        here = ans >= qcount[c]
        cstart = jnp.where(here, qstart[c], cstart)
        csize = jnp.where(here, qrows_ref[0, c], csize)
    cstart_ref[...] = cstart
    csize_ref[...] = csize
    for t in range(tiles):
        q_first = aq_ref[base + order[t * TQ // length]]
        q_last = aq_ref[base + order[(t * TQ + TQ - 1) // length]]
        lo_ref[t] = qstart[q_first] // TK
        hi_ref[t] = (qstart[q_last] + qrows_ref[0, q_last] + TK - 1) // TK

    for c in range(nq):
        head = lax.broadcasted_iota(jnp.int32, (rel_ref.shape[0], 256), 1) // 64
        held = jnp.zeros((rel_ref.shape[0], 256), F32)
        for a in range(4):
            h = c * 4 + a
            held = jnp.where(head == a, rel_ref[:, h : h + 1], held)
        wide[:, c * 256 : (c + 1) * 256] = held
    for d in range(length):
        brow_ref[d : d + 1, :] = wide[pl.ds(bucket_ref[d], 1), :]

    x0 = dot_tn(onehot_rows(src), dec_ref[...])
    x0_ref[...] = x0.astype(BF)
    h1_ref[...] = (x0 * rms(x0) * gain1_ref[...]).astype(BF)
    for i in range(3):
        cs = slice(i * width, (i + 1) * width)
        proj_ref[:, cs] = dot(h1_ref[...], wqkv_ref[:, cs]).astype(BF)
    fill_window(proj_ref, kp, vp, width)
    fill_bias(brow_ref, bias, nq)

    def tile(t, _):
        row = pl.ds(pl.multiple_of(t * TQ, TQ), TQ)
        win = pl.ds(pl.multiple_of(t * TQ, TQ), WIN)
        mask = range_mask(t * TQ - 64, WIN, sstart_ref[pl.ds(t, 1), :], ssize_ref[pl.ds(t, 1), :])
        for c in range(nq):
            cs = slice(c * 256, (c + 1) * 256)
            qs = stack4(proj_ref[row, cs] * jnp.asarray(scale, BF))
            s = jnp.where(mask, dot_nt(kp[win, cs], qs) + bias[c], MASKED)
            m = jnp.max(red(s, jnp.max), axis=0, keepdims=True)
            p = jnp.exp(s - m)
            l = jnp.sum(red(p, jnp.sum), axis=0, keepdims=True)
            p = (p * (1.0 / l)).astype(BF)
            oself_ref[row, cs] = unstack4(dot_tn(p, vp[win, cs])).astype(BF)
            lse_ref[t, c] = m + jnp.log(l)
        return 0

    lax.fori_loop(0, tiles, tile, 0)


def mid_kernel(x0_ref, oself_ref, wso_ref, gain2_ref, wcq_ref, x1_ref, h2_ref, qc_ref, *, scale):
    x1 = x0_ref[...].astype(F32) + dot(oself_ref[...], wso_ref[...])
    x1_ref[...] = x1
    h2_ref[...] = (x1 * rms(x1) * gain2_ref[...]).astype(BF)
    qc_ref[...] = dot(h2_ref[...], wcq_ref[...]).astype(BF) * jnp.asarray(scale, BF)


def mid(x0, oself, wso, gain, wcq, scale):
    rows, width = x0.shape
    return call(
        functools.partial(mid_kernel, scale=scale),
        "mid",
        (sds((rows, width), F32), sds((rows, width), BF), sds((rows, width), BF)),
        [VM] * 5,
        (VM,) * 3,
        [],
        (x0, oself, wso, gain, wcq),
        us=8,
    )


def call(kernel, name, out_shape, in_specs, out_specs, scratch, args, us):
    moved = sum(math.prod(a.shape) * a.dtype.itemsize for a in args)
    moved += sum(math.prod(a.shape) * a.dtype.itemsize for a in out_shape)
    return pl.pallas_call(
        kernel,
        out_shape=out_shape,
        in_specs=in_specs,
        out_specs=out_specs,
        scratch_shapes=scratch,
        compiler_params=pltpu.CompilerParams(vmem_limit_bytes=LIMIT),
        cost_estimate=pl.CostEstimate(flops=int(us * 1e11), bytes_accessed=moved, transcendentals=0),
        name=name,
    )(*args)


def sds(shape, dtype):
    return jax.ShapeDtypeStruct(shape, dtype)


def pre(me, aq, lens, qrows, bucket, dec, g1, rel, wqkv, scale):
    rows, width = dec.shape
    tiles, nq, length = rows // TQ, width // 256, bucket.shape[0]
    i32 = jnp.int32
    meta = sds((tiles, 256), i32)
    out = (
        sds((1, rows), i32),
        meta,
        meta,
        meta,
        meta,
        sds((tiles,), i32),
        sds((tiles,), i32),
        sds((length, width), F32),
        sds((rows, width), BF),
        sds((rows, width), BF),
        sds((rows, 3 * width), BF),
        sds((rows, width), BF),
        sds((tiles, nq, 1, 256), F32),
    )
    return call(
        functools.partial(
            pre_kernel, answers=lens.shape[0], length=length, questions=qrows.shape[1], scale=scale
        ),
        "pre",
        out,
        [SM] * 5 + [VM] * 4,
        (VM,) * 5 + (SM, SM) + (VM,) * 6,
        [
            pltpu.SMEM((lens.shape[0],), i32),
            pltpu.SMEM((qrows.shape[1],), i32),
            pltpu.SMEM((qrows.shape[1],), i32),
            pltpu.VMEM((rel.shape[0], width), F32),
            pltpu.VMEM((rows + 64, width), BF),
            pltpu.VMEM((rows + 64, width), BF),
            pltpu.VMEM((nq, WIN, 256), F32),
        ],
        (me, aq, lens, qrows, bucket, dec, g1, rel, wqkv),
        us=40,
    )


def own_heads(x):
    return jnp.concatenate([x[a * 64 : (a + 1) * 64, a * TQ : (a + 1) * TQ] for a in range(4)], axis=0)


def in_pairs(lo, hi, work):
    def two(i, _):
        work(lo + 2 * i)
        work(lo + 2 * i + 1)
        return 0

    lax.fori_loop(0, (hi - lo) // 2, two, 0)

    @pl.when((hi - lo) % 2 == 1)
    def _():
        work(hi - 1)


def kv_cross_kernel(
    me_ref,
    lo_ref,
    hi_ref,
    start_ref,
    size_ref,
    q_ref,
    *rest,
    pieces,
):
    enc = rest[:pieces]
    wkv_ref, k_any, v_any, kt_any, o_ref, lse_ref, vt, k_ref, v_ref, kt_ref, out_sem, qst, s_scr, m_scr, l_scr, acc = rest[
        pieces:
    ]
    rows, width = q_ref.shape
    nq, tiles = width // 256, rows // TQ
    n = enc[0].shape[0]
    for r in range(pieces):
        at = pl.ds(pl.multiple_of((me_ref[0] ^ r) * n, n), n)
        kk = dot(enc[r][...], wkv_ref[:, :width]).astype(BF)
        k_ref[at, :] = kk
        kt_ref[:, at] = kk.T
        vv = dot(enc[r][...], wkv_ref[:, width:]).astype(BF)
        v_ref[at, :] = vv
        vt[:, at] = vv.T
    leaving = [
        pltpu.make_async_copy(a, b, out_sem.at[i])
        for i, (a, b) in enumerate(((k_ref, k_any), (v_ref, v_any), (kt_ref, kt_any)))
    ]
    for c in leaving:
        c.start()

    def tile(t, _):
        st = start_ref[pl.ds(t, 1), :]
        sz = size_ref[pl.ds(t, 1), :]
        lo = lo_ref[t]
        hi = hi_ref[t]
        row = pl.ds(pl.multiple_of(t * TQ, TQ), TQ)
        for c in range(nq):
            qst[c] = stack4(q_ref[row, c * 256 : (c + 1) * 256])
            m_scr[c] = jnp.full((8, 256), NEG, F32)
            l_scr[c] = jnp.zeros((8, 256), F32)
            acc[c] = jnp.zeros((256, 256), F32)

        def scores(j):
            kr = pl.ds(pl.multiple_of(j * TK, TK), TK)
            mask = range_mask(j * TK, TK, st, sz)
            for c in range(nq):
                s = dot_nt(k_ref[kr, c * 256 : (c + 1) * 256], qst[c])
                s = jnp.where(mask, s, NEG)
                s_scr[c, kr, :] = s
                m_scr[c] = jnp.maximum(m_scr[c], red(s, jnp.max))

        in_pairs(lo, hi, scores)
        for c in range(nq):
            m_scr[c] = jnp.broadcast_to(jnp.max(m_scr[c], axis=0, keepdims=True), (8, 256))

        def mix(j):
            kr = pl.ds(pl.multiple_of(j * TK, TK), TK)
            for c in range(nq):
                p = jnp.exp(s_scr[c, kr, :] - m_scr[c][0:1])
                l_scr[c] += red(p, jnp.sum)
                acc[c] += dot(vt[c * 256 : (c + 1) * 256, kr], p.astype(BF))

        in_pairs(lo, hi, mix)
        for c in range(nq):
            l = jnp.sum(l_scr[c], axis=0, keepdims=True)
            lse_ref[t, c] = m_scr[c][0:1] + jnp.log(l)
            o_ref[row, c * 256 : (c + 1) * 256] = own_heads(acc[c] * (1.0 / l)).T
        return 0

    lax.fori_loop(0, tiles, tile, 0)
    for c in leaving:
        c.wait()


def kv_cross(me, lo, hi, start, size, q, enc, wkv):
    rows, width = q.shape
    tiles, nq = rows // TQ, width // 256
    keys = len(enc) * enc[0].shape[0]
    return call(
        functools.partial(kv_cross_kernel, pieces=len(enc)),
        "kv_cross",
        (
            sds((keys, width), BF),
            sds((keys, width), BF),
            sds((width, keys), BF),
            sds((rows, width), F32),
            sds((tiles, nq, 1, 256), F32),
        ),
        [SM] * 3 + [VM] * (3 + len(enc) + 1),
        (pl.BlockSpec(memory_space=pl.ANY),) * 3 + (VM, VM),
        [
            pltpu.VMEM((width, keys), BF),
            pltpu.VMEM((keys, width), BF),
            pltpu.VMEM((keys, width), BF),
            pltpu.VMEM((width, keys), BF),
            pltpu.SemaphoreType.DMA((3,)),
            pltpu.VMEM((nq, 256, 256), BF),
            pltpu.VMEM((nq, keys, 256), F32),
            pltpu.VMEM((nq, 8, 256), F32),
            pltpu.VMEM((nq, 8, 256), F32),
            pltpu.VMEM((nq, 256, 256), F32),
        ],
        (me, lo, hi, start, size, q, *enc, wkv),
        us=80,
    )


def ffn_kernel(
    me_ref,
    src_ref,
    x1_ref,
    ocross_ref,
    gain_ref,
    cot_ref,
    wco_ref,
    win_ref,
    wout_ref,
    keep_ref,
    send_ref,
    x2_ref,
    dh_ref,
    g_ref,
    oc_ref,
    out_ref,
    h3,
    h3t,
    out_acc,
    *,
    last,
):
    i = pl.program_id(0)
    me_b, me_g = me_ref[0], me_ref[1]
    f = me_b ^ i
    rows, width = x1_ref.shape
    quarter = width // 4
    half = quarter // 2

    @pl.when(i == 0)
    def _():
        hot = onehot_rows(src_ref[...])
        g_ref[...] = dot_tn(hot, cot_ref[...]).astype(BF)
        oc = ocross_ref[...].astype(BF)
        oc_ref[...] = oc
        x2 = x1_ref[...] + dot(oc, wco_ref[...])
        x2_ref[...] = x2
        n = (x2 * rms(x2) * gain_ref[...]).astype(BF)
        h3[...] = n
        h3t[...] = n.T
        out_acc[...] = jnp.zeros_like(out_acc)
        dh_ref[...] = jnp.zeros_like(dh_ref)

    u, slope = gelu_both(dot(h3[...], win_ref[...]))
    u = u.astype(BF)
    out_acc[...] += dot(u, wout_ref[...])
    da = (slope * dot_nt(g_ref[...], wout_ref[...])).astype(BF)
    dh_ref[...] += dot_nt(da, win_ref[...])
    dwo = dot_tn(u, g_ref[...]).astype(BF)
    for s in range(8):
        at = (i >> 1) * 8 + slot_of(me_g ^ s)

        @pl.when((i & 1) == 0)
        def _():
            keep_ref[at, half:, :] = dwo[s * half : (s + 1) * half]

        @pl.when((i & 1) == 1)
        def _():
            send_ref[at, half:, :] = dwo[s * half : (s + 1) * half]

    for r in range(4):
        part = h3t[pl.ds(pl.multiple_of((me_b ^ r) * quarter, quarter), quarter), :]
        dwi = dot(part, da).astype(BF)
        target = send_ref if r & 1 else keep_ref
        for b in range(2):
            rel = me_g ^ (2 * f + b)
            at = (rel & 1) * 8 + (r >> 1) * 4 + (rel & 2) + ((rel >> 2) & 1)
            target[at, :half, :] = dwi[b * half : (b + 1) * half]

    @pl.when(i == last)
    def _():
        out = (x2_ref[...] + out_acc[...]).astype(BF)
        out_ref[...] = dot(onehot_rows(src_ref[...]), out).astype(BF)


def ffn(me, src, x1, ocross, gain, cot, wco, win, wout):
    rows, width = x1.shape
    steps = win.shape[1] // width
    half = width // 8
    full = lambda a: pl.BlockSpec(a.shape, lambda i, m: (0,) * len(a.shape))
    outs = (
        sds((16, 2 * half, width), BF),
        sds((16, 2 * half, width), BF),
        sds((rows, width), F32),
        sds((rows, width), F32),
        sds((rows, width), BF),
        sds((rows, width), BF),
        sds((rows, width), BF),
    )
    ins = (src, x1, ocross, gain, cot, wco)
    grid_spec = pltpu.PrefetchScalarGridSpec(
        num_scalar_prefetch=1,
        grid=(steps,),
        in_specs=[full(a) for a in ins]
        + [
            pl.BlockSpec((width, width), lambda i, m: (0, m[0] ^ i)),
            pl.BlockSpec((width, width), lambda i, m: (m[0] ^ i, 0)),
        ],
        out_specs=tuple(full(a) for a in outs),
        scratch_shapes=[
            pltpu.VMEM((rows, width), BF),
            pltpu.VMEM((width, rows), BF),
            pltpu.VMEM((rows, width), F32),
        ],
    )
    return pl.pallas_call(
        functools.partial(ffn_kernel, last=steps - 1),
        out_shape=outs,
        grid_spec=grid_spec,
        compiler_params=pltpu.CompilerParams(vmem_limit_bytes=LIMIT),
        cost_estimate=pl.CostEstimate(flops=60 * 10**11, bytes_accessed=30 << 20, transcendentals=0),
        name="ffn",
    )(me, *ins, win, wout)


def ffn_back_kernel(x2_ref, dh_ref, g_ref, gain_ref, wco_ref, dx2_ref, dyc_ref, do_ref, dgain_ref):
    x2 = x2_ref[...]
    dx, dgain_ref[...] = rms_back(x2, rms(x2), gain_ref[...], dh_ref[...])
    dx2 = g_ref[...].astype(F32) + dx
    dx2_ref[...] = dx2
    dyc_ref[...] = dx2.astype(BF)
    do_ref[...] = dot_nt(dyc_ref[...], wco_ref[...]).astype(BF)


def ffn_back(x2, dh, g, gain, wco):
    rows, width = x2.shape
    return call(
        ffn_back_kernel,
        "ffn_back",
        (sds((rows, width), F32), sds((rows, width), BF), sds((rows, width), BF), sds((1, width), F32)),
        [VM] * 5,
        (VM,) * 4,
        [],
        (x2, dh, g, gain, wco),
        us=30,
    )


def cross_back_kernel(
    me_ref,
    lo_ref,
    hi_ref,
    start_ref,
    size_ref,
    q_ref,
    do_ref,
    o_ref,
    lse_ref,
    k_ref,
    v_ref,
    kt_ref,
    dq_ref,
    keep_ref,
    send_ref,
    qs,
    dos,
    del_scr,
    dka,
    dva,
    dqt,
    ps,
    dss,
    *,
    scale,
):
    rows, width = q_ref.shape
    nq, tiles = width // 256, rows // TQ
    dka[...] = jnp.zeros_like(dka)
    dva[...] = jnp.zeros_like(dva)

    def tile(t, _):
        st = start_ref[pl.ds(t, 1), :]
        sz = size_ref[pl.ds(t, 1), :]
        row = pl.ds(pl.multiple_of(t * TQ, TQ), TQ)
        for c in range(nq):
            cs = slice(c * 256, (c + 1) * 256)
            qs[c] = stack4(q_ref[row, cs])
            b = do_ref[row, cs]
            dos[c] = stack4(b)
            product = (b.astype(F32) * o_ref[row, cs]).T
            total = jnp.concatenate(
                [jnp.sum(product[h * 64 : (h + 1) * 64], axis=0, keepdims=True) for h in range(4)], axis=1
            )
            del_scr[c] = jnp.broadcast_to(total, (8, 256))
            dqt[c] = jnp.zeros((256, 256), F32)

        def probs(j, slot):
            kr = pl.ds(pl.multiple_of(j * TK, TK), TK)
            mask = range_mask(j * TK, TK, st, sz)
            for c in range(nq):
                cs = slice(c * 256, (c + 1) * 256)
                s = dot_nt(k_ref[kr, cs], qs[c])
                p = jnp.where(mask, jnp.exp(s - lse_ref[t, c]), 0.0)
                dp = dot_nt(v_ref[kr, cs], dos[c])
                ps[slot, c] = p.astype(BF)
                dss[slot, c] = (p * (dp - del_scr[c][0:1])).astype(BF)

        def grads(j, slot):
            kr = pl.ds(pl.multiple_of(j * TK, TK), TK)
            for c in range(nq):
                cs = slice(c * 256, (c + 1) * 256)
                ds = dss[slot, c]
                dva[kr, cs] += dot(ps[slot, c], dos[c])
                dka[kr, cs] += dot(ds, qs[c])
                dqt[c] += dot(kt_ref[cs, kr], ds)

        lo = lo_ref[t]
        hi = hi_ref[t]

        def two(i, _):
            probs(lo + 2 * i, 0)
            probs(lo + 2 * i + 1, 1)
            grads(lo + 2 * i, 0)
            grads(lo + 2 * i + 1, 1)
            return 0

        lax.fori_loop(0, (hi - lo) // 2, two, 0)

        @pl.when((hi - lo) % 2 == 1)
        def _():
            probs(hi - 1, 0)
            grads(hi - 1, 0)

        for c in range(nq):
            cs = slice(c * 256, (c + 1) * 256)
            dq_ref[row, cs] = (own_heads(dqt[c]).T * scale).astype(BF)
        return 0

    lax.fori_loop(0, tiles, tile, 0)
    n = keep_ref.shape[1]
    for r in range(4):
        at = pl.ds(pl.multiple_of((me_ref[0] ^ r) * n, n), n)
        target = send_ref if r & 1 else keep_ref
        target[r >> 1, :, :width] = dka[at, :].astype(BF)
        target[r >> 1, :, width:] = dva[at, :].astype(BF)


def cross_back(me, lo, hi, start, size, q, do, o, lse, k, v, kt, scale, first, nq):
    rows = q.shape[0]
    keys, width = k.shape[0], nq * 256
    tiles = rows // TQ
    at = first // nq
    part = sds((2, keys // 4, 2 * width), BF)
    cols = lambda n: pl.BlockSpec((n, width), lambda i: (0, at))
    whole = lambda a: pl.BlockSpec(a.shape, lambda i: (0,) * len(a.shape))
    outs = (sds((rows, width), BF), part, part)
    return pl.pallas_call(
        functools.partial(cross_back_kernel, scale=scale),
        grid=(1,),
        out_shape=outs,
        in_specs=[
            SM,
            SM,
            SM,
            whole(start),
            whole(size),
            cols(rows),
            cols(rows),
            cols(rows),
            pl.BlockSpec((tiles, nq, 1, 256), lambda i: (0, at, 0, 0)),
            cols(keys),
            cols(keys),
            pl.BlockSpec((width, keys), lambda i: (at, 0)),
        ],
        out_specs=tuple(whole(a) for a in outs),
        scratch_shapes=[pltpu.VMEM((nq, 256, 256), BF)] * 2
        + [
            pltpu.VMEM((nq, 8, 256), F32),
            pltpu.VMEM((keys, width), F32),
            pltpu.VMEM((keys, width), F32),
            pltpu.VMEM((nq, 256, 256), F32),
            pltpu.VMEM((2, nq, 256, 256), BF),
            pltpu.VMEM((2, nq, 256, 256), BF),
        ],
        compiler_params=pltpu.CompilerParams(vmem_limit_bytes=LIMIT),
        cost_estimate=pl.CostEstimate(flops=10**13, bytes_accessed=30 << 20, transcendentals=0),
        name="cross_back",
    )(me, lo, hi, start, size, q, do, o, lse, k, v, kt)


def cross_in_kernel(
    dq0_ref, dq1_ref, x1_ref, dx2_ref, gain_ref, wcq_ref, wso_ref, dx1_ref, dy1_ref, dos_ref, dgain_ref
):
    x1 = x1_ref[...]
    cut = dq0_ref.shape[1]
    back = dot_nt(dq0_ref[...], wcq_ref[:, :cut]) + dot_nt(dq1_ref[...], wcq_ref[:, cut:])
    dx, dgain_ref[...] = rms_back(x1, rms(x1), gain_ref[...], back)
    dx1 = dx2_ref[...] + dx
    dx1_ref[...] = dx1
    dy1_ref[...] = dx1.astype(BF)
    dos_ref[...] = dot_nt(dy1_ref[...], wso_ref[...]).astype(BF)


def cross_in(dq0, dq1, x1, dx2, gain, wcq, wso):
    rows, width = x1.shape
    return call(
        cross_in_kernel,
        "cross_in",
        (sds((rows, width), F32), sds((rows, width), BF), sds((rows, width), BF), sds((1, width), F32)),
        [VM] * 7,
        (VM,) * 4,
        [],
        (dq0, dq1, x1, dx2, gain, wcq, wso),
        us=60,
    )


def late_kernel(
    start_ref,
    size_ref,
    bucket_ref,
    brow_ref,
    proj_any,
    do_any,
    lse_ref,
    h1_any,
    oself_any,
    dy1_any,
    src_ref,
    x0_any,
    gain_ref,
    dx1_any,
    wqkv_any,
    dg2_ref,
    dg3_ref,
    keep0_any,
    came0_any,
    keep1_any,
    came1_any,
    enc0_any,
    enc2_any,
    wkv_any,
    oc_ref,
    dyc_ref,
    h2_ref,
    dq0_ref,
    dq1_ref,
    fkeep_ref,
    fsend_any,
    d_ref,
    small_ref,
    f,
    own_ref,
    came_any,
    ffn_any,
    projs,
    wbuf,
    both,
    stage,
    enc_t,
    enc_out,
    bias,
    dka,
    dva,
    dsum,
    left_t,
    ss,
    drow,
    sm_in,
    dgain,
    fown,
    frecv,
    q,
    r1,
    r2,
    r3,
    r4,
    r5,
    do_ref,
    h1_ref,
    oself_ref,
    dy1_ref,
    x0_ref,
    dx1_ref,
    enc0_ref,
    enc2_ref,
    send_sem,
    recv_sem,
    sm_send,
    sm_recv,
    x_send,
    x_recv,
    f_send,
    f_recv,
    loc,
    *,
    scale,
):
    rows, width = do_ref.shape
    nq, tiles = width // 256, rows // TQ
    length, buckets = brow_ref.shape[0], 32
    count, step_rows, wide = q.shape[0], q.shape[2], q.shape[3]
    each = count // 8
    quarter = width // 4
    tall = quarter // 4
    n = enc0_ref.shape[0]
    cut = dq0_ref.shape[1]
    g, b = lax.axis_index("grp"), lax.axis_index("blk")
    peers = [(g, b ^ 1), (g, b ^ 2), (g ^ 1, b), (g ^ 2, b), (g ^ 4, b), (g ^ 2, b), (g ^ 1, b)]
    mesh_id = pl.DeviceIdType.MESH

    def local(src, dst, k):
        return pltpu.make_async_copy(src, dst, loc.at[k])

    def remote(src, dst, send, recv, k):
        return pltpu.make_async_remote_copy(
            src_ref=src, dst_ref=dst, send_sem=send, recv_sem=recv, device_id=peers[k], device_id_type=mesh_id
        )

    proj_in = local(proj_any, projs.at[pl.ds(64, rows), :], 0)
    wkv_in = local(wkv_any, wbuf.at[:, pl.ds(0, 2 * width)], 1)
    held_in = [
        local(src, dst, 20 + i)
        for i, (src, dst) in enumerate(
            (
                (oself_any, oself_ref),
                (dy1_any, dy1_ref),
                (enc0_any, enc0_ref),
                (enc2_any, enc2_ref),
                (do_any, do_ref),
                (h1_any, h1_ref),
                (x0_any, x0_ref),
                (dx1_any, dx1_ref),
            )
        )
    ]
    wqkv_in = local(wqkv_any, wbuf, 2)
    dkv_in = []
    for r in range(2):
        for i, (keep, came, at, w) in enumerate(
            ((keep0_any, came0_any, 0, cut), (keep1_any, came1_any, cut, width - cut))
        ):
            for half in range(2):
                from_, to = pl.ds(half * w, w), pl.ds(half * width + at, w)
                k = 3 + 8 * r + 4 * i + 2 * half
                dkv_in.append((r, local(keep.at[r, :, from_], both.at[pl.ds(r * n, n), to], k)))
                dkv_in.append((r, local(came.at[r, :, from_], stage.at[:, to], k + 1)))
    for r, c in dkv_in:
        if r == 0:
            c.start()
    for c in held_in[:4] + [wkv_in, proj_in] + held_in[4:]:
        c.start()

    barrier = pltpu.get_barrier_semaphore()
    for p in peers[:5]:
        pl.semaphore_signal(barrier, inc=1, device_id=p, device_id_type=mesh_id)
    pl.semaphore_wait(barrier, 5)

    f_first = remote(fsend_any, frecv, f_send.at[0], f_recv.at[0], 4)
    f_second = remote(fown, ffn_any.at[1], f_send.at[1], f_recv.at[1], 4)
    f_third = remote(ffn_any.at[pl.ds(0, 2)], ffn_any.at[pl.ds(2, 2)], f_send.at[2], f_recv.at[2], 3)
    f_local = local(fown, ffn_any.at[0], 19)
    f_slices = fown.shape[0] // step_rows
    f_first.start()

    def f_copy(i):
        at = pl.ds(pl.multiple_of(i * step_rows, step_rows), step_rows)
        src, dst = ffn_any.at[pl.ds(0, 4), at, :], ffn_any.at[pl.ds(4, 4), at, :]
        return remote(src, dst, f_send.at[3 + i], f_recv.at[3 + i], 2)

    enc_copy = remote(enc_out, came_any, x_send, x_recv, 1)

    def add(x, y):
        return (x.astype(F32) + y.astype(F32)).astype(BF)

    def core_copy(j):
        at = pl.ds(pl.multiple_of(j * step_rows, step_rows), step_rows)
        return remote(ss.at[:, at, :], r1.at[j], send_sem.at[0, j], recv_sem.at[0, j], 0)

    def copy(k, j):
        src, dst = [
            lambda: (q.at[j, pl.ds(8, 8)], r2.at[j]),
            lambda: (q.at[j, pl.ds(4, 4)], r3.at[j]),
            lambda: (q.at[j, pl.ds(2, 2)], r4.at[j]),
            lambda: (q.at[j, pl.ds(0, 2)], r5.at[j]),
            lambda: (f.at[j, pl.ds(0, 2)], f.at[j, pl.ds(2, 2)]),
            lambda: (f.at[j, pl.ds(0, 4)], f.at[j, pl.ds(4, 4)]),
        ][k - 1]()
        return remote(src, dst, send_sem.at[k, j], recv_sem.at[k, j], k)

    def event(k, j):
        @pl.when((j >= 0) & (j < count))
        def _():
            (core_copy(j) if k == 0 else copy(k, j)).wait()
            if k == 0:
                q[j] = add(q[j], r1[j])
            elif k == 1:
                q[j, 0:8] = add(q[j, 0:8], r2[j])
            elif k == 2:
                q[j, 0:4] = add(q[j, 0:4], r3[j])
            elif k == 3:
                q[j, 0:2] = add(q[j, 0:2], r4[j])
            elif k == 4:
                f[j, 0] = add(q[j, 0], r5[j, 1])
                f[j, 1] = add(q[j, 1], r5[j, 0])
            if k < 6:
                copy(k + 1, j).start()

    def step(t):
        t = jnp.asarray(t, jnp.int32)
        event(0, t + 3)
        for k in range(1, 7):
            event(k, t - 2 * (k - 1))

    def put(right, block):
        for r in range(4):
            part = left_t[pl.ds(pl.multiple_of((b ^ r) * quarter, quarter), quarter), :]
            spread(dot(part, right).astype(BF), r, block)
        start_core(block)

    def spread(grad, r, block):
        for s in range(8):
            at = (r >> 1) * 8 + slot_of(g ^ s)
            y, x = (s >> 1) * tall, (s & 1) * wide
            if r & 1:
                ss[at, block * tall : (block + 1) * tall, :] = grad[y : y + tall, x : x + wide]
            else:
                for k in range(each):
                    piece = grad[y + k * step_rows : y + (k + 1) * step_rows, x : x + wide]
                    q[block * each + k, at] = piece

    def start_core(block):
        for k in range(each):
            core_copy(block * each + k).start()

    left_t[...] = oc_ref[...].T
    put(dyc_ref[...], 0)
    left_t[...] = h2_ref[...].T
    for j in range(each):
        event(0, jnp.int32(j))
    put(jnp.concatenate([dq0_ref[...], dq1_ref[...]], axis=1), 1)
    step(0)
    held_in[0].wait()
    held_in[1].wait()
    left_t[...] = oself_ref[...].T
    for r, c in dkv_in:
        if r == 0:
            c.wait()
    both[:n, :] = add(both[:n, :], stage[...])
    for r, c in dkv_in:
        if r == 1:
            c.start()
    put(dy1_ref[...], 2)
    f_first.wait()
    fown[...] = add(fkeep_ref[...], frecv[...])
    f_local.start()
    f_second.start()
    step(1)

    held_in[2].wait()
    held_in[3].wait()
    enc_t[:, :n] = enc0_ref[...].T
    enc_t[:, n:] = enc2_ref[...].T
    for r, c in dkv_in:
        if r == 1:
            c.wait()
    both[n:, :] = add(both[n:, :], stage[...])
    for i in range(2):
        for r in range(4):
            part = enc_t[pl.ds(pl.multiple_of((b ^ r) * quarter, quarter), quarter), :]
            spread(dot(part, both[:, i * width : (i + 1) * width]).astype(BF), r, 3 + i)
        start_core(3 + i)
        step(2 + i)
    wkv_in.wait()
    enc_out[...] = dot_nt(both[n:, :], wbuf[:, : 2 * width]).astype(BF)
    own_ref[...] = dot_nt(both[:n, :], wbuf[:, : 2 * width])
    wqkv_in.start()

    projs[0:64, :] = jnp.zeros((64, 3 * width), BF)
    fill_bias(brow_ref, bias, nq)
    dka[...] = jnp.zeros_like(dka)
    dva[...] = jnp.zeros_like(dva)
    dsum[...] = jnp.zeros_like(dsum)
    proj_in.wait()
    held_in[4].wait()

    def tile(t):
        row = pl.ds(pl.multiple_of(t * TQ, TQ), TQ)
        held = pl.ds(pl.multiple_of(t * TQ + 64, TQ), TQ)
        win = pl.ds(pl.multiple_of(t * TQ, TQ), WIN)
        mask = range_mask(t * TQ - 64, WIN, start_ref[pl.ds(t, 1), :], size_ref[pl.ds(t, 1), :])
        for c in range(nq):
            cols = slice(c * 256, (c + 1) * 256)
            kcols = slice(width + c * 256, width + (c + 1) * 256)
            vcols = slice(2 * width + c * 256, 2 * width + (c + 1) * 256)
            qs = stack4(projs[held, cols] * jnp.asarray(scale, BF))
            dos = stack4(do_ref[row, cols])
            s = dot_nt(projs[win, kcols], qs) + bias[c]
            p = jnp.where(mask, jnp.exp(s - lse_ref[t, c]), 0.0)
            dp = dot_nt(projs[win, vcols], dos)
            delta = jnp.sum(red(p * dp, jnp.sum), axis=0, keepdims=True)
            ds = p * (dp - delta)
            dsum[c] += ds
            ds = ds.astype(BF)
            dva[win, cols] += dot(p.astype(BF), dos)
            dka[win, cols] += dot(ds, qs)
            projs[held, cols] = (unstack4(dot_tn(ds, projs[win, kcols])) * scale).astype(BF)

    def tile_and_step(t, _):
        tile(t)
        step(t + 4)
        return 0

    lax.fori_loop(0, tiles - 2, tile_and_step, 0)

    def tile_alone(t, _):
        tile(t)
        return 0

    lax.fori_loop(tiles - 2, tiles, tile_alone, 0)
    f_second.wait()
    f_local.wait()
    f_third.start()
    done = tiles + 2
    projs[64:, width : 2 * width] = dka[64:, :].astype(BF)
    projs[64:, 2 * width : 3 * width] = dva[64:, :].astype(BF)
    held_in[5].wait()
    left_t[...] = h1_ref[...].T
    for i in range(3):
        put(projs[64:, i * width : (i + 1) * width], 5 + i)
        step(done)
        step(done + 1)
        done += 2

    dgain[...] = jnp.zeros_like(dgain)
    parts = 5
    block = rows // parts
    wqkv_in.wait()
    held_in[6].wait()
    held_in[7].wait()

    def self_in(i, _):
        at = pl.ds(pl.multiple_of(i * block, block), block)
        held = pl.ds(pl.multiple_of(i * block + 64, 64), block)
        x0 = x0_ref[at, :].astype(F32)
        dx, part = rms_back(x0, rms(x0), gain_ref[...], dot_nt(projs[held, :], wbuf[...]))
        dgain[...] += part
        dx0 = dx1_ref[at, :] + dx
        top = dx0.astype(BF)
        both[at, :width] = top
        both[at, width:] = (dx0 - top.astype(F32)).astype(BF)
        step(done + i)

        @pl.when(i == 2)
        def _():
            enc_copy.start()

        return 0

    lax.fori_loop(0, parts, self_in, 0)
    done += parts

    dist = distances()
    for c in range(nq):
        cols = slice(c * 256, (c + 1) * 256)

        def one(d, _):
            x = jnp.where(dist == d, dsum[c], 0.0)
            drow[pl.ds(d, 1), cols] = jnp.sum(red(x, jnp.sum), axis=0, keepdims=True)
            return 0

        lax.fori_loop(0, length, one, 0)
    lane = lax.broadcasted_iota(jnp.int32, (buckets, length), 1)
    place = jnp.zeros((buckets, length), jnp.int32)
    for d in range(length):
        place = jnp.where(lane == d, bucket_ref[d], place)
    hot = (place == lax.broadcasted_iota(jnp.int32, (buckets, length), 0)).astype(F32)
    head = (
        lax.broadcasted_iota(jnp.int32, (width, 128), 0) // 64
        == lax.broadcasted_iota(jnp.int32, (width, 128), 1)
    ).astype(F32)
    by_bucket = jnp.dot(hot, drow[...], preferred_element_type=F32, precision=lax.Precision.HIGHEST)
    small_ref[...] = jnp.zeros_like(small_ref)
    small_ref[24:, :] = jnp.dot(by_bucket, head, preferred_element_type=F32, precision=lax.Precision.HIGHEST)
    for i, ref in enumerate((dgain, dg2_ref, dg3_ref)):
        for k in range(6):
            small_ref[6 * i + k : 6 * i + k + 1, :] = ref[0:1, k * 128 : (k + 1) * 128]

    def small_copy(k):
        src = small_ref if k == 0 else sm_in.at[k + 4]
        return remote(src, sm_in.at[k], sm_send.at[k], sm_recv.at[k], k)

    def small_sum(k):
        small_copy(k).wait()
        held = small_ref[...] if k == 0 else sm_in[k + 4]
        if k < 4:
            sm_in[k + 5] = held + sm_in[k]
            small_copy(k + 1).start()
        else:
            small_ref[...] = held + sm_in[k]

    small_copy(0).start()
    f_third.wait()
    f_copy(0).start()
    f_copy(1).start()
    step(done)
    hot_rows = onehot_rows(src_ref[...])
    d_ref[...] = dot(hot_rows, both[:rows, :width]) + dot(hot_rows, both[:rows, width:])
    for k in range(5):
        small_sum(k)
        for i in range(2):
            f_copy(2 + 2 * k + i).start()
            step(done + 1 + 2 * k + i)

    def rest(t, _):
        step(t)
        return 0

    lax.fori_loop(done + 11, count + 10, rest, 0)

    def f_end(i, _):
        f_copy(i).wait()
        return 0

    lax.fori_loop(0, f_slices, f_end, 0)
    enc_copy.wait()


def late(
    start, size, bucket, brow, proj, do, lse, h1, oself, dy1, src, x0, gain, dx1, wqkv, dg2, dg3,
    keep0, came0, keep1, came1, enc0, enc2, wkv, oc, dyc, h2, dq0, dq1, fkeep, fsend, scale,
):
    rows, width = do.shape
    nq = width // 256
    n = enc0.shape[0]
    step_rows, wide, tall = 16, width // 2, width // 16
    count = 8 * tall // step_rows
    any_spec = pl.BlockSpec(memory_space=pl.ANY)

    def buf(n):
        return pltpu.VMEM((count, n, step_rows, wide), BF)

    return pl.pallas_call(
        functools.partial(late_kernel, scale=scale),
        out_shape=(
            sds((rows, width), F32),
            sds((56, 128), F32),
            sds((count, 8, step_rows, wide), BF),
            sds((n, width), F32),
            sds((n, width), BF),
            sds((8,) + fkeep.shape, BF),
        ),
        in_specs=[VM, VM, SM, VM, any_spec, any_spec, VM]
        + [any_spec] * 3
        + [VM, any_spec, VM, any_spec]
        + [any_spec, VM, VM]
        + [any_spec] * 7
        + [VM] * 6
        + [any_spec],
        out_specs=(VM,) * 4 + (any_spec, any_spec),
        scratch_shapes=[
            pltpu.VMEM((rows + 64, 3 * width), BF),
            pltpu.VMEM((width, 3 * width), BF),
            pltpu.VMEM((2 * n, 2 * width), BF),
            pltpu.VMEM((n, 2 * width), BF),
            pltpu.VMEM((width, 2 * n), BF),
            pltpu.VMEM((n, width), BF),
            pltpu.VMEM((nq, WIN, 256), F32),
            pltpu.VMEM((rows + 64, width), F32),
            pltpu.VMEM((rows + 64, width), F32),
            pltpu.VMEM((nq, WIN, 256), F32),
            pltpu.VMEM((width, rows), BF),
            pltpu.VMEM((16, 8 * tall, wide), BF),
            pltpu.VMEM(brow.shape, F32),
            pltpu.VMEM((9, 56, 128), F32),
            pltpu.VMEM((1, width), F32),
            pltpu.VMEM(fkeep.shape, BF),
            pltpu.VMEM(fkeep.shape, BF),
            buf(16),
            buf(16),
            buf(8),
            buf(4),
            buf(2),
            buf(2),
        ]
        + [pltpu.VMEM(a.shape, a.dtype) for a in (do, h1, oself, dy1, x0, dx1, enc0, enc2)]
        + [
            pltpu.SemaphoreType.DMA((7, count)),
            pltpu.SemaphoreType.DMA((7, count)),
            pltpu.SemaphoreType.DMA((5,)),
            pltpu.SemaphoreType.DMA((5,)),
            pltpu.SemaphoreType.DMA,
            pltpu.SemaphoreType.DMA,
            pltpu.SemaphoreType.DMA((15,)),
            pltpu.SemaphoreType.DMA((15,)),
            pltpu.SemaphoreType.DMA((28,)),
        ],
        compiler_params=pltpu.CompilerParams(
            vmem_limit_bytes=63 << 20, collective_id=0, has_side_effects=True
        ),
        cost_estimate=pl.CostEstimate(flops=10**13, bytes_accessed=30 << 20, transcendentals=0),
        name="late",
    )(
        start, size, bucket, brow, proj, do, lse, h1, oself, dy1, src, x0, gain, dx1, wqkv, dg2, dg3,
        keep0, came0, keep1, came1, enc0, enc2, wkv, oc, dyc, h2, dq0, dq1, fkeep, fsend,
    )


def last_kernel(
    me_ref, small_ref, ffn_ref, f_ref, own_ref, came_ref, win_ref, wout_ref, co_ref, cq_ref, ckv_ref, qkv_ref, so_ref, enc_ref, g1_ref, g2_ref, g3_ref, rel_ref
):
    half = ffn_ref.shape[1] // 2
    for slot in range(8):
        s = me_ref[1] ^ ((slot >> 2) + (slot & 2) + 4 * (slot & 1))
        rows = pl.ds(pl.multiple_of((s & 1) * half, half), half)
        cols = pl.ds(pl.multiple_of((s >> 1) * 768, 768), 768)
        win_ref[rows, cols] = ffn_ref[slot, :half].astype(F32)
        wout_ref[pl.ds(pl.multiple_of(s * half, half), half), :] = ffn_ref[slot, half:].astype(F32)
    count, _, step_rows, wide = f_ref.shape
    width = 2 * wide
    places = (
        (co_ref, 0), (cq_ref, 0), (so_ref, 0), (ckv_ref, 0), (ckv_ref, width),
        (qkv_ref, 0), (qkv_ref, width), (qkv_ref, 2 * width),
    )
    each = count // 8
    tall = each * step_rows
    for slot in range(8):
        s = me_ref[1] ^ ((slot >> 2) + (slot & 2) + 4 * (slot & 1))
        for n, (out, col) in enumerate(places):
            for k in range(each):
                at = pl.ds(pl.multiple_of((s >> 1) * tall + k * step_rows, step_rows), step_rows)
                cols = pl.ds(pl.multiple_of(col + (s & 1) * wide, 128), wide)
                out[at, cols] = f_ref[n * each + k, slot].astype(F32)
    enc_ref[...] = own_ref[...] + came_ref[...].astype(F32)
    quarter = g1_ref.shape[1]
    for i, ref in enumerate((g1_ref, g2_ref, g3_ref)):
        whole = jnp.concatenate([small_ref[6 * i + k : 6 * i + k + 1, :] for k in range(6)], axis=1)
        for j in range(4):

            @pl.when(me_ref[0] == j)
            def _():
                ref[...] = whole[:, j * quarter : (j + 1) * quarter]

    part, heads = rel_ref.shape
    rel_ref[...] = small_ref[pl.ds(pl.multiple_of(24 + me_ref[0] * part, 8), part), :heads]


def last(me, small, ffn, f, own, came, buckets, heads):
    width = own.shape[1]
    quarter = width // 4
    cols = lambda n: sds((quarter, n * width), F32)
    return call(
        last_kernel,
        "last",
        (cols(4), sds((width, width), F32), cols(1), cols(1), cols(2), cols(3), cols(1), sds(own.shape, F32))
        + (sds((1, quarter), F32),) * 3
        + (sds((buckets // 4, heads), F32),),
        [SM] + [VM] * 5,
        (VM,) * 12,
        [],
        (me, small, ffn, f, own, came),
        us=8,
    )


def hop(x, core=0, xb=0, yb=0, z1=0, z2=0):
    b, g = core | (xb << 1), yb | (z1 << 1) | (z2 << 2)
    groups, blocks = lax.axis_size("grp"), lax.axis_size("blk")
    pairs = [(i * blocks + j, (i ^ g) * blocks + (j ^ b)) for i in range(groups) for j in range(blocks)]
    return lax.ppermute(x, ("grp", "blk"), pairs)


def total(*parts):
    out = parts[0].astype(F32)
    for p in parts[1:]:
        out = out + p.astype(F32)
    return out.astype(BF)


def after(x, *deps):
    return lax.optimization_barrier((x,) + deps)[0]


def fused_body(
    dec_in,
    encodings,
    answer_len,
    answer_question,
    question_rows,
    bucket_table,
    gain_self,
    w_qkv,
    w_self_out,
    rel_bias,
    gain_cross,
    w_cross_q,
    w_cross_kv,
    w_cross_out,
    gain_ffn,
    w_in,
    w_out,
    cotangent,
):
    rows, width = dec_in.shape
    buckets, heads = rel_bias.shape
    scale = 1.0 / math.sqrt(width // heads)
    me_b, me_g = lax.axis_index("blk"), lax.axis_index("grp")
    me = jnp.stack([me_b, me_g]).astype(jnp.int32)
    g1, g2, g3 = (g.reshape(1, width) for g in (gain_self, gain_cross, gain_ffn))

    enc2 = hop(encodings, xb=1)
    enc1 = hop(encodings, core=1)
    src, cstart, csize, sstart, ssize, lo, hi, brow, x0, h1, proj, oself, lse_self = pre(
        me, answer_question, answer_len, question_rows, bucket_table, dec_in, g1, rel_bias, w_qkv, scale
    )
    enc2, oself = lax.optimization_barrier((enc2, oself))
    enc3 = hop(enc2, core=1)
    enc1 = after(enc1, x0)
    x1, h2, qc = mid(x0, oself, w_self_out, g2, w_cross_q, scale)
    k, v, kt, ocross, lse = kv_cross(
        me, lo, hi, cstart, csize, qc, (encodings, enc1, enc2, enc3), w_cross_kv
    )
    f_keep, f_send, x2, dh3, g_low, oc, layer_out = ffn(
        me, src, x1, ocross, g3, cotangent, w_cross_out, w_in, w_out
    )
    f_came = hop(f_send, core=1)
    dx2, dyc, do, dgain3 = ffn_back(x2, dh3, g_low, g3, w_cross_out)
    f_came = after(f_came, do)
    half = width // 8
    i_keep, i_send, o_keep, o_send = (
        total(f_keep[n : n + 8, rows_], f_came[n : n + 8, rows_])
        for rows_ in (slice(0, half), slice(half, 2 * half))
        for n in (0, 8)
    )
    do, o_send, i_send = lax.optimization_barrier((do, o_send, i_send))
    i_came, o_came = hop(i_send, yb=1), hop(o_send, xb=1)
    dq0, keep0, send0 = cross_back(
        me, lo, hi, cstart, csize, qc, do, ocross, lse, k, v, kt, scale, 0, 2
    )
    came0 = hop(send0, core=1)
    i_came, o_came, dq0 = lax.optimization_barrier((i_came, o_came, dq0))
    i_q = [total(i_keep[2 * j : 2 * j + 2], i_came[2 * j : 2 * j + 2]) for j in range(4)]
    o_q = [total(o_keep[2 * j : 2 * j + 2], o_came[2 * j : 2 * j + 2]) for j in range(4)]
    z_send = jnp.concatenate([i_q[1], o_q[1]], axis=1)
    do1, z_send, i_q[2], i_q[3], o_q[2], o_q[3] = lax.optimization_barrier(
        (do, z_send, i_q[2], i_q[3], o_q[2], o_q[3])
    )
    z_came = hop(z_send, z1=1)
    ix, ixz = hop(i_q[2], xb=1), hop(i_q[3], xb=1, z1=1)
    oy, oyz = hop(o_q[2], yb=1), hop(o_q[3], yb=1, z1=1)
    dq1, keep1, send1 = cross_back(
        me, lo, hi, cstart, csize, qc, do1, ocross, lse, k, v, kt, scale, 2, 1
    )
    came1 = hop(send1, core=1)
    z_came, ix, ixz, oy, oyz, dq1 = lax.optimization_barrier((z_came, ix, ixz, oy, oyz, dq1))

    def line(n):
        return jnp.concatenate(
            [
                total(i_q[0][n], z_came[n, :half], ix[n], ixz[n]),
                total(o_q[0][n], z_came[n, half:], oy[n], oyz[n]),
            ],
            axis=0,
        )

    f_keep, f_send = line(0), line(1)
    dx1, dy1, dos, dgain2 = cross_in(dq0, dq1, x1, dx2, g2, w_cross_q, w_self_out)
    came0, came1, dos = lax.optimization_barrier((came0, came1, dos))
    d_dec_in, small, gathered, enc_own, enc_came, f_all = late(
        sstart, ssize, bucket_table, brow, proj, dos, lse_self, h1, oself, dy1, src, x0, g1, dx1, w_qkv,
        dgain2, dgain3, keep0, came0, keep1, came1, encodings, enc2, w_cross_kv, oc, dyc, h2, dq0, dq1,
        f_keep, f_send, scale,
    )
    (
        o_win, o_wout, o_wco, o_wcq, o_wckv, o_wqkv, o_wso, d_encodings, g_self, g_cross, g_ffn, g_rel,
    ) = last(me, small, f_all, gathered, enc_own, enc_came, buckets, heads)
    g_self, g_cross, g_ffn = (g.reshape(-1) for g in (g_self, g_cross, g_ffn))
    return (
        layer_out,
        d_dec_in,
        d_encodings,
        g_self,
        o_wqkv,
        o_wso,
        g_rel,
        g_cross,
        o_wcq,
        o_wckv,
        o_wco,
        g_ffn,
        o_win,
        o_wout,
    )


def solution(mesh):
    rows = P(("grp", "blk"), None)
    fused = mesh.shape["grp"] == 8 and mesh.shape["blk"] == 4
    return jax.shard_map(
        fused_body if fused else body,
        mesh=mesh,
        in_specs=(rows, rows, P(("grp", "blk")), P("grp"), P("grp", None)) + (P(),) * 12 + (rows,),
        out_specs=(rows, rows, rows, P("blk"))
        + (P("blk", None),) * 3
        + (P("blk"),)
        + (P("blk", None),) * 3
        + (P("blk"),)
        + (P("blk", None),) * 2,
        check_vma=False,
    )
```

```python
import functools
import math

import jax
import jax.numpy as jnp
from jax import lax
from jax.experimental import pallas as pl
from jax.experimental.pallas import tpu as pltpu
from jax.sharding import PartitionSpec as P

EPSILON = 1e-06
NEG = -1e30
MASKED = -1e9
TQ = 64
TK = 256
WIN = 128
F32 = jnp.float32
BF = jnp.bfloat16
VM = pl.BlockSpec(memory_space=pltpu.VMEM)
SM = pl.BlockSpec(memory_space=pltpu.SMEM)
LIMIT = 60 << 20


def dot(a, b):
    return jnp.dot(a, b, preferred_element_type=F32)


def dot_tn(a, b):
    return lax.dot_general(a, b, (((0,), (0,)), ((), ())), preferred_element_type=F32)


def dot_nt(a, b):
    return lax.dot_general(a, b, (((1,), (1,)), ((), ())), preferred_element_type=F32)


def stack4(t):
    lane = lax.broadcasted_iota(jnp.int32, t.shape, 1) // 64
    return jnp.concatenate([jnp.where(lane == a, t, jnp.zeros_like(t)) for a in range(4)], axis=0)


def unstack4(s):
    n = s.shape[0] // 4
    lane = lax.broadcasted_iota(jnp.int32, (n, 256), 1) // 64
    out = s[:n]
    for a in range(1, 4):
        out = jnp.where(lane == a, s[a * n : (a + 1) * n], out)
    return out


def range_mask(base, rows, start, size):
    idx = lax.broadcasted_iota(jnp.int32, (rows, start.shape[1]), 0)
    rel = idx - (start - base)
    return (rel >= 0) & (rel < size)


def red(x, op):
    return op(x.reshape(x.shape[0] // 8, 8, x.shape[1]), axis=0)


def cross_fwd_kernel(
    lo_ref, hi_ref, start_ref, size_ref, q_ref, k_ref, vt_ref, o_ref, lse_ref, qst, s_scr, m_scr, l_scr, acc, *, nq, tiles
):
    def tile(t, _):
        st = start_ref[t]
        sz = size_ref[t]
        lo = lo_ref[t]
        hi = hi_ref[t]
        row = pl.ds(pl.multiple_of(t * TQ, TQ), TQ)
        for c in range(nq):
            qst[c] = stack4(q_ref[row, c * 256 : (c + 1) * 256]).T
            m_scr[c] = jnp.full((8, 256), NEG, F32)
            l_scr[c] = jnp.zeros((8, 256), F32)
            acc[c] = jnp.zeros((256, 256), F32)

        def scores(j, _):
            kr = pl.ds(pl.multiple_of(j * TK, TK), TK)
            mask = range_mask(j * TK, TK, st, sz)
            for c in range(nq):
                s = dot(k_ref[kr, c * 256 : (c + 1) * 256], qst[c])
                s = jnp.where(mask, s, NEG)
                s_scr[c, kr, :] = s
                m_scr[c] = jnp.maximum(m_scr[c], red(s, jnp.max))
            return 0

        lax.fori_loop(lo, hi, scores, 0)
        for c in range(nq):
            m_scr[c] = jnp.broadcast_to(jnp.max(m_scr[c], axis=0, keepdims=True), (8, 256))

        def mix(j, _):
            kr = pl.ds(pl.multiple_of(j * TK, TK), TK)
            for c in range(nq):
                p = jnp.exp(s_scr[c, kr, :] - m_scr[c][0:1])
                l_scr[c] += red(p, jnp.sum)
                acc[c] += dot(vt_ref[c * 256 : (c + 1) * 256, kr], p.astype(BF))
            return 0

        lax.fori_loop(lo, hi, mix, 0)
        for c in range(nq):
            l = jnp.sum(l_scr[c], axis=0, keepdims=True)
            lse_ref[t, c] = m_scr[c][0:1] + jnp.log(l)
            o_ref[row, c * 256 : (c + 1) * 256] = unstack4((acc[c] * (1.0 / l)).T)
        return 0

    lax.fori_loop(0, tiles, tile, 0)


def quads_per_step(nq, keys):
    return nq if keys <= 2048 else 1


def cross_fwd(lo, hi, start, size, q, k, vt):
    rows, width = q.shape
    tiles, keys = rows // TQ, k.shape[0]
    nq = quads_per_step(width // 256, keys)
    full = pl.BlockSpec(start.shape, lambda g: (0, 0, 0))
    return pl.pallas_call(
        functools.partial(cross_fwd_kernel, nq=nq, tiles=tiles),
        grid=(width // 256 // nq,),
        out_shape=(
            jax.ShapeDtypeStruct(q.shape, F32),
            jax.ShapeDtypeStruct((tiles, width // 256, 1, 256), F32),
        ),
        in_specs=[
            SM,
            SM,
            full,
            full,
            pl.BlockSpec((rows, nq * 256), lambda g: (0, g)),
            pl.BlockSpec((keys, nq * 256), lambda g: (0, g)),
            pl.BlockSpec((nq * 256, keys), lambda g: (g, 0)),
        ],
        out_specs=(
            pl.BlockSpec((rows, nq * 256), lambda g: (0, g)),
            pl.BlockSpec((tiles, nq, 1, 256), lambda g: (0, g, 0, 0)),
        ),
        scratch_shapes=[
            pltpu.VMEM((nq, 256, 256), BF),
            pltpu.VMEM((nq, keys, 256), F32),
            pltpu.VMEM((nq, 8, 256), F32),
            pltpu.VMEM((nq, 8, 256), F32),
            pltpu.VMEM((nq, 256, 256), F32),
        ],
        compiler_params=pltpu.CompilerParams(vmem_limit_bytes=LIMIT),
        name="cross_fwd",
    )(lo, hi, start, size, q, k, vt)


def cross_bwd_kernel(
    lo_ref,
    hi_ref,
    start_ref,
    size_ref,
    q_ref,
    do_ref,
    o_ref,
    lse_ref,
    k_ref,
    v_ref,
    kt_ref,
    dq_ref,
    dk_ref,
    dv_ref,
    qs,
    qst,
    dos,
    dost,
    del_scr,
    dka,
    dva,
    dqt,
    *,
    nq,
    tiles,
    scale,
):
    dka[...] = jnp.zeros_like(dka)
    dva[...] = jnp.zeros_like(dva)

    def tile(t, _):
        st = start_ref[t]
        sz = size_ref[t]
        row = pl.ds(pl.multiple_of(t * TQ, TQ), TQ)
        for c in range(nq):
            cs = slice(c * 256, (c + 1) * 256)
            a = stack4(q_ref[row, cs])
            qs[c] = a
            qst[c] = a.T
            b = stack4(do_ref[row, cs])
            dos[c] = b
            dost[c] = b.T
            product = do_ref[row, cs].astype(F32) * o_ref[row, cs]
            total = jnp.sum(red(stack4(product).T, jnp.sum), axis=0, keepdims=True)
            del_scr[c] = jnp.broadcast_to(total, (8, 256))
            dqt[c] = jnp.zeros((256, 256), F32)

        def step(j, _):
            kr = pl.ds(pl.multiple_of(j * TK, TK), TK)
            mask = range_mask(j * TK, TK, st, sz)
            for c in range(nq):
                cs = slice(c * 256, (c + 1) * 256)
                s = dot(k_ref[kr, cs], qst[c])
                p = jnp.where(mask, jnp.exp(s - lse_ref[t, c]), 0.0)
                dp = dot(v_ref[kr, cs], dost[c])
                ds = (p * (dp - del_scr[c][0:1])).astype(BF)
                dva[kr, cs] += dot(p.astype(BF), dos[c])
                dka[kr, cs] += dot(ds, qs[c])
                dqt[c] += dot(kt_ref[cs, kr], ds)
            return 0

        lax.fori_loop(lo_ref[t], hi_ref[t], step, 0)
        for c in range(nq):
            cs = slice(c * 256, (c + 1) * 256)
            dq_ref[row, cs] = (unstack4(dqt[c].T) * scale).astype(BF)
        return 0

    lax.fori_loop(0, tiles, tile, 0)
    dk_ref[...] = dka[...].astype(BF)
    dv_ref[...] = dva[...].astype(BF)


def cross_bwd(lo, hi, start, size, q, do, o, lse, k, v, kt, scale):
    rows, width = q.shape
    tiles, keys = rows // TQ, k.shape[0]
    nq = quads_per_step(width // 256, keys)
    full = pl.BlockSpec(start.shape, lambda g: (0, 0, 0))
    own = pl.BlockSpec((rows, nq * 256), lambda g: (0, g))
    held = pl.BlockSpec((keys, nq * 256), lambda g: (0, g), pipeline_mode=pl.Buffered(1))
    out_kv = pl.BlockSpec((keys, nq * 256), lambda g: (0, g), pipeline_mode=pl.Buffered(1))
    return pl.pallas_call(
        functools.partial(cross_bwd_kernel, nq=nq, tiles=tiles, scale=scale),
        grid=(width // 256 // nq,),
        out_shape=(
            jax.ShapeDtypeStruct(q.shape, BF),
            jax.ShapeDtypeStruct(k.shape, BF),
            jax.ShapeDtypeStruct(k.shape, BF),
        ),
        in_specs=[
            SM,
            SM,
            full,
            full,
            own,
            own,
            own,
            pl.BlockSpec((tiles, nq, 1, 256), lambda g: (0, g, 0, 0)),
            held,
            held,
            pl.BlockSpec((nq * 256, keys), lambda g: (g, 0), pipeline_mode=pl.Buffered(1)),
        ],
        out_specs=(own, out_kv, out_kv),
        scratch_shapes=[pltpu.VMEM((nq, 256, 256), BF)] * 4
        + [
            pltpu.VMEM((nq, 8, 256), F32),
            pltpu.VMEM((keys, nq * 256), F32),
            pltpu.VMEM((keys, nq * 256), F32),
            pltpu.VMEM((nq, 256, 256), F32),
        ],
        compiler_params=pltpu.CompilerParams(vmem_limit_bytes=LIMIT),
        name="cross_bwd",
    )(lo, hi, start, size, q, do, o, lse, k, v, kt)


def distances():
    j = lax.broadcasted_iota(jnp.int32, (WIN, 256), 0)
    i = lax.broadcasted_iota(jnp.int32, (WIN, 256), 1) % 64
    return WIN - TQ + i - j


def fill_window(proj_ref, kp, vp, width):
    kp[0:64, :] = jnp.zeros((64, width), BF)
    vp[0:64, :] = jnp.zeros((64, width), BF)
    kp[64:, :] = proj_ref[:, width : 2 * width]
    vp[64:, :] = proj_ref[:, 2 * width : 3 * width]


def fill_bias(brow_ref, bias, nq):
    dist = distances()
    for c in range(nq):
        cs = slice(c * 256, (c + 1) * 256)

        def add(d, held):
            return jnp.where(dist == d, brow_ref[pl.ds(d, 1), cs], held)

        bias[c] = lax.fori_loop(0, brow_ref.shape[0], add, jnp.full((WIN, 256), MASKED, F32))


def self_fwd_kernel(start_ref, size_ref, brow_ref, proj_ref, o_ref, lse_ref, kp, vp, bias, *, nq, tiles, scale):
    width = nq * 256
    fill_window(proj_ref, kp, vp, width)
    fill_bias(brow_ref, bias, nq)

    def tile(t, _):
        row = pl.ds(pl.multiple_of(t * TQ, TQ), TQ)
        win = pl.ds(pl.multiple_of(t * TQ, TQ), WIN)
        mask = range_mask(t * TQ - 64, WIN, start_ref[t], size_ref[t])
        for c in range(nq):
            cs = slice(c * 256, (c + 1) * 256)
            qst = stack4(proj_ref[row, cs] * jnp.asarray(scale, BF)).T
            s = jnp.where(mask, dot(kp[win, cs], qst) + bias[c], MASKED)
            m = jnp.max(red(s, jnp.max), axis=0, keepdims=True)
            p = jnp.exp(s - m)
            l = jnp.sum(red(p, jnp.sum), axis=0, keepdims=True)
            p = (p * (1.0 / l)).astype(BF)
            o_ref[row, cs] = unstack4(dot_tn(p, vp[win, cs])).astype(BF)
            lse_ref[t, c] = m + jnp.log(l)
        return 0

    lax.fori_loop(0, tiles, tile, 0)


def self_fwd(start, size, brow, proj, scale):
    rows, width = proj.shape[0], proj.shape[1] // 3
    nq, tiles = width // 256, rows // TQ
    return pl.pallas_call(
        functools.partial(self_fwd_kernel, nq=nq, tiles=tiles, scale=scale),
        out_shape=(
            jax.ShapeDtypeStruct((rows, width), BF),
            jax.ShapeDtypeStruct((tiles, nq, 1, 256), F32),
        ),
        in_specs=[VM] * 4,
        out_specs=(VM, VM),
        scratch_shapes=[
            pltpu.VMEM((rows + 64, width), BF),
            pltpu.VMEM((rows + 64, width), BF),
            pltpu.VMEM((nq, WIN, 256), F32),
        ],
        compiler_params=pltpu.CompilerParams(vmem_limit_bytes=LIMIT),
        name="self_fwd",
    )(start, size, brow, proj)


def self_bwd_kernel(
    start_ref,
    size_ref,
    brow_ref,
    proj_ref,
    do_ref,
    lse_ref,
    dproj_ref,
    dbrow_ref,
    kp,
    vp,
    bias,
    dka,
    dva,
    dsum,
    *,
    nq,
    tiles,
    scale,
):
    width = nq * 256
    fill_window(proj_ref, kp, vp, width)
    fill_bias(brow_ref, bias, nq)
    dka[...] = jnp.zeros_like(dka)
    dva[...] = jnp.zeros_like(dva)
    dsum[...] = jnp.zeros_like(dsum)

    def tile(t, _):
        row = pl.ds(pl.multiple_of(t * TQ, TQ), TQ)
        win = pl.ds(pl.multiple_of(t * TQ, TQ), WIN)
        mask = range_mask(t * TQ - 64, WIN, start_ref[t], size_ref[t])
        for c in range(nq):
            cs = slice(c * 256, (c + 1) * 256)
            qs = stack4(proj_ref[row, cs] * jnp.asarray(scale, BF))
            dos = stack4(do_ref[row, cs])
            s = dot(kp[win, cs], qs.T) + bias[c]
            p = jnp.where(mask, jnp.exp(s - lse_ref[t, c]), 0.0)
            dp = dot(vp[win, cs], dos.T)
            delta = jnp.sum(red(p * dp, jnp.sum), axis=0, keepdims=True)
            ds = p * (dp - delta)
            dsum[c] += ds
            ds = ds.astype(BF)
            dva[win, cs] += dot(p.astype(BF), dos)
            dka[win, cs] += dot(ds, qs)
            dproj_ref[row, cs] = (unstack4(dot_tn(ds, kp[win, cs])) * scale).astype(BF)
        return 0

    lax.fori_loop(0, tiles, tile, 0)
    dproj_ref[:, width : 2 * width] = dka[64:, :].astype(BF)
    dproj_ref[:, 2 * width : 3 * width] = dva[64:, :].astype(BF)
    dist = distances()
    for c in range(nq):
        cs = slice(c * 256, (c + 1) * 256)

        def one(d, _):
            x = jnp.where(dist == d, dsum[c], 0.0)
            dbrow_ref[pl.ds(d, 1), cs] = jnp.sum(red(x, jnp.sum), axis=0, keepdims=True)
            return 0

        lax.fori_loop(0, brow_ref.shape[0], one, 0)


def self_bwd(start, size, brow, proj, do, lse, scale):
    rows, width = proj.shape[0], proj.shape[1] // 3
    nq, tiles = width // 256, rows // TQ
    return pl.pallas_call(
        functools.partial(self_bwd_kernel, nq=nq, tiles=tiles, scale=scale),
        out_shape=(jax.ShapeDtypeStruct((rows, 3 * width), BF), jax.ShapeDtypeStruct(brow.shape, F32)),
        in_specs=[VM] * 6,
        out_specs=(VM, VM),
        scratch_shapes=[
            pltpu.VMEM((rows + 64, width), BF),
            pltpu.VMEM((rows + 64, width), BF),
            pltpu.VMEM((nq, WIN, 256), F32),
            pltpu.VMEM((rows + 64, width), F32),
            pltpu.VMEM((rows + 64, width), F32),
            pltpu.VMEM((nq, WIN, 256), F32),
        ],
        compiler_params=pltpu.CompilerParams(vmem_limit_bytes=LIMIT),
        name="self_bwd",
    )(start, size, brow, proj, do, lse)


def norm_rows(x, gain):
    inverse = lax.rsqrt(jnp.mean(x * x, axis=-1, keepdims=True) + EPSILON)
    return x * inverse * gain, inverse


def norm_back(x, inverse, gain, grad):
    scaled = grad * gain
    mean = jnp.mean(x * scaled, axis=-1, keepdims=True)
    return inverse * scaled - x * inverse * inverse * inverse * mean, jnp.sum(grad * x * inverse, axis=0)


def swap(x, axis, bit):
    size = lax.axis_size(axis)
    return lax.ppermute(x, axis, [(i, i ^ bit) for i in range(size)])


def bits_of(axis):
    size = lax.axis_size(axis)
    return [1 << b for b in range(size.bit_length() - 1)]


def gather_parts(x, axis):
    parts = {0: x}
    for bit in reversed(bits_of(axis)):
        for r in list(parts):
            parts[r ^ bit] = swap(parts[r], axis, bit)
    return parts


def add_low(a, b):
    return (a.astype(F32) + b.astype(F32)).astype(BF)


def scatter_sum(x, axis, order):
    size = x.shape[0]
    live = list(range(size))
    block = x
    for bit in order:
        keep = [r for r in live if not r & bit]
        send = [r for r in live if r & bit]
        k = jnp.stack([block[live.index(r)] for r in keep])
        s = jnp.stack([block[live.index(r)] for r in send])
        block = add_low(k, swap(s, axis, bit))
        live = keep
    return block[0]


def gather_sum(x, axis, order):
    parts = [0]
    block = x[None]
    for bit in order:
        block = jnp.concatenate([block, swap(block, axis, bit)], axis=0)
        parts = parts + [r ^ bit for r in parts]
    inverse = [parts.index(r) for r in range(len(parts))]
    return block, inverse


def relative(x, axis):
    size = lax.axis_size(axis)
    me = lax.axis_index(axis)
    return jnp.stack([lax.dynamic_index_in_dim(x, me ^ r, 0, keepdims=False) for r in range(size)])


def reduce_all(x):
    blocks, rows, width = x.shape
    groups = lax.axis_size("grp")
    part = scatter_sum(relative(x, "blk"), "blk", bits_of("blk"))
    part = relative(part.reshape(groups, rows // groups, width), "grp")
    part = scatter_sum(part, "grp", bits_of("grp"))
    whole, inverse = gather_sum(part, "grp", list(reversed(bits_of("grp"))))
    me = lax.axis_index("grp")
    index = jnp.asarray(inverse, jnp.int32)[jnp.arange(groups) ^ me]
    return jnp.take(whole, index, axis=0).reshape(rows, width)


def sum_everywhere(x):
    for axis in ("blk", "grp"):
        for bit in bits_of(axis):
            x = x + swap(x, axis, bit)
    return x


def pack(grads, blocks):
    out = []
    for g in grads:
        k, n = g.shape
        r = g.reshape(blocks, k // blocks, n // 768, 768).transpose(0, 2, 1, 3)
        out.append(r.reshape(blocks, -1, 768))
    return jnp.concatenate(out, axis=1)


def unpack(rows, shapes, blocks):
    out, at = [], 0
    for k, n in shapes:
        count = k // blocks * (n // 768)
        piece = rows[at : at + count].reshape(n // 768, k // blocks, 768)
        out.append(piece.transpose(1, 0, 2).reshape(k // blocks, n).astype(F32))
        at += count
    return out


def body(
    dec_in,
    encodings,
    answer_len,
    answer_question,
    question_rows,
    bucket_table,
    gain_self,
    w_qkv,
    w_self_out,
    rel_bias,
    gain_cross,
    w_cross_q,
    w_cross_kv,
    w_cross_out,
    gain_ffn,
    w_in,
    w_out,
    cotangent,
):
    answers = answer_len.shape[0]
    length = bucket_table.shape[0]
    rows, width = dec_in.shape
    heads = rel_bias.shape[1]
    buckets = rel_bias.shape[0]
    scale = 1.0 / math.sqrt(width // heads)
    enc_rows = encodings.shape[0]
    blocks = lax.axis_size("blk")
    me = lax.axis_index("blk")
    tiles = rows // TQ
    nq = width // 256

    enc_parts = gather_parts(encodings, "blk")

    own_q = lax.dynamic_slice_in_dim(answer_question, me * answers, answers, 0)
    a_index = jnp.arange(answers)
    before = (own_q[None, :] < own_q[:, None]) | (
        (own_q[None, :] == own_q[:, None]) & (a_index[None, :] < a_index[:, None])
    )
    rank = jnp.sum(before.astype(jnp.int32), axis=1)
    target = (rank[:, None] * length + jnp.arange(length)[None, :]).reshape(rows)
    forward_perm = (jnp.arange(rows)[:, None] == target[None, :]).astype(BF)
    sorted_len = jnp.sum(jnp.where(rank[:, None] == a_index[None, :], answer_len[:, None], 0), axis=0)
    ends_q = jnp.cumsum(question_rows[0])
    starts_q = ends_q - question_rows[0]
    sorted_q = jnp.sum(jnp.where(rank[:, None] == a_index[None, :], own_q[:, None], 0), axis=0)
    token_q = jnp.repeat(sorted_q, length)
    pick = token_q[:, None] == jnp.arange(question_rows.shape[1])[None, :]
    token_start = jnp.sum(jnp.where(pick, starts_q[None, :], 0), axis=1)
    token_size = jnp.sum(jnp.where(pick, question_rows[0][None, :], 0), axis=1)

    def stacked(v):
        return jnp.tile(v.reshape(tiles, 1, TQ), (1, 1, 4)).astype(jnp.int32)

    c_start, c_size = stacked(token_start), stacked(token_size)
    lo = (token_start.reshape(tiles, TQ)[:, 0] // TK).astype(jnp.int32)
    hi = ((token_start + token_size).reshape(tiles, TQ)[:, -1] + TK - 1) // TK
    hi = hi.astype(jnp.int32)
    s_start = stacked(jnp.arange(rows) // length * length)
    s_size = stacked(jnp.repeat(sorted_len, length))

    bucket_hot = (bucket_table[:, None] == jnp.arange(buckets)[None, :]).astype(F32)
    brow = jnp.repeat(
        jnp.dot(bucket_hot, rel_bias, precision=lax.Precision.HIGHEST), width // heads, axis=1
    )

    x0 = dot(forward_perm, dec_in)
    grad_top = dot(forward_perm, cotangent)
    grad_low = grad_top.astype(BF)
    n1, r1 = norm_rows(x0, gain_self)
    h1 = n1.astype(BF)
    proj = dot(h1, w_qkv).astype(BF)
    o_self, lse_self = self_fwd(s_start, s_size, brow, proj, scale)
    x1 = x0 + dot(o_self, w_self_out)
    n2, r2 = norm_rows(x1, gain_cross)
    h2 = n2.astype(BF)
    qc = (dot(h2, w_cross_q).astype(BF) * jnp.asarray(scale, BF)).astype(BF)

    enc_rel = jnp.stack([enc_parts[r] for r in range(blocks)])
    enc_all = relative(enc_rel, "blk").reshape(blocks * enc_rows, width)
    kv = dot(enc_all, w_cross_kv).astype(BF)
    k_all, v_all = kv[:, :width], kv[:, width:]
    kvt = lax.dot_general(w_cross_kv, enc_all, (((0,), (1,)), ((), ())), preferred_element_type=F32).astype(BF)
    kt_all, vt_all = kvt[:width], kvt[width:]

    o_cross, lse_cross = cross_fwd(lo, hi, c_start, c_size, qc, k_all, vt_all)
    oc = o_cross.astype(BF)
    x2 = x1 + dot(oc, w_cross_out)
    n3, r3 = norm_rows(x2, gain_ffn)
    h3 = n3.astype(BF)
    hidden, gelu_back = jax.vjp(jax.nn.gelu, dot(h3, w_in))
    u = hidden.astype(BF)
    out = (x2 + dot(u, w_out)).astype(BF)
    layer_out = dot_tn(forward_perm, out).astype(BF)

    d_w_out = dot_tn(u, grad_low).astype(BF)
    da = gelu_back(dot_nt(grad_low, w_out))[0].astype(BF)
    d_w_in = dot_tn(h3, da).astype(BF)
    sums_out = reduce_all(pack([d_w_out], blocks))
    sums_in = reduce_all(pack([d_w_in], blocks))
    dx3, d_gain_ffn = norm_back(x2, r3, gain_ffn, dot_nt(da, w_in))
    dx2 = grad_top + dx3
    dyc = dx2.astype(BF)
    d_w_cross_out = dot_tn(oc, dyc).astype(BF)
    d_o = dot_nt(dyc, w_cross_out).astype(BF)
    dqc, dk, dv = cross_bwd(
        lo, hi, c_start, c_size, qc, d_o, o_cross, lse_cross, k_all, v_all, kt_all, scale
    )

    dkv = jnp.concatenate([dk, dv], axis=1).reshape(blocks, enc_rows, 2 * width)
    dkv = relative(dkv, "blk")
    dkv = add_low(dkv[0::2], swap(dkv[1::2], "blk", 1))
    enc_half = enc_rel[0::2]
    dkv_flat = dkv.reshape(-1, 2 * width)
    d_w_cross_kv = dot_tn(enc_half.reshape(-1, width), dkv_flat).astype(BF)
    d_enc = dot_nt(dkv_flat, w_cross_kv).reshape(blocks // 2, enc_rows, width)
    d_enc_parts = {2 * r: d_enc[r] for r in range(blocks // 2)}
    for bit in reversed(bits_of("blk")[1:]):
        for r in [r for r in d_enc_parts if r & bit]:
            came = swap(d_enc_parts.pop(r).astype(BF), "blk", bit)
            d_enc_parts[r ^ bit] = d_enc_parts[r ^ bit] + came.astype(F32)
    d_encodings = d_enc_parts[0]

    d_w_cross_q = dot_tn(h2, dqc).astype(BF)
    sums_cross = reduce_all(pack([d_w_cross_out, d_w_cross_q, d_w_cross_kv], blocks))
    dx_two, d_gain_cross = norm_back(x1, r2, gain_cross, dot_nt(dqc, w_cross_q))
    dx1 = dx2 + dx_two
    dy1 = dx1.astype(BF)
    d_w_self_out = dot_tn(o_self, dy1).astype(BF)
    d_os = dot_nt(dy1, w_self_out).astype(BF)
    dproj, dbrow = self_bwd(s_start, s_size, brow, proj, d_os, lse_self, scale)
    d_w_qkv = dot_tn(h1, dproj).astype(BF)
    sums_self = reduce_all(pack([d_w_qkv, d_w_self_out], blocks))
    dx_one, d_gain_self = norm_back(x0, r1, gain_self, dot_nt(dproj, w_qkv))
    d_rel = jnp.dot(
        bucket_hot.T, jnp.sum(dbrow.reshape(length, heads, -1), axis=2), precision=lax.Precision.HIGHEST
    )
    d_x0 = dx1 + dx_one
    high = d_x0.astype(BF)
    low = (d_x0 - high.astype(F32)).astype(BF)
    d_dec_in = dot_tn(forward_perm, high) + dot_tn(forward_perm, low)

    small = jnp.concatenate([d_gain_self, d_gain_cross, d_gain_ffn, d_rel.reshape(-1)])
    small = sum_everywhere(small.reshape(-1, 128)).reshape(-1)

    def own(v):
        return lax.dynamic_slice_in_dim(v, me * (v.shape[0] // blocks), v.shape[0] // blocks, 0)

    g_self, g_cross, g_ffn = (own(small[i * width : (i + 1) * width]) for i in range(3))
    g_rel = own(small[3 * width :].reshape(buckets, heads))
    (o_wout,) = unpack(sums_out, [w_out.shape], blocks)
    (o_win,) = unpack(sums_in, [w_in.shape], blocks)
    o_wco, o_wcq, o_wckv = unpack(sums_cross, [w_cross_out.shape, w_cross_q.shape, w_cross_kv.shape], blocks)
    o_wqkv, o_wso = unpack(sums_self, [w_qkv.shape, w_self_out.shape], blocks)
    return (
        layer_out,
        d_dec_in,
        d_encodings,
        g_self,
        o_wqkv,
        o_wso,
        g_rel,
        g_cross,
        o_wcq,
        o_wckv,
        o_wco,
        g_ffn,
        o_win,
        o_wout,
    )


def slot_of(rel):
    return (rel & 1) * 4 + (rel & 2) + ((rel >> 2) & 1)


def fill_bias_all(brow_ref, bias, nq):
    dist = distances()

    def add(d, held):
        here = dist == d
        row = pl.ds(d, 1)
        return tuple(jnp.where(here, brow_ref[row, c * 256 : (c + 1) * 256], held[c]) for c in range(nq))

    held = lax.fori_loop(0, brow_ref.shape[0], add, (jnp.full((WIN, 256), MASKED, F32),) * nq)
    for c in range(nq):
        bias[c] = held[c]


def gelu_both(a):
    c = math.sqrt(2.0 / math.pi)
    a2 = a * a
    t = jnp.tanh(c * (a + 0.044715 * (a2 * a)))
    half = 0.5 * (1.0 + t)
    return a * half, half + 0.5 * a * (1.0 - t * t) * (c * (1.0 + 3.0 * 0.044715 * a2))


def rms(x):
    return lax.rsqrt(jnp.mean(x * x, axis=-1, keepdims=True) + EPSILON)


def rms_back(x, inverse, gain, grad):
    scaled = grad * gain
    mean = jnp.mean(x * scaled, axis=-1, keepdims=True)
    unit = x * inverse
    return inverse * (scaled - unit * (inverse * mean)), jnp.sum(grad * unit, axis=0, keepdims=True)


def onehot_rows(src):
    n = src.shape[1]
    return (lax.broadcasted_iota(jnp.int32, (n, n), 0) == src).astype(F32).astype(BF)


def pre_kernel(
    me_ref,
    aq_ref,
    len_ref,
    qrows_ref,
    bucket_ref,
    dec_ref,
    gain1_ref,
    rel_ref,
    wqkv_ref,
    src_ref,
    cstart_ref,
    csize_ref,
    sstart_ref,
    ssize_ref,
    lo_ref,
    hi_ref,
    brow_ref,
    x0_ref,
    h1_ref,
    proj_ref,
    oself_ref,
    lse_ref,
    order,
    qstart,
    qcount,
    place,
    wide,
    kp,
    vp,
    bias,
    *,
    answers,
    length,
    questions,
    scale,
):
    rows, width = dec_ref.shape
    nq, tiles = width // 256, rows // TQ
    base = me_ref[0] * answers
    own = [aq_ref[base + a] for a in range(answers)]
    n = jnp.int32(0)
    first_row = jnp.int32(0)
    for c in range(questions):
        qstart[c] = first_row
        first_row = first_row + qrows_ref[0, c]
        qcount[c] = n
        place[c] = n
        for q in own:
            n = n + (q == c).astype(jnp.int32)
    for a, q in enumerate(own):
        at = place[q]
        order[at] = a
        place[q] = at + 1

    def answer_of(tok):
        ans = jnp.zeros_like(tok)
        for k in range(1, answers):
            ans = ans + (tok >= k * length).astype(jnp.int32)
        return ans

    tok = lax.broadcasted_iota(jnp.int32, (1, rows), 1)
    ans = answer_of(tok)
    src = tok - ans * length
    for k in range(answers):
        src = src + jnp.where(ans == k, order[k] * length, 0)
    src_ref[...] = src

    lane = lax.broadcasted_iota(jnp.int32, (tiles, 256), 1) % TQ
    tok = lane + TQ * lax.broadcasted_iota(jnp.int32, (tiles, 256), 0)
    ans = answer_of(tok)
    sstart_ref[...] = ans * length
    size = jnp.zeros_like(ans)
    for k in range(answers):
        size = size + jnp.where(ans == k, len_ref[order[k]], 0)
    ssize_ref[...] = size
    cstart = jnp.zeros_like(ans)
    csize = jnp.zeros_like(ans) + qrows_ref[0, 0]
    for c in range(1, questions):
        here = ans >= qcount[c]
        cstart = jnp.where(here, qstart[c], cstart)
        csize = jnp.where(here, qrows_ref[0, c], csize)
    cstart_ref[...] = cstart
    csize_ref[...] = csize
    for t in range(tiles):
        q_first = aq_ref[base + order[t * TQ // length]]
        q_last = aq_ref[base + order[(t * TQ + TQ - 1) // length]]
        lo_ref[t] = qstart[q_first] // TK
        hi_ref[t] = (qstart[q_last] + qrows_ref[0, q_last] + TK - 1) // TK

    for c in range(nq):
        head = lax.broadcasted_iota(jnp.int32, (rel_ref.shape[0], 256), 1) // 64
        held = jnp.zeros((rel_ref.shape[0], 256), F32)
        for a in range(4):
            h = c * 4 + a
            held = jnp.where(head == a, rel_ref[:, h : h + 1], held)
        wide[:, c * 256 : (c + 1) * 256] = held
    for d in range(length):
        brow_ref[d : d + 1, :] = wide[pl.ds(bucket_ref[d], 1), :]

    x0 = dot_tn(onehot_rows(src), dec_ref[...])
    x0_ref[...] = x0.astype(BF)
    h1_ref[...] = (x0 * rms(x0) * gain1_ref[...]).astype(BF)
    for i in range(3):
        cs = slice(i * width, (i + 1) * width)
        proj_ref[:, cs] = dot(h1_ref[...], wqkv_ref[:, cs]).astype(BF)
    fill_window(proj_ref, kp, vp, width)
    fill_bias_all(brow_ref, bias, nq)

    def scores(t, c):
        row = pl.ds(pl.multiple_of(t * TQ, TQ), TQ)
        win = pl.ds(pl.multiple_of(t * TQ, TQ), WIN)
        cs = slice(c * 256, (c + 1) * 256)
        qs = stack4(proj_ref[row, cs] * jnp.asarray(scale, BF))
        return dot_nt(kp[win, cs], qs) + bias[c]

    def probs(t, c, s):
        mask = range_mask(t * TQ - 64, WIN, sstart_ref[pl.ds(t, 1), :], ssize_ref[pl.ds(t, 1), :])
        s = jnp.where(mask, s, MASKED)
        m = jnp.max(red(s, jnp.max), axis=0, keepdims=True)
        p = jnp.exp(s - m)
        l = jnp.sum(red(p, jnp.sum), axis=0, keepdims=True)
        lse_ref[t, c] = m + jnp.log(l)
        return (p * (1.0 / l)).astype(BF)

    def mix(t, c, p):
        row = pl.ds(pl.multiple_of(t * TQ, TQ), TQ)
        win = pl.ds(pl.multiple_of(t * TQ, TQ), WIN)
        cs = slice(c * 256, (c + 1) * 256)
        oself_ref[row, cs] = unstack4(dot_tn(p, vp[win, cs])).astype(BF)

    def two_tiles(i, _):
        work = [(2 * i + k, c) for k in range(2) for c in range(nq)]
        s = [scores(t, c) for t, c in work]
        p = [probs(t, c, x) for (t, c), x in zip(work, s)]
        for (t, c), x in zip(work, p):
            mix(t, c, x)
        return 0

    lax.fori_loop(0, tiles // 2, two_tiles, 0)


def mid_kernel(x0_ref, oself_ref, wso_ref, gain2_ref, wcq_ref, x1_ref, h2_ref, qc_ref, *, scale):
    x1 = x0_ref[...].astype(F32) + dot(oself_ref[...], wso_ref[...])
    x1_ref[...] = x1
    h2_ref[...] = (x1 * rms(x1) * gain2_ref[...]).astype(BF)
    qc_ref[...] = dot(h2_ref[...], wcq_ref[...]).astype(BF) * jnp.asarray(scale, BF)


def mid(x0, oself, wso, gain, wcq, scale):
    rows, width = x0.shape
    return call(
        functools.partial(mid_kernel, scale=scale),
        "mid",
        (sds((rows, width), F32), sds((rows, width), BF), sds((rows, width), BF)),
        [VM] * 5,
        (VM,) * 3,
        [],
        (x0, oself, wso, gain, wcq),
        us=8,
    )


def call(kernel, name, out_shape, in_specs, out_specs, scratch, args, us):
    moved = sum(math.prod(a.shape) * a.dtype.itemsize for a in args)
    moved += sum(math.prod(a.shape) * a.dtype.itemsize for a in out_shape)
    return pl.pallas_call(
        kernel,
        out_shape=out_shape,
        in_specs=in_specs,
        out_specs=out_specs,
        scratch_shapes=scratch,
        compiler_params=pltpu.CompilerParams(vmem_limit_bytes=LIMIT),
        cost_estimate=pl.CostEstimate(flops=int(us * 1e11), bytes_accessed=moved, transcendentals=0),
        name=name,
    )(*args)


def sds(shape, dtype):
    return jax.ShapeDtypeStruct(shape, dtype)


def pre(me, aq, lens, qrows, bucket, dec, g1, rel, wqkv, scale):
    rows, width = dec.shape
    tiles, nq, length = rows // TQ, width // 256, bucket.shape[0]
    i32 = jnp.int32
    meta = sds((tiles, 256), i32)
    out = (
        sds((1, rows), i32),
        meta,
        meta,
        meta,
        meta,
        sds((tiles,), i32),
        sds((tiles,), i32),
        sds((length, width), F32),
        sds((rows, width), BF),
        sds((rows, width), BF),
        sds((rows, 3 * width), BF),
        sds((rows, width), BF),
        sds((tiles, nq, 1, 256), F32),
    )
    return call(
        functools.partial(
            pre_kernel, answers=lens.shape[0], length=length, questions=qrows.shape[1], scale=scale
        ),
        "pre",
        out,
        [SM] * 5 + [VM] * 4,
        (VM,) * 5 + (SM, SM) + (VM,) * 6,
        [
            pltpu.SMEM((lens.shape[0],), i32),
            pltpu.SMEM((qrows.shape[1],), i32),
            pltpu.SMEM((qrows.shape[1],), i32),
            pltpu.SMEM((qrows.shape[1],), i32),
            pltpu.VMEM((rel.shape[0], width), F32),
            pltpu.VMEM((rows + 64, width), BF),
            pltpu.VMEM((rows + 64, width), BF),
            pltpu.VMEM((nq, WIN, 256), F32),
        ],
        (me, aq, lens, qrows, bucket, dec, g1, rel, wqkv),
        us=40,
    )


def own_heads(x):
    return jnp.concatenate([x[a * 64 : (a + 1) * 64, a * TQ : (a + 1) * TQ] for a in range(4)], axis=0)


def in_pairs(lo, hi, work):
    def two(i, _):
        work(lo + 2 * i)
        work(lo + 2 * i + 1)
        return 0

    lax.fori_loop(0, (hi - lo) // 2, two, 0)

    @pl.when((hi - lo) % 2 == 1)
    def _():
        work(hi - 1)


def kv_cross_kernel(
    me_ref,
    lo_ref,
    hi_ref,
    start_ref,
    size_ref,
    q_ref,
    *rest,
    pieces,
):
    enc = rest[:pieces]
    wkv_ref, k_any, v_any, kt_any, o_ref, lse_ref, vt, k_ref, v_ref, kt_ref, out_sem, qst, s_scr, m_scr, l_scr, acc = rest[
        pieces:
    ]
    rows, width = q_ref.shape
    nq, tiles = width // 256, rows // TQ
    n = enc[0].shape[0]
    for r in range(pieces):
        at = pl.ds(pl.multiple_of((me_ref[0] ^ r) * n, n), n)
        kk = dot(enc[r][...], wkv_ref[:, :width]).astype(BF)
        k_ref[at, :] = kk
        kt_ref[:, at] = kk.T
        vv = dot(enc[r][...], wkv_ref[:, width:]).astype(BF)
        v_ref[at, :] = vv
        vt[:, at] = vv.T
    leaving = [
        pltpu.make_async_copy(a, b, out_sem.at[i])
        for i, (a, b) in enumerate(((k_ref, k_any), (v_ref, v_any), (kt_ref, kt_any)))
    ]
    for c in leaving:
        c.start()

    def tile(t, _):
        st = start_ref[pl.ds(t, 1), :]
        sz = size_ref[pl.ds(t, 1), :]
        lo = lo_ref[t]
        hi = hi_ref[t]
        row = pl.ds(pl.multiple_of(t * TQ, TQ), TQ)
        for c in range(nq):
            qst[c] = stack4(q_ref[row, c * 256 : (c + 1) * 256])
            m_scr[c] = jnp.full((8, 256), NEG, F32)
            l_scr[c] = jnp.zeros((8, 256), F32)
            acc[c] = jnp.zeros((256, 256), F32)

        def scores(j):
            kr = pl.ds(pl.multiple_of(j * TK, TK), TK)
            mask = range_mask(j * TK, TK, st, sz)
            for c in range(nq):
                s = dot_nt(k_ref[kr, c * 256 : (c + 1) * 256], qst[c])
                s = jnp.where(mask, s, NEG)
                s_scr[c, kr, :] = s
                m_scr[c] = jnp.maximum(m_scr[c], red(s, jnp.max))

        in_pairs(lo, hi, scores)
        for c in range(nq):
            m_scr[c] = jnp.broadcast_to(jnp.max(m_scr[c], axis=0, keepdims=True), (8, 256))

        def mix(j):
            kr = pl.ds(pl.multiple_of(j * TK, TK), TK)
            for c in range(nq):
                p = jnp.exp(s_scr[c, kr, :] - m_scr[c][0:1])
                l_scr[c] += red(p, jnp.sum)
                acc[c] += dot(vt[c * 256 : (c + 1) * 256, kr], p.astype(BF))

        in_pairs(lo, hi, mix)
        for c in range(nq):
            l = jnp.sum(l_scr[c], axis=0, keepdims=True)
            lse_ref[t, c] = m_scr[c][0:1] + jnp.log(l)
            o_ref[row, c * 256 : (c + 1) * 256] = own_heads(acc[c] * (1.0 / l)).T
        return 0

    lax.fori_loop(0, tiles, tile, 0)
    for c in leaving:
        c.wait()


def kv_cross(me, lo, hi, start, size, q, enc, wkv):
    rows, width = q.shape
    tiles, nq = rows // TQ, width // 256
    keys = len(enc) * enc[0].shape[0]
    return call(
        functools.partial(kv_cross_kernel, pieces=len(enc)),
        "kv_cross",
        (
            sds((keys, width), BF),
            sds((keys, width), BF),
            sds((width, keys), BF),
            sds((rows, width), F32),
            sds((tiles, nq, 1, 256), F32),
        ),
        [SM] * 3 + [VM] * (3 + len(enc) + 1),
        (pl.BlockSpec(memory_space=pl.ANY),) * 3 + (VM, VM),
        [
            pltpu.VMEM((width, keys), BF),
            pltpu.VMEM((keys, width), BF),
            pltpu.VMEM((keys, width), BF),
            pltpu.VMEM((width, keys), BF),
            pltpu.SemaphoreType.DMA((3,)),
            pltpu.VMEM((nq, 256, 256), BF),
            pltpu.VMEM((nq, keys, 256), F32),
            pltpu.VMEM((nq, 8, 256), F32),
            pltpu.VMEM((nq, 8, 256), F32),
            pltpu.VMEM((nq, 256, 256), F32),
        ],
        (me, lo, hi, start, size, q, *enc, wkv),
        us=80,
    )


def ffn_kernel(
    src_ref,
    x1_ref,
    ocross_ref,
    gain_ref,
    cot_ref,
    wco_ref,
    win_any,
    wout_any,
    okeep_ref,
    osend_ref,
    wi_ref,
    oc_ref,
    out_ref,
    dx2_ref,
    dyc_ref,
    do_ref,
    dgain_ref,
    win,
    wout,
    h3,
    h3t,
    g_low,
    dh,
    out_acc,
    u_all,
    ik,
    ss,
    ic,
    iy,
    ix,
    even,
    odd,
    came,
    w_sem,
    send_sem,
    recv_sem,
    o_send,
    o_recv,
):
    rows, width = x1_ref.shape
    steps = win.shape[1] // width
    quarter = width // 4
    half = quarter // 2
    g, b = lax.axis_index("grp"), lax.axis_index("blk")
    mesh_id = pl.DeviceIdType.MESH
    peers = [(g, b ^ 1), (g ^ 1, b), (g, b ^ 2)]

    def part(f):
        return pl.ds(pl.multiple_of(f * width, width), width)

    def weights(f):
        return (
            pltpu.make_async_copy(win_any.at[:, part(f)], win.at[:, part(f)], w_sem.at[0, f]),
            pltpu.make_async_copy(wout_any.at[part(f), :], wout.at[part(f), :], w_sem.at[1, f]),
        )

    for f in range(steps):
        for c in weights(f):
            c.start()
    barrier = pltpu.get_barrier_semaphore()
    for p in peers:
        pl.semaphore_signal(barrier, inc=1, device_id=p, device_id_type=mesh_id)
    pl.semaphore_wait(barrier, 3)

    def remote(k, f):
        src, dst = ((ss.at[f], ic.at[f]), (ik.at[f, pl.ds(2, 2)], iy.at[f]), (ik.at[f, pl.ds(1, 1)], ix.at[f]))[k]
        return pltpu.make_async_remote_copy(
            src_ref=src,
            dst_ref=dst,
            send_sem=send_sem.at[k, f],
            recv_sem=recv_sem.at[k, f],
            device_id=peers[k],
            device_id_type=mesh_id,
        )

    o_copy = pltpu.make_async_remote_copy(
        src_ref=odd, dst_ref=came, send_sem=o_send, recv_sem=o_recv, device_id=peers[0], device_id_type=mesh_id
    )

    def add(x, y):
        return (x.astype(F32) + y.astype(F32)).astype(BF)

    def event(k, f):
        @pl.when((f >= 0) & (f < steps))
        def _():
            remote(k, f).wait()
            if k == 0:
                ik[f] = add(ik[f], ic[f])
            elif k == 1:
                ik[f, 0:2] = add(ik[f, 0:2], iy[f])
            else:
                rel = (g >> 1) ^ f
                wi_ref[(rel & 1) * 2 + (rel >> 1)] = add(ik[f, 0], ix[f, 0])
            if k < 2:
                remote(k + 1, f).start()

    hot = onehot_rows(src_ref[...])
    g_low[...] = dot_tn(hot, cot_ref[...]).astype(BF)
    oc_ref[...] = ocross_ref[...].astype(BF)
    x2 = x1_ref[...] + dot(oc_ref[...], wco_ref[...])
    dx2_ref[...] = x2
    n = (x2 * rms(x2) * gain_ref[...]).astype(BF)
    h3[...] = n
    h3t[...] = n.T
    out_acc[...] = jnp.zeros_like(out_acc)
    dh[...] = jnp.zeros_like(dh)

    def hidden(f, _):
        for c in weights(f):
            c.wait()
        u, slope = gelu_both(dot(h3[...], win[:, part(f)]))
        u = u.astype(BF)
        u_all[:, part(f)] = u
        da = (slope * dot_nt(g_low[...], wout[part(f), :])).astype(BF)
        for r in range(4):
            left = h3t[pl.ds(pl.multiple_of((b ^ r) * quarter, quarter), quarter), :]
            dwi = dot(left, da).astype(BF)
            target = ss if r & 1 else ik
            for i in range(2):
                y = (g ^ (2 * f + i)) & 1
                target[f, y * 2 + (r >> 1)] = dwi[i * half : (i + 1) * half]
        remote(0, f).start()
        out_acc[...] += dot(u, wout[part(f), :])
        event(0, f)
        dh[...] += dot_nt(da, win[:, part(f)])
        event(1, f - 1)
        event(2, f - 2)
        return 0

    lax.fori_loop(0, steps, hidden, 0)

    def last_rows(f, _):
        dwo = dot_tn(u_all[:, part(f)], g_low[...]).astype(BF)
        r = b ^ f
        for s in range(8):
            at = (r >> 1) * 8 + slot_of(g ^ s)

            @pl.when((r & 1) == 0)
            def _():
                even[at] = dwo[s * half : (s + 1) * half]

            @pl.when((r & 1) == 1)
            def _():
                odd[at] = dwo[s * half : (s + 1) * half]

        return 0

    lax.fori_loop(0, steps, last_rows, 0)
    o_copy.start()
    event(1, jnp.int32(steps - 1))
    event(2, jnp.int32(steps - 2))
    x2 = dx2_ref[...]
    out = (x2 + out_acc[...]).astype(BF)
    out_ref[...] = dot(onehot_rows(src_ref[...]), out).astype(BF)
    dx, dgain_ref[...] = rms_back(x2, rms(x2), gain_ref[...], dh[...])
    dx2 = g_low[...].astype(F32) + dx
    dx2_ref[...] = dx2
    dyc_ref[...] = dx2.astype(BF)
    do_ref[...] = dot_nt(dyc_ref[...], wco_ref[...]).astype(BF)
    o_copy.wait()
    okeep_ref[...] = add(even[0:8], came[0:8])
    osend_ref[...] = add(even[8:16], came[8:16])
    event(2, jnp.int32(steps - 1))


def ffn(src, x1, ocross, gain, cot, wco, win, wout):
    rows, width = x1.shape
    steps = win.shape[1] // width
    half = width // 8
    any_spec = pl.BlockSpec(memory_space=pl.ANY)
    buf = lambda *n: pltpu.VMEM(n + (half, width), BF)
    tok = lambda d: pltpu.VMEM((rows, width), d)
    return pl.pallas_call(
        ffn_kernel,
        out_shape=(
            sds((8, half, width), BF),
            sds((8, half, width), BF),
            sds((4, half, width), BF),
            sds((rows, width), BF),
            sds((rows, width), BF),
            sds((rows, width), F32),
            sds((rows, width), BF),
            sds((rows, width), BF),
            sds((1, width), F32),
        ),
        in_specs=[VM] * 6 + [any_spec] * 2,
        out_specs=(VM,) * 9,
        scratch_shapes=[
            pltpu.VMEM(win.shape, BF),
            pltpu.VMEM(wout.shape, BF),
            tok(BF),
            pltpu.VMEM((width, rows), BF),
            tok(BF),
            tok(F32),
            tok(F32),
            pltpu.VMEM((rows, win.shape[1]), BF),
            buf(steps, 4),
            buf(steps, 4),
            buf(steps, 4),
            buf(steps, 2),
            buf(steps, 1),
            buf(16),
            buf(16),
            buf(16),
            pltpu.SemaphoreType.DMA((2, steps)),
            pltpu.SemaphoreType.DMA((3, steps)),
            pltpu.SemaphoreType.DMA((3, steps)),
            pltpu.SemaphoreType.DMA,
            pltpu.SemaphoreType.DMA,
        ],
        compiler_params=pltpu.CompilerParams(
            vmem_limit_bytes=63 << 20, collective_id=1, has_side_effects=True
        ),
        cost_estimate=pl.CostEstimate(flops=10**13, bytes_accessed=30 << 20, transcendentals=0),
        name="ffn",
    )(src, x1, ocross, gain, cot, wco, win, wout)


def cross_back_kernel(
    me_ref,
    lo_ref,
    hi_ref,
    start_ref,
    size_ref,
    q_ref,
    do_ref,
    o_ref,
    lse_ref,
    k_ref,
    v_ref,
    kt_ref,
    dq_ref,
    keep_ref,
    send_ref,
    qs,
    dos,
    del_scr,
    dka,
    dva,
    dqt,
    ps,
    dss,
    *,
    scale,
):
    rows, width = q_ref.shape
    nq, tiles = width // 256, rows // TQ
    dka[...] = jnp.zeros_like(dka)
    dva[...] = jnp.zeros_like(dva)

    def tile(t, _):
        st = start_ref[pl.ds(t, 1), :]
        sz = size_ref[pl.ds(t, 1), :]
        row = pl.ds(pl.multiple_of(t * TQ, TQ), TQ)
        for c in range(nq):
            cs = slice(c * 256, (c + 1) * 256)
            qs[c] = stack4(q_ref[row, cs])
            b = do_ref[row, cs]
            dos[c] = stack4(b)
            product = (b.astype(F32) * o_ref[row, cs]).T
            total = jnp.concatenate(
                [jnp.sum(product[h * 64 : (h + 1) * 64], axis=0, keepdims=True) for h in range(4)], axis=1
            )
            del_scr[c] = jnp.broadcast_to(total, (8, 256))
            dqt[c] = jnp.zeros((256, 256), F32)

        def probs(j, slot):
            kr = pl.ds(pl.multiple_of(j * TK, TK), TK)
            mask = range_mask(j * TK, TK, st, sz)
            for c in range(nq):
                cs = slice(c * 256, (c + 1) * 256)
                s = dot_nt(k_ref[kr, cs], qs[c])
                p = jnp.where(mask, jnp.exp(s - lse_ref[t, c]), 0.0)
                dp = dot_nt(v_ref[kr, cs], dos[c])
                ps[slot, c] = p.astype(BF)
                dss[slot, c] = (p * (dp - del_scr[c][0:1])).astype(BF)

        def grads(j, slot):
            kr = pl.ds(pl.multiple_of(j * TK, TK), TK)
            for c in range(nq):
                cs = slice(c * 256, (c + 1) * 256)
                ds = dss[slot, c]
                dva[kr, cs] += dot(ps[slot, c], dos[c])
                dka[kr, cs] += dot(ds, qs[c])
                dqt[c] += dot(kt_ref[cs, kr], ds)

        lo = lo_ref[t]
        hi = hi_ref[t]
        slots = ps.shape[0]

        def two(i, _):
            probs(lo + 2 * i, 0)
            probs(lo + 2 * i + 1, 1)
            grads(lo + 2 * i, 0)
            grads(lo + 2 * i + 1, 1)
            return 0

        if slots == 4:

            def four(i, _):
                for k in range(4):
                    probs(lo + 4 * i + k, k)
                for k in range(4):
                    grads(lo + 4 * i + k, k)
                return 0

            lax.fori_loop(0, (hi - lo) // 4, four, 0)
            lo = lo + (hi - lo) // 4 * 4
        lax.fori_loop(0, (hi - lo) // 2, two, 0)

        @pl.when((hi - lo) % 2 == 1)
        def _():
            probs(hi - 1, 0)
            grads(hi - 1, 0)

        for c in range(nq):
            cs = slice(c * 256, (c + 1) * 256)
            dq_ref[row, cs] = (own_heads(dqt[c]).T * scale).astype(BF)
        return 0

    lax.fori_loop(0, tiles, tile, 0)
    n = keep_ref.shape[1]
    for r in range(4):
        at = pl.ds(pl.multiple_of((me_ref[0] ^ r) * n, n), n)
        target = send_ref if r & 1 else keep_ref
        target[r >> 1, :, :width] = dka[at, :].astype(BF)
        target[r >> 1, :, width:] = dva[at, :].astype(BF)


def cross_back(me, lo, hi, start, size, q, do, o, lse, k, v, kt, scale, first, nq):
    rows = q.shape[0]
    keys, width = k.shape[0], nq * 256
    tiles = rows // TQ
    at = first // nq
    part = sds((2, keys // 4, 2 * width), BF)
    cols = lambda n: pl.BlockSpec((n, width), lambda i: (0, at))
    whole = lambda a: pl.BlockSpec(a.shape, lambda i: (0,) * len(a.shape))
    outs = (sds((rows, width), BF), part, part)
    return pl.pallas_call(
        functools.partial(cross_back_kernel, scale=scale),
        grid=(1,),
        out_shape=outs,
        in_specs=[
            SM,
            SM,
            SM,
            whole(start),
            whole(size),
            cols(rows),
            cols(rows),
            cols(rows),
            pl.BlockSpec((tiles, nq, 1, 256), lambda i: (0, at, 0, 0)),
            cols(keys),
            cols(keys),
            pl.BlockSpec((width, keys), lambda i: (at, 0)),
        ],
        out_specs=tuple(whole(a) for a in outs),
        scratch_shapes=[pltpu.VMEM((nq, 256, 256), BF)] * 2
        + [
            pltpu.VMEM((nq, 8, 256), F32),
            pltpu.VMEM((keys, width), F32),
            pltpu.VMEM((keys, width), F32),
            pltpu.VMEM((nq, 256, 256), F32),
            pltpu.VMEM((4 if nq == 1 else 2, nq, 256, 256), BF),
            pltpu.VMEM((4 if nq == 1 else 2, nq, 256, 256), BF),
        ],
        compiler_params=pltpu.CompilerParams(vmem_limit_bytes=LIMIT),
        cost_estimate=pl.CostEstimate(flops=10**13, bytes_accessed=30 << 20, transcendentals=0),
        name="cross_back",
    )(me, lo, hi, start, size, q, do, o, lse, k, v, kt)


def cross_in_kernel(
    dq0_ref, dq1_ref, x1_ref, dx2_ref, gain_ref, wcq_ref, wso_ref, dx1_ref, dy1_ref, dos_ref, dgain_ref
):
    x1 = x1_ref[...]
    cut = dq0_ref.shape[1]
    back = dot_nt(dq0_ref[...], wcq_ref[:, :cut]) + dot_nt(dq1_ref[...], wcq_ref[:, cut:])
    dx, dgain_ref[...] = rms_back(x1, rms(x1), gain_ref[...], back)
    dx1 = dx2_ref[...] + dx
    dx1_ref[...] = dx1
    dy1_ref[...] = dx1.astype(BF)
    dos_ref[...] = dot_nt(dy1_ref[...], wso_ref[...]).astype(BF)


def cross_in(dq0, dq1, x1, dx2, gain, wcq, wso):
    rows, width = x1.shape
    return call(
        cross_in_kernel,
        "cross_in",
        (sds((rows, width), F32), sds((rows, width), BF), sds((rows, width), BF), sds((1, width), F32)),
        [VM] * 7,
        (VM,) * 4,
        [],
        (dq0, dq1, x1, dx2, gain, wcq, wso),
        us=60,
    )


def late_kernel(
    start_ref,
    size_ref,
    bucket_ref,
    brow_ref,
    proj_any,
    do_any,
    lse_ref,
    h1_any,
    oself_any,
    dy1_any,
    src_ref,
    x0_any,
    gain_ref,
    dx1_any,
    wqkv_any,
    dg2_ref,
    dg3_ref,
    keep0_any,
    came0_any,
    keep1_any,
    came1_any,
    enc0_any,
    enc2_any,
    wkv_any,
    oc_ref,
    dyc_ref,
    h2_ref,
    dq0_ref,
    dq1_ref,
    wpair_any,
    fkeep_ref,
    fsend_any,
    d_ref,
    small_ref,
    f,
    own_ref,
    came_any,
    ffn_any,
    projs,
    wbuf,
    both,
    stage,
    enc_t,
    enc_out,
    bias,
    dka,
    dva,
    dsum,
    left_t,
    ss,
    drow,
    sm_in,
    dgain,
    fown,
    frecv,
    q,
    r1,
    r2,
    r3,
    r4,
    r5,
    do_ref,
    h1_ref,
    oself_ref,
    dy1_ref,
    x0_ref,
    dx1_ref,
    enc0_ref,
    enc2_ref,
    send_sem,
    recv_sem,
    sm_send,
    sm_recv,
    x_send,
    x_recv,
    f_send,
    f_recv,
    loc,
    *,
    scale,
):
    rows, width = do_ref.shape
    nq, tiles = width // 256, rows // TQ
    length, buckets = brow_ref.shape[0], 32
    count, step_rows, wide = q.shape[0], q.shape[2], q.shape[3]
    each = count // 8
    quarter = width // 4
    tall = quarter // 4
    n = enc0_ref.shape[0]
    cut = dq0_ref.shape[1]
    g, b = lax.axis_index("grp"), lax.axis_index("blk")
    peers = [(g, b ^ 1), (g, b ^ 2), (g ^ 1, b), (g ^ 2, b), (g ^ 4, b), (g ^ 2, b), (g ^ 1, b)]
    mesh_id = pl.DeviceIdType.MESH

    def local(src, dst, k):
        return pltpu.make_async_copy(src, dst, loc.at[k])

    def remote(src, dst, send, recv, k):
        return pltpu.make_async_remote_copy(
            src_ref=src, dst_ref=dst, send_sem=send, recv_sem=recv, device_id=peers[k], device_id_type=mesh_id
        )

    proj_in = local(proj_any, projs.at[pl.ds(64, rows), :], 0)
    wkv_in = local(wkv_any, wbuf.at[:, pl.ds(0, 2 * width)], 1)
    held_in = [
        local(src, dst, 20 + i)
        for i, (src, dst) in enumerate(
            (
                (oself_any, oself_ref),
                (dy1_any, dy1_ref),
                (enc0_any, enc0_ref),
                (enc2_any, enc2_ref),
                (do_any, do_ref),
                (h1_any, h1_ref),
                (x0_any, x0_ref),
                (dx1_any, dx1_ref),
            )
        )
    ]
    wqkv_in = local(wqkv_any, wbuf, 2)
    dkv_in = []
    for r in range(2):
        for i, (keep, came, at, w) in enumerate(
            ((keep0_any, came0_any, 0, cut), (keep1_any, came1_any, cut, width - cut))
        ):
            for half in range(2):
                from_, to = pl.ds(half * w, w), pl.ds(half * width + at, w)
                k = 3 + 8 * r + 4 * i + 2 * half
                dkv_in.append((r, local(keep.at[r, :, from_], both.at[pl.ds(r * n, n), to], k)))
                dkv_in.append((r, local(came.at[r, :, from_], stage.at[:, to], k + 1)))
    for r, c in dkv_in:
        if r == 0:
            c.start()
    for c in held_in[:4] + [wkv_in, proj_in] + held_in[4:]:
        c.start()

    barrier = pltpu.get_barrier_semaphore()
    for p in peers[:5]:
        pl.semaphore_signal(barrier, inc=1, device_id=p, device_id_type=mesh_id)
    pl.semaphore_wait(barrier, 5)

    f_half = fown.shape[0]
    w_at, o_at = pl.ds(0, f_half), pl.ds(f_half, f_half)
    w_local = local(wpair_any, ffn_any.at[pl.ds(0, 2), w_at, :], 28)
    w_copies = [
        remote(wpair_any, ffn_any.at[pl.ds(2, 2), w_at, :], f_send.at[0], f_recv.at[0], 3),
        remote(ffn_any.at[pl.ds(0, 4), w_at, :], ffn_any.at[pl.ds(4, 4), w_at, :], f_send.at[1], f_recv.at[1], 2),
    ]
    f_first = remote(fsend_any, frecv, f_send.at[2], f_recv.at[2], 4)
    f_second = remote(fown, ffn_any.at[1, o_at, :], f_send.at[3], f_recv.at[3], 4)
    f_third = remote(
        ffn_any.at[pl.ds(0, 2), o_at, :], ffn_any.at[pl.ds(2, 2), o_at, :], f_send.at[4], f_recv.at[4], 3
    )
    f_local = local(fown, ffn_any.at[0, o_at, :], 19)
    f_slices = f_half // step_rows
    w_copies[0].start()
    f_first.start()
    w_local.start()

    def f_copy(i):
        at = pl.ds(pl.multiple_of(f_half + i * step_rows, step_rows), step_rows)
        src, dst = ffn_any.at[pl.ds(0, 4), at, :], ffn_any.at[pl.ds(4, 4), at, :]
        return remote(src, dst, f_send.at[5 + i], f_recv.at[5 + i], 2)

    enc_copy = remote(enc_out, came_any, x_send, x_recv, 1)

    def add(x, y):
        return (x.astype(F32) + y.astype(F32)).astype(BF)

    def core_copy(j):
        at = pl.ds(pl.multiple_of(j * step_rows, step_rows), step_rows)
        return remote(ss.at[:, at, :], r1.at[j], send_sem.at[0, j], recv_sem.at[0, j], 0)

    def copy(k, j):
        src, dst = [
            lambda: (q.at[j, pl.ds(8, 8)], r2.at[j]),
            lambda: (q.at[j, pl.ds(4, 4)], r3.at[j]),
            lambda: (q.at[j, pl.ds(2, 2)], r4.at[j]),
            lambda: (q.at[j, pl.ds(0, 2)], r5.at[j]),
            lambda: (f.at[j, pl.ds(0, 2)], f.at[j, pl.ds(2, 2)]),
            lambda: (f.at[j, pl.ds(0, 4)], f.at[j, pl.ds(4, 4)]),
        ][k - 1]()
        return remote(src, dst, send_sem.at[k, j], recv_sem.at[k, j], k)

    def event(k, j):
        @pl.when((j >= 0) & (j < count))
        def _():
            (core_copy(j) if k == 0 else copy(k, j)).wait()
            if k == 0:
                q[j] = add(q[j], r1[j])
            elif k == 1:
                q[j, 0:8] = add(q[j, 0:8], r2[j])
            elif k == 2:
                q[j, 0:4] = add(q[j, 0:4], r3[j])
            elif k == 3:
                q[j, 0:2] = add(q[j, 0:2], r4[j])
            elif k == 4:
                f[j, 0] = add(q[j, 0], r5[j, 1])
                f[j, 1] = add(q[j, 1], r5[j, 0])
            if k < 6:
                copy(k + 1, j).start()

    def step(t):
        t = jnp.asarray(t, jnp.int32)
        event(0, t + 3)
        for k in range(1, 7):
            event(k, t - 2 * (k - 1))

    def put(right, block):
        for r in range(4):
            part = left_t[pl.ds(pl.multiple_of((b ^ r) * quarter, quarter), quarter), :]
            spread(dot(part, right).astype(BF), r, block)
        start_core(block)

    def spread(grad, r, block):
        for s in range(8):
            at = (r >> 1) * 8 + slot_of(g ^ s)
            y, x = (s >> 1) * tall, (s & 1) * wide
            if r & 1:
                ss[at, block * tall : (block + 1) * tall, :] = grad[y : y + tall, x : x + wide]
            else:
                for k in range(each):
                    piece = grad[y + k * step_rows : y + (k + 1) * step_rows, x : x + wide]
                    q[block * each + k, at] = piece

    def start_core(block):
        for k in range(each):
            core_copy(block * each + k).start()

    left_t[...] = oc_ref[...].T
    put(dyc_ref[...], 0)
    left_t[...] = h2_ref[...].T
    for j in range(each):
        event(0, jnp.int32(j))
    put(jnp.concatenate([dq0_ref[...], dq1_ref[...]], axis=1), 1)
    step(0)
    w_local.wait()
    w_copies[0].wait()
    w_copies[1].start()
    held_in[0].wait()
    held_in[1].wait()
    left_t[...] = oself_ref[...].T
    for r, c in dkv_in:
        if r == 0:
            c.wait()
    both[:n, :] = add(both[:n, :], stage[...])
    for r, c in dkv_in:
        if r == 1:
            c.start()
    put(dy1_ref[...], 2)
    f_first.wait()
    fown[...] = add(fkeep_ref[...], frecv[...])
    f_local.start()
    f_second.start()
    step(1)

    held_in[2].wait()
    held_in[3].wait()
    enc_t[:, :n] = enc0_ref[...].T
    enc_t[:, n:] = enc2_ref[...].T
    for r, c in dkv_in:
        if r == 1:
            c.wait()
    both[n:, :] = add(both[n:, :], stage[...])
    for i in range(2):
        for r in range(4):
            part = enc_t[pl.ds(pl.multiple_of((b ^ r) * quarter, quarter), quarter), :]
            spread(dot(part, both[:, i * width : (i + 1) * width]).astype(BF), r, 3 + i)
        start_core(3 + i)
        step(2 + i)
    wkv_in.wait()
    enc_out[...] = dot_nt(both[n:, :], wbuf[:, : 2 * width]).astype(BF)
    own_ref[...] = dot_nt(both[:n, :], wbuf[:, : 2 * width])
    wqkv_in.start()

    projs[0:64, :] = jnp.zeros((64, 3 * width), BF)
    fill_bias_all(brow_ref, bias, nq)
    dka[...] = jnp.zeros_like(dka)
    dva[...] = jnp.zeros_like(dva)
    dsum[...] = jnp.zeros_like(dsum)
    proj_in.wait()
    held_in[4].wait()

    def tile(t):
        row = pl.ds(pl.multiple_of(t * TQ, TQ), TQ)
        held = pl.ds(pl.multiple_of(t * TQ + 64, TQ), TQ)
        win = pl.ds(pl.multiple_of(t * TQ, TQ), WIN)
        mask = range_mask(t * TQ - 64, WIN, start_ref[pl.ds(t, 1), :], size_ref[pl.ds(t, 1), :])
        for c in range(nq):
            cols = slice(c * 256, (c + 1) * 256)
            kcols = slice(width + c * 256, width + (c + 1) * 256)
            vcols = slice(2 * width + c * 256, 2 * width + (c + 1) * 256)
            qs = stack4(projs[held, cols] * jnp.asarray(scale, BF))
            dos = stack4(do_ref[row, cols])
            s = dot_nt(projs[win, kcols], qs) + bias[c]
            p = jnp.where(mask, jnp.exp(s - lse_ref[t, c]), 0.0)
            dp = dot_nt(projs[win, vcols], dos)
            delta = jnp.sum(red(p * dp, jnp.sum), axis=0, keepdims=True)
            ds = p * (dp - delta)
            dsum[c] += ds
            ds = ds.astype(BF)
            dva[win, cols] += dot(p.astype(BF), dos)
            dka[win, cols] += dot(ds, qs)
            projs[held, cols] = (unstack4(dot_tn(ds, projs[win, kcols])) * scale).astype(BF)

    def tile_and_step(t, _):
        tile(t)
        step(t + 4)
        return 0

    lax.fori_loop(0, tiles - 2, tile_and_step, 0)

    def tile_alone(t, _):
        tile(t)
        return 0

    lax.fori_loop(tiles - 2, tiles, tile_alone, 0)
    f_second.wait()
    f_local.wait()
    f_third.start()
    done = tiles + 2
    projs[64:, width : 2 * width] = dka[64:, :].astype(BF)
    projs[64:, 2 * width : 3 * width] = dva[64:, :].astype(BF)
    held_in[5].wait()
    left_t[...] = h1_ref[...].T
    for i in range(3):
        put(projs[64:, i * width : (i + 1) * width], 5 + i)
        step(done)
        step(done + 1)
        done += 2

    dgain[...] = jnp.zeros_like(dgain)
    parts = 5
    block = rows // parts
    wqkv_in.wait()
    held_in[6].wait()
    held_in[7].wait()

    def self_in(i, _):
        at = pl.ds(pl.multiple_of(i * block, block), block)
        held = pl.ds(pl.multiple_of(i * block + 64, 64), block)
        x0 = x0_ref[at, :].astype(F32)
        dx, part = rms_back(x0, rms(x0), gain_ref[...], dot_nt(projs[held, :], wbuf[...]))
        dgain[...] += part
        dx0 = dx1_ref[at, :] + dx
        top = dx0.astype(BF)
        both[at, :width] = top
        both[at, width:] = (dx0 - top.astype(F32)).astype(BF)
        step(done + i)

        @pl.when(i == 2)
        def _():
            enc_copy.start()

        return 0

    lax.fori_loop(0, parts, self_in, 0)
    done += parts

    dist = distances()
    for c in range(nq):
        cols = slice(c * 256, (c + 1) * 256)

        def one(d, _):
            x = jnp.where(dist == d, dsum[c], 0.0)
            drow[pl.ds(d, 1), cols] = jnp.sum(red(x, jnp.sum), axis=0, keepdims=True)
            return 0

        lax.fori_loop(0, length, one, 0)
    lane = lax.broadcasted_iota(jnp.int32, (buckets, length), 1)
    place = jnp.zeros((buckets, length), jnp.int32)
    for d in range(length):
        place = jnp.where(lane == d, bucket_ref[d], place)
    hot = (place == lax.broadcasted_iota(jnp.int32, (buckets, length), 0)).astype(F32)
    head = (
        lax.broadcasted_iota(jnp.int32, (width, 128), 0) // 64
        == lax.broadcasted_iota(jnp.int32, (width, 128), 1)
    ).astype(F32)
    by_bucket = jnp.dot(hot, drow[...], preferred_element_type=F32, precision=lax.Precision.HIGHEST)
    small_ref[...] = jnp.zeros_like(small_ref)
    small_ref[24:, :] = jnp.dot(by_bucket, head, preferred_element_type=F32, precision=lax.Precision.HIGHEST)
    for i, ref in enumerate((dgain, dg2_ref, dg3_ref)):
        for k in range(6):
            small_ref[6 * i + k : 6 * i + k + 1, :] = ref[0:1, k * 128 : (k + 1) * 128]

    def small_copy(k):
        src = small_ref if k == 0 else sm_in.at[k + 4]
        return remote(src, sm_in.at[k], sm_send.at[k], sm_recv.at[k], k)

    def small_sum(k):
        small_copy(k).wait()
        held = small_ref[...] if k == 0 else sm_in[k + 4]
        if k < 4:
            sm_in[k + 5] = held + sm_in[k]
            small_copy(k + 1).start()
        else:
            small_ref[...] = held + sm_in[k]

    small_copy(0).start()
    f_third.wait()
    f_copy(0).start()
    step(done)
    hot_rows = onehot_rows(src_ref[...])
    d_ref[...] = dot(hot_rows, both[:rows, :width]) + dot(hot_rows, both[:rows, width:])
    for k in range(5):
        small_sum(k)
        for i in range(2):
            step(done + 1 + 2 * k + i)
        f_copy(1 + k).start()

    def rest(t, _):
        step(t)
        return 0

    lax.fori_loop(done + 11, count + 10, rest, 0)

    def f_end(i, _):
        f_copy(i).wait()
        return 0

    lax.fori_loop(0, f_slices, f_end, 0)
    w_copies[1].wait()
    enc_copy.wait()


def late(
    start, size, bucket, brow, proj, do, lse, h1, oself, dy1, src, x0, gain, dx1, wqkv, dg2, dg3,
    keep0, came0, keep1, came1, enc0, enc2, wkv, oc, dyc, h2, dq0, dq1, wpair, fkeep, fsend, scale,
):
    rows, width = do.shape
    nq = width // 256
    n = enc0.shape[0]
    step_rows, wide, tall = 16, width // 2, width // 16
    count = 8 * tall // step_rows
    any_spec = pl.BlockSpec(memory_space=pl.ANY)

    def buf(n):
        return pltpu.VMEM((count, n, step_rows, wide), BF)

    return pl.pallas_call(
        functools.partial(late_kernel, scale=scale),
        out_shape=(
            sds((rows, width), F32),
            sds((56, 128), F32),
            sds((count, 8, step_rows, wide), BF),
            sds((n, width), F32),
            sds((n, width), BF),
            sds((8, 2 * fkeep.shape[0], width), BF),
        ),
        in_specs=[VM, VM, SM, VM, any_spec, any_spec, VM]
        + [any_spec] * 3
        + [VM, any_spec, VM, any_spec]
        + [any_spec, VM, VM]
        + [any_spec] * 7
        + [VM] * 5
        + [any_spec, VM, any_spec],
        out_specs=(VM,) * 4 + (any_spec, any_spec),
        scratch_shapes=[
            pltpu.VMEM((rows + 64, 3 * width), BF),
            pltpu.VMEM((width, 3 * width), BF),
            pltpu.VMEM((2 * n, 2 * width), BF),
            pltpu.VMEM((n, 2 * width), BF),
            pltpu.VMEM((width, 2 * n), BF),
            pltpu.VMEM((n, width), BF),
            pltpu.VMEM((nq, WIN, 256), F32),
            pltpu.VMEM((rows + 64, width), F32),
            pltpu.VMEM((rows + 64, width), F32),
            pltpu.VMEM((nq, WIN, 256), F32),
            pltpu.VMEM((width, rows), BF),
            pltpu.VMEM((16, 8 * tall, wide), BF),
            pltpu.VMEM(brow.shape, F32),
            pltpu.VMEM((9, 56, 128), F32),
            pltpu.VMEM((1, width), F32),
            pltpu.VMEM(fkeep.shape, BF),
            pltpu.VMEM(fkeep.shape, BF),
            buf(16),
            buf(16),
            buf(8),
            buf(4),
            buf(2),
            buf(2),
        ]
        + [pltpu.VMEM(a.shape, a.dtype) for a in (do, h1, oself, dy1, x0, dx1, enc0, enc2)]
        + [
            pltpu.SemaphoreType.DMA((7, count)),
            pltpu.SemaphoreType.DMA((7, count)),
            pltpu.SemaphoreType.DMA((5,)),
            pltpu.SemaphoreType.DMA((5,)),
            pltpu.SemaphoreType.DMA,
            pltpu.SemaphoreType.DMA,
            pltpu.SemaphoreType.DMA((11,)),
            pltpu.SemaphoreType.DMA((11,)),
            pltpu.SemaphoreType.DMA((29,)),
        ],
        compiler_params=pltpu.CompilerParams(
            vmem_limit_bytes=63 << 20, collective_id=0, has_side_effects=True
        ),
        cost_estimate=pl.CostEstimate(flops=10**13, bytes_accessed=30 << 20, transcendentals=0),
        name="late",
    )(
        start, size, bucket, brow, proj, do, lse, h1, oself, dy1, src, x0, gain, dx1, wqkv, dg2, dg3,
        keep0, came0, keep1, came1, enc0, enc2, wkv, oc, dyc, h2, dq0, dq1, wpair, fkeep, fsend,
    )


def last_kernel(
    me_ref, small_ref, ffn_ref, f_ref, own_ref, came_ref, win_ref, wout_ref, co_ref, cq_ref, ckv_ref, qkv_ref, so_ref, enc_ref, g1_ref, g2_ref, g3_ref, rel_ref
):
    half = ffn_ref.shape[1] // 2
    for slot in range(8):
        s = me_ref[1] ^ ((slot >> 2) + (slot & 2) + 4 * (slot & 1))
        rows = pl.ds(pl.multiple_of((s & 1) * half, half), half)
        cols = pl.ds(pl.multiple_of((s >> 1) * 768, 768), 768)
        win_ref[rows, cols] = ffn_ref[slot, :half].astype(F32)
        wout_ref[pl.ds(pl.multiple_of(s * half, half), half), :] = ffn_ref[slot, half:].astype(F32)
    count, _, step_rows, wide = f_ref.shape
    width = 2 * wide
    places = (
        (co_ref, 0), (cq_ref, 0), (so_ref, 0), (ckv_ref, 0), (ckv_ref, width),
        (qkv_ref, 0), (qkv_ref, width), (qkv_ref, 2 * width),
    )
    each = count // 8
    tall = each * step_rows
    for slot in range(8):
        s = me_ref[1] ^ ((slot >> 2) + (slot & 2) + 4 * (slot & 1))
        for n, (out, col) in enumerate(places):
            for k in range(each):
                at = pl.ds(pl.multiple_of((s >> 1) * tall + k * step_rows, step_rows), step_rows)
                cols = pl.ds(pl.multiple_of(col + (s & 1) * wide, 128), wide)
                out[at, cols] = f_ref[n * each + k, slot].astype(F32)
    enc_ref[...] = own_ref[...] + came_ref[...].astype(F32)
    quarter = g1_ref.shape[1]
    for i, ref in enumerate((g1_ref, g2_ref, g3_ref)):
        whole = jnp.concatenate([small_ref[6 * i + k : 6 * i + k + 1, :] for k in range(6)], axis=1)
        for j in range(4):

            @pl.when(me_ref[0] == j)
            def _():
                ref[...] = whole[:, j * quarter : (j + 1) * quarter]

    part, heads = rel_ref.shape
    rel_ref[...] = small_ref[pl.ds(pl.multiple_of(24 + me_ref[0] * part, 8), part), :heads]


def last(me, small, ffn, f, own, came, buckets, heads):
    width = own.shape[1]
    quarter = width // 4
    cols = lambda n: sds((quarter, n * width), F32)
    return call(
        last_kernel,
        "last",
        (cols(4), sds((width, width), F32), cols(1), cols(1), cols(2), cols(3), cols(1), sds(own.shape, F32))
        + (sds((1, quarter), F32),) * 3
        + (sds((buckets // 4, heads), F32),),
        [SM] + [VM] * 5,
        (VM,) * 12,
        [],
        (me, small, ffn, f, own, came),
        us=8,
    )


def hop(x, core=0, xb=0, yb=0, z1=0, z2=0):
    b, g = core | (xb << 1), yb | (z1 << 1) | (z2 << 2)
    groups, blocks = lax.axis_size("grp"), lax.axis_size("blk")
    pairs = [(i * blocks + j, (i ^ g) * blocks + (j ^ b)) for i in range(groups) for j in range(blocks)]
    return lax.ppermute(x, ("grp", "blk"), pairs)


def total(*parts):
    out = parts[0].astype(F32)
    for p in parts[1:]:
        out = out + p.astype(F32)
    return out.astype(BF)


def after(x, *deps):
    return lax.optimization_barrier((x,) + deps)[0]


def fused_body(
    dec_in,
    encodings,
    answer_len,
    answer_question,
    question_rows,
    bucket_table,
    gain_self,
    w_qkv,
    w_self_out,
    rel_bias,
    gain_cross,
    w_cross_q,
    w_cross_kv,
    w_cross_out,
    gain_ffn,
    w_in,
    w_out,
    cotangent,
):
    rows, width = dec_in.shape
    buckets, heads = rel_bias.shape
    scale = 1.0 / math.sqrt(width // heads)
    me_b, me_g = lax.axis_index("blk"), lax.axis_index("grp")
    me = jnp.stack([me_b, me_g]).astype(jnp.int32)
    g1, g2, g3 = (g.reshape(1, width) for g in (gain_self, gain_cross, gain_ffn))

    enc2 = hop(encodings, xb=1)
    enc1 = hop(encodings, core=1)
    src, cstart, csize, sstart, ssize, lo, hi, brow, x0, h1, proj, oself, lse_self = pre(
        me, answer_question, answer_len, question_rows, bucket_table, dec_in, g1, rel_bias, w_qkv, scale
    )
    enc2, oself = lax.optimization_barrier((enc2, oself))
    enc3 = hop(enc2, core=1)
    enc1 = after(enc1, x0)
    x1, h2, qc = mid(x0, oself, w_self_out, g2, w_cross_q, scale)
    k, v, kt, ocross, lse = kv_cross(
        me, lo, hi, cstart, csize, qc, (encodings, enc1, enc2, enc3), w_cross_kv
    )
    o_keep, o_send, w_part, oc, layer_out, dx2, dyc, do, dgain3 = ffn(
        src, x1, ocross, g3, cotangent, w_cross_out, w_in, w_out
    )
    do, o_send, w_part = lax.optimization_barrier((do, o_send, w_part))
    o_came = hop(o_send, xb=1)
    w_came = hop(w_part[2:], z1=1)
    dq0, keep0, send0 = cross_back(
        me, lo, hi, cstart, csize, qc, do, ocross, lse, k, v, kt, scale, 0, 2
    )
    came0 = hop(send0, core=1)
    o_came, w_came, dq0 = lax.optimization_barrier((o_came, w_came, dq0))
    o_q = [total(o_keep[2 * j : 2 * j + 2], o_came[2 * j : 2 * j + 2]) for j in range(4)]
    w_two = total(w_part[:2], w_came)
    do1, o_q[1], o_q[2], o_q[3], w_two = lax.optimization_barrier((do, o_q[1], o_q[2], o_q[3], w_two))
    oz, oy, oyz = hop(o_q[1], z1=1), hop(o_q[2], yb=1), hop(o_q[3], yb=1, z1=1)
    w_came = hop(w_two, z2=1)
    dq1, keep1, send1 = cross_back(
        me, lo, hi, cstart, csize, qc, do1, ocross, lse, k, v, kt, scale, 2, 1
    )
    came1 = hop(send1, core=1)
    oz, oy, oyz, w_came, dq1 = lax.optimization_barrier((oz, oy, oyz, w_came, dq1))
    w_pair = total(w_two, w_came[::-1])
    f_keep, f_send = (total(o_q[0][n], oz[n], oy[n], oyz[n]) for n in range(2))
    dx1, dy1, dos, dgain2 = cross_in(dq0, dq1, x1, dx2, g2, w_cross_q, w_self_out)
    came0, came1, dos = lax.optimization_barrier((came0, came1, dos))
    d_dec_in, small, gathered, enc_own, enc_came, f_all = late(
        sstart, ssize, bucket_table, brow, proj, dos, lse_self, h1, oself, dy1, src, x0, g1, dx1, w_qkv,
        dgain2, dgain3, keep0, came0, keep1, came1, encodings, enc2, w_cross_kv, oc, dyc, h2, dq0, dq1,
        w_pair, f_keep, f_send, scale,
    )
    (
        o_win, o_wout, o_wco, o_wcq, o_wckv, o_wqkv, o_wso, d_encodings, g_self, g_cross, g_ffn, g_rel,
    ) = last(me, small, f_all, gathered, enc_own, enc_came, buckets, heads)
    g_self, g_cross, g_ffn = (g.reshape(-1) for g in (g_self, g_cross, g_ffn))
    return (
        layer_out,
        d_dec_in,
        d_encodings,
        g_self,
        o_wqkv,
        o_wso,
        g_rel,
        g_cross,
        o_wcq,
        o_wckv,
        o_wco,
        g_ffn,
        o_win,
        o_wout,
    )


def solution(mesh):
    rows = P(("grp", "blk"), None)
    fused = mesh.shape["grp"] == 8 and mesh.shape["blk"] == 4
    return jax.shard_map(
        fused_body if fused else body,
        mesh=mesh,
        in_specs=(rows, rows, P(("grp", "blk")), P("grp"), P("grp", None)) + (P(),) * 12 + (rows,),
        out_specs=(rows, rows, rows, P("blk"))
        + (P("blk", None),) * 3
        + (P("blk"),)
        + (P("blk", None),) * 3
        + (P("blk"),)
        + (P("blk", None),) * 2,
        check_vma=False,
    )
```

```python
import functools
import math

import jax
import jax.numpy as jnp
from jax import lax
from jax.experimental import pallas as pl
from jax.experimental.pallas import tpu as pltpu
from jax.sharding import PartitionSpec as P

EPSILON = 1e-06
NEG = -1e30
MASKED = -1e9
TQ = 64
TK = 256
WIN = 128
F32 = jnp.float32
BF = jnp.bfloat16
VM = pl.BlockSpec(memory_space=pltpu.VMEM)
SM = pl.BlockSpec(memory_space=pltpu.SMEM)
LIMIT = 60 << 20


def dot(a, b):
    return jnp.dot(a, b, preferred_element_type=F32)


def dot_tn(a, b):
    return lax.dot_general(a, b, (((0,), (0,)), ((), ())), preferred_element_type=F32)


def dot_nt(a, b):
    return lax.dot_general(a, b, (((1,), (1,)), ((), ())), preferred_element_type=F32)


def stack4(t):
    lane = lax.broadcasted_iota(jnp.int32, t.shape, 1) // 64
    return jnp.concatenate([jnp.where(lane == a, t, jnp.zeros_like(t)) for a in range(4)], axis=0)


def unstack4(s):
    n = s.shape[0] // 4
    lane = lax.broadcasted_iota(jnp.int32, (n, 256), 1) // 64
    out = s[:n]
    for a in range(1, 4):
        out = jnp.where(lane == a, s[a * n : (a + 1) * n], out)
    return out


def range_mask(base, rows, start, size):
    idx = lax.broadcasted_iota(jnp.int32, (rows, start.shape[1]), 0)
    rel = idx - (start - base)
    return (rel >= 0) & (rel < size)


def red(x, op):
    return op(x.reshape(x.shape[0] // 8, 8, x.shape[1]), axis=0)


def cross_fwd_kernel(
    lo_ref, hi_ref, start_ref, size_ref, q_ref, k_ref, vt_ref, o_ref, lse_ref, qst, s_scr, m_scr, l_scr, acc, *, nq, tiles
):
    def tile(t, _):
        st = start_ref[t]
        sz = size_ref[t]
        lo = lo_ref[t]
        hi = hi_ref[t]
        row = pl.ds(pl.multiple_of(t * TQ, TQ), TQ)
        for c in range(nq):
            qst[c] = stack4(q_ref[row, c * 256 : (c + 1) * 256]).T
            m_scr[c] = jnp.full((8, 256), NEG, F32)
            l_scr[c] = jnp.zeros((8, 256), F32)
            acc[c] = jnp.zeros((256, 256), F32)

        def scores(j, _):
            kr = pl.ds(pl.multiple_of(j * TK, TK), TK)
            mask = range_mask(j * TK, TK, st, sz)
            for c in range(nq):
                s = dot(k_ref[kr, c * 256 : (c + 1) * 256], qst[c])
                s = jnp.where(mask, s, NEG)
                s_scr[c, kr, :] = s
                m_scr[c] = jnp.maximum(m_scr[c], red(s, jnp.max))
            return 0

        lax.fori_loop(lo, hi, scores, 0)
        for c in range(nq):
            m_scr[c] = jnp.broadcast_to(jnp.max(m_scr[c], axis=0, keepdims=True), (8, 256))

        def mix(j, _):
            kr = pl.ds(pl.multiple_of(j * TK, TK), TK)
            for c in range(nq):
                p = jnp.exp(s_scr[c, kr, :] - m_scr[c][0:1])
                l_scr[c] += red(p, jnp.sum)
                acc[c] += dot(vt_ref[c * 256 : (c + 1) * 256, kr], p.astype(BF))
            return 0

        lax.fori_loop(lo, hi, mix, 0)
        for c in range(nq):
            l = jnp.sum(l_scr[c], axis=0, keepdims=True)
            lse_ref[t, c] = m_scr[c][0:1] + jnp.log(l)
            o_ref[row, c * 256 : (c + 1) * 256] = unstack4((acc[c] * (1.0 / l)).T)
        return 0

    lax.fori_loop(0, tiles, tile, 0)


def quads_per_step(nq, keys):
    return nq if keys <= 2048 else 1


def cross_fwd(lo, hi, start, size, q, k, vt):
    rows, width = q.shape
    tiles, keys = rows // TQ, k.shape[0]
    nq = quads_per_step(width // 256, keys)
    full = pl.BlockSpec(start.shape, lambda g: (0, 0, 0))
    return pl.pallas_call(
        functools.partial(cross_fwd_kernel, nq=nq, tiles=tiles),
        grid=(width // 256 // nq,),
        out_shape=(
            jax.ShapeDtypeStruct(q.shape, F32),
            jax.ShapeDtypeStruct((tiles, width // 256, 1, 256), F32),
        ),
        in_specs=[
            SM,
            SM,
            full,
            full,
            pl.BlockSpec((rows, nq * 256), lambda g: (0, g)),
            pl.BlockSpec((keys, nq * 256), lambda g: (0, g)),
            pl.BlockSpec((nq * 256, keys), lambda g: (g, 0)),
        ],
        out_specs=(
            pl.BlockSpec((rows, nq * 256), lambda g: (0, g)),
            pl.BlockSpec((tiles, nq, 1, 256), lambda g: (0, g, 0, 0)),
        ),
        scratch_shapes=[
            pltpu.VMEM((nq, 256, 256), BF),
            pltpu.VMEM((nq, keys, 256), F32),
            pltpu.VMEM((nq, 8, 256), F32),
            pltpu.VMEM((nq, 8, 256), F32),
            pltpu.VMEM((nq, 256, 256), F32),
        ],
        compiler_params=pltpu.CompilerParams(vmem_limit_bytes=LIMIT),
        name="cross_fwd",
    )(lo, hi, start, size, q, k, vt)


def cross_bwd_kernel(
    lo_ref,
    hi_ref,
    start_ref,
    size_ref,
    q_ref,
    do_ref,
    o_ref,
    lse_ref,
    k_ref,
    v_ref,
    kt_ref,
    dq_ref,
    dk_ref,
    dv_ref,
    qs,
    qst,
    dos,
    dost,
    del_scr,
    dka,
    dva,
    dqt,
    *,
    nq,
    tiles,
    scale,
):
    dka[...] = jnp.zeros_like(dka)
    dva[...] = jnp.zeros_like(dva)

    def tile(t, _):
        st = start_ref[t]
        sz = size_ref[t]
        row = pl.ds(pl.multiple_of(t * TQ, TQ), TQ)
        for c in range(nq):
            cs = slice(c * 256, (c + 1) * 256)
            a = stack4(q_ref[row, cs])
            qs[c] = a
            qst[c] = a.T
            b = stack4(do_ref[row, cs])
            dos[c] = b
            dost[c] = b.T
            product = do_ref[row, cs].astype(F32) * o_ref[row, cs]
            total = jnp.sum(red(stack4(product).T, jnp.sum), axis=0, keepdims=True)
            del_scr[c] = jnp.broadcast_to(total, (8, 256))
            dqt[c] = jnp.zeros((256, 256), F32)

        def step(j, _):
            kr = pl.ds(pl.multiple_of(j * TK, TK), TK)
            mask = range_mask(j * TK, TK, st, sz)
            for c in range(nq):
                cs = slice(c * 256, (c + 1) * 256)
                s = dot(k_ref[kr, cs], qst[c])
                p = jnp.where(mask, jnp.exp(s - lse_ref[t, c]), 0.0)
                dp = dot(v_ref[kr, cs], dost[c])
                ds = (p * (dp - del_scr[c][0:1])).astype(BF)
                dva[kr, cs] += dot(p.astype(BF), dos[c])
                dka[kr, cs] += dot(ds, qs[c])
                dqt[c] += dot(kt_ref[cs, kr], ds)
            return 0

        lax.fori_loop(lo_ref[t], hi_ref[t], step, 0)
        for c in range(nq):
            cs = slice(c * 256, (c + 1) * 256)
            dq_ref[row, cs] = (unstack4(dqt[c].T) * scale).astype(BF)
        return 0

    lax.fori_loop(0, tiles, tile, 0)
    dk_ref[...] = dka[...].astype(BF)
    dv_ref[...] = dva[...].astype(BF)


def cross_bwd(lo, hi, start, size, q, do, o, lse, k, v, kt, scale):
    rows, width = q.shape
    tiles, keys = rows // TQ, k.shape[0]
    nq = quads_per_step(width // 256, keys)
    full = pl.BlockSpec(start.shape, lambda g: (0, 0, 0))
    own = pl.BlockSpec((rows, nq * 256), lambda g: (0, g))
    held = pl.BlockSpec((keys, nq * 256), lambda g: (0, g), pipeline_mode=pl.Buffered(1))
    out_kv = pl.BlockSpec((keys, nq * 256), lambda g: (0, g), pipeline_mode=pl.Buffered(1))
    return pl.pallas_call(
        functools.partial(cross_bwd_kernel, nq=nq, tiles=tiles, scale=scale),
        grid=(width // 256 // nq,),
        out_shape=(
            jax.ShapeDtypeStruct(q.shape, BF),
            jax.ShapeDtypeStruct(k.shape, BF),
            jax.ShapeDtypeStruct(k.shape, BF),
        ),
        in_specs=[
            SM,
            SM,
            full,
            full,
            own,
            own,
            own,
            pl.BlockSpec((tiles, nq, 1, 256), lambda g: (0, g, 0, 0)),
            held,
            held,
            pl.BlockSpec((nq * 256, keys), lambda g: (g, 0), pipeline_mode=pl.Buffered(1)),
        ],
        out_specs=(own, out_kv, out_kv),
        scratch_shapes=[pltpu.VMEM((nq, 256, 256), BF)] * 4
        + [
            pltpu.VMEM((nq, 8, 256), F32),
            pltpu.VMEM((keys, nq * 256), F32),
            pltpu.VMEM((keys, nq * 256), F32),
            pltpu.VMEM((nq, 256, 256), F32),
        ],
        compiler_params=pltpu.CompilerParams(vmem_limit_bytes=LIMIT),
        name="cross_bwd",
    )(lo, hi, start, size, q, do, o, lse, k, v, kt)


def distances():
    j = lax.broadcasted_iota(jnp.int32, (WIN, 256), 0)
    i = lax.broadcasted_iota(jnp.int32, (WIN, 256), 1) % 64
    return WIN - TQ + i - j


def fill_window(proj_ref, kp, vp, width):
    kp[0:64, :] = jnp.zeros((64, width), BF)
    vp[0:64, :] = jnp.zeros((64, width), BF)
    kp[64:, :] = proj_ref[:, width : 2 * width]
    vp[64:, :] = proj_ref[:, 2 * width : 3 * width]


def fill_bias(brow_ref, bias, nq):
    dist = distances()
    for c in range(nq):
        cs = slice(c * 256, (c + 1) * 256)

        def add(d, held):
            return jnp.where(dist == d, brow_ref[pl.ds(d, 1), cs], held)

        bias[c] = lax.fori_loop(0, brow_ref.shape[0], add, jnp.full((WIN, 256), MASKED, F32))


def self_fwd_kernel(start_ref, size_ref, brow_ref, proj_ref, o_ref, lse_ref, kp, vp, bias, *, nq, tiles, scale):
    width = nq * 256
    fill_window(proj_ref, kp, vp, width)
    fill_bias(brow_ref, bias, nq)

    def tile(t, _):
        row = pl.ds(pl.multiple_of(t * TQ, TQ), TQ)
        win = pl.ds(pl.multiple_of(t * TQ, TQ), WIN)
        mask = range_mask(t * TQ - 64, WIN, start_ref[t], size_ref[t])
        for c in range(nq):
            cs = slice(c * 256, (c + 1) * 256)
            qst = stack4(proj_ref[row, cs] * jnp.asarray(scale, BF)).T
            s = jnp.where(mask, dot(kp[win, cs], qst) + bias[c], MASKED)
            m = jnp.max(red(s, jnp.max), axis=0, keepdims=True)
            p = jnp.exp(s - m)
            l = jnp.sum(red(p, jnp.sum), axis=0, keepdims=True)
            p = (p * (1.0 / l)).astype(BF)
            o_ref[row, cs] = unstack4(dot_tn(p, vp[win, cs])).astype(BF)
            lse_ref[t, c] = m + jnp.log(l)
        return 0

    lax.fori_loop(0, tiles, tile, 0)


def self_fwd(start, size, brow, proj, scale):
    rows, width = proj.shape[0], proj.shape[1] // 3
    nq, tiles = width // 256, rows // TQ
    return pl.pallas_call(
        functools.partial(self_fwd_kernel, nq=nq, tiles=tiles, scale=scale),
        out_shape=(
            jax.ShapeDtypeStruct((rows, width), BF),
            jax.ShapeDtypeStruct((tiles, nq, 1, 256), F32),
        ),
        in_specs=[VM] * 4,
        out_specs=(VM, VM),
        scratch_shapes=[
            pltpu.VMEM((rows + 64, width), BF),
            pltpu.VMEM((rows + 64, width), BF),
            pltpu.VMEM((nq, WIN, 256), F32),
        ],
        compiler_params=pltpu.CompilerParams(vmem_limit_bytes=LIMIT),
        name="self_fwd",
    )(start, size, brow, proj)


def self_bwd_kernel(
    start_ref,
    size_ref,
    brow_ref,
    proj_ref,
    do_ref,
    lse_ref,
    dproj_ref,
    dbrow_ref,
    kp,
    vp,
    bias,
    dka,
    dva,
    dsum,
    *,
    nq,
    tiles,
    scale,
):
    width = nq * 256
    fill_window(proj_ref, kp, vp, width)
    fill_bias(brow_ref, bias, nq)
    dka[...] = jnp.zeros_like(dka)
    dva[...] = jnp.zeros_like(dva)
    dsum[...] = jnp.zeros_like(dsum)

    def tile(t, _):
        row = pl.ds(pl.multiple_of(t * TQ, TQ), TQ)
        win = pl.ds(pl.multiple_of(t * TQ, TQ), WIN)
        mask = range_mask(t * TQ - 64, WIN, start_ref[t], size_ref[t])
        for c in range(nq):
            cs = slice(c * 256, (c + 1) * 256)
            qs = stack4(proj_ref[row, cs] * jnp.asarray(scale, BF))
            dos = stack4(do_ref[row, cs])
            s = dot(kp[win, cs], qs.T) + bias[c]
            p = jnp.where(mask, jnp.exp(s - lse_ref[t, c]), 0.0)
            dp = dot(vp[win, cs], dos.T)
            delta = jnp.sum(red(p * dp, jnp.sum), axis=0, keepdims=True)
            ds = p * (dp - delta)
            dsum[c] += ds
            ds = ds.astype(BF)
            dva[win, cs] += dot(p.astype(BF), dos)
            dka[win, cs] += dot(ds, qs)
            dproj_ref[row, cs] = (unstack4(dot_tn(ds, kp[win, cs])) * scale).astype(BF)
        return 0

    lax.fori_loop(0, tiles, tile, 0)
    dproj_ref[:, width : 2 * width] = dka[64:, :].astype(BF)
    dproj_ref[:, 2 * width : 3 * width] = dva[64:, :].astype(BF)
    dist = distances()
    for c in range(nq):
        cs = slice(c * 256, (c + 1) * 256)

        def one(d, _):
            x = jnp.where(dist == d, dsum[c], 0.0)
            dbrow_ref[pl.ds(d, 1), cs] = jnp.sum(red(x, jnp.sum), axis=0, keepdims=True)
            return 0

        lax.fori_loop(0, brow_ref.shape[0], one, 0)


def self_bwd(start, size, brow, proj, do, lse, scale):
    rows, width = proj.shape[0], proj.shape[1] // 3
    nq, tiles = width // 256, rows // TQ
    return pl.pallas_call(
        functools.partial(self_bwd_kernel, nq=nq, tiles=tiles, scale=scale),
        out_shape=(jax.ShapeDtypeStruct((rows, 3 * width), BF), jax.ShapeDtypeStruct(brow.shape, F32)),
        in_specs=[VM] * 6,
        out_specs=(VM, VM),
        scratch_shapes=[
            pltpu.VMEM((rows + 64, width), BF),
            pltpu.VMEM((rows + 64, width), BF),
            pltpu.VMEM((nq, WIN, 256), F32),
            pltpu.VMEM((rows + 64, width), F32),
            pltpu.VMEM((rows + 64, width), F32),
            pltpu.VMEM((nq, WIN, 256), F32),
        ],
        compiler_params=pltpu.CompilerParams(vmem_limit_bytes=LIMIT),
        name="self_bwd",
    )(start, size, brow, proj, do, lse)


def norm_rows(x, gain):
    inverse = lax.rsqrt(jnp.mean(x * x, axis=-1, keepdims=True) + EPSILON)
    return x * inverse * gain, inverse


def norm_back(x, inverse, gain, grad):
    scaled = grad * gain
    mean = jnp.mean(x * scaled, axis=-1, keepdims=True)
    return inverse * scaled - x * inverse * inverse * inverse * mean, jnp.sum(grad * x * inverse, axis=0)


def swap(x, axis, bit):
    size = lax.axis_size(axis)
    return lax.ppermute(x, axis, [(i, i ^ bit) for i in range(size)])


def bits_of(axis):
    size = lax.axis_size(axis)
    return [1 << b for b in range(size.bit_length() - 1)]


def gather_parts(x, axis):
    parts = {0: x}
    for bit in reversed(bits_of(axis)):
        for r in list(parts):
            parts[r ^ bit] = swap(parts[r], axis, bit)
    return parts


def add_low(a, b):
    return (a.astype(F32) + b.astype(F32)).astype(BF)


def scatter_sum(x, axis, order):
    size = x.shape[0]
    live = list(range(size))
    block = x
    for bit in order:
        keep = [r for r in live if not r & bit]
        send = [r for r in live if r & bit]
        k = jnp.stack([block[live.index(r)] for r in keep])
        s = jnp.stack([block[live.index(r)] for r in send])
        block = add_low(k, swap(s, axis, bit))
        live = keep
    return block[0]


def gather_sum(x, axis, order):
    parts = [0]
    block = x[None]
    for bit in order:
        block = jnp.concatenate([block, swap(block, axis, bit)], axis=0)
        parts = parts + [r ^ bit for r in parts]
    inverse = [parts.index(r) for r in range(len(parts))]
    return block, inverse


def relative(x, axis):
    size = lax.axis_size(axis)
    me = lax.axis_index(axis)
    return jnp.stack([lax.dynamic_index_in_dim(x, me ^ r, 0, keepdims=False) for r in range(size)])


def reduce_all(x):
    blocks, rows, width = x.shape
    groups = lax.axis_size("grp")
    part = scatter_sum(relative(x, "blk"), "blk", bits_of("blk"))
    part = relative(part.reshape(groups, rows // groups, width), "grp")
    part = scatter_sum(part, "grp", bits_of("grp"))
    whole, inverse = gather_sum(part, "grp", list(reversed(bits_of("grp"))))
    me = lax.axis_index("grp")
    index = jnp.asarray(inverse, jnp.int32)[jnp.arange(groups) ^ me]
    return jnp.take(whole, index, axis=0).reshape(rows, width)


def sum_everywhere(x):
    for axis in ("blk", "grp"):
        for bit in bits_of(axis):
            x = x + swap(x, axis, bit)
    return x


def pack(grads, blocks):
    out = []
    for g in grads:
        k, n = g.shape
        r = g.reshape(blocks, k // blocks, n // 768, 768).transpose(0, 2, 1, 3)
        out.append(r.reshape(blocks, -1, 768))
    return jnp.concatenate(out, axis=1)


def unpack(rows, shapes, blocks):
    out, at = [], 0
    for k, n in shapes:
        count = k // blocks * (n // 768)
        piece = rows[at : at + count].reshape(n // 768, k // blocks, 768)
        out.append(piece.transpose(1, 0, 2).reshape(k // blocks, n).astype(F32))
        at += count
    return out


def body(
    dec_in,
    encodings,
    answer_len,
    answer_question,
    question_rows,
    bucket_table,
    gain_self,
    w_qkv,
    w_self_out,
    rel_bias,
    gain_cross,
    w_cross_q,
    w_cross_kv,
    w_cross_out,
    gain_ffn,
    w_in,
    w_out,
    cotangent,
):
    answers = answer_len.shape[0]
    length = bucket_table.shape[0]
    rows, width = dec_in.shape
    heads = rel_bias.shape[1]
    buckets = rel_bias.shape[0]
    scale = 1.0 / math.sqrt(width // heads)
    enc_rows = encodings.shape[0]
    blocks = lax.axis_size("blk")
    me = lax.axis_index("blk")
    tiles = rows // TQ
    nq = width // 256

    enc_parts = gather_parts(encodings, "blk")

    own_q = lax.dynamic_slice_in_dim(answer_question, me * answers, answers, 0)
    a_index = jnp.arange(answers)
    before = (own_q[None, :] < own_q[:, None]) | (
        (own_q[None, :] == own_q[:, None]) & (a_index[None, :] < a_index[:, None])
    )
    rank = jnp.sum(before.astype(jnp.int32), axis=1)
    target = (rank[:, None] * length + jnp.arange(length)[None, :]).reshape(rows)
    forward_perm = (jnp.arange(rows)[:, None] == target[None, :]).astype(BF)
    sorted_len = jnp.sum(jnp.where(rank[:, None] == a_index[None, :], answer_len[:, None], 0), axis=0)
    ends_q = jnp.cumsum(question_rows[0])
    starts_q = ends_q - question_rows[0]
    sorted_q = jnp.sum(jnp.where(rank[:, None] == a_index[None, :], own_q[:, None], 0), axis=0)
    token_q = jnp.repeat(sorted_q, length)
    pick = token_q[:, None] == jnp.arange(question_rows.shape[1])[None, :]
    token_start = jnp.sum(jnp.where(pick, starts_q[None, :], 0), axis=1)
    token_size = jnp.sum(jnp.where(pick, question_rows[0][None, :], 0), axis=1)

    def stacked(v):
        return jnp.tile(v.reshape(tiles, 1, TQ), (1, 1, 4)).astype(jnp.int32)

    c_start, c_size = stacked(token_start), stacked(token_size)
    lo = (token_start.reshape(tiles, TQ)[:, 0] // TK).astype(jnp.int32)
    hi = ((token_start + token_size).reshape(tiles, TQ)[:, -1] + TK - 1) // TK
    hi = hi.astype(jnp.int32)
    s_start = stacked(jnp.arange(rows) // length * length)
    s_size = stacked(jnp.repeat(sorted_len, length))

    bucket_hot = (bucket_table[:, None] == jnp.arange(buckets)[None, :]).astype(F32)
    brow = jnp.repeat(
        jnp.dot(bucket_hot, rel_bias, precision=lax.Precision.HIGHEST), width // heads, axis=1
    )

    x0 = dot(forward_perm, dec_in)
    grad_top = dot(forward_perm, cotangent)
    grad_low = grad_top.astype(BF)
    n1, r1 = norm_rows(x0, gain_self)
    h1 = n1.astype(BF)
    proj = dot(h1, w_qkv).astype(BF)
    o_self, lse_self = self_fwd(s_start, s_size, brow, proj, scale)
    x1 = x0 + dot(o_self, w_self_out)
    n2, r2 = norm_rows(x1, gain_cross)
    h2 = n2.astype(BF)
    qc = (dot(h2, w_cross_q).astype(BF) * jnp.asarray(scale, BF)).astype(BF)

    enc_rel = jnp.stack([enc_parts[r] for r in range(blocks)])
    enc_all = relative(enc_rel, "blk").reshape(blocks * enc_rows, width)
    kv = dot(enc_all, w_cross_kv).astype(BF)
    k_all, v_all = kv[:, :width], kv[:, width:]
    kvt = lax.dot_general(w_cross_kv, enc_all, (((0,), (1,)), ((), ())), preferred_element_type=F32).astype(BF)
    kt_all, vt_all = kvt[:width], kvt[width:]

    o_cross, lse_cross = cross_fwd(lo, hi, c_start, c_size, qc, k_all, vt_all)
    oc = o_cross.astype(BF)
    x2 = x1 + dot(oc, w_cross_out)
    n3, r3 = norm_rows(x2, gain_ffn)
    h3 = n3.astype(BF)
    hidden, gelu_back = jax.vjp(jax.nn.gelu, dot(h3, w_in))
    u = hidden.astype(BF)
    out = (x2 + dot(u, w_out)).astype(BF)
    layer_out = dot_tn(forward_perm, out).astype(BF)

    d_w_out = dot_tn(u, grad_low).astype(BF)
    da = gelu_back(dot_nt(grad_low, w_out))[0].astype(BF)
    d_w_in = dot_tn(h3, da).astype(BF)
    sums_out = reduce_all(pack([d_w_out], blocks))
    sums_in = reduce_all(pack([d_w_in], blocks))
    dx3, d_gain_ffn = norm_back(x2, r3, gain_ffn, dot_nt(da, w_in))
    dx2 = grad_top + dx3
    dyc = dx2.astype(BF)
    d_w_cross_out = dot_tn(oc, dyc).astype(BF)
    d_o = dot_nt(dyc, w_cross_out).astype(BF)
    dqc, dk, dv = cross_bwd(
        lo, hi, c_start, c_size, qc, d_o, o_cross, lse_cross, k_all, v_all, kt_all, scale
    )

    dkv = jnp.concatenate([dk, dv], axis=1).reshape(blocks, enc_rows, 2 * width)
    dkv = relative(dkv, "blk")
    dkv = add_low(dkv[0::2], swap(dkv[1::2], "blk", 1))
    enc_half = enc_rel[0::2]
    dkv_flat = dkv.reshape(-1, 2 * width)
    d_w_cross_kv = dot_tn(enc_half.reshape(-1, width), dkv_flat).astype(BF)
    d_enc = dot_nt(dkv_flat, w_cross_kv).reshape(blocks // 2, enc_rows, width)
    d_enc_parts = {2 * r: d_enc[r] for r in range(blocks // 2)}
    for bit in reversed(bits_of("blk")[1:]):
        for r in [r for r in d_enc_parts if r & bit]:
            came = swap(d_enc_parts.pop(r).astype(BF), "blk", bit)
            d_enc_parts[r ^ bit] = d_enc_parts[r ^ bit] + came.astype(F32)
    d_encodings = d_enc_parts[0]

    d_w_cross_q = dot_tn(h2, dqc).astype(BF)
    sums_cross = reduce_all(pack([d_w_cross_out, d_w_cross_q, d_w_cross_kv], blocks))
    dx_two, d_gain_cross = norm_back(x1, r2, gain_cross, dot_nt(dqc, w_cross_q))
    dx1 = dx2 + dx_two
    dy1 = dx1.astype(BF)
    d_w_self_out = dot_tn(o_self, dy1).astype(BF)
    d_os = dot_nt(dy1, w_self_out).astype(BF)
    dproj, dbrow = self_bwd(s_start, s_size, brow, proj, d_os, lse_self, scale)
    d_w_qkv = dot_tn(h1, dproj).astype(BF)
    sums_self = reduce_all(pack([d_w_qkv, d_w_self_out], blocks))
    dx_one, d_gain_self = norm_back(x0, r1, gain_self, dot_nt(dproj, w_qkv))
    d_rel = jnp.dot(
        bucket_hot.T, jnp.sum(dbrow.reshape(length, heads, -1), axis=2), precision=lax.Precision.HIGHEST
    )
    d_x0 = dx1 + dx_one
    high = d_x0.astype(BF)
    low = (d_x0 - high.astype(F32)).astype(BF)
    d_dec_in = dot_tn(forward_perm, high) + dot_tn(forward_perm, low)

    small = jnp.concatenate([d_gain_self, d_gain_cross, d_gain_ffn, d_rel.reshape(-1)])
    small = sum_everywhere(small.reshape(-1, 128)).reshape(-1)

    def own(v):
        return lax.dynamic_slice_in_dim(v, me * (v.shape[0] // blocks), v.shape[0] // blocks, 0)

    g_self, g_cross, g_ffn = (own(small[i * width : (i + 1) * width]) for i in range(3))
    g_rel = own(small[3 * width :].reshape(buckets, heads))
    (o_wout,) = unpack(sums_out, [w_out.shape], blocks)
    (o_win,) = unpack(sums_in, [w_in.shape], blocks)
    o_wco, o_wcq, o_wckv = unpack(sums_cross, [w_cross_out.shape, w_cross_q.shape, w_cross_kv.shape], blocks)
    o_wqkv, o_wso = unpack(sums_self, [w_qkv.shape, w_self_out.shape], blocks)
    return (
        layer_out,
        d_dec_in,
        d_encodings,
        g_self,
        o_wqkv,
        o_wso,
        g_rel,
        g_cross,
        o_wcq,
        o_wckv,
        o_wco,
        g_ffn,
        o_win,
        o_wout,
    )


def slot_of(rel):
    return (rel & 1) * 4 + (rel & 2) + ((rel >> 2) & 1)


def fill_bias_all(brow_ref, bias, nq):
    dist = distances()

    def add(d, held):
        here = dist == d
        row = pl.ds(d, 1)
        return tuple(jnp.where(here, brow_ref[row, c * 256 : (c + 1) * 256], held[c]) for c in range(nq))

    held = lax.fori_loop(0, brow_ref.shape[0], add, (jnp.full((WIN, 256), MASKED, F32),) * nq)
    for c in range(nq):
        bias[c] = held[c]


def gelu_both(a):
    c = math.sqrt(2.0 / math.pi)
    a2 = a * a
    t = jnp.tanh(c * (a + 0.044715 * (a2 * a)))
    half = 0.5 * (1.0 + t)
    return a * half, half + 0.5 * a * (1.0 - t * t) * (c * (1.0 + 3.0 * 0.044715 * a2))


def rms(x):
    return lax.rsqrt(jnp.mean(x * x, axis=-1, keepdims=True) + EPSILON)


def rms_back(x, inverse, gain, grad):
    scaled = grad * gain
    mean = jnp.mean(x * scaled, axis=-1, keepdims=True)
    unit = x * inverse
    return inverse * (scaled - unit * (inverse * mean)), jnp.sum(grad * unit, axis=0, keepdims=True)


def onehot_rows(src):
    n = src.shape[1]
    return (lax.broadcasted_iota(jnp.int32, (n, n), 0) == src).astype(F32).astype(BF)


def pre_kernel(
    me_ref,
    aq_ref,
    len_ref,
    qrows_ref,
    bucket_ref,
    dec_ref,
    gain1_ref,
    rel_ref,
    wqkv_ref,
    src_ref,
    cstart_ref,
    csize_ref,
    sstart_ref,
    ssize_ref,
    lo_ref,
    hi_ref,
    brow_ref,
    x0_ref,
    h1_ref,
    proj_ref,
    oself_ref,
    lse_ref,
    order,
    qstart,
    qcount,
    place,
    wide,
    kp,
    vp,
    bias,
    *,
    answers,
    length,
    questions,
    scale,
):
    rows, width = dec_ref.shape
    nq, tiles = width // 256, rows // TQ
    base = me_ref[0] * answers
    own = [aq_ref[base + a] for a in range(answers)]
    n = jnp.int32(0)
    first_row = jnp.int32(0)
    for c in range(questions):
        qstart[c] = first_row
        first_row = first_row + qrows_ref[0, c]
        qcount[c] = n
        place[c] = n
        for q in own:
            n = n + (q == c).astype(jnp.int32)
    for a, q in enumerate(own):
        at = place[q]
        order[at] = a
        place[q] = at + 1

    def answer_of(tok):
        ans = jnp.zeros_like(tok)
        for k in range(1, answers):
            ans = ans + (tok >= k * length).astype(jnp.int32)
        return ans

    tok = lax.broadcasted_iota(jnp.int32, (1, rows), 1)
    ans = answer_of(tok)
    src = tok - ans * length
    for k in range(answers):
        src = src + jnp.where(ans == k, order[k] * length, 0)
    src_ref[...] = src

    lane = lax.broadcasted_iota(jnp.int32, (tiles, 256), 1) % TQ
    tok = lane + TQ * lax.broadcasted_iota(jnp.int32, (tiles, 256), 0)
    ans = answer_of(tok)
    sstart_ref[...] = ans * length
    size = jnp.zeros_like(ans)
    for k in range(answers):
        size = size + jnp.where(ans == k, len_ref[order[k]], 0)
    ssize_ref[...] = size
    cstart = jnp.zeros_like(ans)
    csize = jnp.zeros_like(ans) + qrows_ref[0, 0]
    for c in range(1, questions):
        here = ans >= qcount[c]
        cstart = jnp.where(here, qstart[c], cstart)
        csize = jnp.where(here, qrows_ref[0, c], csize)
    cstart_ref[...] = cstart
    csize_ref[...] = csize
    for t in range(tiles):
        q_first = aq_ref[base + order[t * TQ // length]]
        q_last = aq_ref[base + order[(t * TQ + TQ - 1) // length]]
        lo_ref[t] = qstart[q_first] // TK
        hi_ref[t] = (qstart[q_last] + qrows_ref[0, q_last] + TK - 1) // TK

    for c in range(nq):
        head = lax.broadcasted_iota(jnp.int32, (rel_ref.shape[0], 256), 1) // 64
        held = jnp.zeros((rel_ref.shape[0], 256), F32)
        for a in range(4):
            h = c * 4 + a
            held = jnp.where(head == a, rel_ref[:, h : h + 1], held)
        wide[:, c * 256 : (c + 1) * 256] = held
    for d in range(length):
        brow_ref[d : d + 1, :] = wide[pl.ds(bucket_ref[d], 1), :]

    x0 = dot_tn(onehot_rows(src), dec_ref[...])
    x0_ref[...] = x0.astype(BF)
    h1_ref[...] = (x0 * rms(x0) * gain1_ref[0:1, :]).astype(BF)
    for i in range(3):
        cs = slice(i * width, (i + 1) * width)
        proj_ref[:, cs] = dot(h1_ref[...], wqkv_ref[:, cs]).astype(BF)
    fill_window(proj_ref, kp, vp, width)
    fill_bias_all(brow_ref, bias, nq)

    def scores(t, c):
        row = pl.ds(pl.multiple_of(t * TQ, TQ), TQ)
        win = pl.ds(pl.multiple_of(t * TQ, TQ), WIN)
        cs = slice(c * 256, (c + 1) * 256)
        qs = stack4(proj_ref[row, cs] * jnp.asarray(scale, BF))
        return dot_nt(kp[win, cs], qs) + bias[c]

    def probs(t, c, s):
        mask = range_mask(t * TQ - 64, WIN, sstart_ref[pl.ds(t, 1), :], ssize_ref[pl.ds(t, 1), :])
        s = jnp.where(mask, s, MASKED)
        m = jnp.max(red(s, jnp.max), axis=0, keepdims=True)
        p = jnp.exp(s - m)
        l = jnp.sum(red(p, jnp.sum), axis=0, keepdims=True)
        lse_ref[t, c] = m + jnp.log(l)
        return (p * (1.0 / l)).astype(BF)

    def mix(t, c, p):
        row = pl.ds(pl.multiple_of(t * TQ, TQ), TQ)
        win = pl.ds(pl.multiple_of(t * TQ, TQ), WIN)
        cs = slice(c * 256, (c + 1) * 256)
        oself_ref[row, cs] = unstack4(dot_tn(p, vp[win, cs])).astype(BF)

    def two_tiles(i, _):
        work = [(2 * i + k, c) for k in range(2) for c in range(nq)]
        s = [scores(t, c) for t, c in work]
        p = [probs(t, c, x) for (t, c), x in zip(work, s)]
        for (t, c), x in zip(work, p):
            mix(t, c, x)
        return 0

    lax.fori_loop(0, tiles // 2, two_tiles, 0)


def mid_kernel(x0_ref, oself_ref, wso_ref, gain2_ref, wcq_ref, x1_ref, h2_ref, qc_ref, *, scale):
    x1 = x0_ref[...].astype(F32) + dot(oself_ref[...], wso_ref[...])
    x1_ref[...] = x1
    h2_ref[...] = (x1 * rms(x1) * gain2_ref[1:2, :]).astype(BF)
    qc_ref[...] = dot(h2_ref[...], wcq_ref[...]).astype(BF) * jnp.asarray(scale, BF)


def mid(x0, oself, wso, gain, wcq, scale):
    rows, width = x0.shape
    return call(
        functools.partial(mid_kernel, scale=scale),
        "mid",
        (sds((rows, width), F32), sds((rows, width), BF), sds((rows, width), BF)),
        [VM] * 5,
        (VM,) * 3,
        [],
        (x0, oself, wso, gain, wcq),
        us=8,
    )


def call(kernel, name, out_shape, in_specs, out_specs, scratch, args, us):
    moved = sum(math.prod(a.shape) * a.dtype.itemsize for a in args)
    moved += sum(math.prod(a.shape) * a.dtype.itemsize for a in out_shape)
    return pl.pallas_call(
        kernel,
        out_shape=out_shape,
        in_specs=in_specs,
        out_specs=out_specs,
        scratch_shapes=scratch,
        compiler_params=pltpu.CompilerParams(vmem_limit_bytes=LIMIT),
        cost_estimate=pl.CostEstimate(flops=int(us * 1e11), bytes_accessed=moved, transcendentals=0),
        name=name,
    )(*args)


def sds(shape, dtype):
    return jax.ShapeDtypeStruct(shape, dtype)


def pre(me, aq, lens, qrows, bucket, dec, g1, rel, wqkv, scale):
    rows, width = dec.shape
    tiles, nq, length = rows // TQ, width // 256, bucket.shape[0]
    i32 = jnp.int32
    meta = sds((tiles, 256), i32)
    out = (
        sds((1, rows), i32),
        meta,
        meta,
        meta,
        meta,
        sds((tiles,), i32),
        sds((tiles,), i32),
        sds((length, width), F32),
        sds((rows, width), BF),
        sds((rows, width), BF),
        sds((rows, 3 * width), BF),
        sds((rows, width), BF),
        sds((tiles, nq, 1, 256), F32),
    )
    return call(
        functools.partial(
            pre_kernel, answers=lens.shape[0], length=length, questions=qrows.shape[1], scale=scale
        ),
        "pre",
        out,
        [SM] * 5 + [VM] * 4,
        (VM,) * 5 + (SM, SM) + (VM,) * 6,
        [
            pltpu.SMEM((lens.shape[0],), i32),
            pltpu.SMEM((qrows.shape[1],), i32),
            pltpu.SMEM((qrows.shape[1],), i32),
            pltpu.SMEM((qrows.shape[1],), i32),
            pltpu.VMEM((rel.shape[0], width), F32),
            pltpu.VMEM((rows + 64, width), BF),
            pltpu.VMEM((rows + 64, width), BF),
            pltpu.VMEM((nq, WIN, 256), F32),
        ],
        (me, aq, lens, qrows, bucket, dec, g1, rel, wqkv),
        us=40,
    )


def own_heads(x):
    return jnp.concatenate([x[a * 64 : (a + 1) * 64, a * TQ : (a + 1) * TQ] for a in range(4)], axis=0)


def in_pairs(lo, hi, work):
    def two(i, _):
        work(lo + 2 * i)
        work(lo + 2 * i + 1)
        return 0

    lax.fori_loop(0, (hi - lo) // 2, two, 0)

    @pl.when((hi - lo) % 2 == 1)
    def _():
        work(hi - 1)


def kv_cross_kernel(
    me_ref,
    lo_ref,
    hi_ref,
    start_ref,
    size_ref,
    q_ref,
    *rest,
    pieces,
):
    enc = rest[:pieces]
    wkv_ref, k_any, v_any, kt_any, o_ref, lse_ref, vt, k_ref, v_ref, kt_ref, out_sem, qst, s_scr, m_scr, l_scr, acc = rest[
        pieces:
    ]
    rows, width = q_ref.shape
    nq, tiles = width // 256, rows // TQ
    n = enc[0].shape[0]
    for r in range(pieces):
        at = pl.ds(pl.multiple_of((me_ref[0] ^ r) * n, n), n)
        kk = dot(enc[r][...], wkv_ref[:, :width]).astype(BF)
        k_ref[at, :] = kk
        kt_ref[:, at] = kk.T
        vv = dot(enc[r][...], wkv_ref[:, width:]).astype(BF)
        v_ref[at, :] = vv
        vt[:, at] = vv.T
    leaving = [
        pltpu.make_async_copy(a, b, out_sem.at[i])
        for i, (a, b) in enumerate(((k_ref, k_any), (v_ref, v_any), (kt_ref, kt_any)))
    ]
    for c in leaving:
        c.start()

    def tile(t, _):
        st = start_ref[pl.ds(t, 1), :]
        sz = size_ref[pl.ds(t, 1), :]
        lo = lo_ref[t]
        hi = hi_ref[t]
        row = pl.ds(pl.multiple_of(t * TQ, TQ), TQ)
        for c in range(nq):
            qst[c] = stack4(q_ref[row, c * 256 : (c + 1) * 256])
            m_scr[c] = jnp.full((8, 256), NEG, F32)
            l_scr[c] = jnp.zeros((8, 256), F32)
            acc[c] = jnp.zeros((256, 256), F32)

        def scores(j):
            kr = pl.ds(pl.multiple_of(j * TK, TK), TK)
            mask = range_mask(j * TK, TK, st, sz)
            for c in range(nq):
                s = dot_nt(k_ref[kr, c * 256 : (c + 1) * 256], qst[c])
                s = jnp.where(mask, s, NEG)
                s_scr[c, kr, :] = s
                m_scr[c] = jnp.maximum(m_scr[c], red(s, jnp.max))

        in_pairs(lo, hi, scores)
        for c in range(nq):
            m_scr[c] = jnp.broadcast_to(jnp.max(m_scr[c], axis=0, keepdims=True), (8, 256))

        def mix(j):
            kr = pl.ds(pl.multiple_of(j * TK, TK), TK)
            for c in range(nq):
                p = jnp.exp(s_scr[c, kr, :] - m_scr[c][0:1])
                l_scr[c] += red(p, jnp.sum)
                acc[c] += dot(vt[c * 256 : (c + 1) * 256, kr], p.astype(BF))

        in_pairs(lo, hi, mix)
        for c in range(nq):
            l = jnp.sum(l_scr[c], axis=0, keepdims=True)
            lse_ref[t, c] = m_scr[c][0:1] + jnp.log(l)
            o_ref[row, c * 256 : (c + 1) * 256] = own_heads(acc[c] * (1.0 / l)).T
        return 0

    lax.fori_loop(0, tiles, tile, 0)
    for c in leaving:
        c.wait()


def kv_cross(me, lo, hi, start, size, q, enc, wkv):
    rows, width = q.shape
    tiles, nq = rows // TQ, width // 256
    keys = len(enc) * enc[0].shape[0]
    return call(
        functools.partial(kv_cross_kernel, pieces=len(enc)),
        "kv_cross",
        (
            sds((keys, width), BF),
            sds((keys, width), BF),
            sds((width, keys), BF),
            sds((rows, width), F32),
            sds((tiles, nq, 1, 256), F32),
        ),
        [SM] * 3 + [VM] * (3 + len(enc) + 1),
        (pl.BlockSpec(memory_space=pl.ANY),) * 3 + (VM, VM),
        [
            pltpu.VMEM((width, keys), BF),
            pltpu.VMEM((keys, width), BF),
            pltpu.VMEM((keys, width), BF),
            pltpu.VMEM((width, keys), BF),
            pltpu.SemaphoreType.DMA((3,)),
            pltpu.VMEM((nq, 256, 256), BF),
            pltpu.VMEM((nq, keys, 256), F32),
            pltpu.VMEM((nq, 8, 256), F32),
            pltpu.VMEM((nq, 8, 256), F32),
            pltpu.VMEM((nq, 256, 256), F32),
        ],
        (me, lo, hi, start, size, q, *enc, wkv),
        us=80,
    )


def ffn_kernel(
    src_ref,
    x1_ref,
    ocross_ref,
    gain_ref,
    cot_ref,
    wco_ref,
    win_any,
    wout_any,
    okeep_ref,
    osend_ref,
    wi_ref,
    wj_ref,
    oc_ref,
    out_ref,
    dx2_ref,
    dyc_ref,
    do_ref,
    dgain_ref,
    win,
    wout,
    h3,
    h3t,
    g_low,
    dh,
    out_acc,
    u_all,
    ik,
    ss,
    ic,
    iy,
    ix,
    even,
    odd,
    came,
    w_sem,
    send_sem,
    recv_sem,
    o_send,
    o_recv,
):
    rows, width = x1_ref.shape
    steps = win.shape[1] // width
    quarter = width // 4
    half = quarter // 2
    g, b = lax.axis_index("grp"), lax.axis_index("blk")
    mesh_id = pl.DeviceIdType.MESH
    peers = [(g, b ^ 1), (g ^ 1, b), (g, b ^ 2)]

    def part(f):
        return pl.ds(pl.multiple_of(f * width, width), width)

    def weights(f):
        return (
            pltpu.make_async_copy(win_any.at[:, part(f)], win.at[:, part(f)], w_sem.at[0, f]),
            pltpu.make_async_copy(wout_any.at[part(f), :], wout.at[part(f), :], w_sem.at[1, f]),
        )

    for f in range(steps):
        for c in weights(f):
            c.start()
    barrier = pltpu.get_barrier_semaphore()
    for p in peers:
        pl.semaphore_signal(barrier, inc=1, device_id=p, device_id_type=mesh_id)
    pl.semaphore_wait(barrier, 3)

    def remote(k, f):
        src, dst = ((ss.at[f], ic.at[f]), (ik.at[f, pl.ds(2, 2)], iy.at[f]), (ik.at[f, pl.ds(1, 1)], ix.at[f]))[k]
        return pltpu.make_async_remote_copy(
            src_ref=src,
            dst_ref=dst,
            send_sem=send_sem.at[k, f],
            recv_sem=recv_sem.at[k, f],
            device_id=peers[k],
            device_id_type=mesh_id,
        )

    o_copy = pltpu.make_async_remote_copy(
        src_ref=odd, dst_ref=came, send_sem=o_send, recv_sem=o_recv, device_id=peers[0], device_id_type=mesh_id
    )

    def add(x, y):
        return (x.astype(F32) + y.astype(F32)).astype(BF)

    def event(k, f):
        @pl.when((f >= 0) & (f < steps))
        def _():
            remote(k, f).wait()
            if k == 0:
                ik[f] = add(ik[f], ic[f])
            elif k == 1:
                ik[f, 0:2] = add(ik[f, 0:2], iy[f])
            else:
                rel = (g >> 1) ^ f
                whole = add(ik[f, 0], ix[f, 0])

                @pl.when((rel & 1) == 0)
                def _():
                    wi_ref[rel >> 1] = whole

                @pl.when((rel & 1) == 1)
                def _():
                    wj_ref[rel >> 1] = whole

            if k < 2:
                remote(k + 1, f).start()

    hot = onehot_rows(src_ref[...])
    g_low[...] = dot_tn(hot, cot_ref[...]).astype(BF)
    oc_ref[...] = ocross_ref[...].astype(BF)
    x2 = x1_ref[...] + dot(oc_ref[...], wco_ref[...])
    dx2_ref[...] = x2
    n = (x2 * rms(x2) * gain_ref[2:3, :]).astype(BF)
    h3[...] = n
    h3t[...] = n.T
    out_acc[...] = jnp.zeros_like(out_acc)
    dh[...] = jnp.zeros_like(dh)

    def hidden(f, _):
        for c in weights(f):
            c.wait()
        u, slope = gelu_both(dot(h3[...], win[:, part(f)]))
        u = u.astype(BF)
        u_all[:, part(f)] = u
        da = (slope * dot_nt(g_low[...], wout[part(f), :])).astype(BF)
        for r in range(4):
            left = h3t[pl.ds(pl.multiple_of((b ^ r) * quarter, quarter), quarter), :]
            dwi = dot(left, da).astype(BF)
            target = ss if r & 1 else ik
            for i in range(2):
                y, x = (g ^ (2 * f + i)) & 1, r >> 1
                target[f, 2 * y + x] = dwi[i * half : (i + 1) * half]
        remote(0, f).start()
        out_acc[...] += dot(u, wout[part(f), :])
        event(0, f)
        dh[...] += dot_nt(da, win[:, part(f)])
        event(1, f - 1)
        event(2, f - 2)
        return 0

    lax.fori_loop(0, steps, hidden, 0)

    def last_rows(f, _):
        dwo = dot_tn(u_all[:, part(f)], g_low[...]).astype(BF)
        r = b ^ f
        for s in range(8):
            at = (r >> 1) * 8 + slot_of(g ^ s)

            @pl.when((r & 1) == 0)
            def _():
                even[at] = dwo[s * half : (s + 1) * half]

            @pl.when((r & 1) == 1)
            def _():
                odd[at] = dwo[s * half : (s + 1) * half]

        return 0

    lax.fori_loop(0, steps, last_rows, 0)
    o_copy.start()
    event(1, jnp.int32(steps - 1))
    event(2, jnp.int32(steps - 2))
    x2 = dx2_ref[...]
    out = (x2 + out_acc[...]).astype(BF)
    out_ref[...] = dot(onehot_rows(src_ref[...]), out).astype(BF)
    dx, dgain_ref[...] = rms_back(x2, rms(x2), gain_ref[2:3, :], dh[...])
    dx2 = g_low[...].astype(F32) + dx
    dx2_ref[...] = dx2
    dyc_ref[...] = dx2.astype(BF)
    do_ref[...] = dot_nt(dyc_ref[...], wco_ref[...]).astype(BF)
    o_copy.wait()
    okeep_ref[...] = add(even[0:8], came[0:8])
    osend_ref[...] = add(even[8:16], came[8:16])
    event(2, jnp.int32(steps - 1))


def ffn(src, x1, ocross, gain, cot, wco, win, wout):
    rows, width = x1.shape
    steps = win.shape[1] // width
    half = width // 8
    any_spec = pl.BlockSpec(memory_space=pl.ANY)
    buf = lambda *n: pltpu.VMEM(n + (half, width), BF)
    tok = lambda d: pltpu.VMEM((rows, width), d)
    return pl.pallas_call(
        ffn_kernel,
        out_shape=(
            sds((8, half, width), BF),
            sds((8, half, width), BF),
            sds((2, half, width), BF),
            sds((2, half, width), BF),
            sds((rows, width), BF),
            sds((rows, width), BF),
            sds((rows, width), F32),
            sds((rows, width), BF),
            sds((rows, width), BF),
            sds((1, width), F32),
        ),
        in_specs=[VM] * 6 + [any_spec] * 2,
        out_specs=(VM,) * 10,
        scratch_shapes=[
            pltpu.VMEM(win.shape, BF),
            pltpu.VMEM(wout.shape, BF),
            tok(BF),
            pltpu.VMEM((width, rows), BF),
            tok(BF),
            tok(F32),
            tok(F32),
            pltpu.VMEM((rows, win.shape[1]), BF),
            buf(steps, 4),
            buf(steps, 4),
            buf(steps, 4),
            buf(steps, 2),
            buf(steps, 1),
            buf(16),
            buf(16),
            buf(16),
            pltpu.SemaphoreType.DMA((2, steps)),
            pltpu.SemaphoreType.DMA((3, steps)),
            pltpu.SemaphoreType.DMA((3, steps)),
            pltpu.SemaphoreType.DMA,
            pltpu.SemaphoreType.DMA,
        ],
        compiler_params=pltpu.CompilerParams(
            vmem_limit_bytes=63 << 20, collective_id=1, has_side_effects=True
        ),
        cost_estimate=pl.CostEstimate(flops=10**13, bytes_accessed=30 << 20, transcendentals=0),
        name="ffn",
    )(src, x1, ocross, gain, cot, wco, win, wout)


def cross_back_kernel(
    me_ref,
    lo_ref,
    hi_ref,
    start_ref,
    size_ref,
    q_ref,
    do_ref,
    o_ref,
    lse_ref,
    k_ref,
    v_ref,
    kt_ref,
    dq_ref,
    keep_ref,
    send_ref,
    qs,
    dos,
    del_scr,
    dka,
    dva,
    dqt,
    ps,
    dss,
    *,
    scale,
):
    rows, width = q_ref.shape
    nq, tiles = width // 256, rows // TQ
    dka[...] = jnp.zeros_like(dka)
    dva[...] = jnp.zeros_like(dva)

    def tile(t, _):
        st = start_ref[pl.ds(t, 1), :]
        sz = size_ref[pl.ds(t, 1), :]
        row = pl.ds(pl.multiple_of(t * TQ, TQ), TQ)
        for c in range(nq):
            cs = slice(c * 256, (c + 1) * 256)
            qs[c] = stack4(q_ref[row, cs])
            b = do_ref[row, cs]
            dos[c] = stack4(b)
            product = (b.astype(F32) * o_ref[row, cs]).T
            total = jnp.concatenate(
                [jnp.sum(product[h * 64 : (h + 1) * 64], axis=0, keepdims=True) for h in range(4)], axis=1
            )
            del_scr[c] = jnp.broadcast_to(total, (8, 256))
            dqt[c] = jnp.zeros((256, 256), F32)

        def probs(j, slot):
            kr = pl.ds(pl.multiple_of(j * TK, TK), TK)
            mask = range_mask(j * TK, TK, st, sz)
            for c in range(nq):
                cs = slice(c * 256, (c + 1) * 256)
                s = dot_nt(k_ref[kr, cs], qs[c])
                p = jnp.where(mask, jnp.exp(s - lse_ref[t, c]), 0.0)
                dp = dot_nt(v_ref[kr, cs], dos[c])
                ps[slot, c] = p.astype(BF)
                dss[slot, c] = (p * (dp - del_scr[c][0:1])).astype(BF)

        def grads(j, slot):
            kr = pl.ds(pl.multiple_of(j * TK, TK), TK)
            for c in range(nq):
                cs = slice(c * 256, (c + 1) * 256)
                ds = dss[slot, c]
                dva[kr, cs] += dot(ps[slot, c], dos[c])
                dka[kr, cs] += dot(ds, qs[c])
                dqt[c] += dot(kt_ref[cs, kr], ds)

        lo = lo_ref[t]
        hi = hi_ref[t]
        slots = ps.shape[0]

        def two(i, _):
            probs(lo + 2 * i, 0)
            probs(lo + 2 * i + 1, 1)
            grads(lo + 2 * i, 0)
            grads(lo + 2 * i + 1, 1)
            return 0

        if slots == 4:

            def four(i, _):
                for k in range(4):
                    probs(lo + 4 * i + k, k)
                for k in range(4):
                    grads(lo + 4 * i + k, k)
                return 0

            lax.fori_loop(0, (hi - lo) // 4, four, 0)
            lo = lo + (hi - lo) // 4 * 4
        lax.fori_loop(0, (hi - lo) // 2, two, 0)

        @pl.when((hi - lo) % 2 == 1)
        def _():
            probs(hi - 1, 0)
            grads(hi - 1, 0)

        for c in range(nq):
            cs = slice(c * 256, (c + 1) * 256)
            dq_ref[row, cs] = (own_heads(dqt[c]).T * scale).astype(BF)
        return 0

    lax.fori_loop(0, tiles, tile, 0)
    n = keep_ref.shape[1]
    for r in range(4):
        at = pl.ds(pl.multiple_of((me_ref[0] ^ r) * n, n), n)
        target = send_ref if r & 1 else keep_ref
        target[r >> 1, :, :width] = dka[at, :].astype(BF)
        target[r >> 1, :, width:] = dva[at, :].astype(BF)


def cross_back(me, lo, hi, start, size, q, do, o, lse, k, v, kt, scale, first, nq):
    rows = q.shape[0]
    keys, width = k.shape[0], nq * 256
    tiles = rows // TQ
    at = first // nq
    part = sds((2, keys // 4, 2 * width), BF)
    cols = lambda n: pl.BlockSpec((n, width), lambda i: (0, at))
    whole = lambda a: pl.BlockSpec(a.shape, lambda i: (0,) * len(a.shape))
    outs = (sds((rows, width), BF), part, part)
    return pl.pallas_call(
        functools.partial(cross_back_kernel, scale=scale),
        grid=(1,),
        out_shape=outs,
        in_specs=[
            SM,
            SM,
            SM,
            whole(start),
            whole(size),
            cols(rows),
            cols(rows),
            cols(rows),
            pl.BlockSpec((tiles, nq, 1, 256), lambda i: (0, at, 0, 0)),
            cols(keys),
            cols(keys),
            pl.BlockSpec((width, keys), lambda i: (at, 0)),
        ],
        out_specs=tuple(whole(a) for a in outs),
        scratch_shapes=[pltpu.VMEM((nq, 256, 256), BF)] * 2
        + [
            pltpu.VMEM((nq, 8, 256), F32),
            pltpu.VMEM((keys, width), F32),
            pltpu.VMEM((keys, width), F32),
            pltpu.VMEM((nq, 256, 256), F32),
            pltpu.VMEM((4 if nq == 1 else 2, nq, 256, 256), BF),
            pltpu.VMEM((4 if nq == 1 else 2, nq, 256, 256), BF),
        ],
        compiler_params=pltpu.CompilerParams(vmem_limit_bytes=LIMIT),
        cost_estimate=pl.CostEstimate(flops=10**13, bytes_accessed=30 << 20, transcendentals=0),
        name="cross_back",
    )(me, lo, hi, start, size, q, do, o, lse, k, v, kt)


def cross_in_kernel(
    dq0_ref, dq1_ref, x1_ref, dx2_ref, gain_ref, wcq_ref, wso_ref, own_ref, oz_ref, oy_ref, oyz_ref, two_ref, came_ref,
    dx1_ref, dy1_ref, dos_ref, dgain_ref, pair_ref, keep_ref, send_ref,
):
    x1 = x1_ref[...]
    cut = dq0_ref.shape[1]
    back = dot_nt(dq0_ref[...], wcq_ref[:, :cut]) + dot_nt(dq1_ref[...], wcq_ref[:, cut:])
    dx, dgain_ref[...] = rms_back(x1, rms(x1), gain_ref[1:2, :], back)
    dx1 = dx2_ref[...] + dx
    dx1_ref[...] = dx1
    dy1_ref[...] = dx1.astype(BF)
    dos_ref[...] = dot_nt(dy1_ref[...], wso_ref[...]).astype(BF)
    for n, ref in ((0, keep_ref), (1, send_ref)):
        parts = [r[n].astype(F32) for r in (own_ref, oz_ref, oy_ref, oyz_ref)]
        ref[...] = (parts[0] + parts[1] + parts[2] + parts[3]).astype(BF)
        pair_ref[n] = (two_ref[n].astype(F32) + came_ref[1 - n].astype(F32)).astype(BF)


def cross_in(dq0, dq1, x1, dx2, gain, wcq, wso, own, oz, oy, oyz, two, came):
    rows, width = x1.shape
    return call(
        cross_in_kernel,
        "cross_in",
        (
            sds((rows, width), F32),
            sds((rows, width), BF),
            sds((rows, width), BF),
            sds((1, width), F32),
            sds(two.shape, BF),
            sds(two.shape[1:], BF),
            sds(two.shape[1:], BF),
        ),
        [VM] * 13,
        (VM,) * 7,
        [],
        (dq0, dq1, x1, dx2, gain, wcq, wso, own, oz, oy, oyz, two, came),
        us=60,
    )


def late_kernel(
    start_ref,
    size_ref,
    bucket_ref,
    brow_ref,
    proj_any,
    do_any,
    lse_ref,
    h1_any,
    oself_any,
    dy1_any,
    src_ref,
    x0_any,
    gain_ref,
    dx1_any,
    wqkv_any,
    dg2_ref,
    dg3_ref,
    keep0_any,
    came0_any,
    keep1_any,
    came1_any,
    enc0_any,
    enc2_any,
    wkv_any,
    oc_ref,
    dyc_ref,
    h2_ref,
    dq0_ref,
    dq1_ref,
    wpair_any,
    fkeep_ref,
    fsend_any,
    d_ref,
    small_ref,
    f,
    own_ref,
    came_any,
    ffn_any,
    projs,
    wbuf,
    both,
    stage,
    enc_t,
    enc_out,
    bias,
    dka,
    dva,
    dsum,
    left_t,
    ss,
    drow,
    sm_in,
    dgain,
    fown,
    frecv,
    q,
    r1,
    r2,
    r3,
    r4,
    r5,
    do_ref,
    h1_ref,
    oself_ref,
    dy1_ref,
    x0_ref,
    dx1_ref,
    enc0_ref,
    enc2_ref,
    send_sem,
    recv_sem,
    sm_send,
    sm_recv,
    x_send,
    x_recv,
    f_send,
    f_recv,
    loc,
    *,
    scale,
):
    rows, width = do_ref.shape
    nq, tiles = width // 256, rows // TQ
    length, buckets = brow_ref.shape[0], 32
    count, step_rows, wide = q.shape[0], q.shape[2], q.shape[3]
    each = count // 8
    quarter = width // 4
    tall = quarter // 4
    n = enc0_ref.shape[0]
    cut = dq0_ref.shape[1]
    g, b = lax.axis_index("grp"), lax.axis_index("blk")
    peers = [(g, b ^ 1), (g, b ^ 2), (g ^ 1, b), (g ^ 2, b), (g ^ 4, b), (g ^ 2, b), (g ^ 1, b)]
    mesh_id = pl.DeviceIdType.MESH

    def local(src, dst, k):
        return pltpu.make_async_copy(src, dst, loc.at[k])

    def remote(src, dst, send, recv, k):
        return pltpu.make_async_remote_copy(
            src_ref=src, dst_ref=dst, send_sem=send, recv_sem=recv, device_id=peers[k], device_id_type=mesh_id
        )

    proj_in = local(proj_any, projs.at[pl.ds(64, rows), :], 0)
    wkv_in = local(wkv_any, wbuf.at[:, pl.ds(0, 2 * width)], 1)
    held_in = [
        local(src, dst, 20 + i)
        for i, (src, dst) in enumerate(
            (
                (oself_any, oself_ref),
                (dy1_any, dy1_ref),
                (enc0_any, enc0_ref),
                (enc2_any, enc2_ref),
                (do_any, do_ref),
                (h1_any, h1_ref),
                (x0_any, x0_ref),
                (dx1_any, dx1_ref),
            )
        )
    ]
    wqkv_in = local(wqkv_any, wbuf, 2)
    dkv_in = []
    for r in range(2):
        for i, (keep, came, at, w) in enumerate(
            ((keep0_any, came0_any, 0, cut), (keep1_any, came1_any, cut, width - cut))
        ):
            for half in range(2):
                from_, to = pl.ds(half * w, w), pl.ds(half * width + at, w)
                k = 3 + 8 * r + 4 * i + 2 * half
                dkv_in.append((r, local(keep.at[r, :, from_], both.at[pl.ds(r * n, n), to], k)))
                dkv_in.append((r, local(came.at[r, :, from_], stage.at[:, to], k + 1)))
    for r, c in dkv_in:
        if r == 0:
            c.start()
    for c in held_in[:4] + [wkv_in, proj_in] + held_in[4:]:
        c.start()

    barrier = pltpu.get_barrier_semaphore()
    for p in peers[:5]:
        pl.semaphore_signal(barrier, inc=1, device_id=p, device_id_type=mesh_id)
    pl.semaphore_wait(barrier, 5)

    f_half = fown.shape[0]
    w_at, o_at = pl.ds(0, f_half), pl.ds(f_half, f_half)
    w_local = local(wpair_any, ffn_any.at[pl.ds(0, 2), w_at, :], 28)
    w_copies = [
        remote(wpair_any, ffn_any.at[pl.ds(2, 2), w_at, :], f_send.at[0], f_recv.at[0], 3),
    ]
    f_first = remote(fsend_any, frecv, f_send.at[2], f_recv.at[2], 4)
    f_second = remote(fown, ffn_any.at[1, o_at, :], f_send.at[3], f_recv.at[3], 4)
    f_third = remote(
        ffn_any.at[pl.ds(0, 2), o_at, :], ffn_any.at[pl.ds(2, 2), o_at, :], f_send.at[4], f_recv.at[4], 3
    )
    f_local = local(fown, ffn_any.at[0, o_at, :], 19)
    f_slices = f_half // step_rows
    w_copies[0].start()
    f_first.start()
    w_local.start()

    def w_copy(i):
        at = pl.ds(pl.multiple_of(i * step_rows, step_rows), step_rows)
        src, dst = ffn_any.at[pl.ds(0, 4), at, :], ffn_any.at[pl.ds(4, 4), at, :]
        return remote(src, dst, f_send.at[11 + i], f_recv.at[11 + i], 2)

    def f_copy(i):
        at = pl.ds(pl.multiple_of(f_half + i * step_rows, step_rows), step_rows)
        src, dst = ffn_any.at[pl.ds(0, 4), at, :], ffn_any.at[pl.ds(4, 4), at, :]
        return remote(src, dst, f_send.at[5 + i], f_recv.at[5 + i], 2)

    enc_copy = remote(enc_out, came_any, x_send, x_recv, 1)

    def add(x, y):
        return (x.astype(F32) + y.astype(F32)).astype(BF)

    def core_copy(j):
        at = pl.ds(pl.multiple_of(j * step_rows, step_rows), step_rows)
        return remote(ss.at[:, at, :], r1.at[j], send_sem.at[0, j], recv_sem.at[0, j], 0)

    def copy(k, j):
        src, dst = [
            lambda: (q.at[j, pl.ds(8, 8)], r2.at[j]),
            lambda: (q.at[j, pl.ds(4, 4)], r3.at[j]),
            lambda: (q.at[j, pl.ds(2, 2)], r4.at[j]),
            lambda: (q.at[j, pl.ds(0, 2)], r5.at[j]),
            lambda: (f.at[j, pl.ds(0, 2)], f.at[j, pl.ds(2, 2)]),
            lambda: (f.at[j, pl.ds(0, 4)], f.at[j, pl.ds(4, 4)]),
        ][k - 1]()
        return remote(src, dst, send_sem.at[k, j], recv_sem.at[k, j], k)

    def event(k, j):
        @pl.when((j >= 0) & (j < count))
        def _():
            (core_copy(j) if k == 0 else copy(k, j)).wait()
            if k == 0:
                q[j] = add(q[j], r1[j])
            elif k == 1:
                q[j, 0:8] = add(q[j, 0:8], r2[j])
            elif k == 2:
                q[j, 0:4] = add(q[j, 0:4], r3[j])
            elif k == 3:
                q[j, 0:2] = add(q[j, 0:2], r4[j])
            elif k == 4:
                f[j, 0] = add(q[j, 0], r5[j, 1])
                f[j, 1] = add(q[j, 1], r5[j, 0])
            if k < 6:
                copy(k + 1, j).start()

    def step(t):
        t = jnp.asarray(t, jnp.int32)
        event(0, t + 3)
        for k in range(1, 7):
            event(k, t - 2 * (k - 1))

    def put(right, block):
        for r in range(4):
            part = left_t[pl.ds(pl.multiple_of((b ^ r) * quarter, quarter), quarter), :]
            spread(dot(part, right).astype(BF), r, block)
        start_core(block)

    def spread(grad, r, block):
        for s in range(8):
            at = (r >> 1) * 8 + slot_of(g ^ s)
            y, x = (s >> 1) * tall, (s & 1) * wide
            if r & 1:
                ss[at, block * tall : (block + 1) * tall, :] = grad[y : y + tall, x : x + wide]
            else:
                for k in range(each):
                    piece = grad[y + k * step_rows : y + (k + 1) * step_rows, x : x + wide]
                    q[block * each + k, at] = piece

    def start_core(block):
        for k in range(each):
            core_copy(block * each + k).start()

    left_t[...] = oc_ref[...].T
    put(dyc_ref[...], 0)
    left_t[...] = h2_ref[...].T
    for j in range(each):
        event(0, jnp.int32(j))
    put(jnp.concatenate([dq0_ref[...], dq1_ref[...]], axis=1), 1)
    step(0)
    w_local.wait()
    w_copies[0].wait()
    w_copy(0).start()
    held_in[0].wait()
    held_in[1].wait()
    left_t[...] = oself_ref[...].T
    for r, c in dkv_in:
        if r == 0:
            c.wait()
    both[:n, :] = add(both[:n, :], stage[...])
    for r, c in dkv_in:
        if r == 1:
            c.start()
    put(dy1_ref[...], 2)
    f_first.wait()
    fown[...] = add(fkeep_ref[...], frecv[...])
    f_local.start()
    f_second.start()
    step(1)
    w_copy(1).start()

    held_in[2].wait()
    held_in[3].wait()
    enc_t[:, :n] = enc0_ref[...].T
    enc_t[:, n:] = enc2_ref[...].T
    for r, c in dkv_in:
        if r == 1:
            c.wait()
    both[n:, :] = add(both[n:, :], stage[...])
    for i in range(2):
        for r in range(4):
            part = enc_t[pl.ds(pl.multiple_of((b ^ r) * quarter, quarter), quarter), :]
            spread(dot(part, both[:, i * width : (i + 1) * width]).astype(BF), r, 3 + i)
        start_core(3 + i)
        step(2 + i)
        w_copy(2 + i).start()
    wkv_in.wait()
    enc_out[...] = dot_nt(both[n:, :], wbuf[:, : 2 * width]).astype(BF)
    own_ref[...] = dot_nt(both[:n, :], wbuf[:, : 2 * width])
    wqkv_in.start()

    projs[0:64, :] = jnp.zeros((64, 3 * width), BF)
    fill_bias_all(brow_ref, bias, nq)
    dka[...] = jnp.zeros_like(dka)
    dva[...] = jnp.zeros_like(dva)
    dsum[...] = jnp.zeros_like(dsum)
    proj_in.wait()
    held_in[4].wait()

    def tile(t):
        row = pl.ds(pl.multiple_of(t * TQ, TQ), TQ)
        held = pl.ds(pl.multiple_of(t * TQ + 64, TQ), TQ)
        win = pl.ds(pl.multiple_of(t * TQ, TQ), WIN)
        mask = range_mask(t * TQ - 64, WIN, start_ref[pl.ds(t, 1), :], size_ref[pl.ds(t, 1), :])
        for c in range(nq):
            cols = slice(c * 256, (c + 1) * 256)
            kcols = slice(width + c * 256, width + (c + 1) * 256)
            vcols = slice(2 * width + c * 256, 2 * width + (c + 1) * 256)
            qs = stack4(projs[held, cols] * jnp.asarray(scale, BF))
            dos = stack4(do_ref[row, cols])
            s = dot_nt(projs[win, kcols], qs) + bias[c]
            p = jnp.where(mask, jnp.exp(s - lse_ref[t, c]), 0.0)
            dp = dot_nt(projs[win, vcols], dos)
            delta = jnp.sum(red(p * dp, jnp.sum), axis=0, keepdims=True)
            ds = p * (dp - delta)
            dsum[c] += ds
            ds = ds.astype(BF)
            dva[win, cols] += dot(p.astype(BF), dos)
            dka[win, cols] += dot(ds, qs)
            projs[held, cols] = (unstack4(dot_tn(ds, projs[win, kcols])) * scale).astype(BF)

    def tile_and_step(t, _):
        tile(t)
        step(t + 4)

        @pl.when(t < f_slices - 4)
        def _():
            w_copy(t + 4).start()

        return 0

    lax.fori_loop(0, tiles - 2, tile_and_step, 0)

    def tile_alone(t, _):
        tile(t)
        return 0

    lax.fori_loop(tiles - 2, tiles, tile_alone, 0)
    f_second.wait()
    f_local.wait()
    f_third.start()
    dist = distances()
    for c in range(nq):
        cols = slice(c * 256, (c + 1) * 256)

        def one(d, _):
            x = jnp.where(dist == d, dsum[c], 0.0)
            drow[pl.ds(d, 1), cols] = jnp.sum(red(x, jnp.sum), axis=0, keepdims=True)
            return 0

        lax.fori_loop(0, length, one, 0)
    lane = lax.broadcasted_iota(jnp.int32, (buckets, length), 1)
    place = jnp.zeros((buckets, length), jnp.int32)
    for d in range(length):
        place = jnp.where(lane == d, bucket_ref[d], place)
    hot = (place == lax.broadcasted_iota(jnp.int32, (buckets, length), 0)).astype(F32)
    head = (
        lax.broadcasted_iota(jnp.int32, (width, 128), 0) // 64
        == lax.broadcasted_iota(jnp.int32, (width, 128), 1)
    ).astype(F32)
    by_bucket = jnp.dot(hot, drow[...], preferred_element_type=F32, precision=lax.Precision.HIGHEST)
    small_ref[...] = jnp.zeros_like(small_ref)
    small_ref[24:, :] = jnp.dot(by_bucket, head, preferred_element_type=F32, precision=lax.Precision.HIGHEST)
    done = tiles + 2
    projs[64:, width : 2 * width] = dka[64:, :].astype(BF)
    projs[64:, 2 * width : 3 * width] = dva[64:, :].astype(BF)
    held_in[5].wait()
    left_t[...] = h1_ref[...].T
    for i in range(3):
        put(projs[64:, i * width : (i + 1) * width], 5 + i)
        step(done)
        step(done + 1)
        done += 2

    dgain[...] = jnp.zeros_like(dgain)
    parts = 5
    block = rows // parts
    wqkv_in.wait()
    held_in[6].wait()
    held_in[7].wait()

    def self_in(i, _):
        at = pl.ds(pl.multiple_of(i * block, block), block)
        held = pl.ds(pl.multiple_of(i * block + 64, 64), block)
        x0 = x0_ref[at, :].astype(F32)
        dx, part = rms_back(x0, rms(x0), gain_ref[0:1, :], dot_nt(projs[held, :], wbuf[...]))
        dgain[...] += part
        dx0 = dx1_ref[at, :] + dx
        top = dx0.astype(BF)
        both[at, :width] = top
        both[at, width:] = (dx0 - top.astype(F32)).astype(BF)
        step(done + i)

        @pl.when(i == 2)
        def _():
            enc_copy.start()

        return 0

    lax.fori_loop(0, parts, self_in, 0)
    done += parts

    for i, ref in enumerate((dgain, dg2_ref, dg3_ref)):
        for k in range(6):
            small_ref[6 * i + k : 6 * i + k + 1, :] = ref[0:1, k * 128 : (k + 1) * 128]

    def small_copy(k):
        src = small_ref if k == 0 else sm_in.at[k + 4]
        return remote(src, sm_in.at[k], sm_send.at[k], sm_recv.at[k], k)

    def small_sum(k):
        small_copy(k).wait()
        held = small_ref[...] if k == 0 else sm_in[k + 4]
        if k < 4:
            sm_in[k + 5] = held + sm_in[k]
            small_copy(k + 1).start()
        else:
            small_ref[...] = held + sm_in[k]

    small_copy(0).start()
    f_third.wait()
    f_copy(0).start()
    step(done)
    chunk = rows // 5
    for k in range(5):
        small_sum(k)
        hot_rows = (lax.broadcasted_iota(jnp.int32, (chunk, rows), 0) + k * chunk == src_ref[...]).astype(F32).astype(BF)
        d_ref[k * chunk : (k + 1) * chunk, :] = dot(hot_rows, both[:rows, :width]) + dot(hot_rows, both[:rows, width:])
        for i in range(2):
            step(done + 1 + 2 * k + i)
        f_copy(1 + k).start()

    def rest(t, _):
        step(t)
        return 0

    lax.fori_loop(done + 11, count + 10, rest, 0)

    def f_end(i, _):
        f_copy(i).wait()
        return 0

    lax.fori_loop(0, f_slices, f_end, 0)

    def w_end(i, _):
        w_copy(i).wait()
        return 0

    lax.fori_loop(0, f_slices, w_end, 0)
    enc_copy.wait()


def late(
    start, size, bucket, brow, proj, do, lse, h1, oself, dy1, src, x0, gain, dx1, wqkv, dg2, dg3,
    keep0, came0, keep1, came1, enc0, enc2, wkv, oc, dyc, h2, dq0, dq1, wpair, fkeep, fsend, scale,
):
    rows, width = do.shape
    nq = width // 256
    n = enc0.shape[0]
    step_rows, wide, tall = 16, width // 2, width // 16
    count = 8 * tall // step_rows
    any_spec = pl.BlockSpec(memory_space=pl.ANY)

    def buf(n):
        return pltpu.VMEM((count, n, step_rows, wide), BF)

    return pl.pallas_call(
        functools.partial(late_kernel, scale=scale),
        out_shape=(
            sds((rows, width), F32),
            sds((56, 128), F32),
            sds((count, 8, step_rows, wide), BF),
            sds((n, width), F32),
            sds((n, width), BF),
            sds((8, 2 * fkeep.shape[0], width), BF),
        ),
        in_specs=[VM, VM, SM, VM, any_spec, any_spec, VM]
        + [any_spec] * 3
        + [VM, any_spec, VM, any_spec]
        + [any_spec, VM, VM]
        + [any_spec] * 7
        + [VM] * 5
        + [any_spec, VM, any_spec],
        out_specs=(VM,) * 4 + (any_spec, any_spec),
        scratch_shapes=[
            pltpu.VMEM((rows + 64, 3 * width), BF),
            pltpu.VMEM((width, 3 * width), BF),
            pltpu.VMEM((2 * n, 2 * width), BF),
            pltpu.VMEM((n, 2 * width), BF),
            pltpu.VMEM((width, 2 * n), BF),
            pltpu.VMEM((n, width), BF),
            pltpu.VMEM((nq, WIN, 256), F32),
            pltpu.VMEM((rows + 64, width), F32),
            pltpu.VMEM((rows + 64, width), F32),
            pltpu.VMEM((nq, WIN, 256), F32),
            pltpu.VMEM((width, rows), BF),
            pltpu.VMEM((16, 8 * tall, wide), BF),
            pltpu.VMEM(brow.shape, F32),
            pltpu.VMEM((9, 56, 128), F32),
            pltpu.VMEM((1, width), F32),
            pltpu.VMEM(fkeep.shape, BF),
            pltpu.VMEM(fkeep.shape, BF),
            buf(16),
            buf(16),
            buf(8),
            buf(4),
            buf(2),
            buf(2),
        ]
        + [pltpu.VMEM(a.shape, a.dtype) for a in (do, h1, oself, dy1, x0, dx1, enc0, enc2)]
        + [
            pltpu.SemaphoreType.DMA((7, count)),
            pltpu.SemaphoreType.DMA((7, count)),
            pltpu.SemaphoreType.DMA((5,)),
            pltpu.SemaphoreType.DMA((5,)),
            pltpu.SemaphoreType.DMA,
            pltpu.SemaphoreType.DMA,
            pltpu.SemaphoreType.DMA((17,)),
            pltpu.SemaphoreType.DMA((17,)),
            pltpu.SemaphoreType.DMA((29,)),
        ],
        compiler_params=pltpu.CompilerParams(
            vmem_limit_bytes=63 << 20, collective_id=0, has_side_effects=True
        ),
        cost_estimate=pl.CostEstimate(flops=10**13, bytes_accessed=30 << 20, transcendentals=0),
        name="late",
    )(
        start, size, bucket, brow, proj, do, lse, h1, oself, dy1, src, x0, gain, dx1, wqkv, dg2, dg3,
        keep0, came0, keep1, came1, enc0, enc2, wkv, oc, dyc, h2, dq0, dq1, wpair, fkeep, fsend,
    )


def last_kernel(
    me_ref, small_ref, ffn_any, f_any, own_any, came_any,
    win_any, wout_any, co_any, cq_any, ckv_any, qkv_any, so_any, enc_any,
    g1_ref, g2_ref, g3_ref, rel_ref,
    ffn_ref, f_ref, own_ref, came_ref, win_ref, wout_ref, co_ref, cq_ref, ckv_ref, qkv_ref, so_ref, enc_ref, sem,
):
    def move(src, dst, k):
        return pltpu.make_async_copy(src, dst, sem.at[k])

    arriving = [
        move(a, b, i)
        for i, (a, b) in enumerate(
            ((ffn_any, ffn_ref), (own_any, own_ref), (came_any, came_ref), (f_any, f_ref))
        )
    ]
    outs = ((win_ref, win_any), (wout_ref, wout_any), (enc_ref, enc_any), (co_ref, co_any), (cq_ref, cq_any))
    outs = outs + ((so_ref, so_any), (ckv_ref, ckv_any), (qkv_ref, qkv_any))
    leaving = [move(a, b, 4 + i) for i, (a, b) in enumerate(outs)]
    for c in arriving:
        c.start()

    arriving[0].wait()
    half = ffn_ref.shape[1] // 2
    for slot in range(8):
        s = me_ref[1] ^ ((slot >> 2) + (slot & 2) + 4 * (slot & 1))
        rows = pl.ds(pl.multiple_of((s & 1) * half, half), half)
        cols = pl.ds(pl.multiple_of((s >> 1) * 768, 768), 768)
        win_ref[rows, cols] = ffn_ref[slot, :half].astype(F32)
        wout_ref[pl.ds(pl.multiple_of(s * half, half), half), :] = ffn_ref[slot, half:].astype(F32)
    leaving[0].start()
    leaving[1].start()
    arriving[1].wait()
    arriving[2].wait()
    enc_ref[...] = own_ref[...] + came_ref[...].astype(F32)
    leaving[2].start()
    arriving[3].wait()
    count, _, step_rows, wide = f_ref.shape
    width = 2 * wide
    places = (
        (co_ref, 0, 3), (cq_ref, 0, 4), (so_ref, 0, 5), (ckv_ref, 0, None), (ckv_ref, width, 6),
        (qkv_ref, 0, None), (qkv_ref, width, None), (qkv_ref, 2 * width, 7),
    )
    each = count // 8
    tall = each * step_rows
    for n, (out, col, done) in enumerate(places):
        for slot in range(8):
            s = me_ref[1] ^ ((slot >> 2) + (slot & 2) + 4 * (slot & 1))
            for k in range(each):
                at = pl.ds(pl.multiple_of((s >> 1) * tall + k * step_rows, step_rows), step_rows)
                cols = pl.ds(pl.multiple_of(col + (s & 1) * wide, 128), wide)
                out[at, cols] = f_ref[n * each + k, slot].astype(F32)
        if done is not None:
            leaving[done].start()
    quarter = g1_ref.shape[1]
    for i, ref in enumerate((g1_ref, g2_ref, g3_ref)):
        whole = jnp.concatenate([small_ref[6 * i + k : 6 * i + k + 1, :] for k in range(6)], axis=1)
        for j in range(4):

            @pl.when(me_ref[0] == j)
            def _():
                ref[...] = whole[:, j * quarter : (j + 1) * quarter]

    part, heads = rel_ref.shape
    rel_ref[...] = small_ref[pl.ds(pl.multiple_of(24 + me_ref[0] * part, 8), part), :heads]
    for c in leaving:
        c.wait()


def last(me, small, ffn, f, own, came, buckets, heads):
    width = own.shape[1]
    quarter = width // 4
    cols = lambda n: sds((quarter, n * width), F32)
    any_spec = pl.BlockSpec(memory_space=pl.ANY)
    big = (cols(4), sds((width, width), F32), cols(1), cols(1), cols(2), cols(3), cols(1), sds(own.shape, F32))
    held = (ffn, f, own, came) + big
    return call(
        last_kernel,
        "last",
        big
        + (sds((1, quarter), F32),) * 3
        + (sds((buckets // 4, heads), F32),),
        [SM, VM] + [any_spec] * 4,
        (any_spec,) * 8 + (VM,) * 4,
        [pltpu.VMEM(a.shape, a.dtype) for a in held] + [pltpu.SemaphoreType.DMA((12,))],
        (me, small, ffn, f, own, came),
        us=8,
    )


def hop(x, core=0, xb=0, yb=0, z1=0, z2=0):
    b, g = core | (xb << 1), yb | (z1 << 1) | (z2 << 2)
    groups, blocks = lax.axis_size("grp"), lax.axis_size("blk")
    pairs = [(i * blocks + j, (i ^ g) * blocks + (j ^ b)) for i in range(groups) for j in range(blocks)]
    return lax.ppermute(x, ("grp", "blk"), pairs)


def total(*parts):
    out = parts[0].astype(F32)
    for p in parts[1:]:
        out = out + p.astype(F32)
    return out.astype(BF)


def after(x, *deps):
    return lax.optimization_barrier((x,) + deps)[0]


def fused_body(
    dec_in,
    encodings,
    answer_len,
    answer_question,
    question_rows,
    bucket_table,
    gain_self,
    w_qkv,
    w_self_out,
    rel_bias,
    gain_cross,
    w_cross_q,
    w_cross_kv,
    w_cross_out,
    gain_ffn,
    w_in,
    w_out,
    cotangent,
):
    rows, width = dec_in.shape
    buckets, heads = rel_bias.shape
    scale = 1.0 / math.sqrt(width // heads)
    me_b, me_g = lax.axis_index("blk"), lax.axis_index("grp")
    me = jnp.stack([me_b, me_g]).astype(jnp.int32)
    row = lax.broadcasted_iota(jnp.int32, (3, width), 0)
    gains = jnp.where(row == 0, gain_self[None], jnp.where(row == 1, gain_cross[None], gain_ffn[None]))
    g1, g2, g3 = gains, gains, gains

    enc2 = hop(encodings, xb=1)
    enc1 = hop(encodings, core=1)
    src, cstart, csize, sstart, ssize, lo, hi, brow, x0, h1, proj, oself, lse_self = pre(
        me, answer_question, answer_len, question_rows, bucket_table, dec_in, g1, rel_bias, w_qkv, scale
    )
    enc2, oself = lax.optimization_barrier((enc2, oself))
    enc3 = hop(enc2, core=1)
    enc1 = after(enc1, x0)
    x1, h2, qc = mid(x0, oself, w_self_out, g2, w_cross_q, scale)
    k, v, kt, ocross, lse = kv_cross(
        me, lo, hi, cstart, csize, qc, (encodings, enc1, enc2, enc3), w_cross_kv
    )
    o_keep, o_send, w_keep, w_send, oc, layer_out, dx2, dyc, do, dgain3 = ffn(
        src, x1, ocross, g3, cotangent, w_cross_out, w_in, w_out
    )
    do, o_send, w_send = lax.optimization_barrier((do, o_send, w_send))
    o_came = hop(o_send, xb=1)
    w_came = hop(w_send, z1=1)
    dq0, keep0, send0 = cross_back(
        me, lo, hi, cstart, csize, qc, do, ocross, lse, k, v, kt, scale, 0, 2
    )
    came0 = hop(send0, core=1)
    o_came, w_came, dq0 = lax.optimization_barrier((o_came, w_came, dq0))
    o_q = [total(o_keep[2 * j : 2 * j + 2], o_came[2 * j : 2 * j + 2]) for j in range(4)]
    w_two = total(w_keep, w_came)
    do1, o_q[1], o_q[2], o_q[3], w_two = lax.optimization_barrier((do, o_q[1], o_q[2], o_q[3], w_two))
    oz, oy, oyz = hop(o_q[1], z1=1), hop(o_q[2], yb=1), hop(o_q[3], yb=1, z1=1)
    w_came = hop(w_two, z2=1)
    dq1, keep1, send1 = cross_back(
        me, lo, hi, cstart, csize, qc, do1, ocross, lse, k, v, kt, scale, 2, 1
    )
    came1 = hop(send1, core=1)
    oz, oy, oyz, w_came, dq1 = lax.optimization_barrier((oz, oy, oyz, w_came, dq1))
    dx1, dy1, dos, dgain2, w_pair, f_keep, f_send = cross_in(
        dq0, dq1, x1, dx2, g2, w_cross_q, w_self_out, o_q[0], oz, oy, oyz, w_two, w_came
    )
    came0, came1, dos = lax.optimization_barrier((came0, came1, dos))
    d_dec_in, small, gathered, enc_own, enc_came, f_all = late(
        sstart, ssize, bucket_table, brow, proj, dos, lse_self, h1, oself, dy1, src, x0, g1, dx1, w_qkv,
        dgain2, dgain3, keep0, came0, keep1, came1, encodings, enc2, w_cross_kv, oc, dyc, h2, dq0, dq1,
        w_pair, f_keep, f_send, scale,
    )
    (
        o_win, o_wout, o_wco, o_wcq, o_wckv, o_wqkv, o_wso, d_encodings, g_self, g_cross, g_ffn, g_rel,
    ) = last(me, small, f_all, gathered, enc_own, enc_came, buckets, heads)
    g_self, g_cross, g_ffn = (g.reshape(-1) for g in (g_self, g_cross, g_ffn))
    return (
        layer_out,
        d_dec_in,
        d_encodings,
        g_self,
        o_wqkv,
        o_wso,
        g_rel,
        g_cross,
        o_wcq,
        o_wckv,
        o_wco,
        g_ffn,
        o_win,
        o_wout,
    )


def solution(mesh):
    rows = P(("grp", "blk"), None)
    fused = mesh.shape["grp"] == 8 and mesh.shape["blk"] == 4
    return jax.shard_map(
        fused_body if fused else body,
        mesh=mesh,
        in_specs=(rows, rows, P(("grp", "blk")), P("grp"), P("grp", None)) + (P(),) * 12 + (rows,),
        out_specs=(rows, rows, rows, P("blk"))
        + (P("blk", None),) * 3
        + (P("blk"),)
        + (P("blk", None),) * 3
        + (P("blk"),)
        + (P("blk", None),) * 2,
        check_vma=False,
    )
```

```python
import functools
import math

import jax
import jax.numpy as jnp
from jax import lax
from jax.experimental import pallas as pl
from jax.experimental.pallas import tpu as pltpu
from jax.sharding import PartitionSpec as P

EPSILON = 1e-06
NEG = -1e30
MASKED = -1e9
TQ = 64
TK = 256
WIN = 128
F32 = jnp.float32
BF = jnp.bfloat16
VM = pl.BlockSpec(memory_space=pltpu.VMEM)
SM = pl.BlockSpec(memory_space=pltpu.SMEM)
LIMIT = 60 << 20


def dot(a, b):
    return jnp.dot(a, b, preferred_element_type=F32)


def dot_tn(a, b):
    return lax.dot_general(a, b, (((0,), (0,)), ((), ())), preferred_element_type=F32)


def dot_nt(a, b):
    return lax.dot_general(a, b, (((1,), (1,)), ((), ())), preferred_element_type=F32)


def stack4(t):
    lane = lax.broadcasted_iota(jnp.int32, t.shape, 1) // 64
    return jnp.concatenate([jnp.where(lane == a, t, jnp.zeros_like(t)) for a in range(4)], axis=0)


def unstack4(s):
    n = s.shape[0] // 4
    lane = lax.broadcasted_iota(jnp.int32, (n, 256), 1) // 64
    out = s[:n]
    for a in range(1, 4):
        out = jnp.where(lane == a, s[a * n : (a + 1) * n], out)
    return out


def range_mask(base, rows, start, size):
    idx = lax.broadcasted_iota(jnp.int32, (rows, start.shape[1]), 0)
    rel = idx - (start - base)
    return (rel >= 0) & (rel < size)


def red(x, op):
    return op(x.reshape(x.shape[0] // 8, 8, x.shape[1]), axis=0)


def cross_fwd_kernel(
    lo_ref, hi_ref, start_ref, size_ref, q_ref, k_ref, vt_ref, o_ref, lse_ref, qst, s_scr, m_scr, l_scr, acc, *, nq, tiles
):
    def tile(t, _):
        st = start_ref[t]
        sz = size_ref[t]
        lo = lo_ref[t]
        hi = hi_ref[t]
        row = pl.ds(pl.multiple_of(t * TQ, TQ), TQ)
        for c in range(nq):
            qst[c] = stack4(q_ref[row, c * 256 : (c + 1) * 256]).T
            m_scr[c] = jnp.full((8, 256), NEG, F32)
            l_scr[c] = jnp.zeros((8, 256), F32)
            acc[c] = jnp.zeros((256, 256), F32)

        def scores(j, _):
            kr = pl.ds(pl.multiple_of(j * TK, TK), TK)
            mask = range_mask(j * TK, TK, st, sz)
            for c in range(nq):
                s = dot(k_ref[kr, c * 256 : (c + 1) * 256], qst[c])
                s = jnp.where(mask, s, NEG)
                s_scr[c, kr, :] = s
                m_scr[c] = jnp.maximum(m_scr[c], red(s, jnp.max))
            return 0

        lax.fori_loop(lo, hi, scores, 0)
        for c in range(nq):
            m_scr[c] = jnp.broadcast_to(jnp.max(m_scr[c], axis=0, keepdims=True), (8, 256))

        def mix(j, _):
            kr = pl.ds(pl.multiple_of(j * TK, TK), TK)
            for c in range(nq):
                p = jnp.exp(s_scr[c, kr, :] - m_scr[c][0:1])
                l_scr[c] += red(p, jnp.sum)
                acc[c] += dot(vt_ref[c * 256 : (c + 1) * 256, kr], p.astype(BF))
            return 0

        lax.fori_loop(lo, hi, mix, 0)
        for c in range(nq):
            l = jnp.sum(l_scr[c], axis=0, keepdims=True)
            lse_ref[t, c] = m_scr[c][0:1] + jnp.log(l)
            o_ref[row, c * 256 : (c + 1) * 256] = unstack4((acc[c] * (1.0 / l)).T)
        return 0

    lax.fori_loop(0, tiles, tile, 0)


def quads_per_step(nq, keys):
    return nq if keys <= 2048 else 1


def cross_fwd(lo, hi, start, size, q, k, vt):
    rows, width = q.shape
    tiles, keys = rows // TQ, k.shape[0]
    nq = quads_per_step(width // 256, keys)
    full = pl.BlockSpec(start.shape, lambda g: (0, 0, 0))
    return pl.pallas_call(
        functools.partial(cross_fwd_kernel, nq=nq, tiles=tiles),
        grid=(width // 256 // nq,),
        out_shape=(
            jax.ShapeDtypeStruct(q.shape, F32),
            jax.ShapeDtypeStruct((tiles, width // 256, 1, 256), F32),
        ),
        in_specs=[
            SM,
            SM,
            full,
            full,
            pl.BlockSpec((rows, nq * 256), lambda g: (0, g)),
            pl.BlockSpec((keys, nq * 256), lambda g: (0, g)),
            pl.BlockSpec((nq * 256, keys), lambda g: (g, 0)),
        ],
        out_specs=(
            pl.BlockSpec((rows, nq * 256), lambda g: (0, g)),
            pl.BlockSpec((tiles, nq, 1, 256), lambda g: (0, g, 0, 0)),
        ),
        scratch_shapes=[
            pltpu.VMEM((nq, 256, 256), BF),
            pltpu.VMEM((nq, keys, 256), F32),
            pltpu.VMEM((nq, 8, 256), F32),
            pltpu.VMEM((nq, 8, 256), F32),
            pltpu.VMEM((nq, 256, 256), F32),
        ],
        compiler_params=pltpu.CompilerParams(vmem_limit_bytes=LIMIT),
        name="cross_fwd",
    )(lo, hi, start, size, q, k, vt)


def cross_bwd_kernel(
    lo_ref,
    hi_ref,
    start_ref,
    size_ref,
    q_ref,
    do_ref,
    o_ref,
    lse_ref,
    k_ref,
    v_ref,
    kt_ref,
    dq_ref,
    dk_ref,
    dv_ref,
    qs,
    qst,
    dos,
    dost,
    del_scr,
    dka,
    dva,
    dqt,
    *,
    nq,
    tiles,
    scale,
):
    dka[...] = jnp.zeros_like(dka)
    dva[...] = jnp.zeros_like(dva)

    def tile(t, _):
        st = start_ref[t]
        sz = size_ref[t]
        row = pl.ds(pl.multiple_of(t * TQ, TQ), TQ)
        for c in range(nq):
            cs = slice(c * 256, (c + 1) * 256)
            a = stack4(q_ref[row, cs])
            qs[c] = a
            qst[c] = a.T
            b = stack4(do_ref[row, cs])
            dos[c] = b
            dost[c] = b.T
            product = do_ref[row, cs].astype(F32) * o_ref[row, cs]
            total = jnp.sum(red(stack4(product).T, jnp.sum), axis=0, keepdims=True)
            del_scr[c] = jnp.broadcast_to(total, (8, 256))
            dqt[c] = jnp.zeros((256, 256), F32)

        def step(j, _):
            kr = pl.ds(pl.multiple_of(j * TK, TK), TK)
            mask = range_mask(j * TK, TK, st, sz)
            for c in range(nq):
                cs = slice(c * 256, (c + 1) * 256)
                s = dot(k_ref[kr, cs], qst[c])
                p = jnp.where(mask, jnp.exp(s - lse_ref[t, c]), 0.0)
                dp = dot(v_ref[kr, cs], dost[c])
                ds = (p * (dp - del_scr[c][0:1])).astype(BF)
                dva[kr, cs] += dot(p.astype(BF), dos[c])
                dka[kr, cs] += dot(ds, qs[c])
                dqt[c] += dot(kt_ref[cs, kr], ds)
            return 0

        lax.fori_loop(lo_ref[t], hi_ref[t], step, 0)
        for c in range(nq):
            cs = slice(c * 256, (c + 1) * 256)
            dq_ref[row, cs] = (unstack4(dqt[c].T) * scale).astype(BF)
        return 0

    lax.fori_loop(0, tiles, tile, 0)
    dk_ref[...] = dka[...].astype(BF)
    dv_ref[...] = dva[...].astype(BF)


def cross_bwd(lo, hi, start, size, q, do, o, lse, k, v, kt, scale):
    rows, width = q.shape
    tiles, keys = rows // TQ, k.shape[0]
    nq = quads_per_step(width // 256, keys)
    full = pl.BlockSpec(start.shape, lambda g: (0, 0, 0))
    own = pl.BlockSpec((rows, nq * 256), lambda g: (0, g))
    held = pl.BlockSpec((keys, nq * 256), lambda g: (0, g), pipeline_mode=pl.Buffered(1))
    out_kv = pl.BlockSpec((keys, nq * 256), lambda g: (0, g), pipeline_mode=pl.Buffered(1))
    return pl.pallas_call(
        functools.partial(cross_bwd_kernel, nq=nq, tiles=tiles, scale=scale),
        grid=(width // 256 // nq,),
        out_shape=(
            jax.ShapeDtypeStruct(q.shape, BF),
            jax.ShapeDtypeStruct(k.shape, BF),
            jax.ShapeDtypeStruct(k.shape, BF),
        ),
        in_specs=[
            SM,
            SM,
            full,
            full,
            own,
            own,
            own,
            pl.BlockSpec((tiles, nq, 1, 256), lambda g: (0, g, 0, 0)),
            held,
            held,
            pl.BlockSpec((nq * 256, keys), lambda g: (g, 0), pipeline_mode=pl.Buffered(1)),
        ],
        out_specs=(own, out_kv, out_kv),
        scratch_shapes=[pltpu.VMEM((nq, 256, 256), BF)] * 4
        + [
            pltpu.VMEM((nq, 8, 256), F32),
            pltpu.VMEM((keys, nq * 256), F32),
            pltpu.VMEM((keys, nq * 256), F32),
            pltpu.VMEM((nq, 256, 256), F32),
        ],
        compiler_params=pltpu.CompilerParams(vmem_limit_bytes=LIMIT),
        name="cross_bwd",
    )(lo, hi, start, size, q, do, o, lse, k, v, kt)


def distances():
    j = lax.broadcasted_iota(jnp.int32, (WIN, 256), 0)
    i = lax.broadcasted_iota(jnp.int32, (WIN, 256), 1) % 64
    return WIN - TQ + i - j


def fill_window(proj_ref, kp, vp, width):
    kp[0:64, :] = jnp.zeros((64, width), BF)
    vp[0:64, :] = jnp.zeros((64, width), BF)
    kp[64:, :] = proj_ref[:, width : 2 * width]
    vp[64:, :] = proj_ref[:, 2 * width : 3 * width]


def fill_bias(brow_ref, bias, nq):
    dist = distances()
    for c in range(nq):
        cs = slice(c * 256, (c + 1) * 256)

        def add(d, held):
            return jnp.where(dist == d, brow_ref[pl.ds(d, 1), cs], held)

        bias[c] = lax.fori_loop(0, brow_ref.shape[0], add, jnp.full((WIN, 256), MASKED, F32))


def self_fwd_kernel(start_ref, size_ref, brow_ref, proj_ref, o_ref, lse_ref, kp, vp, bias, *, nq, tiles, scale):
    width = nq * 256
    fill_window(proj_ref, kp, vp, width)
    fill_bias(brow_ref, bias, nq)

    def tile(t, _):
        row = pl.ds(pl.multiple_of(t * TQ, TQ), TQ)
        win = pl.ds(pl.multiple_of(t * TQ, TQ), WIN)
        mask = range_mask(t * TQ - 64, WIN, start_ref[t], size_ref[t])
        for c in range(nq):
            cs = slice(c * 256, (c + 1) * 256)
            qst = stack4(proj_ref[row, cs] * jnp.asarray(scale, BF)).T
            s = jnp.where(mask, dot(kp[win, cs], qst) + bias[c], MASKED)
            m = jnp.max(red(s, jnp.max), axis=0, keepdims=True)
            p = jnp.exp(s - m)
            l = jnp.sum(red(p, jnp.sum), axis=0, keepdims=True)
            p = (p * (1.0 / l)).astype(BF)
            o_ref[row, cs] = unstack4(dot_tn(p, vp[win, cs])).astype(BF)
            lse_ref[t, c] = m + jnp.log(l)
        return 0

    lax.fori_loop(0, tiles, tile, 0)


def self_fwd(start, size, brow, proj, scale):
    rows, width = proj.shape[0], proj.shape[1] // 3
    nq, tiles = width // 256, rows // TQ
    return pl.pallas_call(
        functools.partial(self_fwd_kernel, nq=nq, tiles=tiles, scale=scale),
        out_shape=(
            jax.ShapeDtypeStruct((rows, width), BF),
            jax.ShapeDtypeStruct((tiles, nq, 1, 256), F32),
        ),
        in_specs=[VM] * 4,
        out_specs=(VM, VM),
        scratch_shapes=[
            pltpu.VMEM((rows + 64, width), BF),
            pltpu.VMEM((rows + 64, width), BF),
            pltpu.VMEM((nq, WIN, 256), F32),
        ],
        compiler_params=pltpu.CompilerParams(vmem_limit_bytes=LIMIT),
        name="self_fwd",
    )(start, size, brow, proj)


def self_bwd_kernel(
    start_ref,
    size_ref,
    brow_ref,
    proj_ref,
    do_ref,
    lse_ref,
    dproj_ref,
    dbrow_ref,
    kp,
    vp,
    bias,
    dka,
    dva,
    dsum,
    *,
    nq,
    tiles,
    scale,
):
    width = nq * 256
    fill_window(proj_ref, kp, vp, width)
    fill_bias(brow_ref, bias, nq)
    dka[...] = jnp.zeros_like(dka)
    dva[...] = jnp.zeros_like(dva)
    dsum[...] = jnp.zeros_like(dsum)

    def tile(t, _):
        row = pl.ds(pl.multiple_of(t * TQ, TQ), TQ)
        win = pl.ds(pl.multiple_of(t * TQ, TQ), WIN)
        mask = range_mask(t * TQ - 64, WIN, start_ref[t], size_ref[t])
        for c in range(nq):
            cs = slice(c * 256, (c + 1) * 256)
            qs = stack4(proj_ref[row, cs] * jnp.asarray(scale, BF))
            dos = stack4(do_ref[row, cs])
            s = dot(kp[win, cs], qs.T) + bias[c]
            p = jnp.where(mask, jnp.exp(s - lse_ref[t, c]), 0.0)
            dp = dot(vp[win, cs], dos.T)
            delta = jnp.sum(red(p * dp, jnp.sum), axis=0, keepdims=True)
            ds = p * (dp - delta)
            dsum[c] += ds
            ds = ds.astype(BF)
            dva[win, cs] += dot(p.astype(BF), dos)
            dka[win, cs] += dot(ds, qs)
            dproj_ref[row, cs] = (unstack4(dot_tn(ds, kp[win, cs])) * scale).astype(BF)
        return 0

    lax.fori_loop(0, tiles, tile, 0)
    dproj_ref[:, width : 2 * width] = dka[64:, :].astype(BF)
    dproj_ref[:, 2 * width : 3 * width] = dva[64:, :].astype(BF)
    dist = distances()
    for c in range(nq):
        cs = slice(c * 256, (c + 1) * 256)

        def one(d, _):
            x = jnp.where(dist == d, dsum[c], 0.0)
            dbrow_ref[pl.ds(d, 1), cs] = jnp.sum(red(x, jnp.sum), axis=0, keepdims=True)
            return 0

        lax.fori_loop(0, brow_ref.shape[0], one, 0)


def self_bwd(start, size, brow, proj, do, lse, scale):
    rows, width = proj.shape[0], proj.shape[1] // 3
    nq, tiles = width // 256, rows // TQ
    return pl.pallas_call(
        functools.partial(self_bwd_kernel, nq=nq, tiles=tiles, scale=scale),
        out_shape=(jax.ShapeDtypeStruct((rows, 3 * width), BF), jax.ShapeDtypeStruct(brow.shape, F32)),
        in_specs=[VM] * 6,
        out_specs=(VM, VM),
        scratch_shapes=[
            pltpu.VMEM((rows + 64, width), BF),
            pltpu.VMEM((rows + 64, width), BF),
            pltpu.VMEM((nq, WIN, 256), F32),
            pltpu.VMEM((rows + 64, width), F32),
            pltpu.VMEM((rows + 64, width), F32),
            pltpu.VMEM((nq, WIN, 256), F32),
        ],
        compiler_params=pltpu.CompilerParams(vmem_limit_bytes=LIMIT),
        name="self_bwd",
    )(start, size, brow, proj, do, lse)


def norm_rows(x, gain):
    inverse = lax.rsqrt(jnp.mean(x * x, axis=-1, keepdims=True) + EPSILON)
    return x * inverse * gain, inverse


def norm_back(x, inverse, gain, grad):
    scaled = grad * gain
    mean = jnp.mean(x * scaled, axis=-1, keepdims=True)
    return inverse * scaled - x * inverse * inverse * inverse * mean, jnp.sum(grad * x * inverse, axis=0)


def swap(x, axis, bit):
    size = lax.axis_size(axis)
    return lax.ppermute(x, axis, [(i, i ^ bit) for i in range(size)])


def bits_of(axis):
    size = lax.axis_size(axis)
    return [1 << b for b in range(size.bit_length() - 1)]


def gather_parts(x, axis):
    parts = {0: x}
    for bit in reversed(bits_of(axis)):
        for r in list(parts):
            parts[r ^ bit] = swap(parts[r], axis, bit)
    return parts


def add_low(a, b):
    return (a.astype(F32) + b.astype(F32)).astype(BF)


def scatter_sum(x, axis, order):
    size = x.shape[0]
    live = list(range(size))
    block = x
    for bit in order:
        keep = [r for r in live if not r & bit]
        send = [r for r in live if r & bit]
        k = jnp.stack([block[live.index(r)] for r in keep])
        s = jnp.stack([block[live.index(r)] for r in send])
        block = add_low(k, swap(s, axis, bit))
        live = keep
    return block[0]


def gather_sum(x, axis, order):
    parts = [0]
    block = x[None]
    for bit in order:
        block = jnp.concatenate([block, swap(block, axis, bit)], axis=0)
        parts = parts + [r ^ bit for r in parts]
    inverse = [parts.index(r) for r in range(len(parts))]
    return block, inverse


def relative(x, axis):
    size = lax.axis_size(axis)
    me = lax.axis_index(axis)
    return jnp.stack([lax.dynamic_index_in_dim(x, me ^ r, 0, keepdims=False) for r in range(size)])


def reduce_all(x):
    blocks, rows, width = x.shape
    groups = lax.axis_size("grp")
    part = scatter_sum(relative(x, "blk"), "blk", bits_of("blk"))
    part = relative(part.reshape(groups, rows // groups, width), "grp")
    part = scatter_sum(part, "grp", bits_of("grp"))
    whole, inverse = gather_sum(part, "grp", list(reversed(bits_of("grp"))))
    me = lax.axis_index("grp")
    index = jnp.asarray(inverse, jnp.int32)[jnp.arange(groups) ^ me]
    return jnp.take(whole, index, axis=0).reshape(rows, width)


def sum_everywhere(x):
    for axis in ("blk", "grp"):
        for bit in bits_of(axis):
            x = x + swap(x, axis, bit)
    return x


def pack(grads, blocks):
    out = []
    for g in grads:
        k, n = g.shape
        r = g.reshape(blocks, k // blocks, n // 768, 768).transpose(0, 2, 1, 3)
        out.append(r.reshape(blocks, -1, 768))
    return jnp.concatenate(out, axis=1)


def unpack(rows, shapes, blocks):
    out, at = [], 0
    for k, n in shapes:
        count = k // blocks * (n // 768)
        piece = rows[at : at + count].reshape(n // 768, k // blocks, 768)
        out.append(piece.transpose(1, 0, 2).reshape(k // blocks, n).astype(F32))
        at += count
    return out


def body(
    dec_in,
    encodings,
    answer_len,
    answer_question,
    question_rows,
    bucket_table,
    gain_self,
    w_qkv,
    w_self_out,
    rel_bias,
    gain_cross,
    w_cross_q,
    w_cross_kv,
    w_cross_out,
    gain_ffn,
    w_in,
    w_out,
    cotangent,
):
    answers = answer_len.shape[0]
    length = bucket_table.shape[0]
    rows, width = dec_in.shape
    heads = rel_bias.shape[1]
    buckets = rel_bias.shape[0]
    scale = 1.0 / math.sqrt(width // heads)
    enc_rows = encodings.shape[0]
    blocks = lax.axis_size("blk")
    me = lax.axis_index("blk")
    tiles = rows // TQ
    nq = width // 256

    enc_parts = gather_parts(encodings, "blk")

    own_q = lax.dynamic_slice_in_dim(answer_question, me * answers, answers, 0)
    a_index = jnp.arange(answers)
    before = (own_q[None, :] < own_q[:, None]) | (
        (own_q[None, :] == own_q[:, None]) & (a_index[None, :] < a_index[:, None])
    )
    rank = jnp.sum(before.astype(jnp.int32), axis=1)
    target = (rank[:, None] * length + jnp.arange(length)[None, :]).reshape(rows)
    forward_perm = (jnp.arange(rows)[:, None] == target[None, :]).astype(BF)
    sorted_len = jnp.sum(jnp.where(rank[:, None] == a_index[None, :], answer_len[:, None], 0), axis=0)
    ends_q = jnp.cumsum(question_rows[0])
    starts_q = ends_q - question_rows[0]
    sorted_q = jnp.sum(jnp.where(rank[:, None] == a_index[None, :], own_q[:, None], 0), axis=0)
    token_q = jnp.repeat(sorted_q, length)
    pick = token_q[:, None] == jnp.arange(question_rows.shape[1])[None, :]
    token_start = jnp.sum(jnp.where(pick, starts_q[None, :], 0), axis=1)
    token_size = jnp.sum(jnp.where(pick, question_rows[0][None, :], 0), axis=1)

    def stacked(v):
        return jnp.tile(v.reshape(tiles, 1, TQ), (1, 1, 4)).astype(jnp.int32)

    c_start, c_size = stacked(token_start), stacked(token_size)
    lo = (token_start.reshape(tiles, TQ)[:, 0] // TK).astype(jnp.int32)
    hi = ((token_start + token_size).reshape(tiles, TQ)[:, -1] + TK - 1) // TK
    hi = hi.astype(jnp.int32)
    s_start = stacked(jnp.arange(rows) // length * length)
    s_size = stacked(jnp.repeat(sorted_len, length))

    bucket_hot = (bucket_table[:, None] == jnp.arange(buckets)[None, :]).astype(F32)
    brow = jnp.repeat(
        jnp.dot(bucket_hot, rel_bias, precision=lax.Precision.HIGHEST), width // heads, axis=1
    )

    x0 = dot(forward_perm, dec_in)
    grad_top = dot(forward_perm, cotangent)
    grad_low = grad_top.astype(BF)
    n1, r1 = norm_rows(x0, gain_self)
    h1 = n1.astype(BF)
    proj = dot(h1, w_qkv).astype(BF)
    o_self, lse_self = self_fwd(s_start, s_size, brow, proj, scale)
    x1 = x0 + dot(o_self, w_self_out)
    n2, r2 = norm_rows(x1, gain_cross)
    h2 = n2.astype(BF)
    qc = (dot(h2, w_cross_q).astype(BF) * jnp.asarray(scale, BF)).astype(BF)

    enc_rel = jnp.stack([enc_parts[r] for r in range(blocks)])
    enc_all = relative(enc_rel, "blk").reshape(blocks * enc_rows, width)
    kv = dot(enc_all, w_cross_kv).astype(BF)
    k_all, v_all = kv[:, :width], kv[:, width:]
    kvt = lax.dot_general(w_cross_kv, enc_all, (((0,), (1,)), ((), ())), preferred_element_type=F32).astype(BF)
    kt_all, vt_all = kvt[:width], kvt[width:]

    o_cross, lse_cross = cross_fwd(lo, hi, c_start, c_size, qc, k_all, vt_all)
    oc = o_cross.astype(BF)
    x2 = x1 + dot(oc, w_cross_out)
    n3, r3 = norm_rows(x2, gain_ffn)
    h3 = n3.astype(BF)
    hidden, gelu_back = jax.vjp(jax.nn.gelu, dot(h3, w_in))
    u = hidden.astype(BF)
    out = (x2 + dot(u, w_out)).astype(BF)
    layer_out = dot_tn(forward_perm, out).astype(BF)

    d_w_out = dot_tn(u, grad_low).astype(BF)
    da = gelu_back(dot_nt(grad_low, w_out))[0].astype(BF)
    d_w_in = dot_tn(h3, da).astype(BF)
    sums_out = reduce_all(pack([d_w_out], blocks))
    sums_in = reduce_all(pack([d_w_in], blocks))
    dx3, d_gain_ffn = norm_back(x2, r3, gain_ffn, dot_nt(da, w_in))
    dx2 = grad_top + dx3
    dyc = dx2.astype(BF)
    d_w_cross_out = dot_tn(oc, dyc).astype(BF)
    d_o = dot_nt(dyc, w_cross_out).astype(BF)
    dqc, dk, dv = cross_bwd(
        lo, hi, c_start, c_size, qc, d_o, o_cross, lse_cross, k_all, v_all, kt_all, scale
    )

    dkv = jnp.concatenate([dk, dv], axis=1).reshape(blocks, enc_rows, 2 * width)
    dkv = relative(dkv, "blk")
    dkv = add_low(dkv[0::2], swap(dkv[1::2], "blk", 1))
    enc_half = enc_rel[0::2]
    dkv_flat = dkv.reshape(-1, 2 * width)
    d_w_cross_kv = dot_tn(enc_half.reshape(-1, width), dkv_flat).astype(BF)
    d_enc = dot_nt(dkv_flat, w_cross_kv).reshape(blocks // 2, enc_rows, width)
    d_enc_parts = {2 * r: d_enc[r] for r in range(blocks // 2)}
    for bit in reversed(bits_of("blk")[1:]):
        for r in [r for r in d_enc_parts if r & bit]:
            came = swap(d_enc_parts.pop(r).astype(BF), "blk", bit)
            d_enc_parts[r ^ bit] = d_enc_parts[r ^ bit] + came.astype(F32)
    d_encodings = d_enc_parts[0]

    d_w_cross_q = dot_tn(h2, dqc).astype(BF)
    sums_cross = reduce_all(pack([d_w_cross_out, d_w_cross_q, d_w_cross_kv], blocks))
    dx_two, d_gain_cross = norm_back(x1, r2, gain_cross, dot_nt(dqc, w_cross_q))
    dx1 = dx2 + dx_two
    dy1 = dx1.astype(BF)
    d_w_self_out = dot_tn(o_self, dy1).astype(BF)
    d_os = dot_nt(dy1, w_self_out).astype(BF)
    dproj, dbrow = self_bwd(s_start, s_size, brow, proj, d_os, lse_self, scale)
    d_w_qkv = dot_tn(h1, dproj).astype(BF)
    sums_self = reduce_all(pack([d_w_qkv, d_w_self_out], blocks))
    dx_one, d_gain_self = norm_back(x0, r1, gain_self, dot_nt(dproj, w_qkv))
    d_rel = jnp.dot(
        bucket_hot.T, jnp.sum(dbrow.reshape(length, heads, -1), axis=2), precision=lax.Precision.HIGHEST
    )
    d_x0 = dx1 + dx_one
    high = d_x0.astype(BF)
    low = (d_x0 - high.astype(F32)).astype(BF)
    d_dec_in = dot_tn(forward_perm, high) + dot_tn(forward_perm, low)

    small = jnp.concatenate([d_gain_self, d_gain_cross, d_gain_ffn, d_rel.reshape(-1)])
    small = sum_everywhere(small.reshape(-1, 128)).reshape(-1)

    def own(v):
        return lax.dynamic_slice_in_dim(v, me * (v.shape[0] // blocks), v.shape[0] // blocks, 0)

    g_self, g_cross, g_ffn = (own(small[i * width : (i + 1) * width]) for i in range(3))
    g_rel = own(small[3 * width :].reshape(buckets, heads))
    (o_wout,) = unpack(sums_out, [w_out.shape], blocks)
    (o_win,) = unpack(sums_in, [w_in.shape], blocks)
    o_wco, o_wcq, o_wckv = unpack(sums_cross, [w_cross_out.shape, w_cross_q.shape, w_cross_kv.shape], blocks)
    o_wqkv, o_wso = unpack(sums_self, [w_qkv.shape, w_self_out.shape], blocks)
    return (
        layer_out,
        d_dec_in,
        d_encodings,
        g_self,
        o_wqkv,
        o_wso,
        g_rel,
        g_cross,
        o_wcq,
        o_wckv,
        o_wco,
        g_ffn,
        o_win,
        o_wout,
    )


def slot_of(rel):
    return (rel & 1) * 4 + (rel & 2) + ((rel >> 2) & 1)


def fill_bias_all(brow_ref, bias, nq):
    dist = distances()

    def add(d, held):
        here = dist == d
        row = pl.ds(d, 1)
        return tuple(jnp.where(here, brow_ref[row, c * 256 : (c + 1) * 256], held[c]) for c in range(nq))

    held = lax.fori_loop(0, brow_ref.shape[0], add, (jnp.full((WIN, 256), MASKED, F32),) * nq)
    for c in range(nq):
        bias[c] = held[c]


def gelu_both(a):
    c = math.sqrt(2.0 / math.pi)
    a2 = a * a
    t = jnp.tanh(c * (a + 0.044715 * (a2 * a)))
    half = 0.5 * (1.0 + t)
    return a * half, half + 0.5 * a * (1.0 - t * t) * (c * (1.0 + 3.0 * 0.044715 * a2))


def rms(x):
    return lax.rsqrt(jnp.mean(x * x, axis=-1, keepdims=True) + EPSILON)


def rms_back(x, inverse, gain, grad):
    scaled = grad * gain
    mean = jnp.mean(x * scaled, axis=-1, keepdims=True)
    unit = x * inverse
    return inverse * (scaled - unit * (inverse * mean)), jnp.sum(grad * unit, axis=0, keepdims=True)


def onehot_rows(src):
    n = src.shape[1]
    return (lax.broadcasted_iota(jnp.int32, (n, n), 0) == src).astype(F32).astype(BF)


def pre_kernel(
    me_ref,
    aq_ref,
    len_ref,
    qrows_ref,
    bucket_ref,
    dec_ref,
    gain1_ref,
    rel_ref,
    wqkv_ref,
    src_ref,
    cstart_ref,
    csize_ref,
    sstart_ref,
    ssize_ref,
    lo_ref,
    hi_ref,
    brow_ref,
    x0_ref,
    h1_ref,
    proj_ref,
    oself_ref,
    lse_ref,
    order,
    qstart,
    qcount,
    place,
    wide,
    kp,
    vp,
    bias,
    *,
    answers,
    length,
    questions,
    scale,
):
    rows, width = dec_ref.shape
    nq, tiles = width // 256, rows // TQ
    base = me_ref[0] * answers
    own = [aq_ref[base + a] for a in range(answers)]
    n = jnp.int32(0)
    first_row = jnp.int32(0)
    for c in range(questions):
        qstart[c] = first_row
        first_row = first_row + qrows_ref[0, c]
        qcount[c] = n
        place[c] = n
        for q in own:
            n = n + (q == c).astype(jnp.int32)
    for a, q in enumerate(own):
        at = place[q]
        order[at] = a
        place[q] = at + 1

    def answer_of(tok):
        ans = jnp.zeros_like(tok)
        for k in range(1, answers):
            ans = ans + (tok >= k * length).astype(jnp.int32)
        return ans

    tok = lax.broadcasted_iota(jnp.int32, (1, rows), 1)
    ans = answer_of(tok)
    src = tok - ans * length
    for k in range(answers):
        src = src + jnp.where(ans == k, order[k] * length, 0)
    src_ref[...] = src

    lane = lax.broadcasted_iota(jnp.int32, (tiles, 256), 1) % TQ
    tok = lane + TQ * lax.broadcasted_iota(jnp.int32, (tiles, 256), 0)
    ans = answer_of(tok)
    sstart_ref[...] = ans * length
    size = jnp.zeros_like(ans)
    for k in range(answers):
        size = size + jnp.where(ans == k, len_ref[order[k]], 0)
    ssize_ref[...] = size
    cstart = jnp.zeros_like(ans)
    csize = jnp.zeros_like(ans) + qrows_ref[0, 0]
    for c in range(1, questions):
        here = ans >= qcount[c]
        cstart = jnp.where(here, qstart[c], cstart)
        csize = jnp.where(here, qrows_ref[0, c], csize)
    cstart_ref[...] = cstart
    csize_ref[...] = csize
    for t in range(tiles):
        q_first = aq_ref[base + order[t * TQ // length]]
        q_last = aq_ref[base + order[(t * TQ + TQ - 1) // length]]
        lo_ref[t] = qstart[q_first] // TK
        hi_ref[t] = (qstart[q_last] + qrows_ref[0, q_last] + TK - 1) // TK

    for c in range(nq):
        head = lax.broadcasted_iota(jnp.int32, (rel_ref.shape[0], 256), 1) // 64
        held = jnp.zeros((rel_ref.shape[0], 256), F32)
        for a in range(4):
            h = c * 4 + a
            held = jnp.where(head == a, rel_ref[:, h : h + 1], held)
        wide[:, c * 256 : (c + 1) * 256] = held
    for d in range(length):
        brow_ref[d : d + 1, :] = wide[pl.ds(bucket_ref[d], 1), :]

    x0 = dot_tn(onehot_rows(src), dec_ref[...])
    x0_ref[...] = x0.astype(BF)
    h1_ref[...] = (x0 * rms(x0) * gain1_ref[0:1, :]).astype(BF)
    for i in range(3):
        cs = slice(i * width, (i + 1) * width)
        proj_ref[:, cs] = dot(h1_ref[...], wqkv_ref[:, cs]).astype(BF)
    fill_window(proj_ref, kp, vp, width)
    fill_bias_all(brow_ref, bias, nq)

    def scores(t, c):
        row = pl.ds(pl.multiple_of(t * TQ, TQ), TQ)
        win = pl.ds(pl.multiple_of(t * TQ, TQ), WIN)
        cs = slice(c * 256, (c + 1) * 256)
        qs = stack4(proj_ref[row, cs] * jnp.asarray(scale, BF))
        return dot_nt(kp[win, cs], qs) + bias[c]

    def probs(t, c, s):
        mask = range_mask(t * TQ - 64, WIN, sstart_ref[pl.ds(t, 1), :], ssize_ref[pl.ds(t, 1), :])
        s = jnp.where(mask, s, MASKED)
        m = jnp.max(red(s, jnp.max), axis=0, keepdims=True)
        p = jnp.exp(s - m)
        l = jnp.sum(red(p, jnp.sum), axis=0, keepdims=True)
        lse_ref[t, c] = m + jnp.log(l)
        return (p * (1.0 / l)).astype(BF)

    def mix(t, c, p):
        row = pl.ds(pl.multiple_of(t * TQ, TQ), TQ)
        win = pl.ds(pl.multiple_of(t * TQ, TQ), WIN)
        cs = slice(c * 256, (c + 1) * 256)
        oself_ref[row, cs] = unstack4(dot_tn(p, vp[win, cs])).astype(BF)

    def two_tiles(i, _):
        work = [(2 * i + k, c) for k in range(2) for c in range(nq)]
        s = [scores(t, c) for t, c in work]
        p = [probs(t, c, x) for (t, c), x in zip(work, s)]
        for (t, c), x in zip(work, p):
            mix(t, c, x)
        return 0

    lax.fori_loop(0, tiles // 2, two_tiles, 0)


def mid_kernel(x0_ref, oself_ref, wso_ref, gain2_ref, wcq_ref, x1_ref, h2_ref, qc_ref, *, scale):
    x1 = x0_ref[...].astype(F32) + dot(oself_ref[...], wso_ref[...])
    x1_ref[...] = x1
    h2_ref[...] = (x1 * rms(x1) * gain2_ref[1:2, :]).astype(BF)
    qc_ref[...] = dot(h2_ref[...], wcq_ref[...]).astype(BF) * jnp.asarray(scale, BF)


def mid(x0, oself, wso, gain, wcq, scale):
    rows, width = x0.shape
    return call(
        functools.partial(mid_kernel, scale=scale),
        "mid",
        (sds((rows, width), F32), sds((rows, width), BF), sds((rows, width), BF)),
        [VM] * 5,
        (VM,) * 3,
        [],
        (x0, oself, wso, gain, wcq),
        us=8,
    )


def call(kernel, name, out_shape, in_specs, out_specs, scratch, args, us):
    moved = sum(math.prod(a.shape) * a.dtype.itemsize for a in args)
    moved += sum(math.prod(a.shape) * a.dtype.itemsize for a in out_shape)
    return pl.pallas_call(
        kernel,
        out_shape=out_shape,
        in_specs=in_specs,
        out_specs=out_specs,
        scratch_shapes=scratch,
        compiler_params=pltpu.CompilerParams(vmem_limit_bytes=LIMIT),
        cost_estimate=pl.CostEstimate(flops=int(us * 1e11), bytes_accessed=moved, transcendentals=0),
        name=name,
    )(*args)


def sds(shape, dtype):
    return jax.ShapeDtypeStruct(shape, dtype)


def pre(me, aq, lens, qrows, bucket, dec, g1, rel, wqkv, scale):
    rows, width = dec.shape
    tiles, nq, length = rows // TQ, width // 256, bucket.shape[0]
    i32 = jnp.int32
    meta = sds((tiles, 256), i32)
    out = (
        sds((1, rows), i32),
        meta,
        meta,
        meta,
        meta,
        sds((tiles,), i32),
        sds((tiles,), i32),
        sds((length, width), F32),
        sds((rows, width), BF),
        sds((rows, width), BF),
        sds((rows, 3 * width), BF),
        sds((rows, width), BF),
        sds((tiles, nq, 1, 256), F32),
    )
    return call(
        functools.partial(
            pre_kernel, answers=lens.shape[0], length=length, questions=qrows.shape[1], scale=scale
        ),
        "pre",
        out,
        [SM] * 5 + [VM] * 4,
        (VM,) * 5 + (SM, SM) + (VM,) * 6,
        [
            pltpu.SMEM((lens.shape[0],), i32),
            pltpu.SMEM((qrows.shape[1],), i32),
            pltpu.SMEM((qrows.shape[1],), i32),
            pltpu.SMEM((qrows.shape[1],), i32),
            pltpu.VMEM((rel.shape[0], width), F32),
            pltpu.VMEM((rows + 64, width), BF),
            pltpu.VMEM((rows + 64, width), BF),
            pltpu.VMEM((nq, WIN, 256), F32),
        ],
        (me, aq, lens, qrows, bucket, dec, g1, rel, wqkv),
        us=40,
    )


def own_heads(x):
    return jnp.concatenate([x[a * 64 : (a + 1) * 64, a * TQ : (a + 1) * TQ] for a in range(4)], axis=0)


def in_pairs(lo, hi, work):
    def two(i, _):
        work(lo + 2 * i)
        work(lo + 2 * i + 1)
        return 0

    lax.fori_loop(0, (hi - lo) // 2, two, 0)

    @pl.when((hi - lo) % 2 == 1)
    def _():
        work(hi - 1)


def kv_cross_kernel(
    me_ref,
    lo_ref,
    hi_ref,
    start_ref,
    size_ref,
    q_ref,
    *rest,
    pieces,
):
    enc = rest[:pieces]
    wkv_ref, k_any, v_any, kt_any, o_ref, lse_ref, vt, k_ref, v_ref, kt_ref, out_sem, qst, s_scr, m_scr, l_scr, acc = rest[
        pieces:
    ]
    rows, width = q_ref.shape
    nq, tiles = width // 256, rows // TQ
    n = enc[0].shape[0]
    for r in range(pieces):
        at = pl.ds(pl.multiple_of((me_ref[0] ^ r) * n, n), n)
        kk = dot(enc[r][...], wkv_ref[:, :width]).astype(BF)
        k_ref[at, :] = kk
        kt_ref[:, at] = kk.T
        vv = dot(enc[r][...], wkv_ref[:, width:]).astype(BF)
        v_ref[at, :] = vv
        vt[:, at] = vv.T
    leaving = [
        pltpu.make_async_copy(a, b, out_sem.at[i])
        for i, (a, b) in enumerate(((k_ref, k_any), (v_ref, v_any), (kt_ref, kt_any)))
    ]
    for c in leaving:
        c.start()

    def tile(t, _):
        st = start_ref[pl.ds(t, 1), :]
        sz = size_ref[pl.ds(t, 1), :]
        lo = lo_ref[t]
        hi = hi_ref[t]
        row = pl.ds(pl.multiple_of(t * TQ, TQ), TQ)
        for c in range(nq):
            qst[c] = stack4(q_ref[row, c * 256 : (c + 1) * 256])
            m_scr[c] = jnp.full((8, 256), NEG, F32)
            l_scr[c] = jnp.zeros((8, 256), F32)
            acc[c] = jnp.zeros((256, 256), F32)

        def scores(j):
            kr = pl.ds(pl.multiple_of(j * TK, TK), TK)
            mask = range_mask(j * TK, TK, st, sz)
            for c in range(nq):
                s = dot_nt(k_ref[kr, c * 256 : (c + 1) * 256], qst[c])
                s = jnp.where(mask, s, NEG)
                s_scr[c, kr, :] = s
                m_scr[c] = jnp.maximum(m_scr[c], red(s, jnp.max))

        in_pairs(lo, hi, scores)
        for c in range(nq):
            m_scr[c] = jnp.broadcast_to(jnp.max(m_scr[c], axis=0, keepdims=True), (8, 256))

        def mix(j):
            kr = pl.ds(pl.multiple_of(j * TK, TK), TK)
            for c in range(nq):
                p = jnp.exp(s_scr[c, kr, :] - m_scr[c][0:1])
                l_scr[c] += red(p, jnp.sum)
                acc[c] += dot(vt[c * 256 : (c + 1) * 256, kr], p.astype(BF))

        in_pairs(lo, hi, mix)
        for c in range(nq):
            l = jnp.sum(l_scr[c], axis=0, keepdims=True)
            lse_ref[t, c] = m_scr[c][0:1] + jnp.log(l)
            o_ref[row, c * 256 : (c + 1) * 256] = own_heads(acc[c] * (1.0 / l)).T
        return 0

    lax.fori_loop(0, tiles, tile, 0)
    for c in leaving:
        c.wait()


def kv_cross(me, lo, hi, start, size, q, enc, wkv):
    rows, width = q.shape
    tiles, nq = rows // TQ, width // 256
    keys = len(enc) * enc[0].shape[0]
    return call(
        functools.partial(kv_cross_kernel, pieces=len(enc)),
        "kv_cross",
        (
            sds((keys, width), BF),
            sds((keys, width), BF),
            sds((width, keys), BF),
            sds((rows, width), F32),
            sds((tiles, nq, 1, 256), F32),
        ),
        [SM] * 3 + [VM] * (3 + len(enc) + 1),
        (pl.BlockSpec(memory_space=pl.ANY),) * 3 + (VM, VM),
        [
            pltpu.VMEM((width, keys), BF),
            pltpu.VMEM((keys, width), BF),
            pltpu.VMEM((keys, width), BF),
            pltpu.VMEM((width, keys), BF),
            pltpu.SemaphoreType.DMA((3,)),
            pltpu.VMEM((nq, 256, 256), BF),
            pltpu.VMEM((nq, keys, 256), F32),
            pltpu.VMEM((nq, 8, 256), F32),
            pltpu.VMEM((nq, 8, 256), F32),
            pltpu.VMEM((nq, 256, 256), F32),
        ],
        (me, lo, hi, start, size, q, *enc, wkv),
        us=80,
    )


def ffn_kernel(
    src_ref,
    x1_ref,
    ocross_ref,
    gain_ref,
    cot_ref,
    wco_ref,
    win_any,
    wout_any,
    okeep_ref,
    osend_ref,
    wi_ref,
    wj_ref,
    oc_ref,
    out_ref,
    dx2_ref,
    dyc_ref,
    do_ref,
    dgain_ref,
    win,
    wout,
    h3,
    h3t,
    g_low,
    dh,
    out_acc,
    u_all,
    ik,
    ss,
    ic,
    iy,
    ix,
    even,
    odd,
    came,
    w_sem,
    send_sem,
    recv_sem,
    o_send,
    o_recv,
):
    rows, width = x1_ref.shape
    steps = win.shape[1] // width
    quarter = width // 4
    half = quarter // 2
    g, b = lax.axis_index("grp"), lax.axis_index("blk")
    mesh_id = pl.DeviceIdType.MESH
    peers = [(g, b ^ 1), (g ^ 1, b), (g, b ^ 2)]

    def part(f):
        return pl.ds(pl.multiple_of(f * width, width), width)

    def weights(f):
        return (
            pltpu.make_async_copy(win_any.at[:, part(f)], win.at[:, part(f)], w_sem.at[0, f]),
            pltpu.make_async_copy(wout_any.at[part(f), :], wout.at[part(f), :], w_sem.at[1, f]),
        )

    for f in range(steps):
        for c in weights(f):
            c.start()
    barrier = pltpu.get_barrier_semaphore()
    for p in peers:
        pl.semaphore_signal(barrier, inc=1, device_id=p, device_id_type=mesh_id)
    pl.semaphore_wait(barrier, 3)

    def remote(k, f):
        src, dst = ((ss.at[f], ic.at[f]), (ik.at[f, pl.ds(2, 2)], iy.at[f]), (ik.at[f, pl.ds(1, 1)], ix.at[f]))[k]
        return pltpu.make_async_remote_copy(
            src_ref=src,
            dst_ref=dst,
            send_sem=send_sem.at[k, f],
            recv_sem=recv_sem.at[k, f],
            device_id=peers[k],
            device_id_type=mesh_id,
        )

    o_copy = pltpu.make_async_remote_copy(
        src_ref=odd, dst_ref=came, send_sem=o_send, recv_sem=o_recv, device_id=peers[0], device_id_type=mesh_id
    )

    def add(x, y):
        return (x.astype(F32) + y.astype(F32)).astype(BF)

    def event(k, f):
        @pl.when((f >= 0) & (f < steps))
        def _():
            remote(k, f).wait()
            if k == 0:
                ik[f] = add(ik[f], ic[f])
            elif k == 1:
                ik[f, 0:2] = add(ik[f, 0:2], iy[f])
            else:
                rel = (g >> 1) ^ f
                whole = add(ik[f, 0], ix[f, 0])

                @pl.when((rel & 1) == 0)
                def _():
                    wi_ref[rel >> 1] = whole

                @pl.when((rel & 1) == 1)
                def _():
                    wj_ref[rel >> 1] = whole

            if k < 2:
                remote(k + 1, f).start()

    hot = onehot_rows(src_ref[...])
    g_low[...] = dot_tn(hot, cot_ref[...]).astype(BF)
    oc_ref[...] = ocross_ref[...].astype(BF)
    x2 = x1_ref[...] + dot(oc_ref[...], wco_ref[...])
    dx2_ref[...] = x2
    n = (x2 * rms(x2) * gain_ref[2:3, :]).astype(BF)
    h3[...] = n
    h3t[...] = n.T
    out_acc[...] = jnp.zeros_like(out_acc)
    dh[...] = jnp.zeros_like(dh)

    def hidden(f, _):
        for c in weights(f):
            c.wait()
        u, slope = gelu_both(dot(h3[...], win[:, part(f)]))
        u = u.astype(BF)
        u_all[:, part(f)] = u
        da = (slope * dot_nt(g_low[...], wout[part(f), :])).astype(BF)
        for r in range(4):
            left = h3t[pl.ds(pl.multiple_of((b ^ r) * quarter, quarter), quarter), :]
            dwi = dot(left, da).astype(BF)
            target = ss if r & 1 else ik
            for i in range(2):
                y, x = (g ^ (2 * f + i)) & 1, r >> 1
                target[f, 2 * y + x] = dwi[i * half : (i + 1) * half]
        remote(0, f).start()
        out_acc[...] += dot(u, wout[part(f), :])
        event(0, f)
        dh[...] += dot_nt(da, win[:, part(f)])
        event(1, f - 1)
        event(2, f - 2)
        return 0

    lax.fori_loop(0, steps, hidden, 0)

    def last_rows(f, _):
        dwo = dot_tn(u_all[:, part(f)], g_low[...]).astype(BF)
        r = b ^ f
        for s in range(8):
            at = (r >> 1) * 8 + slot_of(g ^ s)

            @pl.when((r & 1) == 0)
            def _():
                even[at] = dwo[s * half : (s + 1) * half]

            @pl.when((r & 1) == 1)
            def _():
                odd[at] = dwo[s * half : (s + 1) * half]

        return 0

    lax.fori_loop(0, steps, last_rows, 0)
    o_copy.start()
    event(1, jnp.int32(steps - 1))
    event(2, jnp.int32(steps - 2))
    x2 = dx2_ref[...]
    out = (x2 + out_acc[...]).astype(BF)
    out_ref[...] = dot(onehot_rows(src_ref[...]), out).astype(BF)
    dx, dgain_ref[...] = rms_back(x2, rms(x2), gain_ref[2:3, :], dh[...])
    dx2 = g_low[...].astype(F32) + dx
    dx2_ref[...] = dx2
    dyc_ref[...] = dx2.astype(BF)
    do_ref[...] = dot_nt(dyc_ref[...], wco_ref[...]).astype(BF)
    o_copy.wait()
    okeep_ref[...] = add(even[0:8], came[0:8])
    osend_ref[...] = add(even[8:16], came[8:16])
    event(2, jnp.int32(steps - 1))


def ffn(src, x1, ocross, gain, cot, wco, win, wout):
    rows, width = x1.shape
    steps = win.shape[1] // width
    half = width // 8
    any_spec = pl.BlockSpec(memory_space=pl.ANY)
    buf = lambda *n: pltpu.VMEM(n + (half, width), BF)
    tok = lambda d: pltpu.VMEM((rows, width), d)
    return pl.pallas_call(
        ffn_kernel,
        out_shape=(
            sds((8, half, width), BF),
            sds((8, half, width), BF),
            sds((2, half, width), BF),
            sds((2, half, width), BF),
            sds((rows, width), BF),
            sds((rows, width), BF),
            sds((rows, width), F32),
            sds((rows, width), BF),
            sds((rows, width), BF),
            sds((1, width), F32),
        ),
        in_specs=[VM] * 6 + [any_spec] * 2,
        out_specs=(VM,) * 10,
        scratch_shapes=[
            pltpu.VMEM(win.shape, BF),
            pltpu.VMEM(wout.shape, BF),
            tok(BF),
            pltpu.VMEM((width, rows), BF),
            tok(BF),
            tok(F32),
            tok(F32),
            pltpu.VMEM((rows, win.shape[1]), BF),
            buf(steps, 4),
            buf(steps, 4),
            buf(steps, 4),
            buf(steps, 2),
            buf(steps, 1),
            buf(16),
            buf(16),
            buf(16),
            pltpu.SemaphoreType.DMA((2, steps)),
            pltpu.SemaphoreType.DMA((3, steps)),
            pltpu.SemaphoreType.DMA((3, steps)),
            pltpu.SemaphoreType.DMA,
            pltpu.SemaphoreType.DMA,
        ],
        compiler_params=pltpu.CompilerParams(
            vmem_limit_bytes=63 << 20, collective_id=1, has_side_effects=True
        ),
        cost_estimate=pl.CostEstimate(flops=10**13, bytes_accessed=30 << 20, transcendentals=0),
        name="ffn",
    )(src, x1, ocross, gain, cot, wco, win, wout)


def cross_back_kernel(
    me_ref,
    lo_ref,
    hi_ref,
    start_ref,
    size_ref,
    q_ref,
    do_ref,
    o_ref,
    lse_ref,
    k_ref,
    v_ref,
    kt_ref,
    dq_ref,
    keep_ref,
    send_ref,
    qs,
    dos,
    del_scr,
    dka,
    dva,
    dqt,
    ps,
    dss,
    *,
    scale,
):
    rows, width = q_ref.shape
    nq, tiles = width // 256, rows // TQ
    dka[...] = jnp.zeros_like(dka)
    dva[...] = jnp.zeros_like(dva)

    def tile(t, _):
        st = start_ref[pl.ds(t, 1), :]
        sz = size_ref[pl.ds(t, 1), :]
        row = pl.ds(pl.multiple_of(t * TQ, TQ), TQ)
        for c in range(nq):
            cs = slice(c * 256, (c + 1) * 256)
            qs[c] = stack4(q_ref[row, cs])
            b = do_ref[row, cs]
            dos[c] = stack4(b)
            product = (b.astype(F32) * o_ref[row, cs]).T
            total = jnp.concatenate(
                [jnp.sum(product[h * 64 : (h + 1) * 64], axis=0, keepdims=True) for h in range(4)], axis=1
            )
            del_scr[c] = jnp.broadcast_to(total, (8, 256))
            dqt[c] = jnp.zeros((256, 256), F32)

        def probs(j, slot):
            kr = pl.ds(pl.multiple_of(j * TK, TK), TK)
            mask = range_mask(j * TK, TK, st, sz)
            for c in range(nq):
                cs = slice(c * 256, (c + 1) * 256)
                s = dot_nt(k_ref[kr, cs], qs[c])
                p = jnp.where(mask, jnp.exp(s - lse_ref[t, c]), 0.0)
                dp = dot_nt(v_ref[kr, cs], dos[c])
                ps[slot, c] = p.astype(BF)
                dss[slot, c] = (p * (dp - del_scr[c][0:1])).astype(BF)

        def grads(j, slot):
            kr = pl.ds(pl.multiple_of(j * TK, TK), TK)
            for c in range(nq):
                cs = slice(c * 256, (c + 1) * 256)
                ds = dss[slot, c]
                dva[kr, cs] += dot(ps[slot, c], dos[c])
                dka[kr, cs] += dot(ds, qs[c])
                dqt[c] += dot(kt_ref[cs, kr], ds)

        lo = lo_ref[t]
        hi = hi_ref[t]
        slots = ps.shape[0]

        def two(i, _):
            probs(lo + 2 * i, 0)
            probs(lo + 2 * i + 1, 1)
            grads(lo + 2 * i, 0)
            grads(lo + 2 * i + 1, 1)
            return 0

        if slots == 4:

            def four(i, _):
                for k in range(4):
                    probs(lo + 4 * i + k, k)
                for k in range(4):
                    grads(lo + 4 * i + k, k)
                return 0

            lax.fori_loop(0, (hi - lo) // 4, four, 0)
            lo = lo + (hi - lo) // 4 * 4
        lax.fori_loop(0, (hi - lo) // 2, two, 0)

        @pl.when((hi - lo) % 2 == 1)
        def _():
            probs(hi - 1, 0)
            grads(hi - 1, 0)

        for c in range(nq):
            cs = slice(c * 256, (c + 1) * 256)
            dq_ref[row, cs] = (own_heads(dqt[c]).T * scale).astype(BF)
        return 0

    lax.fori_loop(0, tiles, tile, 0)
    n = keep_ref.shape[1]
    for r in range(4):
        at = pl.ds(pl.multiple_of((me_ref[0] ^ r) * n, n), n)
        target = send_ref if r & 1 else keep_ref
        target[r >> 1, :, :width] = dka[at, :].astype(BF)
        target[r >> 1, :, width:] = dva[at, :].astype(BF)


def cross_back(me, lo, hi, start, size, q, do, o, lse, k, v, kt, scale, first, nq):
    rows = q.shape[0]
    keys, width = k.shape[0], nq * 256
    tiles = rows // TQ
    at = first // nq
    part = sds((2, keys // 4, 2 * width), BF)
    cols = lambda n: pl.BlockSpec((n, width), lambda i: (0, at))
    whole = lambda a: pl.BlockSpec(a.shape, lambda i: (0,) * len(a.shape))
    outs = (sds((rows, width), BF), part, part)
    return pl.pallas_call(
        functools.partial(cross_back_kernel, scale=scale),
        grid=(1,),
        out_shape=outs,
        in_specs=[
            SM,
            SM,
            SM,
            whole(start),
            whole(size),
            cols(rows),
            cols(rows),
            cols(rows),
            pl.BlockSpec((tiles, nq, 1, 256), lambda i: (0, at, 0, 0)),
            cols(keys),
            cols(keys),
            pl.BlockSpec((width, keys), lambda i: (at, 0)),
        ],
        out_specs=tuple(whole(a) for a in outs),
        scratch_shapes=[pltpu.VMEM((nq, 256, 256), BF)] * 2
        + [
            pltpu.VMEM((nq, 8, 256), F32),
            pltpu.VMEM((keys, width), F32),
            pltpu.VMEM((keys, width), F32),
            pltpu.VMEM((nq, 256, 256), F32),
            pltpu.VMEM((4 if nq == 1 else 2, nq, 256, 256), BF),
            pltpu.VMEM((4 if nq == 1 else 2, nq, 256, 256), BF),
        ],
        compiler_params=pltpu.CompilerParams(vmem_limit_bytes=LIMIT),
        cost_estimate=pl.CostEstimate(flops=10**13, bytes_accessed=30 << 20, transcendentals=0),
        name="cross_back",
    )(me, lo, hi, start, size, q, do, o, lse, k, v, kt)


def cross_in_kernel(
    dq0_ref, dq1_ref, x1_ref, dx2_ref, gain_ref, wcq_ref, wso_ref, own_ref, oz_ref, oy_ref, oyz_ref, two_ref, came_ref,
    dx1_ref, dy1_ref, dos_ref, dgain_ref, pair_ref, keep_ref, send_ref,
):
    x1 = x1_ref[...]
    cut = dq0_ref.shape[1]
    back = dot_nt(dq0_ref[...], wcq_ref[:, :cut]) + dot_nt(dq1_ref[...], wcq_ref[:, cut:])
    dx, dgain_ref[...] = rms_back(x1, rms(x1), gain_ref[1:2, :], back)
    dx1 = dx2_ref[...] + dx
    dx1_ref[...] = dx1
    dy1_ref[...] = dx1.astype(BF)
    dos_ref[...] = dot_nt(dy1_ref[...], wso_ref[...]).astype(BF)
    for n, ref in ((0, keep_ref), (1, send_ref)):
        parts = [r[n].astype(F32) for r in (own_ref, oz_ref, oy_ref, oyz_ref)]
        ref[...] = (parts[0] + parts[1] + parts[2] + parts[3]).astype(BF)
        pair_ref[n] = (two_ref[n].astype(F32) + came_ref[1 - n].astype(F32)).astype(BF)


def cross_in(dq0, dq1, x1, dx2, gain, wcq, wso, own, oz, oy, oyz, two, came):
    rows, width = x1.shape
    return call(
        cross_in_kernel,
        "cross_in",
        (
            sds((rows, width), F32),
            sds((rows, width), BF),
            sds((rows, width), BF),
            sds((1, width), F32),
            sds(two.shape, BF),
            sds(two.shape[1:], BF),
            sds(two.shape[1:], BF),
        ),
        [VM] * 13,
        (VM,) * 7,
        [],
        (dq0, dq1, x1, dx2, gain, wcq, wso, own, oz, oy, oyz, two, came),
        us=60,
    )


def late_kernel(
    start_ref,
    size_ref,
    bucket_ref,
    brow_ref,
    proj_any,
    do_any,
    lse_ref,
    h1_any,
    oself_any,
    dy1_any,
    src_ref,
    x0_any,
    gain_ref,
    dx1_any,
    wqkv_any,
    dg2_ref,
    dg3_ref,
    keep0_any,
    came0_any,
    keep1_any,
    came1_any,
    enc0_any,
    enc2_any,
    wkv_any,
    oc_ref,
    dyc_ref,
    h2_ref,
    dq0_ref,
    dq1_ref,
    wpair_any,
    fkeep_ref,
    fsend_any,
    d_ref,
    small_ref,
    f,
    own_ref,
    came_any,
    ffn_any,
    projs,
    wbuf,
    both,
    stage,
    enc_t,
    enc_out,
    bias,
    dka,
    dva,
    dsum,
    left_t,
    ss,
    drow,
    sm_in,
    dgain,
    fown,
    frecv,
    q,
    r1,
    r2,
    r3,
    r4,
    r5,
    do_ref,
    h1_ref,
    oself_ref,
    dy1_ref,
    x0_ref,
    dx1_ref,
    enc0_ref,
    enc2_ref,
    send_sem,
    recv_sem,
    sm_send,
    sm_recv,
    x_send,
    x_recv,
    f_send,
    f_recv,
    loc,
    *,
    scale,
):
    rows, width = do_ref.shape
    nq, tiles = width // 256, rows // TQ
    length, buckets = brow_ref.shape[0], 32
    count, step_rows, wide = q.shape[0], q.shape[2], q.shape[3]
    each = count // 8
    quarter = width // 4
    tall = quarter // 4
    n = enc0_ref.shape[0]
    cut = dq0_ref.shape[1]
    g, b = lax.axis_index("grp"), lax.axis_index("blk")
    peers = [(g, b ^ 1), (g, b ^ 2), (g ^ 1, b), (g ^ 2, b), (g ^ 4, b), (g ^ 2, b), (g ^ 1, b)]
    mesh_id = pl.DeviceIdType.MESH

    def local(src, dst, k):
        return pltpu.make_async_copy(src, dst, loc.at[k])

    def remote(src, dst, send, recv, k):
        return pltpu.make_async_remote_copy(
            src_ref=src, dst_ref=dst, send_sem=send, recv_sem=recv, device_id=peers[k], device_id_type=mesh_id
        )

    proj_in = local(proj_any, projs.at[pl.ds(64, rows), :], 0)
    wkv_in = local(wkv_any, wbuf.at[:, pl.ds(0, 2 * width)], 1)
    held_in = [
        local(src, dst, 20 + i)
        for i, (src, dst) in enumerate(
            (
                (oself_any, oself_ref),
                (dy1_any, dy1_ref),
                (enc0_any, enc0_ref),
                (enc2_any, enc2_ref),
                (do_any, do_ref),
                (h1_any, h1_ref),
                (x0_any, x0_ref),
                (dx1_any, dx1_ref),
            )
        )
    ]
    wqkv_in = local(wqkv_any, wbuf, 2)
    dkv_in = []
    for r in range(2):
        for i, (keep, came, at, w) in enumerate(
            ((keep0_any, came0_any, 0, cut), (keep1_any, came1_any, cut, width - cut))
        ):
            for half in range(2):
                from_, to = pl.ds(half * w, w), pl.ds(half * width + at, w)
                k = 3 + 8 * r + 4 * i + 2 * half
                dkv_in.append((r, local(keep.at[r, :, from_], both.at[pl.ds(r * n, n), to], k)))
                dkv_in.append((r, local(came.at[r, :, from_], stage.at[:, to], k + 1)))
    for r, c in dkv_in:
        if r == 0:
            c.start()
    for c in held_in[:4] + [wkv_in, proj_in] + held_in[4:]:
        c.start()

    barrier = pltpu.get_barrier_semaphore()
    for p in peers[:5]:
        pl.semaphore_signal(barrier, inc=1, device_id=p, device_id_type=mesh_id)
    pl.semaphore_wait(barrier, 5)

    f_half = fown.shape[0]
    w_at, o_at = pl.ds(0, f_half), pl.ds(f_half, f_half)
    w_local = local(wpair_any, ffn_any.at[pl.ds(0, 2), w_at, :], 28)
    w_copies = [
        remote(wpair_any, ffn_any.at[pl.ds(2, 2), w_at, :], f_send.at[0], f_recv.at[0], 3),
    ]
    f_first = remote(fsend_any, frecv, f_send.at[2], f_recv.at[2], 4)
    f_second = remote(fown, ffn_any.at[1, o_at, :], f_send.at[3], f_recv.at[3], 4)
    f_third = remote(
        ffn_any.at[pl.ds(0, 2), o_at, :], ffn_any.at[pl.ds(2, 2), o_at, :], f_send.at[4], f_recv.at[4], 3
    )
    f_local = local(fown, ffn_any.at[0, o_at, :], 19)
    f_slices = f_half // step_rows
    w_copies[0].start()
    f_first.start()
    w_local.start()

    def w_copy(i):
        at = pl.ds(pl.multiple_of(i * step_rows, step_rows), step_rows)
        src, dst = ffn_any.at[pl.ds(0, 4), at, :], ffn_any.at[pl.ds(4, 4), at, :]
        return remote(src, dst, f_send.at[11 + i], f_recv.at[11 + i], 2)

    def f_copy(i):
        at = pl.ds(pl.multiple_of(f_half + i * step_rows, step_rows), step_rows)
        src, dst = ffn_any.at[pl.ds(0, 4), at, :], ffn_any.at[pl.ds(4, 4), at, :]
        return remote(src, dst, f_send.at[5 + i], f_recv.at[5 + i], 2)

    enc_copy = remote(enc_out, came_any, x_send, x_recv, 1)

    def add(x, y):
        return (x.astype(F32) + y.astype(F32)).astype(BF)

    def core_copy(j):
        at = pl.ds(pl.multiple_of(j * step_rows, step_rows), step_rows)
        return remote(ss.at[:, at, :], r1.at[j], send_sem.at[0, j], recv_sem.at[0, j], 0)

    def copy(k, j):
        src, dst = [
            lambda: (q.at[j, pl.ds(8, 8)], r2.at[j]),
            lambda: (q.at[j, pl.ds(4, 4)], r3.at[j]),
            lambda: (q.at[j, pl.ds(2, 2)], r4.at[j]),
            lambda: (q.at[j, pl.ds(0, 2)], r5.at[j]),
            lambda: (f.at[j, pl.ds(0, 2)], f.at[j, pl.ds(2, 2)]),
            lambda: (f.at[j, pl.ds(0, 4)], f.at[j, pl.ds(4, 4)]),
        ][k - 1]()
        return remote(src, dst, send_sem.at[k, j], recv_sem.at[k, j], k)

    def event(k, j):
        @pl.when((j >= 0) & (j < count))
        def _():
            (core_copy(j) if k == 0 else copy(k, j)).wait()
            if k == 0:
                q[j] = add(q[j], r1[j])
            elif k == 1:
                q[j, 0:8] = add(q[j, 0:8], r2[j])
            elif k == 2:
                q[j, 0:4] = add(q[j, 0:4], r3[j])
            elif k == 3:
                q[j, 0:2] = add(q[j, 0:2], r4[j])
            elif k == 4:
                f[j, 0] = add(q[j, 0], r5[j, 1])
                f[j, 1] = add(q[j, 1], r5[j, 0])
            if k < 6:
                copy(k + 1, j).start()

    def step(t):
        t = jnp.asarray(t, jnp.int32)
        event(0, t + 3)
        for k in range(1, 7):
            event(k, t - 2 * (k - 1))

    def put(right, block):
        for r in range(4):
            part = left_t[pl.ds(pl.multiple_of((b ^ r) * quarter, quarter), quarter), :]
            spread(dot(part, right).astype(BF), r, block)
        start_core(block)

    def spread(grad, r, block):
        for s in range(8):
            at = (r >> 1) * 8 + slot_of(g ^ s)
            y, x = (s >> 1) * tall, (s & 1) * wide
            if r & 1:
                ss[at, block * tall : (block + 1) * tall, :] = grad[y : y + tall, x : x + wide]
            else:
                for k in range(each):
                    piece = grad[y + k * step_rows : y + (k + 1) * step_rows, x : x + wide]
                    q[block * each + k, at] = piece

    def start_core(block):
        for k in range(each):
            core_copy(block * each + k).start()

    left_t[...] = oc_ref[...].T
    put(dyc_ref[...], 0)
    left_t[...] = h2_ref[...].T
    for j in range(each):
        event(0, jnp.int32(j))
    put(jnp.concatenate([dq0_ref[...], dq1_ref[...]], axis=1), 1)
    step(0)
    w_local.wait()
    w_copies[0].wait()
    w_copy(0).start()
    held_in[0].wait()
    held_in[1].wait()
    left_t[...] = oself_ref[...].T
    for r, c in dkv_in:
        if r == 0:
            c.wait()
    both[:n, :] = add(both[:n, :], stage[...])
    for r, c in dkv_in:
        if r == 1:
            c.start()
    put(dy1_ref[...], 2)
    f_first.wait()
    fown[...] = add(fkeep_ref[...], frecv[...])
    f_local.start()
    f_second.start()
    step(1)
    w_copy(1).start()

    held_in[2].wait()
    held_in[3].wait()
    enc_t[:, :n] = enc0_ref[...].T
    enc_t[:, n:] = enc2_ref[...].T
    for r, c in dkv_in:
        if r == 1:
            c.wait()
    both[n:, :] = add(both[n:, :], stage[...])
    for i in range(2):
        for r in range(4):
            part = enc_t[pl.ds(pl.multiple_of((b ^ r) * quarter, quarter), quarter), :]
            spread(dot(part, both[:, i * width : (i + 1) * width]).astype(BF), r, 3 + i)
        start_core(3 + i)
        step(2 + i)
        w_copy(2 + i).start()
    wkv_in.wait()
    enc_out[...] = dot_nt(both[n:, :], wbuf[:, : 2 * width]).astype(BF)
    own_ref[...] = dot_nt(both[:n, :], wbuf[:, : 2 * width])
    wqkv_in.start()

    projs[0:64, :] = jnp.zeros((64, 3 * width), BF)
    fill_bias_all(brow_ref, bias, nq)
    dka[...] = jnp.zeros_like(dka)
    dva[...] = jnp.zeros_like(dva)
    dsum[...] = jnp.zeros_like(dsum)
    proj_in.wait()
    held_in[4].wait()

    def tile(t):
        row = pl.ds(pl.multiple_of(t * TQ, TQ), TQ)
        held = pl.ds(pl.multiple_of(t * TQ + 64, TQ), TQ)
        win = pl.ds(pl.multiple_of(t * TQ, TQ), WIN)
        mask = range_mask(t * TQ - 64, WIN, start_ref[pl.ds(t, 1), :], size_ref[pl.ds(t, 1), :])
        for c in range(nq):
            cols = slice(c * 256, (c + 1) * 256)
            kcols = slice(width + c * 256, width + (c + 1) * 256)
            vcols = slice(2 * width + c * 256, 2 * width + (c + 1) * 256)
            qs = stack4(projs[held, cols] * jnp.asarray(scale, BF))
            dos = stack4(do_ref[row, cols])
            s = dot_nt(projs[win, kcols], qs) + bias[c]
            p = jnp.where(mask, jnp.exp(s - lse_ref[t, c]), 0.0)
            dp = dot_nt(projs[win, vcols], dos)
            delta = jnp.sum(red(p * dp, jnp.sum), axis=0, keepdims=True)
            ds = p * (dp - delta)
            dsum[c] += ds
            ds = ds.astype(BF)
            dva[win, cols] += dot(p.astype(BF), dos)
            dka[win, cols] += dot(ds, qs)
            projs[held, cols] = (unstack4(dot_tn(ds, projs[win, kcols])) * scale).astype(BF)

    def tile_and_step(t, _):
        tile(t)
        step(t + 4)

        @pl.when(t < f_slices - 4)
        def _():
            w_copy(t + 4).start()

        return 0

    lax.fori_loop(0, tiles - 2, tile_and_step, 0)

    def tile_alone(t, _):
        tile(t)
        return 0

    lax.fori_loop(tiles - 2, tiles, tile_alone, 0)
    f_second.wait()
    f_local.wait()
    f_third.start()
    dist = distances()
    for c in range(nq):
        cols = slice(c * 256, (c + 1) * 256)

        def one(d, _):
            x = jnp.where(dist == d, dsum[c], 0.0)
            drow[pl.ds(d, 1), cols] = jnp.sum(red(x, jnp.sum), axis=0, keepdims=True)
            return 0

        lax.fori_loop(0, length, one, 0)
    lane = lax.broadcasted_iota(jnp.int32, (buckets, length), 1)
    place = jnp.zeros((buckets, length), jnp.int32)
    for d in range(length):
        place = jnp.where(lane == d, bucket_ref[d], place)
    hot = (place == lax.broadcasted_iota(jnp.int32, (buckets, length), 0)).astype(F32)
    head = (
        lax.broadcasted_iota(jnp.int32, (width, 128), 0) // 64
        == lax.broadcasted_iota(jnp.int32, (width, 128), 1)
    ).astype(F32)
    by_bucket = jnp.dot(hot, drow[...], preferred_element_type=F32, precision=lax.Precision.HIGHEST)
    small_ref[...] = jnp.zeros_like(small_ref)
    small_ref[24:, :] = jnp.dot(by_bucket, head, preferred_element_type=F32, precision=lax.Precision.HIGHEST)
    done = tiles + 2
    projs[64:, width : 2 * width] = dka[64:, :].astype(BF)
    projs[64:, 2 * width : 3 * width] = dva[64:, :].astype(BF)
    held_in[5].wait()
    left_t[...] = h1_ref[...].T
    for i in range(3):
        put(projs[64:, i * width : (i + 1) * width], 5 + i)
        step(done)
        step(done + 1)
        done += 2

    dgain[...] = jnp.zeros_like(dgain)
    parts = 5
    block = rows // parts
    wqkv_in.wait()
    held_in[6].wait()
    held_in[7].wait()

    def self_in(i, _):
        at = pl.ds(pl.multiple_of(i * block, block), block)
        held = pl.ds(pl.multiple_of(i * block + 64, 64), block)
        x0 = x0_ref[at, :].astype(F32)
        dx, part = rms_back(x0, rms(x0), gain_ref[0:1, :], dot_nt(projs[held, :], wbuf[...]))
        dgain[...] += part
        dx0 = dx1_ref[at, :] + dx
        top = dx0.astype(BF)
        both[at, :width] = top
        both[at, width:] = (dx0 - top.astype(F32)).astype(BF)
        step(done + i)

        @pl.when(i == 2)
        def _():
            enc_copy.start()

        return 0

    lax.fori_loop(0, parts, self_in, 0)
    done += parts

    for i, ref in enumerate((dgain, dg2_ref, dg3_ref)):
        for k in range(6):
            small_ref[6 * i + k : 6 * i + k + 1, :] = ref[0:1, k * 128 : (k + 1) * 128]

    def small_copy(k):
        src = small_ref if k == 0 else sm_in.at[k + 4]
        return remote(src, sm_in.at[k], sm_send.at[k], sm_recv.at[k], k)

    def small_sum(k):
        small_copy(k).wait()
        held = small_ref[...] if k == 0 else sm_in[k + 4]
        if k < 4:
            sm_in[k + 5] = held + sm_in[k]
            small_copy(k + 1).start()
        else:
            small_ref[...] = held + sm_in[k]

    small_copy(0).start()
    f_third.wait()
    f_copy(0).start()
    step(done)
    chunk = rows // 5
    for k in range(5):
        small_sum(k)
        hot_rows = (lax.broadcasted_iota(jnp.int32, (chunk, rows), 0) + k * chunk == src_ref[...]).astype(F32).astype(BF)
        d_ref[k * chunk : (k + 1) * chunk, :] = dot(hot_rows, both[:rows, :width]) + dot(hot_rows, both[:rows, width:])
        for i in range(2):
            step(done + 1 + 2 * k + i)
        f_copy(1 + k).start()

    def rest(t, _):
        step(t)
        return 0

    lax.fori_loop(done + 11, count + 10, rest, 0)

    def f_end(i, _):
        f_copy(i).wait()
        return 0

    lax.fori_loop(0, f_slices, f_end, 0)

    def w_end(i, _):
        w_copy(i).wait()
        return 0

    lax.fori_loop(0, f_slices, w_end, 0)
    enc_copy.wait()


def late(
    start, size, bucket, brow, proj, do, lse, h1, oself, dy1, src, x0, gain, dx1, wqkv, dg2, dg3,
    keep0, came0, keep1, came1, enc0, enc2, wkv, oc, dyc, h2, dq0, dq1, wpair, fkeep, fsend, scale,
):
    rows, width = do.shape
    nq = width // 256
    n = enc0.shape[0]
    step_rows, wide, tall = 16, width // 2, width // 16
    count = 8 * tall // step_rows
    any_spec = pl.BlockSpec(memory_space=pl.ANY)

    def buf(n):
        return pltpu.VMEM((count, n, step_rows, wide), BF)

    return pl.pallas_call(
        functools.partial(late_kernel, scale=scale),
        out_shape=(
            sds((rows, width), F32),
            sds((56, 128), F32),
            sds((count, 8, step_rows, wide), BF),
            sds((n, width), F32),
            sds((n, width), BF),
            sds((8, 2 * fkeep.shape[0], width), BF),
        ),
        in_specs=[VM, VM, SM, VM, any_spec, any_spec, VM]
        + [any_spec] * 3
        + [VM, any_spec, VM, any_spec]
        + [any_spec, VM, VM]
        + [any_spec] * 7
        + [VM] * 5
        + [any_spec, VM, any_spec],
        out_specs=(VM,) * 4 + (any_spec, any_spec),
        scratch_shapes=[
            pltpu.VMEM((rows + 64, 3 * width), BF),
            pltpu.VMEM((width, 3 * width), BF),
            pltpu.VMEM((2 * n, 2 * width), BF),
            pltpu.VMEM((n, 2 * width), BF),
            pltpu.VMEM((width, 2 * n), BF),
            pltpu.VMEM((n, width), BF),
            pltpu.VMEM((nq, WIN, 256), F32),
            pltpu.VMEM((rows + 64, width), F32),
            pltpu.VMEM((rows + 64, width), F32),
            pltpu.VMEM((nq, WIN, 256), F32),
            pltpu.VMEM((width, rows), BF),
            pltpu.VMEM((16, 8 * tall, wide), BF),
            pltpu.VMEM(brow.shape, F32),
            pltpu.VMEM((9, 56, 128), F32),
            pltpu.VMEM((1, width), F32),
            pltpu.VMEM(fkeep.shape, BF),
            pltpu.VMEM(fkeep.shape, BF),
            buf(16),
            buf(16),
            buf(8),
            buf(4),
            buf(2),
            buf(2),
        ]
        + [pltpu.VMEM(a.shape, a.dtype) for a in (do, h1, oself, dy1, x0, dx1, enc0, enc2)]
        + [
            pltpu.SemaphoreType.DMA((7, count)),
            pltpu.SemaphoreType.DMA((7, count)),
            pltpu.SemaphoreType.DMA((5,)),
            pltpu.SemaphoreType.DMA((5,)),
            pltpu.SemaphoreType.DMA,
            pltpu.SemaphoreType.DMA,
            pltpu.SemaphoreType.DMA((17,)),
            pltpu.SemaphoreType.DMA((17,)),
            pltpu.SemaphoreType.DMA((29,)),
        ],
        compiler_params=pltpu.CompilerParams(
            vmem_limit_bytes=63 << 20, collective_id=0, has_side_effects=True
        ),
        cost_estimate=pl.CostEstimate(flops=10**13, bytes_accessed=30 << 20, transcendentals=0),
        name="late",
    )(
        start, size, bucket, brow, proj, do, lse, h1, oself, dy1, src, x0, gain, dx1, wqkv, dg2, dg3,
        keep0, came0, keep1, came1, enc0, enc2, wkv, oc, dyc, h2, dq0, dq1, wpair, fkeep, fsend,
    )


def last_kernel(
    me_ref, small_ref, ffn_any, f_any, own_any, came_any,
    win_any, wout_any, co_any, cq_any, ckv_any, qkv_any, so_any, enc_any,
    g1_ref, g2_ref, g3_ref, rel_ref,
    ffn_ref, f_ref, own_ref, came_ref, win_ref, wout_ref, co_ref, cq_ref, ckv_ref, qkv_ref, so_ref, enc_ref, sem,
):
    def move(src, dst, k):
        return pltpu.make_async_copy(src, dst, sem.at[k])

    arriving = [
        move(a, b, i)
        for i, (a, b) in enumerate(
            ((ffn_any, ffn_ref), (own_any, own_ref), (came_any, came_ref), (f_any, f_ref))
        )
    ]
    outs = ((win_ref, win_any), (wout_ref, wout_any), (enc_ref, enc_any), (co_ref, co_any), (cq_ref, cq_any))
    outs = outs + ((so_ref, so_any), (ckv_ref, ckv_any), (qkv_ref, qkv_any))
    leaving = [move(a, b, 4 + i) for i, (a, b) in enumerate(outs)]
    for c in arriving:
        c.start()

    arriving[0].wait()
    half = ffn_ref.shape[1] // 2
    for slot in range(8):
        s = me_ref[1] ^ ((slot >> 2) + (slot & 2) + 4 * (slot & 1))
        rows = pl.ds(pl.multiple_of((s & 1) * half, half), half)
        cols = pl.ds(pl.multiple_of((s >> 1) * 768, 768), 768)
        win_ref[rows, cols] = ffn_ref[slot, :half].astype(F32)
        wout_ref[pl.ds(pl.multiple_of(s * half, half), half), :] = ffn_ref[slot, half:].astype(F32)
    leaving[0].start()
    leaving[1].start()
    arriving[1].wait()
    arriving[2].wait()
    enc_ref[...] = own_ref[...] + came_ref[...].astype(F32)
    leaving[2].start()
    arriving[3].wait()
    count, _, step_rows, wide = f_ref.shape
    width = 2 * wide
    places = (
        (co_ref, 0, 3), (cq_ref, 0, 4), (so_ref, 0, 5), (ckv_ref, 0, None), (ckv_ref, width, 6),
        (qkv_ref, 0, None), (qkv_ref, width, None), (qkv_ref, 2 * width, 7),
    )
    each = count // 8
    tall = each * step_rows
    for n, (out, col, done) in enumerate(places):
        for slot in range(8):
            s = me_ref[1] ^ ((slot >> 2) + (slot & 2) + 4 * (slot & 1))
            for k in range(each):
                at = pl.ds(pl.multiple_of((s >> 1) * tall + k * step_rows, step_rows), step_rows)
                cols = pl.ds(pl.multiple_of(col + (s & 1) * wide, 128), wide)
                out[at, cols] = f_ref[n * each + k, slot].astype(F32)
        if done is not None:
            leaving[done].start()
    quarter = g1_ref.shape[1]
    for i, ref in enumerate((g1_ref, g2_ref, g3_ref)):
        whole = jnp.concatenate([small_ref[6 * i + k : 6 * i + k + 1, :] for k in range(6)], axis=1)
        for j in range(4):

            @pl.when(me_ref[0] == j)
            def _():
                ref[...] = whole[:, j * quarter : (j + 1) * quarter]

    part, heads = rel_ref.shape
    rel_ref[...] = small_ref[pl.ds(pl.multiple_of(24 + me_ref[0] * part, 8), part), :heads]
    for c in leaving:
        c.wait()


def last(me, small, ffn, f, own, came, buckets, heads):
    width = own.shape[1]
    quarter = width // 4
    cols = lambda n: sds((quarter, n * width), F32)
    any_spec = pl.BlockSpec(memory_space=pl.ANY)
    big = (cols(4), sds((width, width), F32), cols(1), cols(1), cols(2), cols(3), cols(1), sds(own.shape, F32))
    held = (ffn, f, own, came) + big
    return call(
        last_kernel,
        "last",
        big
        + (sds((1, quarter), F32),) * 3
        + (sds((buckets // 4, heads), F32),),
        [SM, VM] + [any_spec] * 4,
        (any_spec,) * 8 + (VM,) * 4,
        [pltpu.VMEM(a.shape, a.dtype) for a in held] + [pltpu.SemaphoreType.DMA((12,))],
        (me, small, ffn, f, own, came),
        us=8,
    )


def hop(x, core=0, xb=0, yb=0, z1=0, z2=0):
    b, g = core | (xb << 1), yb | (z1 << 1) | (z2 << 2)
    groups, blocks = lax.axis_size("grp"), lax.axis_size("blk")
    pairs = [(i * blocks + j, (i ^ g) * blocks + (j ^ b)) for i in range(groups) for j in range(blocks)]
    return lax.ppermute(x, ("grp", "blk"), pairs)


def after(x, *deps):
    return lax.optimization_barrier((x,) + deps)[0]


def split_kernel(okeep_ref, ocame_ref, wkeep_ref, wcame_ref, q0_ref, q1_ref, q2_ref, q3_ref, two_ref):
    for j, ref in enumerate((q0_ref, q1_ref, q2_ref, q3_ref)):
        ref[...] = (okeep_ref[2 * j : 2 * j + 2].astype(F32) + ocame_ref[2 * j : 2 * j + 2].astype(F32)).astype(BF)
    two_ref[...] = (wkeep_ref[...].astype(F32) + wcame_ref[...].astype(F32)).astype(BF)


def split(okeep, ocame, wkeep, wcame):
    part = sds(wkeep.shape, BF)
    return call(
        split_kernel, "split", (part,) * 5, [VM] * 4, (VM,) * 5, [], (okeep, ocame, wkeep, wcame), us=4
    )


def fused_body(
    dec_in,
    encodings,
    answer_len,
    answer_question,
    question_rows,
    bucket_table,
    gain_self,
    w_qkv,
    w_self_out,
    rel_bias,
    gain_cross,
    w_cross_q,
    w_cross_kv,
    w_cross_out,
    gain_ffn,
    w_in,
    w_out,
    cotangent,
):
    rows, width = dec_in.shape
    buckets, heads = rel_bias.shape
    scale = 1.0 / math.sqrt(width // heads)
    me_b, me_g = lax.axis_index("blk"), lax.axis_index("grp")
    me = jnp.stack([me_b, me_g]).astype(jnp.int32)
    row = lax.broadcasted_iota(jnp.int32, (3, width), 0)
    gains = jnp.where(row == 0, gain_self[None], jnp.where(row == 1, gain_cross[None], gain_ffn[None]))
    g1, g2, g3 = gains, gains, gains

    enc2 = hop(encodings, xb=1)
    enc1 = hop(encodings, core=1)
    src, cstart, csize, sstart, ssize, lo, hi, brow, x0, h1, proj, oself, lse_self = pre(
        me, answer_question, answer_len, question_rows, bucket_table, dec_in, g1, rel_bias, w_qkv, scale
    )
    enc2, oself = lax.optimization_barrier((enc2, oself))
    enc3 = hop(enc2, core=1)
    enc1 = after(enc1, x0)
    x1, h2, qc = mid(x0, oself, w_self_out, g2, w_cross_q, scale)
    k, v, kt, ocross, lse = kv_cross(
        me, lo, hi, cstart, csize, qc, (encodings, enc1, enc2, enc3), w_cross_kv
    )
    o_keep, o_send, w_keep, w_send, oc, layer_out, dx2, dyc, do, dgain3 = ffn(
        src, x1, ocross, g3, cotangent, w_cross_out, w_in, w_out
    )
    do, o_send, w_send = lax.optimization_barrier((do, o_send, w_send))
    o_came = hop(o_send, xb=1)
    w_came = hop(w_send, z1=1)
    dq0, keep0, send0 = cross_back(
        me, lo, hi, cstart, csize, qc, do, ocross, lse, k, v, kt, scale, 0, 2
    )
    came0 = hop(send0, core=1)
    o_came, w_came, dq0 = lax.optimization_barrier((o_came, w_came, dq0))
    *o_q, w_two = split(o_keep, o_came, w_keep, w_came)
    do1, o_q[1], o_q[2], o_q[3], w_two = lax.optimization_barrier((do, o_q[1], o_q[2], o_q[3], w_two))
    oz, oy, oyz = hop(o_q[1], z1=1), hop(o_q[2], yb=1), hop(o_q[3], yb=1, z1=1)
    w_came = hop(w_two, z2=1)
    dq1, keep1, send1 = cross_back(
        me, lo, hi, cstart, csize, qc, do1, ocross, lse, k, v, kt, scale, 2, 1
    )
    came1 = hop(send1, core=1)
    oz, oy, oyz, w_came, dq1 = lax.optimization_barrier((oz, oy, oyz, w_came, dq1))
    dx1, dy1, dos, dgain2, w_pair, f_keep, f_send = cross_in(
        dq0, dq1, x1, dx2, g2, w_cross_q, w_self_out, o_q[0], oz, oy, oyz, w_two, w_came
    )
    came0, came1, dos = lax.optimization_barrier((came0, came1, dos))
    d_dec_in, small, gathered, enc_own, enc_came, f_all = late(
        sstart, ssize, bucket_table, brow, proj, dos, lse_self, h1, oself, dy1, src, x0, g1, dx1, w_qkv,
        dgain2, dgain3, keep0, came0, keep1, came1, encodings, enc2, w_cross_kv, oc, dyc, h2, dq0, dq1,
        w_pair, f_keep, f_send, scale,
    )
    (
        o_win, o_wout, o_wco, o_wcq, o_wckv, o_wqkv, o_wso, d_encodings, g_self, g_cross, g_ffn, g_rel,
    ) = last(me, small, f_all, gathered, enc_own, enc_came, buckets, heads)
    g_self, g_cross, g_ffn = (g.reshape(-1) for g in (g_self, g_cross, g_ffn))
    return (
        layer_out,
        d_dec_in,
        d_encodings,
        g_self,
        o_wqkv,
        o_wso,
        g_rel,
        g_cross,
        o_wcq,
        o_wckv,
        o_wco,
        g_ffn,
        o_win,
        o_wout,
    )


def solution(mesh):
    rows = P(("grp", "blk"), None)
    fused = mesh.shape["grp"] == 8 and mesh.shape["blk"] == 4
    return jax.shard_map(
        fused_body if fused else body,
        mesh=mesh,
        in_specs=(rows, rows, P(("grp", "blk")), P("grp"), P("grp", None)) + (P(),) * 12 + (rows,),
        out_specs=(rows, rows, rows, P("blk"))
        + (P("blk", None),) * 3
        + (P("blk"),)
        + (P("blk", None),) * 3
        + (P("blk"),)
        + (P("blk", None),) * 2,
        check_vma=False,
    )
```
